32 devices in a mesh: frame: 4 (over y, x), patch: 8 (over z, core).
Axes of the slice: x: 2, y: 2, z: 4, core: 2. Of those that a mesh axis runs over, the one named last changes fastest.
Arguments:
- latents: bfloat16 [4, 16, 512, 1152], P(None, 'frame', 'patch'), may hold values from -6 to 6
- cotangent: bfloat16 [4, 16, 512, 1152], P(None, 'frame', 'patch'), may hold values from -6 to 6
- spatial_weights: bfloat16 [4, 1152, 1152], replicated, may hold values from -0.1875 to 0.1875
- temporal_weights: bfloat16 [4, 1152, 1152], replicated, may hold values from -0.1875 to 0.1875
- modulation: float32 [2, 3, 4, 1152], replicated, may hold values from -5 to 5
- lengths: int32 [4], replicated, may hold values from 1 to 16, 21 in all
- frame_mask: int32 [4, 16], replicated, may hold values 0 or 1
Outputs:
- output: bfloat16 [4, 16, 512, 1152], P(None, 'frame', 'patch')
- grad_latents: bfloat16 [4, 16, 512, 1152], P(None, 'frame', 'patch')
The draws below stay inside these ranges and needn't reach their ends.
Inputs may be any that keep to these rules, and one draw needn't show every extreme that they name: The lengths sum to 21 and the longest is exactly 16.
All inputs are finite; a program needn't handle non-finite values.
Results may differ from the reference program's by a relative error of at most 0.035.
Values may be sent and summed in bfloat16 or wider, within the bound.
No kernel may reach another device: no remote copies, remote signals or barrier semaphores. Data moves between devices by JAX's collectives and lax.ppermute only.
A program may use at most 256 MiB of HBM per device.

```python
import math
import jax
import jax.numpy as jnp
import numpy as np
from jax import lax

HEAD = 72
D = 1152
CLIPS = 4
FRAMES = 16
PATCHES = 512


def place_ends(entries, own_key, low, high):
    shape = entries.shape
    index_at = [jax.random.randint(jax.random.fold_in(own_key, axis), (), 0, shape[axis]) for axis in range(len(shape))]
    entries = entries.at[tuple(index_at)].set(low)
    longest = shape.index(max(shape))
    index_at[longest] = (index_at[longest] + 1) % shape[longest]
    return entries.at[tuple(index_at)].set(high)


def levels(own_key, dims, cuts, low, high):
    def one(axis_at, blocks):
        heights = jax.random.uniform(jax.random.fold_in(jax.random.fold_in(own_key, 6), axis_at), (blocks,), jnp.float32, low / len(cuts), high / len(cuts))
        return jnp.repeat(jnp.exp(heights), dims[axis_at] // blocks).reshape((-1,) + (1,) * (len(dims) - axis_at - 1))

    loudness = one(*cuts[0])
    for cut in cuts[1:]:
        loudness = loudness * one(*cut)
    return loudness


def profile(number_of, total, most, slope):
    loads = [(1 << 20) // math.isqrt(rank ** slope) + 1 for rank in range(2, number_of + 1)]
    spare, given = total - most - (number_of - 1), [1] * (number_of - 1)
    while spare > 0:
        free = [i for i in range(number_of - 1) if given[i] < most]
        whole, remaining = sum([loads[i] for i in free]), spare
        for i in free:
            more = min(most - given[i], max(1, remaining * loads[i] // whole), spare)
            given[i] = given[i] + more
            spare = spare - more
    return np.array([most] + given)


def uneven_parts(own_key, amount, total, most, slope):
    if amount == 2:
        one = jax.random.randint(own_key, (), max(1, total - most), min(most, total - 1) + 1)
        return jnp.stack([one, total - one])
    sizes = jnp.asarray(profile(amount, total, most, slope), jnp.int32)
    pairs = (amount - 1) // 2
    donor, taker = sizes[1:1 + 2 * pairs:2], sizes[2:2 + 2 * pairs:2]
    slack = jnp.minimum(donor - 1, most - taker)
    passed = jax.random.randint(jax.random.fold_in(own_key, 1), (pairs,), 0, 1 << 20) % (slack + 1)
    sizes = sizes.at[1:1 + 2 * pairs:2].set(donor - passed).at[2:2 + 2 * pairs:2].set(taker + passed)
    return sizes[jax.random.permutation(jax.random.fold_in(own_key, 2), amount)]


def noise(own_key, shape, spread, limit, shards=(), held_as=jnp.bfloat16):
    array = jax.random.normal(own_key, shape, jnp.float32) * spread
    if len(shards) > 0:
        array = levels(own_key, shape, shards, -0.22, 0.18) * array
    return jnp.clip(array, min=-limit, max=limit).astype(held_as)


def setup_inputs(seed: int = 0) -> dict:
    keys = jax.random.split(jax.random.key(seed), 8)
    return {
        "latents": noise(keys[0], (CLIPS, FRAMES, PATCHES, D), 1.0, 6.0, ((1, 4), (2, 8))),
        "cotangent": noise(keys[1], (CLIPS, FRAMES, PATCHES, D), 1.0, 6.0, ((1, 4), (2, 8))),
        "spatial_weights": noise(keys[2], (4, D, D), D ** -0.5, 0.1875),
        "temporal_weights": noise(keys[3], (4, D, D), D ** -0.5, 0.1875),
        "modulation": noise(keys[4], (2, 3, CLIPS, D), 1.0, 5.0, (), jnp.float32),
        "lengths": uneven_parts(keys[5], CLIPS, CLIPS * FRAMES // 3, FRAMES, 2).astype(jnp.int32),
        "frame_mask": place_ends((jax.random.randint(keys[6], (CLIPS, FRAMES), 0, 4) < 3).astype(jnp.int32), jax.random.fold_in(keys[6], 1), 0, 1),
    }


def layer_norm_mod(inputs, shift_vec, scale_vec):
    floats = inputs.astype(jnp.float32)
    average = lax.optimization_barrier(jnp.mean(floats, axis=-1, keepdims=True))
    centred = floats - average
    variance = lax.optimization_barrier(jnp.mean(centred * centred, axis=-1, keepdims=True))
    normed = centred * lax.rsqrt(variance + 1e-06)
    return (normed * (1.0 + scale_vec[:, None, None, :]) + shift_vec[:, None, None, :]).astype(jnp.bfloat16)

def project(modulated, weight):
    flattened = modulated.reshape(-1, modulated.shape[-1])
    product = jnp.dot(flattened, weight, preferred_element_type=jnp.float32)
    return product.reshape(modulated.shape[:-1] + (weight.shape[1],))

def front(inputs, weights, shift_vec, scale_vec):
    modulated = layer_norm_mod(inputs, shift_vec, scale_vec)
    return jnp.stack([project(modulated, weights[member]).astype(jnp.bfloat16) for member in range(3)])

def back(inputs, attended, weights, gate_vec):
    mixed_rows = project(attended[0], weights[3])
    return (inputs.astype(jnp.float32) + gate_vec[:, None, None, :] * mixed_rows).astype(jnp.bfloat16)

def attend(queries, key_rows, value_rows, keys_ok):
    count, length, feat_width = queries.shape
    head_count = feat_width // HEAD
    split_shape = (count, length, head_count, HEAD)
    query_heads = queries.reshape(split_shape).astype(jnp.float32)
    key_heads = key_rows.reshape(split_shape).astype(jnp.float32)
    value_heads = value_rows.reshape(split_shape).astype(jnp.float32)
    scores = jnp.einsum('bqhd,bkhd->bhqk', query_heads, key_heads) * HEAD ** (-0.5)
    if keys_ok is not None:
        allowed = keys_ok[:, None, None, :] | jnp.eye(length, dtype=jnp.bool_)[None, None]
        scores = jnp.where(allowed, scores, -1e+30)
    scores = scores - lax.optimization_barrier(jnp.max(scores, axis=-1, keepdims=True))
    exponent = jnp.exp(scores)
    probabilities = (exponent / lax.optimization_barrier(jnp.sum(exponent, axis=-1, keepdims=True))).astype(jnp.bfloat16)
    result = jnp.einsum('bhqk,bkhd->bqhd', probabilities.astype(jnp.float32), value_heads)
    return result.astype(jnp.bfloat16).reshape(count, length, feat_width)

def temporal_core(queries, key_rows, value_rows, validity):
    clip_count, frames, patches, feat_width = queries.shape

    def to_sequences(array_in):
        return jnp.transpose(array_in, (0, 2, 1, 3)).reshape(clip_count * patches, frames, feat_width)
    keys_ok = jnp.broadcast_to(validity[:, None, :], (clip_count, patches, frames)).reshape(-1, frames)
    result = attend(to_sequences(queries), to_sequences(key_rows), to_sequences(value_rows), keys_ok)
    return jnp.transpose(result.reshape(clip_count, patches, frames, feat_width), (0, 2, 1, 3))[None]

def spatial_full(stacked):

    def per_clip(triple):
        return attend(triple[0], triple[1], triple[2], None)
    moved = jnp.transpose(stacked, (1, 0, 2, 3, 4))
    return lax.map(per_clip, moved)[None]

def reference(latents, cotangent, spatial_weights, temporal_weights, modulation, lengths, frame_mask):
    frame_ids = jnp.arange(FRAMES, dtype=jnp.int32)
    validity = (frame_ids[None, :] < lengths[:, None]) & (frame_mask == 1)
    keep_rows = validity[:, :, None, None]

    def forward(inputs):
        stacked = front(inputs, spatial_weights, modulation[0, 0], modulation[0, 1])
        attended = spatial_full(stacked)
        first = back(inputs, attended, spatial_weights, modulation[0, 2])
        stacked_t = front(first, temporal_weights, modulation[1, 0], modulation[1, 1])
        attended_t = temporal_core(stacked_t[0], stacked_t[1], stacked_t[2], validity)
        second = back(first, attended_t, temporal_weights, modulation[1, 2])
        return jnp.where(keep_rows, second, jnp.zeros((), second.dtype))
    output, pullback = jax.vjp(forward, latents)
    grad_latents = pullback(cotangent)[0]
    return (output, grad_latents)
```

```python
import functools
import math

import jax
import jax.numpy as jnp
from jax import lax
from jax.experimental import pallas as pl
from jax.experimental.pallas import tpu as pltpu
from jax.sharding import PartitionSpec as P

HEAD = 72
EXTRAS = 5
SCALE = HEAD ** -0.5
SCALE2 = SCALE * math.log2(math.e)
BF = jnp.bfloat16
F32 = jnp.float32
VMEM_LIMIT = 56 * 1024 * 1024


def nn(a, b):
    return lax.dot_general(a, b, (((1,), (0,)), ((), ())), preferred_element_type=F32)


def nt(a, b):
    return lax.dot_general(a, b, (((1,), (1,)), ((), ())), preferred_element_type=F32)


def tn(a, b):
    return lax.dot_general(a, b, (((0,), (0,)), ((), ())), preferred_element_type=F32)


def window(head):
    start = head * HEAD // 128 * 128
    offset = head * HEAD - start
    return start, offset, 128 if offset + HEAD <= 128 else 256


def lanes_in(width, low, high):
    lane = lax.broadcasted_iota(jnp.int32, (1, width), 1)
    return (lane >= low) & (lane < high)


def masked(x, keep):
    return jnp.where(keep, x, jnp.zeros((), x.dtype))


def take_head(x_ref, rows, head):
    start, offset, width = window(head)
    part = x_ref[rows, start : start + width].astype(F32)
    if offset:
        part = pltpu.roll(part, width - offset, 1)
    return masked(part[:, :128], lanes_in(128, 0, HEAD))


def put_head(value, head):
    start, offset, width = window(head)
    if width == 256:
        value = jnp.concatenate([value, jnp.zeros_like(value)], axis=1)
    if offset:
        value = pltpu.roll(value, offset, 1)
    return start, width, value


def wide(value):
    return jnp.concatenate([value, jnp.zeros_like(value)], axis=1)


def pack3(parts):
    first, second, third = parts
    return wide(first) + pltpu.roll(wide(second), HEAD, 1) + pltpu.roll(wide(third), 2 * HEAD, 1)


def unpack3(packed, member):
    if member:
        packed = pltpu.roll(packed, 256 - member * HEAD, 1)
    return masked(packed[:, :128], lanes_in(128, 0, HEAD))


def row_vec(vec_ref, member, row):
    at = row // 8
    wide_d = vec_ref.shape[-1]
    low = jnp.broadcast_to(vec_ref[member, pl.ds(at, 1), :], (8, wide_d))
    high = jnp.broadcast_to(vec_ref[member, pl.ds(at + 1, 1), :], (8, wide_d))
    return jnp.concatenate([low, high], axis=0)


def normed_of(x):
    average = jnp.mean(x, axis=-1, keepdims=True)
    centred = x - average
    variance = jnp.mean(centred * centred, axis=-1, keepdims=True)
    inverse = lax.rsqrt(variance + 1e-06)
    return centred * inverse, inverse


def over_rows(count, body):
    def step(i, carry):
        body(pl.multiple_of(i * 16, 16))
        return carry

    lax.fori_loop(0, count // 16, step, 0)


def modulate(dest_ref, base, x_ref, vec_ref):
    def body(row):
        normed, _ = normed_of(x_ref[pl.ds(row, 16), :].astype(F32))
        out = normed * (1.0 + row_vec(vec_ref, 1, base + row)) + row_vec(vec_ref, 0, base + row)
        dest_ref[pl.ds(base + row, 16), :] = out.astype(BF)

    over_rows(x_ref.shape[0], body)


def norm_back(out_ref, x_ref, grad_ref, dmod_ref, base, vec_ref):
    def body(row):
        normed, inverse = normed_of(x_ref[pl.ds(row, 16), :].astype(F32))
        dnormed = dmod_ref[pl.ds(base + row, 16), :] * (1.0 + row_vec(vec_ref, 1, base + row))
        mean_d = jnp.mean(dnormed, axis=-1, keepdims=True)
        mean_dn = jnp.mean(dnormed * normed, axis=-1, keepdims=True)
        dx = (inverse * (dnormed - mean_d - normed * mean_dn)).astype(BF)
        out_ref[pl.ds(row, 16), :] = (dx.astype(F32) + grad_ref[pl.ds(row, 16), :].astype(F32)).astype(BF)

    over_rows(x_ref.shape[0], body)


def col_tiles(width):
    whole, tiles = 512, []
    start = 0
    while start < width:
        tiles.append((start, min(whole, width - start)))
        start += whole
    return tiles


def times(dest_ref, x_ref, w_ref, member, transposed=False, add=False):
    for start, size in col_tiles(w_ref.shape[-1]):
        cols = pl.ds(start, size)
        if transposed:
            product = nt(x_ref[...], w_ref[member, cols, :])
        else:
            product = nn(x_ref[...], w_ref[member, :, cols])
        if add:
            product = dest_ref[:, cols] + product
        dest_ref[:, cols] = product.astype(dest_ref.dtype)


def heads_forward(o_ref, q_ref, k_ref, v_ref, rows, keys, bias, heads):
    for head in range(heads):
        start, offset, width = window(head)
        cols = slice(start, start + width)
        keep = lanes_in(width, offset, offset + HEAD)
        scores = nt(masked(q_ref[rows, cols], keep), k_ref[keys, cols])
        if bias is not None:
            scores = scores + bias
        exponent = jnp.exp2((scores - jnp.max(scores, axis=-1, keepdims=True)) * SCALE2)
        total = jnp.sum(exponent, axis=-1, keepdims=True)
        result = nn(exponent.astype(BF), masked(v_ref[keys, cols], keep)) * (1.0 / total)
        o_ref[rows, cols] = o_ref[rows, cols] + result


def softmax_grads(q, do, k, v, bias):
    scores = nt(k, q)
    if bias is not None:
        scores = scores + bias
    exponent = jnp.exp2((scores - jnp.max(scores, axis=0, keepdims=True)) * SCALE2)
    prob = exponent * (1.0 / jnp.sum(exponent, axis=0, keepdims=True))
    dprob = nt(v, do)
    delta = jnp.sum(prob * dprob, axis=0, keepdims=True)
    dscores = prob * (dprob - delta) * SCALE
    return dscores.astype(BF), prob.astype(BF)


def heads_backward(dq_ref, dk_ref, dv_ref, q_ref, k_ref, v_ref, do_ref, rows, keys, bias, heads):
    for head in range(heads):
        start, offset, width = window(head)
        cols = slice(start, start + width)
        keep = lanes_in(width, offset, offset + HEAD)
        q = masked(q_ref[rows, cols], keep)
        do = masked(do_ref[rows, cols], keep)
        k = masked(k_ref[keys, cols], keep)
        dscores, prob = softmax_grads(q, do, k, v_ref[keys, cols], bias)
        dv_ref[keys, cols] = dv_ref[keys, cols] + nn(prob, do)
        dk_ref[keys, cols] = dk_ref[keys, cols] + nn(dscores, q)
        dq_ref[rows, cols] = dq_ref[rows, cols] + tn(dscores, k)


def front_kernel(xm_ref, xe_ref, vec_ref, w_ref, qkv_ref, pack_ref, mod_ref, ext_ref):
    member = pl.program_id(0)
    main = xm_ref.shape[0]
    heads = pack_ref.shape[0]

    @pl.when(member == 0)
    def _():
        modulate(mod_ref, 0, xm_ref, vec_ref)
        modulate(mod_ref, main, xe_ref, vec_ref)

    for start, size in col_tiles(w_ref.shape[-1]):
        cols = pl.ds(start, size)
        product = nn(mod_ref[...], w_ref[0, :, cols])
        qkv_ref[0, :, cols] = product[:main].astype(BF)
        ext_ref[member, :, cols] = product[main:]

    @pl.when(member == 2)
    def _():
        for head in range(heads):
            parts = [take_head(ext_ref.at[i], slice(None), head) for i in range(3)]
            pack_ref[head] = pack3(parts).astype(BF)


def attend_kernel(qkv_ref, other_ref, o_ref, k_ref, v_ref, acc_ref, *, heads):
    rows = qkv_ref.shape[1]
    k_ref[:rows] = qkv_ref[1]
    v_ref[:rows] = qkv_ref[2]
    for i in range(other_ref.shape[0]):
        k_ref[(i + 1) * rows : (i + 2) * rows] = other_ref[i, 0]
        v_ref[(i + 1) * rows : (i + 2) * rows] = other_ref[i, 1]
    acc_ref[...] = jnp.zeros_like(acc_ref)
    heads_forward(acc_ref, qkv_ref.at[0], k_ref, v_ref, slice(None), slice(None), None, heads)
    o_ref[...] = acc_ref[...].astype(BF)


def extra_rows(ref, index):
    part = ref[:, index]
    return part.reshape(part.shape[0] * part.shape[1], part.shape[2])


def extra_attend_kernel(pack_ref, o_ref):
    for index in range(pack_ref.shape[1]):
        packed = extra_rows(pack_ref, index).astype(F32)
        q, k, v = [unpack3(packed, i).astype(BF) for i in range(3)]
        scores = nt(q, k)
        exponent = jnp.exp2((scores - jnp.max(scores, axis=-1, keepdims=True)) * SCALE2)
        total = jnp.sum(exponent, axis=-1, keepdims=True)
        result = nn(exponent.astype(BF), v) * (1.0 / total)
        o_ref[:, index] = result.astype(BF).reshape(o_ref.shape[0], o_ref.shape[2], 128)


def extra_attend_back_kernel(pack_ref, do_ref, grad_ref):
    for index in range(pack_ref.shape[1]):
        packed = extra_rows(pack_ref, index).astype(F32)
        q, k, v = [unpack3(packed, i).astype(BF) for i in range(3)]
        do = extra_rows(do_ref, index)
        dscores, prob = softmax_grads(q, do, k, v, None)
        out = pack3([tn(dscores, k), nn(dscores, q), nn(prob, do)]).astype(BF)
        grad_ref[:, index] = out.reshape(grad_ref.shape[0], grad_ref.shape[2], 256)


def back_kernel(xm_ref, xe_ref, om_ref, oe_ref, vec_ref, w_ref, fm_ref, fe_ref, o_ref, acc_ref):
    main, heads = xm_ref.shape[0], oe_ref.shape[0]
    o_ref[:main] = om_ref[...]
    acc_ref[main:] = jnp.zeros_like(acc_ref[main:])
    for head in range(heads):
        start, width, value = put_head(oe_ref[head].astype(F32), head)
        acc_ref[main:, start : start + width] = acc_ref[main:, start : start + width] + value
    o_ref[main:] = acc_ref[main:].astype(BF)
    times(acc_ref, o_ref, w_ref, 0)
    residual(fm_ref, xm_ref, acc_ref, 0, vec_ref)
    residual(fe_ref, xe_ref, acc_ref, main, vec_ref)


def residual(out_ref, x_ref, mixed_ref, base, vec_ref):
    def body(row):
        gated = row_vec(vec_ref, 2, base + row) * mixed_ref[pl.ds(base + row, 16), :]
        out_ref[pl.ds(row, 16), :] = (x_ref[pl.ds(row, 16), :].astype(F32) + gated).astype(BF)

    over_rows(x_ref.shape[0], body)


def gate_grad(dest_ref, grad_ref, base, vec_ref):
    def body(row):
        gated = row_vec(vec_ref, 2, base + row) * grad_ref[pl.ds(row, 16), :].astype(F32)
        dest_ref[pl.ds(base + row, 16), :] = gated.astype(BF)

    over_rows(grad_ref.shape[0], body)


def back_grad_kernel(gm_ref, ge_ref, vec_ref, w_ref, dom_ref, pack_ref, dmix_ref, do_ref):
    main, heads = gm_ref.shape[0], pack_ref.shape[0]
    gate_grad(dmix_ref, gm_ref, 0, vec_ref)
    gate_grad(dmix_ref, ge_ref, main, vec_ref)
    times(do_ref, dmix_ref, w_ref, 0, transposed=True)
    dom_ref[...] = do_ref[:main].astype(BF)
    for head in range(heads):
        pack_ref[head] = take_head(do_ref, slice(main, None), head).astype(BF)


def attend_back_kernel(
    qkv_ref, other_ref, do_ref, own_ref, sent_ref, k_ref, v_ref, dq_ref, dk_ref, dv_ref, *, heads
):
    rows = qkv_ref.shape[1]
    k_ref[:rows] = qkv_ref[1]
    v_ref[:rows] = qkv_ref[2]
    for i in range(other_ref.shape[0]):
        k_ref[(i + 1) * rows : (i + 2) * rows] = other_ref[i, 0]
        v_ref[(i + 1) * rows : (i + 2) * rows] = other_ref[i, 1]
    for ref in (dq_ref, dk_ref, dv_ref):
        ref[...] = jnp.zeros_like(ref)
    everything = slice(None)
    heads_backward(
        dq_ref, dk_ref, dv_ref, qkv_ref.at[0], k_ref, v_ref, do_ref, everything, everything, None, heads
    )
    own_ref[0] = dq_ref[...].astype(BF)
    own_ref[1] = dk_ref[:rows].astype(BF)
    own_ref[2] = dv_ref[:rows].astype(BF)
    for i in range(other_ref.shape[0]):
        sent_ref[i, 0] = dk_ref[(i + 1) * rows : (i + 2) * rows].astype(BF)
        sent_ref[i, 1] = dv_ref[(i + 1) * rows : (i + 2) * rows].astype(BF)


def front_grad_kernel(
    own_ref, got_ref, dpack_ref, xm_ref, xe_ref, gm_ref, ge_ref, vec_ref, w_ref,
    outm_ref, oute_ref, d_ref, acc_ref, ext_ref,
):
    member = pl.program_id(0)
    main, heads = xm_ref.shape[0], dpack_ref.shape[0]

    @pl.when(member == 0)
    def _():
        acc_ref[...] = jnp.zeros_like(acc_ref)
        ext_ref[...] = jnp.zeros_like(ext_ref)
        d_ref[0, :main] = own_ref[0]
        for i in range(2):
            total = own_ref[1 + i].astype(F32)
            for j in range(got_ref.shape[0]):
                total = total + got_ref[j, i].astype(F32)
            d_ref[1 + i, :main] = total.astype(BF)
        for head in range(heads):
            packed = dpack_ref[head].astype(F32)
            for i in range(3):
                start, width, value = put_head(unpack3(packed, i), head)
                cols = slice(start, start + width)
                ext_ref[i, :, cols] = ext_ref[i, :, cols] + value
        for i in range(3):
            d_ref[i, main:] = ext_ref[i].astype(BF)

    for start, size in col_tiles(w_ref.shape[-1]):
        cols = pl.ds(start, size)
        acc_ref[:, cols] = acc_ref[:, cols] + nt(d_ref[member], w_ref[0, cols, :])

    @pl.when(member == 2)
    def _():
        norm_back(outm_ref, xm_ref, gm_ref, acc_ref, 0, vec_ref)
        norm_back(oute_ref, xe_ref, ge_ref, acc_ref, main, vec_ref)


def temporal_kernel(
    xm_ref, xe_ref, cm_ref, ce_ref, vec_ref, w_ref, biasm_ref, biase_ref,
    outm_ref, oute_ref, gm_ref, ge_ref,
    low_ref, q_ref, k_ref, v_ref, acc_ref, dq_ref, dk_ref, dv_ref, *, heads,
):
    main = xm_ref.shape[0]
    parts = ((slice(0, main), biasm_ref), (slice(main, None), biase_ref))
    modulate(low_ref, 0, xm_ref, vec_ref)
    modulate(low_ref, main, xe_ref, vec_ref)
    for i, ref in enumerate((q_ref, k_ref, v_ref)):
        times(ref, low_ref, w_ref, i)
    acc_ref[...] = jnp.zeros_like(acc_ref)
    for rows, bias in parts:
        heads_forward(acc_ref, q_ref, k_ref, v_ref, rows, rows, bias[...], heads)
    low_ref[...] = acc_ref[...].astype(BF)
    times(acc_ref, low_ref, w_ref, 3)
    residual(outm_ref, xm_ref, acc_ref, 0, vec_ref)
    residual(oute_ref, xe_ref, acc_ref, main, vec_ref)

    gate_grad(low_ref, cm_ref, 0, vec_ref)
    gate_grad(low_ref, ce_ref, main, vec_ref)
    times(acc_ref, low_ref, w_ref, 3, transposed=True)
    low_ref[...] = acc_ref[...].astype(BF)
    for ref in (dq_ref, dk_ref, dv_ref):
        ref[...] = jnp.zeros_like(ref)
    for rows, bias in parts:
        heads_backward(
            dq_ref, dk_ref, dv_ref, q_ref, k_ref, v_ref, low_ref, rows, rows, bias[...].T, heads
        )
    for i, ref in enumerate((dq_ref, dk_ref, dv_ref)):
        low_ref[...] = ref[...].astype(BF)
        times(acc_ref, low_ref, w_ref, i, transposed=True, add=i > 0)
    norm_back(gm_ref, xm_ref, cm_ref, acc_ref, 0, vec_ref)
    norm_back(ge_ref, xe_ref, ce_ref, acc_ref, main, vec_ref)


def place_kernel(table_ref, main_ref, extra_ref, out_ref):
    kind = table_ref[2, pl.program_id(0)]
    zero = jnp.zeros_like(out_ref)
    out_ref[...] = jnp.where(kind == 1, main_ref[...], jnp.where(kind == 2, extra_ref[...], zero))


def params(steps=0):
    semantics = {"dimension_semantics": ("arbitrary",) * steps} if steps else {}
    return pltpu.CompilerParams(vmem_limit_bytes=VMEM_LIMIT, **semantics)


def whole(array):
    return pl.BlockSpec(array.shape, lambda *_: (0,) * array.ndim)


def shape(*dims, dtype=BF):
    return jax.ShapeDtypeStruct(dims, dtype)


def front(xm, xe, vec, weights, heads):
    main, width = xm.shape
    extra = xe.shape[0]
    return pl.pallas_call(
        front_kernel,
        grid=(3,),
        in_specs=[
            whole(xm), whole(xe), whole(vec),
            pl.BlockSpec((1, width, width), lambda i: (i, 0, 0)),
        ],
        out_specs=[
            pl.BlockSpec((1, main, width), lambda i: (i, 0, 0)),
            pl.BlockSpec((heads, extra, 256), lambda i: (0, 0, 0)),
        ],
        out_shape=[shape(3, main, width), shape(heads, extra, 256)],
        scratch_shapes=[
            pltpu.VMEM((main + extra, width), BF),
            pltpu.VMEM((3, extra, width), F32),
        ],
        compiler_params=params(1),
    )(xm, xe, vec, weights)


def attend(qkv, other, heads):
    _, rows, width = qkv.shape
    keys = rows * (other.shape[0] + 1)
    return pl.pallas_call(
        functools.partial(attend_kernel, heads=heads),
        out_shape=shape(rows, width),
        scratch_shapes=[
            pltpu.VMEM((keys, width), BF),
            pltpu.VMEM((keys, width), BF),
            pltpu.VMEM((rows, width), F32),
        ],
        compiler_params=params(),
    )(qkv, other)


def extra_attend(pack):
    return pl.pallas_call(
        extra_attend_kernel, out_shape=shape(*pack.shape[:-1], 128), compiler_params=params()
    )(pack)


def extra_attend_back(pack, do):
    return pl.pallas_call(
        extra_attend_back_kernel, out_shape=shape(*pack.shape), compiler_params=params()
    )(pack, do)


def back(xm, xe, om, oe, vec, weights):
    main, width = xm.shape
    extra = xe.shape[0]
    return pl.pallas_call(
        back_kernel,
        grid=(1,),
        in_specs=[
            whole(xm), whole(xe), whole(om), whole(oe), whole(vec),
            pl.BlockSpec((1, width, width), lambda i: (3, 0, 0)),
        ],
        out_specs=[whole(xm), whole(xe)],
        out_shape=[shape(main, width), shape(extra, width)],
        scratch_shapes=[
            pltpu.VMEM((main + extra, width), BF),
            pltpu.VMEM((main + extra, width), F32),
        ],
        compiler_params=params(1),
    )(xm, xe, om, oe, vec, weights)


def back_grad(gm, ge, vec, weights, heads):
    main, width = gm.shape
    extra = ge.shape[0]
    return pl.pallas_call(
        back_grad_kernel,
        grid=(1,),
        in_specs=[
            whole(gm), whole(ge), whole(vec),
            pl.BlockSpec((1, width, width), lambda i: (3, 0, 0)),
        ],
        out_specs=[
            whole(gm),
            pl.BlockSpec((heads, extra, 128), lambda i: (0, 0, 0)),
        ],
        out_shape=[shape(main, width), shape(heads, extra, 128)],
        scratch_shapes=[
            pltpu.VMEM((main + extra, width), BF),
            pltpu.VMEM((main + extra, width), F32),
        ],
        compiler_params=params(1),
    )(gm, ge, vec, weights)


def attend_back(qkv, other, do, heads):
    _, rows, width = qkv.shape
    keys = rows * (other.shape[0] + 1)
    return pl.pallas_call(
        functools.partial(attend_back_kernel, heads=heads),
        out_shape=[shape(3, rows, width), shape(*other.shape)],
        scratch_shapes=[
            pltpu.VMEM((keys, width), BF),
            pltpu.VMEM((keys, width), BF),
            pltpu.VMEM((rows, width), F32),
            pltpu.VMEM((keys, width), F32),
            pltpu.VMEM((keys, width), F32),
        ],
        compiler_params=params(),
    )(qkv, other, do)


def front_grad(own, got, dpack, xm, xe, gm, ge, vec, weights):
    main, width = xm.shape
    extra = xe.shape[0]
    operands = (own, got, dpack, xm, xe, gm, ge, vec)
    return pl.pallas_call(
        front_grad_kernel,
        grid=(3,),
        in_specs=[whole(a) for a in operands]
        + [pl.BlockSpec((1, width, width), lambda i: (i, 0, 0))],
        out_specs=[whole(xm), whole(xe)],
        out_shape=[shape(main, width), shape(extra, width)],
        scratch_shapes=[
            pltpu.VMEM((3, main + extra, width), BF),
            pltpu.VMEM((main + extra, width), F32),
            pltpu.VMEM((3, extra, width), F32),
        ],
        compiler_params=params(1),
    )(*operands, weights)


def temporal(xm, xe, cm, ce, vec, weights, bias_m, bias_e, heads):
    main, width = xm.shape
    extra = xe.shape[0]
    rows = main + extra
    return pl.pallas_call(
        functools.partial(temporal_kernel, heads=heads),
        out_shape=[shape(main, width), shape(extra, width)] * 2,
        scratch_shapes=[pltpu.VMEM((rows, width), BF)] * 4 + [pltpu.VMEM((rows, width), F32)] * 4,
        compiler_params=params(),
    )(xm, xe, cm, ce, vec, weights, bias_m, bias_e)


def place(table, main, extra):
    slots = table.shape[1]
    patches, width = main.shape[1:]
    block = (1, patches, width)
    return pl.pallas_call(
        place_kernel,
        grid_spec=pltpu.PrefetchScalarGridSpec(
            num_scalar_prefetch=1,
            grid=(slots,),
            in_specs=[
                pl.BlockSpec(block, lambda i, t: (t[0, i], 0, 0)),
                pl.BlockSpec(block, lambda i, t: (t[1, i], 0, 0)),
            ],
            out_specs=pl.BlockSpec(block, lambda i, t: (i, 0, 0)),
        ),
        out_shape=shape(slots, patches, width),
        compiler_params=params(1),
    )(table, main, extra)


def local(latents, cotangent, spatial_weights, temporal_weights, modulation, lengths, frame_mask):
    clips, frame_dev, patch_dev, width = latents.shape
    heads = width // HEAD
    frame_axis, patch_axis = lax.axis_size("frame"), lax.axis_size("patch")
    everyone = ("frame", "patch")
    frames = frame_dev * frame_axis
    sharers = patch_axis // frame_dev
    sub = patch_dev // sharers
    small = sub // frame_axis
    patch_t = patch_dev // frame_axis
    heads_col = heads // frame_axis
    groups = patch_axis // heads_col
    group_extras = -(-EXTRAS // groups)
    extras = groups * group_extras

    def swap(x, axis):
        return lax.all_to_all(x, axis, split_axis=0, concat_axis=0, tiled=True)

    frame_ids = jnp.arange(frames, dtype=jnp.int32)
    validity = (frame_ids[None, :] < lengths[:, None]) & (frame_mask == 1)
    long = jnp.argmax(lengths).astype(jnp.int32)
    used = (frame_ids[None, :] < lengths[:, None]) & (jnp.arange(clips)[:, None] != long)
    used = used.reshape(-1)
    rank = jnp.cumsum(used.astype(jnp.int32)) - 1
    hit = used[None] & (rank[None] == jnp.arange(EXTRAS, dtype=jnp.int32)[:, None])
    slot = jnp.sum(jnp.where(hit, jnp.arange(clips * frames, dtype=jnp.int32)[None], 0), axis=1)
    extra_clip, extra_frame = slot // frames, slot % frames
    extra_valid = jnp.any(hit & validity.reshape(-1)[None], axis=1)
    extra_col = extra_frame // frame_dev
    long_valid = lax.dynamic_index_in_dim(validity, long, 0, keepdims=False)
    column = lax.axis_index("frame")

    def padded(array, value):
        return jnp.concatenate([array, jnp.full((extras - EXTRAS,), value, array.dtype)])

    main_rows = frame_dev * patch_dev
    clip_rows = jnp.concatenate(
        [jnp.full((main_rows // 8,), long), jnp.repeat(padded(extra_clip, 0), patch_t // 8)]
    )
    vec_s, vec_t = jnp.take(modulation[0], clip_rows, axis=1), jnp.take(modulation[1], clip_rows, axis=1)

    def bias_of(count, keys_ok, same):
        token = jnp.arange(count * patch_t, dtype=jnp.int32)
        patch, item = token % patch_t, token // patch_t
        own = token[:, None] == token[None, :]
        pair = (patch[:, None] == patch[None, :]) & same(item)
        return jnp.where(pair & (keys_ok[item][None, :] | own), 0.0, -1e30).astype(F32)

    all_clip = padded(extra_clip, -1)
    bias_m = bias_of(frames, long_valid, lambda item: True)
    bias_e = bias_of(
        extras, padded(extra_valid, False), lambda item: all_clip[item][:, None] == all_clip[item][None, :]
    )

    def pick(array, e):
        return lax.dynamic_slice(
            array, (extra_clip[e], extra_frame[e] % frame_dev, 0, 0), (1, 1, patch_dev, width)
        )[0, 0]

    def split_home(x):
        x = x.reshape(x.shape[0], sharers, frame_axis, small, width)
        return jnp.transpose(x, (2, 0, 1, 3, 4)).reshape(frame_axis, x.shape[0], patch_t, width)

    def join_home(x):
        items = x.shape[1]
        x = x.reshape(frame_axis, items, sharers, small, width)
        return jnp.transpose(x, (1, 2, 0, 3, 4)).reshape(items, patch_dev, width)

    def extras_in(received):
        rows = [lax.dynamic_index_in_dim(received[:, e], extra_col[e], 0, keepdims=False) for e in range(EXTRAS)]
        rows += [jnp.zeros_like(rows[0])] * (extras - EXTRAS)
        return jnp.concatenate(rows)

    main_home = lax.dynamic_index_in_dim(latents, long, 0, keepdims=False)
    main_s = swap(main_home.reshape(patch_axis, sub, width), "patch").reshape(main_rows, width)
    extra_home = jnp.stack([pick(latents, e) for e in range(EXTRAS)])
    extra_t = extras_in(swap(split_home(extra_home), "frame"))
    cot_main = lax.dynamic_index_in_dim(cotangent, long, 0, keepdims=False)
    cot_home = jnp.concatenate([cot_main, jnp.stack([pick(cotangent, e) for e in range(EXTRAS)])])
    cot_got = swap(split_home(cot_home), "frame")
    cot_m = jnp.where(
        long_valid[:, None, None], cot_got[:, :frame_dev].reshape(frames, patch_t, width), jnp.zeros((), BF)
    ).reshape(frames * patch_t, width)
    cot_e = extras_in(jnp.where(extra_valid[None, :, None, None], cot_got[:, frame_dev:], jnp.zeros((), BF)))

    def rotate(array, by):
        perm = []
        for p in range(patch_axis):
            base = p // sharers * sharers
            perm.append((p, base + (p - base + by) % sharers))
        return lax.ppermute(array, "patch", perm)

    qkv, pack = front(main_s, extra_t, vec_s, spatial_weights, heads)
    chunk = group_extras * patch_t
    pack_got = swap(pack.reshape(frame_axis * patch_axis, chunk, 256), everyone)
    pack_got = pack_got.reshape(frame_axis * patch_axis, group_extras, patch_t, 256)
    other = jnp.stack([rotate(qkv[1:], by) for by in range(1, sharers)])
    attended = attend(qkv, other, heads)
    extra_o = extra_attend(pack_got)
    extra_o = swap(extra_o.reshape(frame_axis * patch_axis, chunk, 128), everyone)
    extra_o = extra_o.reshape(heads, extras * patch_t, 128)
    first_m, first_e = back(main_s, extra_t, attended, extra_o, vec_s, spatial_weights)

    def to_temporal(x):
        x = x.reshape(patch_axis, frame_axis, small, width)
        x = jnp.transpose(x, (1, 0, 2, 3)).reshape(frame_axis * patch_axis, small, width)
        return swap(x, everyone).reshape(frames * patch_t, width)

    def to_spatial(x):
        x = swap(x.reshape(frame_axis * patch_axis, small, width), everyone)
        x = jnp.transpose(x.reshape(frame_axis, patch_axis, small, width), (1, 0, 2, 3))
        return x.reshape(main_rows, width)

    out_m, out_e, grad_m, grad_e = temporal(
        to_temporal(first_m), first_e, cot_m, cot_e, vec_t, temporal_weights, bias_m, bias_e, heads
    )

    def extras_home(x):
        x = x.reshape(extras, patch_t, width)[:EXTRAS]
        return jnp.broadcast_to(x[None], (frame_axis,) + x.shape)

    out_sent = jnp.concatenate(
        [out_m.reshape(frame_axis, frame_dev, patch_t, width), extras_home(out_e)], axis=1
    )
    out_home = join_home(swap(out_sent, "frame"))

    grad_s = to_spatial(grad_m)
    do_main, do_pack = back_grad(grad_s, grad_e, vec_s, spatial_weights, heads)
    do_got = swap(do_pack.reshape(frame_axis * patch_axis, chunk, 128), everyone)
    do_got = do_got.reshape(frame_axis * patch_axis, group_extras, patch_t, 128)
    own, sent = attend_back(qkv, other, do_main, heads)
    got = jnp.stack([rotate(sent[by - 1], -by) for by in range(1, sharers)])
    dpack = extra_attend_back(pack_got, do_got)
    dpack = swap(dpack.reshape(frame_axis * patch_axis, chunk, 256), everyone)
    dpack = dpack.reshape(heads, extras * patch_t, 256)
    lat_m, lat_e = front_grad(own, got, dpack, main_s, extra_t, grad_s, grad_e, vec_s, spatial_weights)
    lat_main = swap(lat_m.reshape(patch_axis, sub, width), "patch").reshape(frame_dev, patch_dev, width)
    lat_extra = join_home(swap(extras_home(lat_e), "frame"))

    slot_clip = jnp.repeat(jnp.arange(clips, dtype=jnp.int32), frame_dev)
    slot_local = jnp.tile(jnp.arange(frame_dev, dtype=jnp.int32), clips)
    slot_frame = column * frame_dev + slot_local
    slot_valid = validity[slot_clip, slot_frame]
    match = (extra_clip[None] == slot_clip[:, None]) & (extra_frame[None] == slot_frame[:, None])
    extra_at = jnp.sum(jnp.where(match, jnp.arange(EXTRAS, dtype=jnp.int32)[None], 0), axis=1)
    kind = jnp.where(slot_valid, jnp.where(slot_clip == long, 1, 2), 0)
    table = jnp.stack([slot_local, extra_at, kind]).astype(jnp.int32)
    output = place(table, out_home[:frame_dev], out_home[frame_dev:])
    grad = place(table, lat_main, lat_extra)
    return output.reshape(latents.shape), grad.reshape(latents.shape)


def solution(mesh):
    tokens = P(None, "frame", "patch", None)
    in_specs = (tokens, tokens, P(), P(), P(), P(), P())
    return jax.shard_map(local, mesh=mesh, in_specs=in_specs, out_specs=(tokens, tokens), check_vma=False)
```

```python
import functools
import math

import jax
import jax.numpy as jnp
from jax import lax
from jax.experimental import pallas as pl
from jax.experimental.pallas import tpu as pltpu
from jax.sharding import PartitionSpec as P

HEAD = 72
EXTRAS = 5
SCALE = HEAD ** -0.5
SCALE2 = SCALE * math.log2(math.e)
BF = jnp.bfloat16
F32 = jnp.float32
VMEM_LIMIT = 56 * 1024 * 1024
LONG, CLIP, FRAME, VALID, LONG_VALID, KIND, EXTRA_AT, TABLE = 0, 8, 16, 24, 32, 48, 64, 80


def nn(a, b):
    return lax.dot_general(a, b, (((1,), (0,)), ((), ())), preferred_element_type=F32)


def nt(a, b):
    return lax.dot_general(a, b, (((1,), (1,)), ((), ())), preferred_element_type=F32)


def tn(a, b):
    return lax.dot_general(a, b, (((0,), (0,)), ((), ())), preferred_element_type=F32)


def window(head):
    start = head * HEAD // 128 * 128
    offset = head * HEAD - start
    return start, offset, 128 if offset + HEAD <= 128 else 256


def lanes_in(width, low, high):
    lane = lax.broadcasted_iota(jnp.int32, (1, width), 1)
    return (lane >= low) & (lane < high)


def masked(x, keep):
    return jnp.where(keep, x, jnp.zeros((), x.dtype))


def take_head(x_ref, rows, head):
    start, offset, width = window(head)
    part = x_ref[rows, start : start + width].astype(F32)
    if offset:
        part = pltpu.roll(part, width - offset, 1)
    return masked(part[:, :128], lanes_in(128, 0, HEAD))


def put_head(value, head):
    start, offset, width = window(head)
    if width == 256:
        value = jnp.concatenate([value, jnp.zeros_like(value)], axis=1)
    if offset:
        value = pltpu.roll(value, offset, 1)
    return start, width, value


def wide(value):
    return jnp.concatenate([value, jnp.zeros_like(value)], axis=1)


def pack3(parts):
    first, second, third = parts
    return wide(first) + pltpu.roll(wide(second), HEAD, 1) + pltpu.roll(wide(third), 2 * HEAD, 1)


def unpack3(packed, member):
    if member:
        packed = pltpu.roll(packed, 256 - member * HEAD, 1)
    return masked(packed[:, :128], lanes_in(128, 0, HEAD))


def main_vec(meta_ref, mod_ref, block, member):
    return mod_ref[block, member, pl.ds(meta_ref[LONG], 1), :]


def extra_vec(meta_ref, mod_ref, block, member, extras, patches):
    rows = [mod_ref[block, member, pl.ds(meta_ref[CLIP + e], 1), :] for e in range(extras)]
    return jnp.concatenate([jnp.broadcast_to(r, (patches, r.shape[1])) for r in rows], axis=0)


def normed_of(x):
    average = jnp.mean(x, axis=-1, keepdims=True)
    centred = x - average
    variance = jnp.mean(centred * centred, axis=-1, keepdims=True)
    inverse = lax.rsqrt(variance + 1e-06)
    return centred * inverse, inverse


def over_rows(count, body):
    size = math.gcd(count, 64)
    if count == size:
        body(slice(0, count))
        return

    def step(i, carry):
        body(pl.ds(pl.multiple_of(i * size, size), size))
        return carry

    lax.fori_loop(0, count // size, step, 0)


def modulate(x, shift, scale):
    normed, _ = normed_of(x.astype(F32))
    return (normed * (1.0 + scale) + shift).astype(BF)


def norm_back(x, grad, dmod, scale):
    normed, inverse = normed_of(x.astype(F32))
    dnormed = dmod * (1.0 + scale)
    mean_d = jnp.mean(dnormed, axis=-1, keepdims=True)
    mean_dn = jnp.mean(dnormed * normed, axis=-1, keepdims=True)
    dx = (inverse * (dnormed - mean_d - normed * mean_dn)).astype(BF)
    return (dx.astype(F32) + grad.astype(F32)).astype(BF)


def gated(x, gate, mixed):
    return (x.astype(F32) + gate * mixed).astype(BF)


def col_tiles(width):
    whole, tiles = 512, []
    start = 0
    while start < width:
        tiles.append((start, min(whole, width - start)))
        start += whole
    return tiles


def times(dest_ref, x_ref, w_ref, member, transposed=False, add=False):
    for start, size in col_tiles(w_ref.shape[-1]):
        cols = pl.ds(start, size)
        if transposed:
            product = nt(x_ref[...], w_ref[member, cols, :])
        else:
            product = nn(x_ref[...], w_ref[member, :, cols])
        if add:
            product = dest_ref[:, cols] + product
        dest_ref[:, cols] = product.astype(dest_ref.dtype)


def heads_forward(o_ref, q_ref, k_ref, v_ref, rows, keys, bias, heads):
    for head in range(heads):
        start, offset, width = window(head)
        cols = slice(start, start + width)
        keep = lanes_in(width, offset, offset + HEAD)
        scores = nt(masked(q_ref[rows, cols], keep), k_ref[keys, cols])
        if bias is not None:
            scores = scores + bias
        exponent = jnp.exp2((scores - jnp.max(scores, axis=-1, keepdims=True)) * SCALE2)
        total = jnp.sum(exponent, axis=-1, keepdims=True)
        result = nn(exponent.astype(BF), masked(v_ref[keys, cols], keep)) * (1.0 / total)
        o_ref[rows, cols] = o_ref[rows, cols] + result


def softmax_grads(q, do, k, v, bias):
    scores = nt(k, q)
    if bias is not None:
        scores = scores + bias
    exponent = jnp.exp2((scores - jnp.max(scores, axis=0, keepdims=True)) * SCALE2)
    prob = exponent * (1.0 / jnp.sum(exponent, axis=0, keepdims=True))
    dprob = nt(v, do)
    delta = jnp.sum(prob * dprob, axis=0, keepdims=True)
    dscores = prob * (dprob - delta) * SCALE
    return dscores.astype(BF), prob.astype(BF)


def heads_backward(dq_ref, dk_ref, dv_ref, q_ref, k_ref, v_ref, do_ref, rows, keys, bias, heads):
    for head in range(heads):
        start, offset, width = window(head)
        cols = slice(start, start + width)
        keep = lanes_in(width, offset, offset + HEAD)
        q = masked(q_ref[rows, cols], keep)
        do = masked(do_ref[rows, cols], keep)
        k = masked(k_ref[keys, cols], keep)
        dscores, prob = softmax_grads(q, do, k, v_ref[keys, cols], bias)
        dv_ref[keys, cols] = dv_ref[keys, cols] + nn(prob, do)
        dk_ref[keys, cols] = dk_ref[keys, cols] + nn(dscores, q)
        dq_ref[rows, cols] = dq_ref[rows, cols] + tn(dscores, k)


def gather_kernel(
    lengths_ref, mask_ref, column_ref, latents_ref, cotangent_ref,
    meta_ref, main_ref, extra_ref, cot_main_ref, cot_extra_ref, sems,
):
    clips, frame_dev = latents_ref.shape[:2]
    frames = mask_ref.shape[1]
    column = column_ref[0]
    long = jnp.int32(0)
    for c in range(clips):
        long = long + jnp.where(lengths_ref[c] == frames, c, 0)
    for i in range(TABLE):
        meta_ref[i] = 0
    meta_ref[LONG] = long
    count = jnp.int32(0)
    for c in range(clips):
        for f in range(EXTRAS - clips + 2):
            used = (c != long) & (f < lengths_ref[c])
            at = jnp.where(used, count, EXTRAS)
            meta_ref[CLIP + at] = jnp.int32(c)
            meta_ref[FRAME + at] = jnp.int32(f)
            meta_ref[VALID + at] = mask_ref[c, f]
            count = count + used.astype(jnp.int32)
    for e in range(EXTRAS, 8):
        for row in (CLIP, FRAME, VALID):
            meta_ref[row + e] = 0
    for f in range(frames):
        meta_ref[LONG_VALID + f] = mask_ref[long, f]
    for c in range(clips):
        for f in range(frame_dev):
            frame = column * frame_dev + f
            valid = (frame < lengths_ref[c]) & (mask_ref[c, frame] == 1)
            meta_ref[KIND + c * frame_dev + f] = jnp.where(valid, jnp.where(c == long, 1, 2), 0)
    for e in range(EXTRAS):
        local_frame = meta_ref[FRAME + e] - column * frame_dev
        here = (local_frame >= 0) & (local_frame < frame_dev)
        slot = meta_ref[CLIP + e] * frame_dev + jnp.where(here, local_frame, 0)

        @pl.when(here)
        def _(e=e, slot=slot):
            meta_ref[EXTRA_AT + slot] = jnp.int32(e)

    copies = []
    pairs = ((latents_ref, main_ref, extra_ref), (cotangent_ref, cot_main_ref, cot_extra_ref))
    for i, (source, main, extra) in enumerate(pairs):
        base = i * (EXTRAS + 1)
        copies.append(pltpu.make_async_copy(source.at[long], main, sems.at[base]))
        copies[-1].start()
        for e in range(EXTRAS):
            frame = lax.rem(meta_ref[FRAME + e], frame_dev)
            part = source.at[meta_ref[CLIP + e], frame]
            copies.append(pltpu.make_async_copy(part, extra.at[e], sems.at[base + 1 + e]))
            copies[-1].start()
    for copy in copies:
        copy.wait()


def front_main_kernel(meta_ref, mod_ref, x_ref, w_ref, qkv_ref, low_ref):
    @pl.when(pl.program_id(0) == 0)
    def _():
        shift, scale = [main_vec(meta_ref, mod_ref, 0, i) for i in range(2)]

        def body(rows):
            low_ref[rows, :] = modulate(x_ref[rows, :], shift, scale)

        over_rows(x_ref.shape[0], body)

    for start, size in col_tiles(w_ref.shape[-1]):
        cols = pl.ds(start, size)
        qkv_ref[0, :, cols] = nn(low_ref[...], w_ref[0, :, cols]).astype(BF)


def front_extra_kernel(meta_ref, mod_ref, x_ref, w_ref, pack_ref, low_ref, out_ref, *, patches):
    member = pl.program_id(0)
    rows = x_ref.shape[0]

    @pl.when(member == 0)
    def _():
        shift, scale = [extra_vec(meta_ref, mod_ref, 0, i, rows // patches, patches) for i in range(2)]
        low_ref[...] = modulate(x_ref[...], shift, scale)

    for start, size in col_tiles(w_ref.shape[-1]):
        cols = pl.ds(start, size)
        out_ref[member, :, cols] = nn(low_ref[...], w_ref[0, :, cols])

    @pl.when(member == 2)
    def _():
        for head in range(pack_ref.shape[0]):
            parts = [take_head(out_ref.at[i], slice(None), head) for i in range(3)]
            pack_ref[head] = pack3(parts).astype(BF)


def fill_keys(k_ref, v_ref, qkv_ref, other_ref):
    rows = qkv_ref.shape[1]
    k_ref[:rows] = qkv_ref[1]
    v_ref[:rows] = qkv_ref[2]
    for i in range(other_ref.shape[0]):
        k_ref[(i + 1) * rows : (i + 2) * rows] = other_ref[i, 0]
        v_ref[(i + 1) * rows : (i + 2) * rows] = other_ref[i, 1]


def attend_kernel(qkv_ref, other_ref, o_ref, k_ref, v_ref, acc_ref, *, heads):
    fill_keys(k_ref, v_ref, qkv_ref, other_ref)
    acc_ref[...] = jnp.zeros_like(acc_ref)
    heads_forward(acc_ref, qkv_ref.at[0], k_ref, v_ref, slice(None), slice(None), None, heads)
    o_ref[...] = acc_ref[...].astype(BF)


def extra_rows(ref, index):
    part = ref[:, index]
    return part.reshape(part.shape[0] * part.shape[1], part.shape[2])


def extra_attend_kernel(pack_ref, o_ref):
    for index in range(pack_ref.shape[1]):
        packed = extra_rows(pack_ref, index).astype(F32)
        q, k, v = [unpack3(packed, i).astype(BF) for i in range(3)]
        scores = nt(q, k)
        exponent = jnp.exp2((scores - jnp.max(scores, axis=-1, keepdims=True)) * SCALE2)
        total = jnp.sum(exponent, axis=-1, keepdims=True)
        result = nn(exponent.astype(BF), v) * (1.0 / total)
        o_ref[:, index] = result.astype(BF).reshape(o_ref.shape[0], o_ref.shape[2], 128)


def extra_attend_back_kernel(pack_ref, do_ref, grad_ref):
    for index in range(pack_ref.shape[1]):
        packed = extra_rows(pack_ref, index).astype(F32)
        q, k, v = [unpack3(packed, i).astype(BF) for i in range(3)]
        do = extra_rows(do_ref, index)
        dscores, prob = softmax_grads(q, do, k, v, None)
        out = pack3([tn(dscores, k), nn(dscores, q), nn(prob, do)]).astype(BF)
        grad_ref[:, index] = out.reshape(grad_ref.shape[0], grad_ref.shape[2], 256)


def back_main_kernel(meta_ref, mod_ref, x_ref, o_ref, w_ref, first_ref, acc_ref):
    times(acc_ref, o_ref, w_ref, 0)
    gate = main_vec(meta_ref, mod_ref, 0, 2)

    def body(rows):
        first_ref[rows, :] = gated(x_ref[rows, :], gate, acc_ref[rows, :])

    over_rows(x_ref.shape[0], body)


def back_extra_kernel(meta_ref, mod_ref, x_ref, o_ref, w_ref, first_ref, low_ref, acc_ref, *, patches):
    rows = x_ref.shape[0]
    acc_ref[...] = jnp.zeros_like(acc_ref)
    for head in range(o_ref.shape[0]):
        start, width, value = put_head(o_ref[head].astype(F32), head)
        acc_ref[:, start : start + width] = acc_ref[:, start : start + width] + value
    low_ref[...] = acc_ref[...].astype(BF)
    times(acc_ref, low_ref, w_ref, 0)
    gate = extra_vec(meta_ref, mod_ref, 0, 2, rows // patches, patches)
    first_ref[...] = gated(x_ref[...], gate, acc_ref[...])


def back_grad_main_kernel(meta_ref, mod_ref, g_ref, w_ref, do_ref, low_ref):
    gate = main_vec(meta_ref, mod_ref, 0, 2)

    def body(rows):
        low_ref[rows, :] = (gate * g_ref[rows, :].astype(F32)).astype(BF)

    over_rows(g_ref.shape[0], body)
    times(do_ref, low_ref, w_ref, 0, transposed=True)


def back_grad_extra_kernel(meta_ref, mod_ref, g_ref, w_ref, pack_ref, low_ref, do_ref, *, patches):
    rows = g_ref.shape[0]
    gate = extra_vec(meta_ref, mod_ref, 0, 2, rows // patches, patches)
    low_ref[...] = (gate * g_ref[...].astype(F32)).astype(BF)
    times(do_ref, low_ref, w_ref, 0, transposed=True)
    for head in range(pack_ref.shape[0]):
        pack_ref[head] = take_head(do_ref, slice(None), head).astype(BF)


def attend_back_kernel(
    qkv_ref, other_ref, do_ref, own_ref, sent_ref, k_ref, v_ref, dq_ref, dk_ref, dv_ref, *, heads
):
    rows = qkv_ref.shape[1]
    fill_keys(k_ref, v_ref, qkv_ref, other_ref)
    for ref in (dq_ref, dk_ref, dv_ref):
        ref[...] = jnp.zeros_like(ref)
    everything = slice(None)
    heads_backward(
        dq_ref, dk_ref, dv_ref, qkv_ref.at[0], k_ref, v_ref, do_ref, everything, everything, None, heads
    )
    own_ref[0] = dq_ref[...].astype(BF)
    own_ref[1] = dk_ref[:rows].astype(BF)
    own_ref[2] = dv_ref[:rows].astype(BF)
    for i in range(other_ref.shape[0]):
        sent_ref[i, 0] = dk_ref[(i + 1) * rows : (i + 2) * rows].astype(BF)
        sent_ref[i, 1] = dv_ref[(i + 1) * rows : (i + 2) * rows].astype(BF)


def add_product(acc_ref, d_ref, member, w_ref):
    for start, size in col_tiles(w_ref.shape[-1]):
        cols = pl.ds(start, size)
        product = nt(d_ref[member], w_ref[0, cols, :])

        @pl.when(member == 0)
        def _(cols=cols, product=product):
            acc_ref[:, cols] = product

        @pl.when(member > 0)
        def _(cols=cols, product=product):
            acc_ref[:, cols] = acc_ref[:, cols] + product


def front_grad_main_kernel(meta_ref, mod_ref, own_ref, got_ref, x_ref, g_ref, w_ref, out_ref, d_ref, acc_ref):
    member = pl.program_id(0)

    @pl.when(member == 0)
    def _():
        d_ref[0] = own_ref[0]
        for i in range(2):
            total = own_ref[1 + i].astype(F32)
            for j in range(got_ref.shape[0]):
                total = total + got_ref[j, i].astype(F32)
            d_ref[1 + i] = total.astype(BF)

    add_product(acc_ref, d_ref, member, w_ref)

    @pl.when(member == 2)
    def _():
        scale = main_vec(meta_ref, mod_ref, 0, 1)

        def body(rows):
            out_ref[rows, :] = norm_back(x_ref[rows, :], g_ref[rows, :], acc_ref[rows, :], scale)

        over_rows(x_ref.shape[0], body)


def front_grad_extra_kernel(
    meta_ref, mod_ref, pack_ref, x_ref, g_ref, w_ref, out_ref, d_ref, acc_ref, ext_ref, *, patches
):
    member = pl.program_id(0)
    rows = x_ref.shape[0]

    @pl.when(member == 0)
    def _():
        ext_ref[...] = jnp.zeros_like(ext_ref)
        for head in range(pack_ref.shape[0]):
            packed = pack_ref[head].astype(F32)
            for i in range(3):
                start, width, value = put_head(unpack3(packed, i), head)
                cols = slice(start, start + width)
                ext_ref[i, :, cols] = ext_ref[i, :, cols] + value
        d_ref[...] = ext_ref[...].astype(BF)

    add_product(acc_ref, d_ref, member, w_ref)

    @pl.when(member == 2)
    def _():
        scale = extra_vec(meta_ref, mod_ref, 0, 1, rows // patches, patches)
        out_ref[...] = norm_back(x_ref[...], g_ref[...], acc_ref[...], scale)


def key_bias(meta_ref, valid_at, clip_at, count, patches, keys_axis):
    tokens = count * patches
    where = lax.broadcasted_iota(jnp.int32, (tokens, tokens), keys_axis)
    other = lax.broadcasted_iota(jnp.int32, (tokens, tokens), 1 - keys_axis)

    def spread(base, axis):
        line = (1, tokens) if axis == 1 else (tokens, 1)
        item = lax.broadcasted_iota(jnp.int32, line, axis) // patches
        out = jnp.zeros(line, jnp.int32)
        for i in range(count):
            out = jnp.where(item == i, meta_ref[base + i], out)
        return out

    admitted = jnp.broadcast_to(spread(valid_at, keys_axis) == 1, (tokens, tokens))
    if clip_at is not None:
        admitted = admitted & (spread(clip_at, 0) == spread(clip_at, 1))
    admitted = admitted & (where % patches == other % patches)
    return jnp.where(admitted | (where == other), 0.0, -1e30).astype(F32)


def temporal_kernel(
    meta_ref, mod_ref, xm_ref, xe_ref, cm_ref, ce_ref, w_ref,
    outm_ref, oute_ref, gm_ref, ge_ref,
    low_ref, q_ref, k_ref, v_ref, cot_ref, acc_ref, dq_ref, dk_ref, dv_ref, *, heads, patches,
):
    main = xm_ref.shape[0]
    frames, extras = main // patches, xe_ref.shape[0] // patches
    last = slice(main, None)
    mvec = [main_vec(meta_ref, mod_ref, 1, i) for i in range(3)]

    def evec(member):
        return extra_vec(meta_ref, mod_ref, 1, member, extras, patches)

    def body(rows):
        low_ref[rows, :] = modulate(xm_ref[rows, :], mvec[0], mvec[1])

    over_rows(main, body)
    low_ref[last] = modulate(xe_ref[...], evec(0), evec(1))
    for i in range(frames):
        rows = slice(i * patches, (i + 1) * patches)
        cot_ref[rows, :] = jnp.where(meta_ref[LONG_VALID + i] == 1, cm_ref[rows, :].astype(F32), 0.0)
    for i in range(extras):
        rows = slice(i * patches, (i + 1) * patches)
        there = slice(main + i * patches, main + (i + 1) * patches)
        cot_ref[there, :] = jnp.where(meta_ref[VALID + i] == 1, ce_ref[rows, :].astype(F32), 0.0)

    for i, ref in enumerate((q_ref, k_ref, v_ref)):
        times(ref, low_ref, w_ref, i)
    acc_ref[...] = jnp.zeros_like(acc_ref)
    parts = ((slice(0, main), LONG_VALID, None, frames), (last, VALID, CLIP, extras))
    for rows, valid_at, clip_at, count in parts:
        bias = key_bias(meta_ref, valid_at, clip_at, count, patches, 1)
        heads_forward(acc_ref, q_ref, k_ref, v_ref, rows, rows, bias, heads)
    low_ref[...] = acc_ref[...].astype(BF)
    times(acc_ref, low_ref, w_ref, 3)

    def body(rows):
        outm_ref[rows, :] = gated(xm_ref[rows, :], mvec[2], acc_ref[rows, :])
        low_ref[rows, :] = (mvec[2] * cot_ref[rows, :]).astype(BF)

    over_rows(main, body)
    gate = evec(2)
    oute_ref[...] = gated(xe_ref[...], gate, acc_ref[last])
    low_ref[last] = (gate * cot_ref[last]).astype(BF)

    times(acc_ref, low_ref, w_ref, 3, transposed=True)
    low_ref[...] = acc_ref[...].astype(BF)
    for ref in (dq_ref, dk_ref, dv_ref):
        ref[...] = jnp.zeros_like(ref)
    for rows, valid_at, clip_at, count in parts:
        bias = key_bias(meta_ref, valid_at, clip_at, count, patches, 0)
        heads_backward(dq_ref, dk_ref, dv_ref, q_ref, k_ref, v_ref, low_ref, rows, rows, bias, heads)
    for i, ref in enumerate((dq_ref, dk_ref, dv_ref)):
        low_ref[...] = ref[...].astype(BF)
        times(acc_ref, low_ref, w_ref, i, transposed=True, add=i > 0)

    def body(rows):
        gm_ref[rows, :] = norm_back(xm_ref[rows, :], cot_ref[rows, :], acc_ref[rows, :], mvec[1])

    over_rows(main, body)
    ge_ref[...] = norm_back(xe_ref[...], cot_ref[last], acc_ref[last], evec(1))


def place_kernel(meta_ref, main_ref, extra_ref, out_ref):
    frame_dev = main_ref.shape[0]
    for slot in range(out_ref.shape[0]):
        kind = meta_ref[KIND + slot]

        @pl.when(kind == 0)
        def _(slot=slot):
            out_ref[slot] = jnp.zeros_like(out_ref[slot])

        @pl.when(kind == 1)
        def _(slot=slot):
            out_ref[slot] = main_ref[slot % frame_dev]

        @pl.when(kind == 2)
        def _(slot=slot):
            out_ref[slot] = extra_ref[meta_ref[EXTRA_AT + slot]]


SCALARS = pl.BlockSpec(memory_space=pltpu.SMEM)
ANYWHERE = pl.BlockSpec(memory_space=pl.ANY)


def params(steps=0):
    semantics = {"dimension_semantics": ("arbitrary",) * steps} if steps else {}
    return pltpu.CompilerParams(vmem_limit_bytes=VMEM_LIMIT, **semantics)


def cost(flops, elements=0):
    return pl.CostEstimate(flops=int(flops), bytes_accessed=int(elements), transcendentals=0)


def whole(array):
    return pl.BlockSpec(array.shape, lambda *_: (0,) * len(array.shape))


def shape(*dims, dtype=BF):
    return jax.ShapeDtypeStruct(dims, dtype)


def weight_call(kernel, name, operands, weights, members, outs, scratch, weigh):
    width = weights.shape[-1]
    first, count = members
    return pl.pallas_call(
        kernel,
        name=name,
        grid=(count,),
        in_specs=[SCALARS]
        + [whole(a) for a in operands[1:]]
        + [pl.BlockSpec((1, width, width), lambda i: (first + i, 0, 0))],
        out_specs=[spec for spec, _ in outs],
        out_shape=[struct for _, struct in outs],
        scratch_shapes=scratch,
        compiler_params=params(1),
        cost_estimate=cost(weigh * count, 2 * width * width * count),
    )(*operands, weights)


def full(*dims):
    return whole(shape(*dims)), shape(*dims)


def gather(lengths, frame_mask, column, latents, cotangent):
    main, extra = latents.shape[1:], (EXTRAS,) + latents.shape[2:]
    return pl.pallas_call(
        gather_kernel,
        name="gather",
        in_specs=[SCALARS] * 3 + [ANYWHERE] * 2,
        out_specs=[SCALARS] + [ANYWHERE] * 4,
        out_shape=[shape(TABLE, dtype=jnp.int32)] + [shape(*main), shape(*extra)] * 2,
        scratch_shapes=[pltpu.SemaphoreType.DMA((2 * (EXTRAS + 1),))],
        compiler_params=params(),
    )(lengths, frame_mask, column, latents, cotangent)


def front_main(meta, mod, x, weights):
    rows, width = x.shape
    spec = pl.BlockSpec((1, rows, width), lambda i: (i, 0, 0))
    return weight_call(
        front_main_kernel, "front_main", (meta, mod, x), weights, (0, 3),
        [(spec, shape(3, rows, width))], [pltpu.VMEM((rows, width), BF)], 2 * rows * width**2,
    )[0]


def front_extra(meta, mod, x, weights, heads, patches):
    rows, width = x.shape
    return weight_call(
        functools.partial(front_extra_kernel, patches=patches), "front_extra", (meta, mod, x), weights, (0, 3),
        [full(heads, rows, 256)], [pltpu.VMEM((rows, width), BF), pltpu.VMEM((3, rows, width), F32)],
        4 * rows * width**2,
    )[0]


def back_main(meta, mod, x, o, weights):
    rows, width = x.shape
    return weight_call(
        back_main_kernel, "back_main", (meta, mod, x, o), weights, (3, 1),
        [full(rows, width)], [pltpu.VMEM((rows, width), F32)], 3 * rows * width**2,
    )[0]


def back_extra(meta, mod, x, o, weights, patches):
    rows, width = x.shape
    return weight_call(
        functools.partial(back_extra_kernel, patches=patches), "back_extra", (meta, mod, x, o), weights, (3, 1),
        [full(rows, width)], [pltpu.VMEM((rows, width), BF), pltpu.VMEM((rows, width), F32)],
        4 * rows * width**2,
    )[0]


def back_grad_main(meta, mod, g, weights):
    rows, width = g.shape
    return weight_call(
        back_grad_main_kernel, "back_grad_main", (meta, mod, g), weights, (3, 1),
        [full(rows, width)], [pltpu.VMEM((rows, width), BF)], 3 * rows * width**2,
    )[0]


def back_grad_extra(meta, mod, g, weights, heads, patches):
    rows, width = g.shape
    return weight_call(
        functools.partial(back_grad_extra_kernel, patches=patches), "back_grad_extra", (meta, mod, g), weights,
        (3, 1), [full(heads, rows, 128)], [pltpu.VMEM((rows, width), BF), pltpu.VMEM((rows, width), F32)],
        4 * rows * width**2,
    )[0]


def front_grad_main(meta, mod, own, got, x, g, weights):
    rows, width = x.shape
    return weight_call(
        front_grad_main_kernel, "front_grad_main", (meta, mod, own, got, x, g), weights, (0, 3),
        [full(rows, width)], [pltpu.VMEM((3, rows, width), BF), pltpu.VMEM((rows, width), F32)],
        3 * rows * width**2,
    )[0]


def front_grad_extra(meta, mod, pack, x, g, weights, patches):
    rows, width = x.shape
    return weight_call(
        functools.partial(front_grad_extra_kernel, patches=patches), "front_grad_extra",
        (meta, mod, pack, x, g), weights, (0, 3), [full(rows, width)],
        [pltpu.VMEM((3, rows, width), BF), pltpu.VMEM((rows, width), F32), pltpu.VMEM((3, rows, width), F32)],
        4 * rows * width**2,
    )[0]


def attend(qkv, other, heads):
    _, rows, width = qkv.shape
    keys = rows * (other.shape[0] + 1)
    return pl.pallas_call(
        functools.partial(attend_kernel, heads=heads),
        name="attend",
        out_shape=shape(rows, width),
        scratch_shapes=[
            pltpu.VMEM((keys, width), BF),
            pltpu.VMEM((keys, width), BF),
            pltpu.VMEM((rows, width), F32),
        ],
        compiler_params=params(),
        cost_estimate=cost(6e9),
    )(qkv, other)


def extra_attend(pack):
    return pl.pallas_call(
        extra_attend_kernel, name="extra_attend", out_shape=shape(*pack.shape[:-1], 128),
        compiler_params=params(), cost_estimate=cost(4e9),
    )(pack)


def extra_attend_back(pack, do):
    return pl.pallas_call(
        extra_attend_back_kernel, name="extra_attend_back", out_shape=shape(*pack.shape),
        compiler_params=params(), cost_estimate=cost(6e9),
    )(pack, do)


def attend_back(qkv, other, do, heads):
    _, rows, width = qkv.shape
    keys = rows * (other.shape[0] + 1)
    return pl.pallas_call(
        functools.partial(attend_back_kernel, heads=heads),
        name="attend_back",
        out_shape=[shape(3, rows, width), shape(*other.shape)],
        scratch_shapes=[
            pltpu.VMEM((keys, width), BF),
            pltpu.VMEM((keys, width), BF),
            pltpu.VMEM((rows, width), F32),
            pltpu.VMEM((keys, width), F32),
            pltpu.VMEM((keys, width), F32),
        ],
        compiler_params=params(),
        cost_estimate=cost(14e9),
    )(qkv, other, do)


def temporal(meta, mod, xm, xe, cm, ce, weights, heads, patches):
    main, width = xm.shape
    extra = xe.shape[0]
    rows = main + extra
    return pl.pallas_call(
        functools.partial(temporal_kernel, heads=heads, patches=patches),
        name="temporal",
        in_specs=[SCALARS] + [whole(a) for a in (mod, xm, xe, cm, ce, weights)],
        out_shape=[shape(main, width), shape(extra, width)] * 2,
        scratch_shapes=[pltpu.VMEM((rows, width), BF)] * 4 + [pltpu.VMEM((rows, width), F32)] * 5,
        compiler_params=params(),
        cost_estimate=cost(30e9),
    )(meta, mod, xm, xe, cm, ce, weights)


def place(meta, main, extra, slots):
    return pl.pallas_call(
        place_kernel,
        name="place",
        in_specs=[SCALARS, whole(main), whole(extra)],
        out_shape=shape(slots, *main.shape[1:]),
        compiler_params=params(),
        cost_estimate=cost(3e9),
    )(meta, main, extra)


def local(latents, cotangent, spatial_weights, temporal_weights, modulation, lengths, frame_mask):
    clips, frame_dev, patch_dev, width = latents.shape
    heads = width // HEAD
    frame_axis, patch_axis = lax.axis_size("frame"), lax.axis_size("patch")
    everyone = ("frame", "patch")
    frames = frame_dev * frame_axis
    sharers = patch_axis // frame_dev
    sub = patch_dev // sharers
    small = sub // frame_axis
    patch_t = patch_dev // frame_axis
    heads_col = heads // frame_axis
    groups = patch_axis // heads_col
    group_extras = -(-EXTRAS // groups)
    extras = groups * group_extras

    def swap(x, axis):
        return lax.all_to_all(x, axis, split_axis=0, concat_axis=0, tiled=True)

    column = lax.axis_index("frame")
    sources = -(-(EXTRAS - clips + 2) // frame_dev)
    main_rows = frame_dev * patch_dev

    def split_home(x):
        x = x.reshape(x.shape[0], sharers, frame_axis, small, width)
        return jnp.transpose(x, (2, 0, 1, 3, 4)).reshape(frame_axis, x.shape[0], patch_t, width)

    def join_home(x):
        items = x.shape[1]
        x = x.reshape(frame_axis, items, sharers, small, width)
        return jnp.transpose(x, (1, 2, 0, 3, 4)).reshape(items, patch_dev, width)

    def extras_out(x, meta):
        x = jnp.transpose(x.reshape(EXTRAS, frame_axis, patch_t, width), (1, 0, 2, 3))
        found = []
        for source in range(sources):
            mine = jnp.where(column == source, x[source], jnp.zeros((), BF))
            for dest in range(frame_axis):
                if dest != source:
                    mine = mine + lax.ppermute(x[dest], "frame", [(source, dest)])
            found.append(mine)
        out = found[0]
        for source in range(1, sources):
            frame = meta[FRAME : FRAME + EXTRAS][:, None, None]
            out = jnp.where(frame // frame_dev == source, found[source], out)
        out = out.reshape(EXTRAS * patch_t, width)
        return jnp.concatenate([out, jnp.zeros(((extras - EXTRAS) * patch_t, width), BF)])

    def extras_home(x):
        x = x.reshape(extras, patch_t, width)[:EXTRAS]
        found = []
        for source in range(frame_axis):
            mine = jnp.where(column == source, x, jnp.zeros((), BF))
            for dest in range(sources):
                if dest != source:
                    mine = mine + lax.ppermute(x, "frame", [(source, dest)])
            found.append(mine)
        return jnp.transpose(jnp.stack(found), (1, 0, 2, 3)).reshape(EXTRAS, patch_dev, width)

    meta, main_home, extra_home, cot_main, cot_extra = gather(
        lengths, frame_mask, column.reshape(1).astype(jnp.int32), latents, cotangent
    )
    extra_t = extras_out(extra_home, meta)
    main_s = swap(main_home.reshape(patch_axis, sub, width), "patch").reshape(main_rows, width)
    cot_m = swap(split_home(cot_main), "frame").reshape(main_rows, width)
    cot_e = extras_out(cot_extra, meta)

    def rotate(array, by):
        perm = []
        for p in range(patch_axis):
            base = p // sharers * sharers
            perm.append((p, base + (p - base + by) % sharers))
        return lax.ppermute(array, "patch", perm)

    mod = modulation
    chunk = group_extras * patch_t
    pack = front_extra(meta, mod, extra_t, spatial_weights, heads, patch_t)
    pack_got = swap(pack.reshape(frame_axis * patch_axis, chunk, 256), everyone)
    pack_got = pack_got.reshape(frame_axis * patch_axis, group_extras, patch_t, 256)
    qkv = front_main(meta, mod, main_s, spatial_weights)
    other = jnp.stack([rotate(qkv[1:], by) for by in range(1, sharers)])
    attended = attend(qkv, other, heads)
    extra_o = extra_attend(pack_got)
    extra_o = swap(extra_o.reshape(frame_axis * patch_axis, chunk, 128), everyone)
    extra_o = extra_o.reshape(heads, extras * patch_t, 128)
    first_m = back_main(meta, mod, main_s, attended, spatial_weights)
    first_e = back_extra(meta, mod, extra_t, extra_o, spatial_weights, patch_t)

    def to_temporal(x):
        x = x.reshape(patch_axis, frame_axis, small, width)
        x = jnp.transpose(x, (1, 0, 2, 3)).reshape(frame_axis * patch_axis, small, width)
        return swap(x, everyone).reshape(frames * patch_t, width)

    def to_spatial(x):
        x = swap(x.reshape(frame_axis * patch_axis, small, width), everyone)
        x = jnp.transpose(x.reshape(frame_axis, patch_axis, small, width), (1, 0, 2, 3))
        return x.reshape(main_rows, width)

    out_m, out_e, grad_m, grad_e = temporal(
        meta, mod, to_temporal(first_m), first_e, cot_m, cot_e, temporal_weights, heads, patch_t
    )

    do_pack = back_grad_extra(meta, mod, grad_e, spatial_weights, heads, patch_t)
    do_got = swap(do_pack.reshape(frame_axis * patch_axis, chunk, 128), everyone)
    do_got = do_got.reshape(frame_axis * patch_axis, group_extras, patch_t, 128)
    grad_s = to_spatial(grad_m)
    do_main = back_grad_main(meta, mod, grad_s, spatial_weights)
    own, sent = attend_back(qkv, other, do_main, heads)
    got = jnp.stack([rotate(sent[by - 1], -by) for by in range(1, sharers)])
    dpack = extra_attend_back(pack_got, do_got)
    dpack = swap(dpack.reshape(frame_axis * patch_axis, chunk, 256), everyone)
    dpack = dpack.reshape(heads, extras * patch_t, 256)
    lat_m = front_grad_main(meta, mod, own, got, main_s, grad_s, spatial_weights)
    lat_e = front_grad_extra(meta, mod, dpack, extra_t, grad_e, spatial_weights, patch_t)
    lat_main = swap(lat_m.reshape(patch_axis, sub, width), "patch").reshape(frame_dev, patch_dev, width)

    out_main = join_home(swap(out_m.reshape(frame_axis, frame_dev, patch_t, width), "frame"))
    slots = clips * frame_dev
    output = place(meta, out_main, extras_home(out_e), slots)
    grad = place(meta, lat_main, extras_home(lat_e), slots)
    return output.reshape(latents.shape), grad.reshape(latents.shape)


def solution(mesh):
    tokens = P(None, "frame", "patch", None)
    in_specs = (tokens, tokens, P(), P(), P(), P(), P())
    return jax.shard_map(local, mesh=mesh, in_specs=in_specs, out_specs=(tokens, tokens), check_vma=False)
```

```python
import functools
import math

import jax
import jax.numpy as jnp
from jax import lax
from jax.experimental import pallas as pl
from jax.experimental.pallas import tpu as pltpu
from jax.sharding import PartitionSpec as P

HEAD = 72
EXTRAS = 5
SCALE = HEAD ** -0.5
SCALE2 = SCALE * math.log2(math.e)
BF = jnp.bfloat16
F32 = jnp.float32
VMEM_LIMIT = 56 * 1024 * 1024
LONG, COLUMN, CLIP, FRAME, VALID, LONG_VALID, KIND, EXTRA_AT, TABLE = 0, 1, 8, 16, 24, 32, 48, 64, 80


def nn(a, b):
    return lax.dot_general(a, b, (((1,), (0,)), ((), ())), preferred_element_type=F32)


def nt(a, b):
    return lax.dot_general(a, b, (((1,), (1,)), ((), ())), preferred_element_type=F32)


def tn(a, b):
    return lax.dot_general(a, b, (((0,), (0,)), ((), ())), preferred_element_type=F32)


def window(head):
    start = head * HEAD // 128 * 128
    offset = head * HEAD - start
    return start, offset, 128 if offset + HEAD <= 128 else 256


def lanes_in(width, low, high):
    lane = lax.broadcasted_iota(jnp.int32, (1, width), 1)
    return (lane >= low) & (lane < high)


def masked(x, keep):
    return jnp.where(keep, x, jnp.zeros((), x.dtype))


def take_head(x_ref, rows, head):
    start, offset, width = window(head)
    part = x_ref[rows, start : start + width].astype(F32)
    if offset:
        part = pltpu.roll(part, width - offset, 1)
    return masked(part[:, :128], lanes_in(128, 0, HEAD))


def put_head(value, head):
    start, offset, width = window(head)
    if width == 256:
        value = jnp.concatenate([value, jnp.zeros_like(value)], axis=1)
    if offset:
        value = pltpu.roll(value, offset, 1)
    return start, width, value


def wide(value):
    return jnp.concatenate([value, jnp.zeros_like(value)], axis=1)


def pack3(parts):
    first, second, third = parts
    return wide(first) + pltpu.roll(wide(second), HEAD, 1) + pltpu.roll(wide(third), 2 * HEAD, 1)


def unpack3(packed, member):
    if member:
        packed = pltpu.roll(packed, 256 - member * HEAD, 1)
    return masked(packed[:, :128], lanes_in(128, 0, HEAD))


def main_vec(meta_ref, mod_ref, block, member):
    return mod_ref[block, member, pl.ds(meta_ref[LONG], 1), :]


def extra_vec(meta_ref, mod_ref, block, member, extras, patches):
    rows = [mod_ref[block, member, pl.ds(meta_ref[CLIP + e], 1), :] for e in range(extras)]
    return jnp.concatenate([jnp.broadcast_to(r, (patches, r.shape[1])) for r in rows], axis=0)


def normed_of(x):
    average = jnp.mean(x, axis=-1, keepdims=True)
    centred = x - average
    variance = jnp.mean(centred * centred, axis=-1, keepdims=True)
    inverse = lax.rsqrt(variance + 1e-06)
    return centred * inverse, inverse


def over_rows(count, body):
    size = math.gcd(count, 64)
    if count == size:
        body(slice(0, count))
        return

    def step(i, carry):
        body(pl.ds(pl.multiple_of(i * size, size), size))
        return carry

    lax.fori_loop(0, count // size, step, 0)


def modulate(x, shift, scale):
    normed, _ = normed_of(x.astype(F32))
    return (normed * (1.0 + scale) + shift).astype(BF)


def norm_back(x, grad, dmod, scale):
    normed, inverse = normed_of(x.astype(F32))
    dnormed = dmod * (1.0 + scale)
    mean_d = jnp.mean(dnormed, axis=-1, keepdims=True)
    mean_dn = jnp.mean(dnormed * normed, axis=-1, keepdims=True)
    dx = (inverse * (dnormed - mean_d - normed * mean_dn)).astype(BF)
    return (dx.astype(F32) + grad.astype(F32)).astype(BF)


def gated(x, gate, mixed):
    return (x.astype(F32) + gate * mixed).astype(BF)


def col_tiles(width):
    whole, tiles = 512, []
    start = 0
    while start < width:
        tiles.append((start, min(whole, width - start)))
        start += whole
    return tiles


def times(dest_ref, x_ref, w_ref, member, transposed=False, add=False):
    for start, size in col_tiles(w_ref.shape[-1]):
        cols = pl.ds(start, size)
        if transposed:
            product = nt(x_ref[...], w_ref[member, cols, :])
        else:
            product = nn(x_ref[...], w_ref[member, :, cols])
        if add:
            product = dest_ref[:, cols] + product
        dest_ref[:, cols] = product.astype(dest_ref.dtype)


def heads_forward(o_ref, q_ref, k_ref, v_ref, rows, keys, bias, heads):
    for head in range(heads):
        start, offset, width = window(head)
        cols = slice(start, start + width)
        keep = lanes_in(width, offset, offset + HEAD)
        scores = nt(masked(q_ref[rows, cols], keep), k_ref[keys, cols])
        if bias is not None:
            scores = scores + bias
        exponent = jnp.exp2((scores - jnp.max(scores, axis=-1, keepdims=True)) * SCALE2)
        total = jnp.sum(exponent, axis=-1, keepdims=True)
        result = nn(exponent.astype(BF), masked(v_ref[keys, cols], keep)) * (1.0 / total)
        o_ref[rows, cols] = o_ref[rows, cols] + result


def softmax_grads(q, do, k, v, bias):
    scores = nt(k, q)
    if bias is not None:
        scores = scores + bias
    exponent = jnp.exp2((scores - jnp.max(scores, axis=0, keepdims=True)) * SCALE2)
    prob = exponent * (1.0 / jnp.sum(exponent, axis=0, keepdims=True))
    dprob = nt(v, do)
    delta = jnp.sum(prob * dprob, axis=0, keepdims=True)
    dscores = prob * (dprob - delta) * SCALE
    return dscores.astype(BF), prob.astype(BF)


def heads_backward(dq_ref, dk_ref, dv_ref, q_ref, k_ref, v_ref, do_ref, rows, keys, bias, heads):
    for head in range(heads):
        start, offset, width = window(head)
        cols = slice(start, start + width)
        keep = lanes_in(width, offset, offset + HEAD)
        q = masked(q_ref[rows, cols], keep)
        do = masked(do_ref[rows, cols], keep)
        k = masked(k_ref[keys, cols], keep)
        dscores, prob = softmax_grads(q, do, k, v_ref[keys, cols], bias)
        dv_ref[keys, cols] = dv_ref[keys, cols] + nn(prob, do)
        dk_ref[keys, cols] = dk_ref[keys, cols] + nn(dscores, q)
        dq_ref[rows, cols] = dq_ref[rows, cols] + tn(dscores, k)


def gather_kernel(
    lengths_ref, mask_ref, column_ref, latents_ref, cotangent_ref,
    meta_ref, main_ref, extra_ref, cot_main_ref, cot_extra_ref,
    main_in, extra_in, sems, *, sharers,
):
    clips, frame_dev, patch_dev, width = latents_ref.shape
    frames = mask_ref.shape[1]
    frame_axis = frames // frame_dev
    patch_t = patch_dev // frame_axis
    small, sub = patch_t // sharers, patch_dev // sharers
    column = column_ref[0]
    long = jnp.int32(0)
    for c in range(clips):
        long = long + jnp.where(lengths_ref[c] == frames, c, 0)
    for i in range(TABLE):
        meta_ref[i] = 0
    meta_ref[LONG] = long
    meta_ref[COLUMN] = column
    count = jnp.int32(0)
    for c in range(clips):
        for f in range(EXTRAS - clips + 2):
            used = (c != long) & (f < lengths_ref[c])
            at = jnp.where(used, count, EXTRAS)
            meta_ref[CLIP + at] = jnp.int32(c)
            meta_ref[FRAME + at] = jnp.int32(f)
            meta_ref[VALID + at] = mask_ref[c, f]
            count = count + used.astype(jnp.int32)
    for e in range(EXTRAS, 8):
        for row in (CLIP, FRAME, VALID):
            meta_ref[row + e] = 0

    copies = []
    pairs = ((latents_ref, main_ref), (cotangent_ref, main_in))
    for i, (source, main) in enumerate(pairs):
        copies.append(pltpu.make_async_copy(source.at[long], main, sems.at[i, EXTRAS]))
        copies[-1].start()
        for e in range(EXTRAS):
            frame = lax.rem(meta_ref[FRAME + e], frame_dev)
            part = source.at[meta_ref[CLIP + e], frame]
            copies.append(pltpu.make_async_copy(part, extra_in.at[i, e], sems.at[i, e]))
            copies[-1].start()

    for f in range(frames):
        meta_ref[LONG_VALID + f] = mask_ref[long, f]
    for c in range(clips):
        for f in range(frame_dev):
            frame = column * frame_dev + f
            valid = (frame < lengths_ref[c]) & (mask_ref[c, frame] == 1)
            meta_ref[KIND + c * frame_dev + f] = jnp.where(valid, jnp.where(c == long, 1, 2), 0)
    for e in range(EXTRAS):
        local_frame = meta_ref[FRAME + e] - column * frame_dev
        here = (local_frame >= 0) & (local_frame < frame_dev)
        slot = meta_ref[CLIP + e] * frame_dev + jnp.where(here, local_frame, 0)

        @pl.when(here)
        def _(e=e, slot=slot):
            meta_ref[EXTRA_AT + slot] = jnp.int32(e)

    for copy in copies:
        copy.wait()
    for i, out in enumerate((extra_ref, cot_extra_ref)):
        for e in range(EXTRAS):
            rows = extra_in[i, e].astype(F32)
            for f in range(frame_axis):
                out[f, e] = rows[f * patch_t : (f + 1) * patch_t].astype(BF)
    for j in range(frame_dev):
        rows = main_in[j].astype(F32)
        for f in range(frame_axis):
            starts = [s * sub + f * small for s in range(sharers)]
            part = jnp.concatenate([rows[at : at + small] for at in starts], axis=0)
            cot_main_ref[f ^ column, j] = part.astype(BF)


def front_main_kernel(meta_ref, mod_ref, x_ref, w_ref, q_ref, kv_ref, low_ref):
    member = pl.program_id(0)

    @pl.when(member == 0)
    def _():
        shift, scale = [main_vec(meta_ref, mod_ref, 0, i) for i in range(2)]

        def body(rows):
            low_ref[rows, :] = modulate(x_ref[rows, :], shift, scale)

        over_rows(x_ref.shape[0], body)
        times(q_ref, low_ref, w_ref, 0)

    @pl.when(member > 0)
    def _():
        times(kv_ref.at[0], low_ref, w_ref, 0)


def front_extra_kernel(meta_ref, mod_ref, x_ref, w_ref, pack_ref, low_ref, out_ref, *, patches):
    member = pl.program_id(0)
    rows = x_ref.shape[0]

    @pl.when(member == 0)
    def _():
        shift, scale = [extra_vec(meta_ref, mod_ref, 0, i, rows // patches, patches) for i in range(2)]
        low_ref[...] = modulate(x_ref[...], shift, scale)

    for start, size in col_tiles(w_ref.shape[-1]):
        cols = pl.ds(start, size)
        out_ref[member, :, cols] = nn(low_ref[...], w_ref[0, :, cols])

    @pl.when(member == 2)
    def _():
        for head in range(pack_ref.shape[0]):
            parts = [take_head(out_ref.at[i], slice(None), head) for i in range(3)]
            pack_ref[head] = pack3(parts).astype(BF)


def fill_keys(k_ref, v_ref, kv_ref, other_ref):
    rows = kv_ref.shape[1]
    k_ref[:rows] = kv_ref[0]
    v_ref[:rows] = kv_ref[1]
    for i in range(other_ref.shape[0]):
        k_ref[(i + 1) * rows : (i + 2) * rows] = other_ref[i, 0]
        v_ref[(i + 1) * rows : (i + 2) * rows] = other_ref[i, 1]


def attend_kernel(q_ref, kv_ref, other_ref, o_ref, k_ref, v_ref, acc_ref, *, heads):
    fill_keys(k_ref, v_ref, kv_ref, other_ref)
    acc_ref[...] = jnp.zeros_like(acc_ref)
    heads_forward(acc_ref, q_ref, k_ref, v_ref, slice(None), slice(None), None, heads)
    o_ref[...] = acc_ref[...].astype(BF)


def extra_rows(ref, index):
    part = ref[:, index]
    return part.reshape(part.shape[0] * part.shape[1], part.shape[2])


def extra_attend_kernel(pack_ref, o_ref):
    for index in range(pack_ref.shape[1]):
        packed = extra_rows(pack_ref, index).astype(F32)
        q, k, v = [unpack3(packed, i).astype(BF) for i in range(3)]
        scores = nt(q, k)
        exponent = jnp.exp2((scores - jnp.max(scores, axis=-1, keepdims=True)) * SCALE2)
        total = jnp.sum(exponent, axis=-1, keepdims=True)
        result = nn(exponent.astype(BF), v) * (1.0 / total)
        o_ref[:, index] = result.astype(BF).reshape(o_ref.shape[0], o_ref.shape[2], 128)


def extra_attend_back_kernel(pack_ref, got_ref, grad_ref):
    patches = pack_ref.shape[2]
    for index in range(pack_ref.shape[1]):
        packed = extra_rows(pack_ref, index).astype(F32)
        q, k, v = [unpack3(packed, i).astype(BF) for i in range(3)]
        do = got_ref[:, index * patches : (index + 1) * patches, :].astype(F32)
        do = do.reshape(do.shape[0] * patches, 128).astype(BF)
        dscores, prob = softmax_grads(q, do, k, v, None)
        out = pack3([tn(dscores, k), nn(dscores, q), nn(prob, do)]).astype(BF)
        grad_ref[:, index] = out.reshape(grad_ref.shape[0], grad_ref.shape[2], 256)


def extra_room(rows):
    return -(-rows // 16) * 16


def write_chunk(sent_ref, dest, room, value):
    pieces = [value[:, at : at + 128] for at in range(0, value.shape[1], 128)]
    rows = value.shape[0] * len(pieces)
    sent_ref[dest, room : room + rows, :] = jnp.concatenate(pieces, axis=0).astype(BF)


def read_chunk(got_ref, source, room, out_ref, row, small):
    count = out_ref.shape[1] // 128
    value = got_ref[source, room : room + small * count, :].astype(F32)
    for i in range(count):
        out_ref[row : row + small, i * 128 : (i + 1) * 128] = value[i * small : (i + 1) * small]


def back_main_kernel(meta_ref, mod_ref, x_ref, o_ref, extra_ref, w_ref, sent_ref, acc_ref, *, columns):
    times(acc_ref, o_ref, w_ref, 0)
    gate = main_vec(meta_ref, mod_ref, 0, 2)

    def body(rows):
        acc_ref[rows, :] = x_ref[rows, :].astype(F32) + gate * acc_ref[rows, :]

    over_rows(x_ref.shape[0], body)
    devices, chunk, _ = extra_ref.shape
    room = extra_room(chunk)
    small = x_ref.shape[0] // devices
    patch_axis = devices // columns
    sent_ref[:, :chunk, :] = extra_ref[...]
    for p in range(patch_axis):
        for f in range(columns):
            row = (p * columns + f) * small
            write_chunk(sent_ref, f * patch_axis + p, room, acc_ref[row : row + small, :])


def back_grad_main_kernel(meta_ref, mod_ref, got_ref, w_ref, do_ref, g_ref, low_ref, acc_ref, *, columns, room):
    devices = got_ref.shape[0]
    small = g_ref.shape[0] // devices
    patch_axis = devices // columns
    for p in range(patch_axis):
        for f in range(columns):
            row = (p * columns + f) * small
            read_chunk(got_ref, f * patch_axis + p, room, acc_ref, row, small)
    gate = main_vec(meta_ref, mod_ref, 0, 2)

    def body(rows):
        g_ref[rows, :] = acc_ref[rows, :].astype(BF)
        low_ref[rows, :] = (gate * acc_ref[rows, :]).astype(BF)

    over_rows(g_ref.shape[0], body)
    times(do_ref, low_ref, w_ref, 0, transposed=True)


def attend_back_kernel(
    q_ref, kv_ref, other_ref, do_ref, own_ref, sent_ref, k_ref, v_ref, dq_ref, dk_ref, dv_ref, *, heads
):
    rows = kv_ref.shape[1]
    fill_keys(k_ref, v_ref, kv_ref, other_ref)
    for ref in (dq_ref, dk_ref, dv_ref):
        ref[...] = jnp.zeros_like(ref)
    everything = slice(None)
    heads_backward(
        dq_ref, dk_ref, dv_ref, q_ref, k_ref, v_ref, do_ref, everything, everything, None, heads
    )
    own_ref[0] = dq_ref[...].astype(BF)
    own_ref[1] = dk_ref[:rows].astype(BF)
    own_ref[2] = dv_ref[:rows].astype(BF)
    for i in range(other_ref.shape[0]):
        sent_ref[i, 0] = dk_ref[(i + 1) * rows : (i + 2) * rows].astype(BF)
        sent_ref[i, 1] = dv_ref[(i + 1) * rows : (i + 2) * rows].astype(BF)


def add_product(acc_ref, d_ref, member, w_ref):
    for start, size in col_tiles(w_ref.shape[-1]):
        cols = pl.ds(start, size)
        product = nt(d_ref[member], w_ref[0, cols, :])

        @pl.when(member == 0)
        def _(cols=cols, product=product):
            acc_ref[:, cols] = product

        @pl.when(member > 0)
        def _(cols=cols, product=product):
            acc_ref[:, cols] = acc_ref[:, cols] + product


def front_grad_main_kernel(meta_ref, mod_ref, own_ref, got_ref, x_ref, g_ref, w_ref, out_ref, d_ref, acc_ref):
    member = pl.program_id(0)

    @pl.when(member == 0)
    def _():
        d_ref[0] = own_ref[0]
        for i in range(2):
            total = own_ref[1 + i].astype(F32)
            for j in range(got_ref.shape[0]):
                total = total + got_ref[j, i].astype(F32)
            d_ref[1 + i] = total.astype(BF)

    add_product(acc_ref, d_ref, member, w_ref)

    @pl.when(member == 2)
    def _():
        scale = main_vec(meta_ref, mod_ref, 0, 1)

        def body(rows):
            out_ref[rows, :] = norm_back(x_ref[rows, :], g_ref[rows, :], acc_ref[rows, :], scale)

        over_rows(x_ref.shape[0], body)


def front_grad_extra_kernel(
    meta_ref, mod_ref, pack_ref, x_ref, g_ref, w_ref, out_ref, d_ref, acc_ref, ext_ref, *, patches
):
    member = pl.program_id(0)
    rows = x_ref.shape[0]

    @pl.when(member == 0)
    def _():
        ext_ref[...] = jnp.zeros_like(ext_ref)
        for head in range(pack_ref.shape[0]):
            packed = pack_ref[head].astype(F32)
            for i in range(3):
                start, width, value = put_head(unpack3(packed, i), head)
                cols = slice(start, start + width)
                ext_ref[i, :, cols] = ext_ref[i, :, cols] + value
        d_ref[...] = ext_ref[...].astype(BF)

    add_product(acc_ref, d_ref, member, w_ref)

    @pl.when(member == 2)
    def _():
        scale = extra_vec(meta_ref, mod_ref, 0, 1, rows // patches, patches)
        out_ref[...] = norm_back(x_ref[...], g_ref[...], acc_ref[...], scale)


def key_bias(meta_ref, valid_at, clip_at, count, patches, keys_axis):
    tokens = count * patches
    where = lax.broadcasted_iota(jnp.int32, (tokens, tokens), keys_axis)
    other = lax.broadcasted_iota(jnp.int32, (tokens, tokens), 1 - keys_axis)

    def spread(base, axis):
        line = (1, tokens) if axis == 1 else (tokens, 1)
        item = lax.broadcasted_iota(jnp.int32, line, axis) // patches
        out = jnp.zeros(line, jnp.int32)
        for i in range(count):
            out = jnp.where(item == i, meta_ref[base + i], out)
        return out

    admitted = jnp.broadcast_to(spread(valid_at, keys_axis) == 1, (tokens, tokens))
    if clip_at is not None:
        admitted = admitted & (spread(clip_at, 0) == spread(clip_at, 1))
    admitted = admitted & (where % patches == other % patches)
    return jnp.where(admitted | (where == other), 0.0, -1e30).astype(F32)


def temporal_kernel(
    meta_ref, mod_ref, got_ref, le_ref, cm_ref, ce_ref, w_ref, ws_ref,
    outm_ref, oute_ref, sent_ref, ge_ref,
    xm_ref, xe_ref, low_ref, q_ref, k_ref, v_ref, cot_ref, acc_ref, dq_ref, dk_ref, dv_ref,
    *, heads, patches, groups,
):
    columns, block, width = cm_ref.shape
    main, extra = columns * block, le_ref.shape[0]
    frames, extras = main // patches, extra // patches
    last = slice(main, None)
    column = meta_ref[COLUMN]
    chunk = extra // groups
    room = extra_room(chunk)
    devices = got_ref.shape[0]
    small = main // devices

    for source in range(devices):
        read_chunk(got_ref, source, room, xm_ref, source * small, small)
    acc_ref[last] = jnp.zeros_like(acc_ref[last])
    for source in range(devices):
        head, group = source // groups, source % groups
        rows = slice(main + group * chunk, main + (group + 1) * chunk)
        start, size, value = put_head(got_ref[source, :chunk, :].astype(F32), head)
        acc_ref[rows, start : start + size] = acc_ref[rows, start : start + size] + value
    gate_s = extra_vec(meta_ref, mod_ref, 0, 2, extras, patches)
    mixed = nn(acc_ref[last].astype(BF), ws_ref[0])
    xe_ref[...] = gated(le_ref[...], gate_s, mixed).astype(F32)

    mvec = [main_vec(meta_ref, mod_ref, 1, i) for i in range(3)]

    def evec(member):
        return extra_vec(meta_ref, mod_ref, 1, member, extras, patches)

    def body(rows):
        low_ref[rows, :] = modulate(xm_ref[rows, :], mvec[0], mvec[1])

    over_rows(main, body)
    low_ref[last] = modulate(xe_ref[...], evec(0), evec(1))
    for f in range(columns):
        values = cm_ref[column ^ f].astype(F32)
        for i in range(block // patches):
            rows = slice(f * block + i * patches, f * block + (i + 1) * patches)
            valid = meta_ref[LONG_VALID + f * (block // patches) + i] == 1
            cot_ref[rows, :] = jnp.where(valid, values[i * patches : (i + 1) * patches], 0.0)
    values = ce_ref[...].astype(F32)
    for i in range(extras):
        rows = slice(i * patches, (i + 1) * patches)
        there = slice(main + i * patches, main + (i + 1) * patches)
        cot_ref[there, :] = jnp.where(meta_ref[VALID + i] == 1, values[rows], 0.0)

    for i, ref in enumerate((q_ref, k_ref, v_ref)):
        times(ref, low_ref, w_ref, i)
    acc_ref[...] = jnp.zeros_like(acc_ref)
    parts = ((slice(0, main), LONG_VALID, None, frames), (last, VALID, CLIP, extras))
    for rows, valid_at, clip_at, count in parts:
        bias = key_bias(meta_ref, valid_at, clip_at, count, patches, 1)
        heads_forward(acc_ref, q_ref, k_ref, v_ref, rows, rows, bias, heads)
    low_ref[...] = acc_ref[...].astype(BF)
    times(acc_ref, low_ref, w_ref, 3)

    def body(rows):
        acc_ref[rows, :] = xm_ref[rows, :] + mvec[2] * acc_ref[rows, :]
        low_ref[rows, :] = (mvec[2] * cot_ref[rows, :]).astype(BF)

    over_rows(main, body)
    for f in range(columns):
        outm_ref[column ^ f] = acc_ref[f * block : (f + 1) * block, :].astype(BF)
    gate = evec(2)
    oute_ref[...] = gated(xe_ref[...], gate, acc_ref[last])
    low_ref[last] = (gate * cot_ref[last]).astype(BF)

    times(acc_ref, low_ref, w_ref, 3, transposed=True)
    low_ref[...] = acc_ref[...].astype(BF)
    for ref in (dq_ref, dk_ref, dv_ref):
        ref[...] = jnp.zeros_like(ref)
    for rows, valid_at, clip_at, count in parts:
        bias = key_bias(meta_ref, valid_at, clip_at, count, patches, 0)
        heads_backward(dq_ref, dk_ref, dv_ref, q_ref, k_ref, v_ref, low_ref, rows, rows, bias, heads)
    for i, ref in enumerate((dq_ref, dk_ref, dv_ref)):
        low_ref[...] = ref[...].astype(BF)
        times(acc_ref, low_ref, w_ref, i, transposed=True, add=i > 0)

    def body(rows):
        acc_ref[rows, :] = norm_back(xm_ref[rows, :], cot_ref[rows, :], acc_ref[rows, :], mvec[1]).astype(F32)

    over_rows(main, body)
    for dest in range(devices):
        write_chunk(sent_ref, dest, room, acc_ref[dest * small : (dest + 1) * small, :])
    grad = norm_back(xe_ref[...], cot_ref[last], acc_ref[last], evec(1))
    ge_ref[...] = grad
    acc_ref[last] = nt((gate_s * grad.astype(F32)).astype(BF), ws_ref[0])
    for dest in range(devices):
        head, group = dest // groups, dest % groups
        rows = slice(main + group * chunk, main + (group + 1) * chunk)
        sent_ref[dest, :chunk, :] = take_head(acc_ref, rows, head).astype(BF)


def place_kernel(meta_ref, main_ref, extra_ref, out_ref, *, sharers):
    frame_dev, patch_dev, width = main_ref.shape[-3], out_ref.shape[1], out_ref.shape[2]
    for slot in range(out_ref.shape[0]):
        kind = meta_ref[KIND + slot]

        @pl.when(kind == 0)
        def _(slot=slot):
            out_ref[slot] = jnp.zeros_like(out_ref[slot])

        @pl.when(kind == 1)
        def _(slot=slot):
            if not sharers:
                out_ref[slot] = main_ref[slot % frame_dev]
                return
            columns, patch_t = main_ref.shape[0], main_ref.shape[2]
            small = patch_t // sharers
            parts = [main_ref[meta_ref[COLUMN] ^ f, slot % frame_dev].astype(F32) for f in range(columns)]
            pieces = [p[s * small : (s + 1) * small] for s in range(sharers) for p in parts]
            out_ref[slot] = jnp.concatenate(pieces, axis=0).astype(BF)

        @pl.when(kind == 2)
        def _(slot=slot):
            out_ref[slot] = extra_ref[meta_ref[EXTRA_AT + slot]]


SCALARS = pl.BlockSpec(memory_space=pltpu.SMEM)
ANYWHERE = pl.BlockSpec(memory_space=pl.ANY)


def params(steps=0):
    semantics = {"dimension_semantics": ("arbitrary",) * steps} if steps else {}
    return pltpu.CompilerParams(vmem_limit_bytes=VMEM_LIMIT, **semantics)


def cost(flops, elements=0):
    return pl.CostEstimate(flops=int(flops), bytes_accessed=int(elements), transcendentals=0)


def whole(array):
    return pl.BlockSpec(array.shape, lambda *_: (0,) * len(array.shape))


def shape(*dims, dtype=BF):
    return jax.ShapeDtypeStruct(dims, dtype)


def weight_call(kernel, name, operands, weights, members, outs, scratch, weigh):
    width = weights.shape[-1]
    first, count = members
    return pl.pallas_call(
        kernel,
        name=name,
        grid=(count,),
        in_specs=[SCALARS]
        + [whole(a) for a in operands[1:]]
        + [pl.BlockSpec((1, width, width), lambda i: (first + i, 0, 0))],
        out_specs=[spec for spec, _ in outs],
        out_shape=[struct for _, struct in outs],
        scratch_shapes=scratch,
        compiler_params=params(1),
        cost_estimate=cost(weigh * count, 2 * width * width * count),
    )(*operands, weights)


def full(*dims):
    return whole(shape(*dims)), shape(*dims)


def gather(lengths, frame_mask, column, latents, cotangent, columns, sharers):
    _, frame_dev, patch_dev, width = latents.shape
    main = (frame_dev, patch_dev, width)
    patch_t = patch_dev // columns
    extra = shape(columns, EXTRAS, patch_t, width)
    return pl.pallas_call(
        functools.partial(gather_kernel, sharers=sharers),
        name="gather",
        in_specs=[SCALARS] * 3 + [ANYWHERE] * 2,
        out_specs=[SCALARS] + [pl.BlockSpec(memory_space=pltpu.VMEM)] * 4,
        out_shape=[
            shape(TABLE, dtype=jnp.int32), shape(*main), extra, shape(columns, frame_dev, patch_t, width), extra,
        ],
        scratch_shapes=[
            pltpu.VMEM(main, BF),
            pltpu.VMEM((2, EXTRAS, patch_dev, width), BF),
            pltpu.SemaphoreType.DMA((2, EXTRAS + 1)),
        ],
        compiler_params=params(),
    )(lengths, frame_mask, column, latents, cotangent)


def front_main(meta, mod, x, weights):
    rows, width = x.shape
    kv = pl.BlockSpec((1, rows, width), lambda i: (jnp.maximum(i - 1, 0), 0, 0)), shape(2, rows, width)
    return weight_call(
        front_main_kernel, "front_main", (meta, mod, x), weights, (0, 3),
        [full(rows, width), kv], [pltpu.VMEM((rows, width), BF)], 2 * rows * width**2,
    )


def front_extra(meta, mod, x, weights, heads, patches):
    rows, width = x.shape
    return weight_call(
        functools.partial(front_extra_kernel, patches=patches), "front_extra", (meta, mod, x), weights, (0, 3),
        [full(heads, rows, 256)], [pltpu.VMEM((rows, width), BF), pltpu.VMEM((3, rows, width), F32)],
        4 * rows * width**2,
    )[0]


def back_main(meta, mod, x, o, extra, weights, columns):
    rows, width = x.shape
    devices, chunk, _ = extra.shape
    sent = full(devices, extra_room(chunk) + rows * width // (devices * 128), 128)
    return weight_call(
        functools.partial(back_main_kernel, columns=columns), "back_main", (meta, mod, x, o, extra), weights,
        (3, 1), [sent], [pltpu.VMEM((rows, width), F32)], 3 * rows * width**2,
    )[0]


def back_grad_main(meta, mod, got, weights, rows, columns, room):
    width = weights.shape[-1]
    return weight_call(
        functools.partial(back_grad_main_kernel, columns=columns, room=room), "back_grad_main",
        (meta, mod, got), weights, (3, 1), [full(rows, width)] * 2,
        [pltpu.VMEM((rows, width), BF), pltpu.VMEM((rows, width), F32)], 3 * rows * width**2,
    )


def front_grad_main(meta, mod, own, got, x, g, weights):
    rows, width = x.shape
    return weight_call(
        front_grad_main_kernel, "front_grad_main", (meta, mod, own, got, x, g), weights, (0, 3),
        [full(rows, width)], [pltpu.VMEM((3, rows, width), BF), pltpu.VMEM((rows, width), F32)],
        3 * rows * width**2,
    )[0]


def front_grad_extra(meta, mod, pack, x, g, weights, patches):
    rows, width = x.shape
    return weight_call(
        functools.partial(front_grad_extra_kernel, patches=patches), "front_grad_extra",
        (meta, mod, pack, x, g), weights, (0, 3), [full(rows, width)],
        [pltpu.VMEM((3, rows, width), BF), pltpu.VMEM((rows, width), F32), pltpu.VMEM((3, rows, width), F32)],
        4 * rows * width**2,
    )[0]


def attend(q, kv, other, heads):
    rows, width = q.shape
    keys = rows * (other.shape[0] + 1)
    return pl.pallas_call(
        functools.partial(attend_kernel, heads=heads),
        name="attend",
        out_shape=shape(rows, width),
        scratch_shapes=[
            pltpu.VMEM((keys, width), BF),
            pltpu.VMEM((keys, width), BF),
            pltpu.VMEM((rows, width), F32),
        ],
        compiler_params=params(),
        cost_estimate=cost(6e9),
    )(q, kv, other)


def extra_attend(pack):
    return pl.pallas_call(
        extra_attend_kernel, name="extra_attend", out_shape=shape(*pack.shape[:-1], 128),
        compiler_params=params(), cost_estimate=cost(4e9),
    )(pack)


def extra_attend_back(pack, got):
    return pl.pallas_call(
        extra_attend_back_kernel, name="extra_attend_back", out_shape=shape(*pack.shape),
        compiler_params=params(), cost_estimate=cost(6e9),
    )(pack, got)


def attend_back(q, kv, other, do, heads):
    rows, width = q.shape
    keys = rows * (other.shape[0] + 1)
    return pl.pallas_call(
        functools.partial(attend_back_kernel, heads=heads),
        name="attend_back",
        out_shape=[shape(3, rows, width), shape(*other.shape)],
        scratch_shapes=[
            pltpu.VMEM((keys, width), BF),
            pltpu.VMEM((keys, width), BF),
            pltpu.VMEM((rows, width), F32),
            pltpu.VMEM((keys, width), F32),
            pltpu.VMEM((keys, width), F32),
        ],
        compiler_params=params(),
        cost_estimate=cost(14e9),
    )(q, kv, other, do)


def temporal(meta, mod, got, le, cm, ce, weights, last_weight, heads, patches, groups):
    columns, block, width = cm.shape
    main, extra = columns * block, le.shape[0]
    rows = main + extra
    operands = (mod, got, le, cm, ce, weights, last_weight)
    return pl.pallas_call(
        functools.partial(temporal_kernel, heads=heads, patches=patches, groups=groups),
        name="temporal",
        in_specs=[SCALARS] + [whole(a) for a in operands],
        out_shape=[shape(*cm.shape), shape(extra, width), shape(*got.shape), shape(extra, width)],
        scratch_shapes=[pltpu.VMEM((main, width), F32), pltpu.VMEM((extra, width), F32)]
        + [pltpu.VMEM((rows, width), BF)] * 4
        + [pltpu.VMEM((rows, width), F32)] * 5,
        compiler_params=params(),
        cost_estimate=cost(34e9),
    )(meta, *operands)


def place(meta, main, extra, slots, sharers):
    return pl.pallas_call(
        functools.partial(place_kernel, sharers=sharers),
        name="place",
        in_specs=[SCALARS, whole(main), whole(extra)],
        out_shape=shape(slots, *extra.shape[1:]),
        compiler_params=params(),
        cost_estimate=cost(3e9),
    )(meta, main, extra)


def local(latents, cotangent, spatial_weights, temporal_weights, modulation, lengths, frame_mask):
    clips, frame_dev, patch_dev, width = latents.shape
    heads = width // HEAD
    frame_axis, patch_axis = lax.axis_size("frame"), lax.axis_size("patch")
    everyone = ("frame", "patch")
    frames = frame_dev * frame_axis
    sharers = patch_axis // frame_dev
    sub = patch_dev // sharers
    small = sub // frame_axis
    patch_t = patch_dev // frame_axis
    heads_col = heads // frame_axis
    groups = patch_axis // heads_col
    group_extras = -(-EXTRAS // groups)
    extras = groups * group_extras

    def swap(x, axis):
        return lax.all_to_all(x, axis, split_axis=0, concat_axis=0, tiled=True)

    column = lax.axis_index("frame")
    sources = -(-(EXTRAS - clips + 2) // frame_dev)
    main_rows = frame_dev * patch_dev

    def cross(blocks):
        got = [blocks[0]]
        for m in range(1, frame_axis):
            got.append(lax.ppermute(blocks[m], "frame", [(f, f ^ m) for f in range(frame_axis)]))
        return jnp.stack(got)

    def extras_out(x, meta):
        found = []
        for source in range(sources):
            mine = jnp.where(column == source, x[source], jnp.zeros((), BF))
            for dest in range(frame_axis):
                if dest != source:
                    mine = mine + lax.ppermute(x[dest], "frame", [(source, dest)])
            found.append(mine)
        out = found[0]
        for source in range(1, sources):
            frame = meta[FRAME : FRAME + EXTRAS][:, None, None]
            out = jnp.where(frame // frame_dev == source, found[source], out)
        out = out.reshape(EXTRAS * patch_t, width)
        return jnp.concatenate([out, jnp.zeros(((extras - EXTRAS) * patch_t, width), BF)])

    def extras_home(x):
        x = x.reshape(extras, patch_t, width)[:EXTRAS]
        found = []
        for source in range(frame_axis):
            mine = jnp.where(column == source, x, jnp.zeros((), BF))
            for dest in range(sources):
                if dest != source:
                    mine = mine + lax.ppermute(x, "frame", [(source, dest)])
            found.append(mine)
        return jnp.transpose(jnp.stack(found), (1, 0, 2, 3)).reshape(EXTRAS, patch_dev, width)

    meta, main_home, extra_home, cot_main, cot_extra = gather(
        lengths, frame_mask, column.reshape(1).astype(jnp.int32), latents, cotangent, frame_axis, sharers
    )
    main_s = swap(main_home.reshape(patch_axis, sub, width), "patch").reshape(main_rows, width)
    extra_t = extras_out(extra_home, meta)
    cot_m = cross(cot_main.reshape(frame_axis, frame_dev * patch_t, width))
    cot_e = extras_out(cot_extra, meta)

    def rotate(array, by):
        perm = []
        for p in range(patch_axis):
            base = p // sharers * sharers
            perm.append((p, base + (p - base + by) % sharers))
        return lax.ppermute(array, "patch", perm)

    mod = modulation
    chunk = group_extras * patch_t
    pack = front_extra(meta, mod, extra_t, spatial_weights, heads, patch_t)
    pack_got = swap(pack.reshape(frame_axis * patch_axis, chunk, 256), everyone)
    pack_got = pack_got.reshape(frame_axis * patch_axis, group_extras, patch_t, 256)
    q, kv = front_main(meta, mod, main_s, spatial_weights)
    other = jnp.stack([rotate(kv, by) for by in range(1, sharers)])
    attended = attend(q, kv, other, heads)
    extra_o = extra_attend(pack_got).reshape(frame_axis * patch_axis, chunk, 128)
    sent = back_main(meta, mod, main_s, attended, extra_o, spatial_weights, frame_axis)

    out_m, out_e, sent, grad_e = temporal(
        meta, mod, swap(sent, everyone), extra_t, cot_m, cot_e, temporal_weights, spatial_weights[3:],
        heads, patch_t, groups,
    )

    grads = swap(sent, everyone)
    do_main, grad_s = back_grad_main(
        meta, mod, grads, spatial_weights, main_rows, frame_axis, extra_room(chunk)
    )
    own, sent = attend_back(q, kv, other, do_main, heads)
    got = jnp.stack([rotate(sent[by - 1], -by) for by in range(1, sharers)])
    dpack = extra_attend_back(pack_got, grads)
    dpack = swap(dpack.reshape(frame_axis * patch_axis, chunk, 256), everyone)
    dpack = dpack.reshape(heads, extras * patch_t, 256)
    lat_m = front_grad_main(meta, mod, own, got, main_s, grad_s, spatial_weights)
    lat_e = front_grad_extra(meta, mod, dpack, extra_t, grad_e, spatial_weights, patch_t)
    lat_main = swap(lat_m.reshape(patch_axis, sub, width), "patch").reshape(frame_dev, patch_dev, width)

    out_main = cross(out_m).reshape(frame_axis, frame_dev, patch_t, width)
    slots = clips * frame_dev
    output = place(meta, out_main, extras_home(out_e), slots, sharers)
    grad = place(meta, lat_main, extras_home(lat_e), slots, 0)
    return output.reshape(latents.shape), grad.reshape(latents.shape)


def solution(mesh):
    tokens = P(None, "frame", "patch", None)
    in_specs = (tokens, tokens, P(), P(), P(), P(), P())
    return jax.shard_map(local, mesh=mesh, in_specs=in_specs, out_specs=(tokens, tokens), check_vma=False)
```

```python
import functools
import math

import jax
import jax.numpy as jnp
from jax import lax
from jax.experimental import pallas as pl
from jax.experimental.pallas import tpu as pltpu
from jax.sharding import PartitionSpec as P

HEAD = 72
EXTRAS = 5
SCALE = HEAD ** -0.5
SCALE2 = SCALE * math.log2(math.e)
BF = jnp.bfloat16
F32 = jnp.float32
VMEM_LIMIT = 56 * 1024 * 1024
LONG, COLUMN, CLIP, FRAME, VALID, LONG_VALID, KIND, EXTRA_AT, TABLE = 0, 1, 8, 16, 24, 32, 48, 64, 80


def nn(a, b):
    return lax.dot_general(a, b, (((1,), (0,)), ((), ())), preferred_element_type=F32)


def nt(a, b):
    return lax.dot_general(a, b, (((1,), (1,)), ((), ())), preferred_element_type=F32)


def tn(a, b):
    return lax.dot_general(a, b, (((0,), (0,)), ((), ())), preferred_element_type=F32)


def window(head):
    start = head * HEAD // 128 * 128
    offset = head * HEAD - start
    return start, offset, 128 if offset + HEAD <= 128 else 256


def lanes_in(width, low, high):
    lane = lax.broadcasted_iota(jnp.int32, (1, width), 1)
    return (lane >= low) & (lane < high)


def masked(x, keep):
    return jnp.where(keep, x, jnp.zeros((), x.dtype))


def take_head(x_ref, rows, head):
    start, offset, width = window(head)
    part = x_ref[rows, start : start + width].astype(F32)
    if offset:
        part = pltpu.roll(part, width - offset, 1)
    return masked(part[:, :128], lanes_in(128, 0, HEAD))


def put_head(value, head):
    start, offset, width = window(head)
    if width == 256:
        value = jnp.concatenate([value, jnp.zeros_like(value)], axis=1)
    if offset:
        value = pltpu.roll(value, offset, 1)
    return start, width, value


def wide(value):
    return jnp.concatenate([value, jnp.zeros_like(value)], axis=1)


def pack3(parts):
    first, second, third = parts
    return wide(first) + pltpu.roll(wide(second), HEAD, 1) + pltpu.roll(wide(third), 2 * HEAD, 1)


def unpack3(packed, member):
    if member:
        packed = pltpu.roll(packed, 256 - member * HEAD, 1)
    return masked(packed[:, :128], lanes_in(128, 0, HEAD))


def main_vec(meta_ref, mod_ref, block, member):
    return mod_ref[block, member, pl.ds(meta_ref[LONG], 1), :]


def extra_vec(meta_ref, mod_ref, block, member, extras, patches):
    rows = [mod_ref[block, member, pl.ds(meta_ref[CLIP + e], 1), :] for e in range(extras)]
    return jnp.concatenate([jnp.broadcast_to(r, (patches, r.shape[1])) for r in rows], axis=0)


def normed_of(x):
    average = jnp.mean(x, axis=-1, keepdims=True)
    centred = x - average
    variance = jnp.mean(centred * centred, axis=-1, keepdims=True)
    inverse = lax.rsqrt(variance + 1e-06)
    return centred * inverse, inverse


def over_rows(count, body):
    size = math.gcd(count, 64)
    if count == size:
        body(slice(0, count))
        return

    def step(i, carry):
        body(pl.ds(pl.multiple_of(i * size, size), size))
        return carry

    lax.fori_loop(0, count // size, step, 0)


def modulate(x, shift, scale):
    normed, _ = normed_of(x.astype(F32))
    return (normed * (1.0 + scale) + shift).astype(BF)


def norm_back(x, grad, dmod, scale):
    normed, inverse = normed_of(x.astype(F32))
    dnormed = dmod * (1.0 + scale)
    mean_d = jnp.mean(dnormed, axis=-1, keepdims=True)
    mean_dn = jnp.mean(dnormed * normed, axis=-1, keepdims=True)
    dx = (inverse * (dnormed - mean_d - normed * mean_dn)).astype(BF)
    return (dx.astype(F32) + grad.astype(F32)).astype(BF)


def gated(x, gate, mixed):
    return (x.astype(F32) + gate * mixed).astype(BF)


def col_tiles(width):
    whole, tiles = 512, []
    start = 0
    while start < width:
        tiles.append((start, min(whole, width - start)))
        start += whole
    return tiles


def times(dest_ref, x_ref, w_ref, member, transposed=False, add=False):
    for start, size in col_tiles(w_ref.shape[-1]):
        cols = pl.ds(start, size)
        if transposed:
            product = nt(x_ref[...], w_ref[member, cols, :])
        else:
            product = nn(x_ref[...], w_ref[member, :, cols])
        if add:
            product = dest_ref[:, cols] + product
        dest_ref[:, cols] = product.astype(dest_ref.dtype)


def heads_forward(o_ref, q_ref, k_ref, v_ref, parts, bias, heads):
    for head in range(heads):
        start, offset, width = window(head)
        cols = slice(start, start + width)
        keep = lanes_in(width, offset, offset + HEAD)
        for rows in parts:
            scores = nt(masked(q_ref[rows, cols], keep), k_ref[rows, cols])
            if bias is not None:
                scores = scores + bias
            exponent = jnp.exp2((scores - jnp.max(scores, axis=-1, keepdims=True)) * SCALE2)
            total = jnp.sum(exponent, axis=-1, keepdims=True)
            result = nn(exponent.astype(BF), masked(v_ref[rows, cols], keep)) * (1.0 / total)
            o_ref[rows, cols] = o_ref[rows, cols] + result


def softmax_grads(q, do, k, v, bias):
    scores = nt(k, q)
    if bias is not None:
        scores = scores + bias
    exponent = jnp.exp2((scores - jnp.max(scores, axis=0, keepdims=True)) * SCALE2)
    prob = exponent * (1.0 / jnp.sum(exponent, axis=0, keepdims=True))
    dprob = nt(v, do)
    delta = jnp.sum(prob * dprob, axis=0, keepdims=True)
    dscores = prob * (dprob - delta) * SCALE
    return dscores.astype(BF), prob.astype(BF)


def heads_backward(dq_ref, dk_ref, dv_ref, q_ref, k_ref, v_ref, do_ref, parts, bias, heads):
    for head in range(heads):
        start, offset, width = window(head)
        cols = slice(start, start + width)
        keep = lanes_in(width, offset, offset + HEAD)
        for rows in parts:
            q = masked(q_ref[rows, cols], keep)
            do = masked(do_ref[rows, cols], keep)
            k = masked(k_ref[rows, cols], keep)
            dscores, prob = softmax_grads(q, do, k, v_ref[rows, cols], bias)
            dv_ref[rows, cols] = dv_ref[rows, cols] + nn(prob, do)
            dk_ref[rows, cols] = dk_ref[rows, cols] + nn(dscores, q)
            dq_ref[rows, cols] = dq_ref[rows, cols] + tn(dscores, k)


def gather_kernel(
    lengths_ref, mask_ref, column_ref, latents_ref, cotangent_ref,
    meta_ref, main_ref, extra_ref, cot_main_ref, cot_extra_ref,
    main_in, extra_in, sems, *, sharers,
):
    clips, frame_dev, patch_dev, width = latents_ref.shape
    frames = mask_ref.shape[1]
    frame_axis = frames // frame_dev
    patch_t = patch_dev // frame_axis
    small, sub = patch_t // sharers, patch_dev // sharers
    column = column_ref[0]
    long = jnp.int32(0)
    for c in range(clips):
        long = long + jnp.where(lengths_ref[c] == frames, c, 0)
    for i in range(TABLE):
        meta_ref[i] = 0
    meta_ref[LONG] = long
    meta_ref[COLUMN] = column
    count = jnp.int32(0)
    for c in range(clips):
        for f in range(EXTRAS - clips + 2):
            used = (c != long) & (f < lengths_ref[c])
            at = jnp.where(used, count, EXTRAS)
            meta_ref[CLIP + at] = jnp.int32(c)
            meta_ref[FRAME + at] = jnp.int32(f)
            meta_ref[VALID + at] = mask_ref[c, f]
            count = count + used.astype(jnp.int32)
    for e in range(EXTRAS, 8):
        for row in (CLIP, FRAME, VALID):
            meta_ref[row + e] = 0

    copies = []
    pairs = ((latents_ref, main_ref), (cotangent_ref, main_in))
    for i, (source, main) in enumerate(pairs):
        copies.append(pltpu.make_async_copy(source.at[long], main, sems.at[i, EXTRAS]))
        copies[-1].start()
        for e in range(EXTRAS):
            frame = lax.rem(meta_ref[FRAME + e], frame_dev)
            part = source.at[meta_ref[CLIP + e], frame]
            copies.append(pltpu.make_async_copy(part, extra_in.at[i, e], sems.at[i, e]))
            copies[-1].start()

    for f in range(frames):
        meta_ref[LONG_VALID + f] = mask_ref[long, f]
    for c in range(clips):
        for f in range(frame_dev):
            frame = column * frame_dev + f
            valid = (frame < lengths_ref[c]) & (mask_ref[c, frame] == 1)
            meta_ref[KIND + c * frame_dev + f] = jnp.where(valid, jnp.where(c == long, 1, 2), 0)
    for e in range(EXTRAS):
        local_frame = meta_ref[FRAME + e] - column * frame_dev
        here = (local_frame >= 0) & (local_frame < frame_dev)
        slot = meta_ref[CLIP + e] * frame_dev + jnp.where(here, local_frame, 0)

        @pl.when(here)
        def _(e=e, slot=slot):
            meta_ref[EXTRA_AT + slot] = jnp.int32(e)

    for copy in copies:
        copy.wait()
    for i, out in enumerate((extra_ref, cot_extra_ref)):
        for e in range(EXTRAS):
            rows = extra_in[i, e].astype(F32)
            for f in range(frame_axis):
                out[f, e] = rows[f * patch_t : (f + 1) * patch_t].astype(BF)
    for j in range(frame_dev):
        rows = main_in[j].astype(F32)
        for f in range(frame_axis):
            starts = [s * sub + f * small for s in range(sharers)]
            part = jnp.concatenate([rows[at : at + small] for at in starts], axis=0)
            cot_main_ref[f ^ column, j] = part.astype(BF)


def front_main_kernel(meta_ref, mod_ref, x_ref, w_ref, q_ref, kv_ref, low_ref):
    member = pl.program_id(0)

    @pl.when(member == 0)
    def _():
        shift, scale = [main_vec(meta_ref, mod_ref, 0, i) for i in range(2)]

        def body(rows):
            low_ref[rows, :] = modulate(x_ref[rows, :], shift, scale)

        over_rows(x_ref.shape[0], body)
        times(q_ref, low_ref, w_ref, 0)

    @pl.when(member > 0)
    def _():
        times(kv_ref.at[0], low_ref, w_ref, 0)


def front_extra_kernel(meta_ref, mod_ref, x_ref, w_ref, pack_ref, low_ref, out_ref, *, patches):
    member = pl.program_id(0)
    rows = x_ref.shape[0]

    @pl.when(member == 0)
    def _():
        shift, scale = [extra_vec(meta_ref, mod_ref, 0, i, rows // patches, patches) for i in range(2)]
        low_ref[...] = modulate(x_ref[...], shift, scale)

    for start, size in col_tiles(w_ref.shape[-1]):
        cols = pl.ds(start, size)
        out_ref[member, :, cols] = nn(low_ref[...], w_ref[0, :, cols])

    @pl.when(member == 2)
    def _():
        for head in range(pack_ref.shape[0]):
            parts = [take_head(out_ref.at[i], slice(None), head) for i in range(3)]
            pack_ref[head] = pack3(parts).astype(BF)


def fill_keys(k_ref, v_ref, kv_ref, other_ref):
    rows = kv_ref.shape[1]
    k_ref[:rows] = kv_ref[0]
    v_ref[:rows] = kv_ref[1]
    for i in range(other_ref.shape[0]):
        k_ref[(i + 1) * rows : (i + 2) * rows] = other_ref[i, 0]
        v_ref[(i + 1) * rows : (i + 2) * rows] = other_ref[i, 1]


def attend_kernel(q_ref, kv_ref, other_ref, o_ref, k_ref, v_ref, acc_ref, *, heads):
    fill_keys(k_ref, v_ref, kv_ref, other_ref)
    acc_ref[...] = jnp.zeros_like(acc_ref)
    heads_forward(acc_ref, q_ref, k_ref, v_ref, [slice(None)], None, heads)
    o_ref[...] = acc_ref[...].astype(BF)


def extra_rows(ref, index):
    part = ref[:, index]
    return part.reshape(part.shape[0] * part.shape[1], part.shape[2])


def extra_attend_kernel(pack_ref, main_ref, sent_ref):
    devices, _, patches, _ = pack_ref.shape
    room = sent_ref.shape[1] - main_ref.shape[1]
    sent_ref[:, room:, :] = main_ref[...]
    for index in range(pack_ref.shape[1]):
        packed = extra_rows(pack_ref, index).astype(F32)
        q, k, v = [unpack3(packed, i).astype(BF) for i in range(3)]
        scores = nt(q, k)
        exponent = jnp.exp2((scores - jnp.max(scores, axis=-1, keepdims=True)) * SCALE2)
        total = jnp.sum(exponent, axis=-1, keepdims=True)
        result = nn(exponent.astype(BF), v) * (1.0 / total)
        result = result.reshape(devices, patches, 128).astype(BF)
        sent_ref[:, index * patches : (index + 1) * patches, :] = result


def extra_attend_back_kernel(pack_ref, got_ref, grad_ref):
    patches = pack_ref.shape[2]
    for index in range(pack_ref.shape[1]):
        packed = extra_rows(pack_ref, index).astype(F32)
        q, k, v = [unpack3(packed, i).astype(BF) for i in range(3)]
        do = got_ref[:, index * patches : (index + 1) * patches, :].astype(F32)
        do = do.reshape(do.shape[0] * patches, 128).astype(BF)
        dscores, prob = softmax_grads(q, do, k, v, None)
        out = pack3([tn(dscores, k), nn(dscores, q), nn(prob, do)]).astype(BF)
        grad_ref[:, index] = out.reshape(grad_ref.shape[0], grad_ref.shape[2], 256)


def extra_room(rows):
    return -(-rows // 16) * 16


def write_chunk(sent_ref, dest, room, value):
    pieces = [value[:, at : at + 128] for at in range(0, value.shape[1], 128)]
    rows = value.shape[0] * len(pieces)
    sent_ref[dest, room : room + rows, :] = jnp.concatenate(pieces, axis=0).astype(BF)


def read_chunk(got_ref, source, room, out_ref, row, small):
    count = out_ref.shape[1] // 128
    value = got_ref[source, room : room + small * count, :].astype(F32)
    for i in range(count):
        out_ref[row : row + small, i * 128 : (i + 1) * 128] = value[i * small : (i + 1) * small]


def back_main_kernel(meta_ref, mod_ref, x_ref, o_ref, w_ref, sent_ref, acc_ref, *, columns):
    times(acc_ref, o_ref, w_ref, 0)
    gate = main_vec(meta_ref, mod_ref, 0, 2)

    def body(rows):
        acc_ref[rows, :] = x_ref[rows, :].astype(F32) + gate * acc_ref[rows, :]

    over_rows(x_ref.shape[0], body)
    devices = sent_ref.shape[0]
    small = x_ref.shape[0] // devices
    patch_axis = devices // columns
    for p in range(patch_axis):
        for f in range(columns):
            row = (p * columns + f) * small
            write_chunk(sent_ref, f * patch_axis + p, 0, acc_ref[row : row + small, :])


def back_grad_main_kernel(meta_ref, mod_ref, got_ref, w_ref, do_ref, g_ref, low_ref, acc_ref, *, columns, room):
    devices = got_ref.shape[0]
    small = g_ref.shape[0] // devices
    patch_axis = devices // columns
    for p in range(patch_axis):
        for f in range(columns):
            row = (p * columns + f) * small
            read_chunk(got_ref, f * patch_axis + p, room, acc_ref, row, small)
    gate = main_vec(meta_ref, mod_ref, 0, 2)

    def body(rows):
        g_ref[rows, :] = acc_ref[rows, :].astype(BF)
        low_ref[rows, :] = (gate * acc_ref[rows, :]).astype(BF)

    over_rows(g_ref.shape[0], body)
    times(do_ref, low_ref, w_ref, 0, transposed=True)


def attend_back_kernel(
    q_ref, kv_ref, other_ref, do_ref, own_ref, sent_ref, k_ref, v_ref, dq_ref, dk_ref, dv_ref, *, heads
):
    rows = kv_ref.shape[1]
    fill_keys(k_ref, v_ref, kv_ref, other_ref)
    for ref in (dq_ref, dk_ref, dv_ref):
        ref[...] = jnp.zeros_like(ref)
    heads_backward(dq_ref, dk_ref, dv_ref, q_ref, k_ref, v_ref, do_ref, [slice(None)], None, heads)
    own_ref[0] = dq_ref[...].astype(BF)
    own_ref[1] = dk_ref[:rows].astype(BF)
    own_ref[2] = dv_ref[:rows].astype(BF)
    for i in range(other_ref.shape[0]):
        sent_ref[i, 0] = dk_ref[(i + 1) * rows : (i + 2) * rows].astype(BF)
        sent_ref[i, 1] = dv_ref[(i + 1) * rows : (i + 2) * rows].astype(BF)


def add_product(acc_ref, d_ref, member, w_ref):
    for start, size in col_tiles(w_ref.shape[-1]):
        cols = pl.ds(start, size)
        product = nt(d_ref[member], w_ref[0, cols, :])

        @pl.when(member == 0)
        def _(cols=cols, product=product):
            acc_ref[:, cols] = product

        @pl.when(member > 0)
        def _(cols=cols, product=product):
            acc_ref[:, cols] = acc_ref[:, cols] + product


def front_grad_main_kernel(meta_ref, mod_ref, own_ref, got_ref, x_ref, g_ref, w_ref, out_ref, d_ref, acc_ref):
    member = pl.program_id(0)

    @pl.when(member == 0)
    def _():
        d_ref[0] = own_ref[0]
        for i in range(2):
            total = own_ref[1 + i].astype(F32)
            for j in range(got_ref.shape[0]):
                total = total + got_ref[j, i].astype(F32)
            d_ref[1 + i] = total.astype(BF)

    add_product(acc_ref, d_ref, member, w_ref)

    @pl.when(member == 2)
    def _():
        scale = main_vec(meta_ref, mod_ref, 0, 1)

        def body(rows):
            out_ref[rows, :] = norm_back(x_ref[rows, :], g_ref[rows, :], acc_ref[rows, :], scale)

        over_rows(x_ref.shape[0], body)


def front_grad_extra_kernel(
    meta_ref, mod_ref, pack_ref, x_ref, g_ref, w_ref, out_ref, d_ref, acc_ref, ext_ref, *, patches
):
    member = pl.program_id(0)
    rows = x_ref.shape[0]

    @pl.when(member == 0)
    def _():
        ext_ref[...] = jnp.zeros_like(ext_ref)
        for head in range(pack_ref.shape[0]):
            packed = pack_ref[head].astype(F32)
            for i in range(3):
                start, width, value = put_head(unpack3(packed, i), head)
                cols = slice(start, start + width)
                ext_ref[i, :, cols] = ext_ref[i, :, cols] + value
        d_ref[...] = ext_ref[...].astype(BF)

    add_product(acc_ref, d_ref, member, w_ref)

    @pl.when(member == 2)
    def _():
        scale = extra_vec(meta_ref, mod_ref, 0, 1, rows // patches, patches)
        out_ref[...] = norm_back(x_ref[...], g_ref[...], acc_ref[...], scale)


def key_bias(meta_ref, valid_at, clip_at, count, patches, keys_axis):
    tokens = count * patches
    where = lax.broadcasted_iota(jnp.int32, (tokens, tokens), keys_axis)
    other = lax.broadcasted_iota(jnp.int32, (tokens, tokens), 1 - keys_axis)

    def spread(base, axis):
        line = (1, tokens) if axis == 1 else (tokens, 1)
        item = lax.broadcasted_iota(jnp.int32, line, axis) // patches
        out = jnp.zeros(line, jnp.int32)
        for i in range(count):
            out = jnp.where(item == i, meta_ref[base + i], out)
        return out

    admitted = jnp.broadcast_to(spread(valid_at, keys_axis) == 1, (tokens, tokens))
    if clip_at is not None:
        admitted = admitted & (spread(clip_at, 0) == spread(clip_at, 1))
    admitted = admitted & (where % patches == other % patches)
    return jnp.where(admitted | (where == other), 0.0, -1e30).astype(F32)


def temporal_kernel(
    meta_ref, mod_ref, got_ref, le_ref, cm_ref, ce_ref, w_ref, ws_ref,
    outm_ref, oute_ref, sent_ref, ge_ref,
    xm_ref, xe_ref, low_ref, q_ref, k_ref, v_ref, cot_ref, acc_ref, dq_ref, dk_ref, dv_ref,
    *, heads, patches, groups,
):
    columns, block, width = cm_ref.shape
    main, extra = columns * block, le_ref.shape[0]
    frames, extras = main // patches, extra // patches
    last = slice(main, None)
    column = meta_ref[COLUMN]
    chunk = extra // groups
    room = extra_room(chunk)
    devices = got_ref.shape[0]
    small = main // devices

    sharers = patches // small
    part = frames * small

    def token(source):
        return source % sharers * part + source // sharers * small

    for source in range(devices):
        read_chunk(got_ref, source, room, xm_ref, token(source), small)
    acc_ref[last] = jnp.zeros_like(acc_ref[last])
    for source in range(devices):
        head, group = source // groups, source % groups
        rows = slice(main + group * chunk, main + (group + 1) * chunk)
        start, size, value = put_head(got_ref[source, :chunk, :].astype(F32), head)
        acc_ref[rows, start : start + size] = acc_ref[rows, start : start + size] + value
    gate_s = extra_vec(meta_ref, mod_ref, 0, 2, extras, patches)
    mixed = nn(acc_ref[last].astype(BF), ws_ref[0])
    xe_ref[...] = gated(le_ref[...], gate_s, mixed).astype(F32)

    mvec = [main_vec(meta_ref, mod_ref, 1, i) for i in range(3)]

    def evec(member):
        return extra_vec(meta_ref, mod_ref, 1, member, extras, patches)

    def body(rows):
        low_ref[rows, :] = modulate(xm_ref[rows, :], mvec[0], mvec[1])

    over_rows(main, body)
    low_ref[last] = modulate(xe_ref[...], evec(0), evec(1))
    each = frames // columns
    for f in range(columns):
        values = cm_ref[column ^ f].astype(F32)
        for j in range(each):
            valid = meta_ref[LONG_VALID + f * each + j] == 1
            for g in range(sharers):
                rows = pl.ds(token((f * each + j) * sharers + g), small)
                at = j * patches + g * small
                cot_ref[rows, :] = jnp.where(valid, values[at : at + small], 0.0)
    values = ce_ref[...].astype(F32)
    for i in range(extras):
        rows = slice(i * patches, (i + 1) * patches)
        there = slice(main + i * patches, main + (i + 1) * patches)
        cot_ref[there, :] = jnp.where(meta_ref[VALID + i] == 1, values[rows], 0.0)

    for i, ref in enumerate((q_ref, k_ref, v_ref)):
        times(ref, low_ref, w_ref, i)
    acc_ref[...] = jnp.zeros_like(acc_ref)
    main_parts = [slice(g * part, (g + 1) * part) for g in range(sharers)]
    extra_parts = [last]
    kinds = ((main_parts, LONG_VALID, None, frames, small), (extra_parts, VALID, CLIP, extras, patches))
    for parts, valid_at, clip_at, count, each_patches in kinds:
        bias = key_bias(meta_ref, valid_at, clip_at, count, each_patches, 1)
        heads_forward(acc_ref, q_ref, k_ref, v_ref, parts, bias, heads)
    low_ref[...] = acc_ref[...].astype(BF)
    times(acc_ref, low_ref, w_ref, 3)

    def body(rows):
        acc_ref[rows, :] = xm_ref[rows, :] + mvec[2] * acc_ref[rows, :]
        low_ref[rows, :] = (mvec[2] * cot_ref[rows, :]).astype(BF)

    over_rows(main, body)
    for f in range(columns):
        starts = [token(f * each * sharers + i) for i in range(each * sharers)]
        pieces = [acc_ref[at : at + small, :] for at in starts]
        outm_ref[column ^ f] = jnp.concatenate(pieces, axis=0).astype(BF)
    gate = evec(2)
    oute_ref[...] = gated(xe_ref[...], gate, acc_ref[last])
    low_ref[last] = (gate * cot_ref[last]).astype(BF)

    times(acc_ref, low_ref, w_ref, 3, transposed=True)
    low_ref[...] = acc_ref[...].astype(BF)
    for ref in (dq_ref, dk_ref, dv_ref):
        ref[...] = jnp.zeros_like(ref)
    for parts, valid_at, clip_at, count, each_patches in kinds:
        bias = key_bias(meta_ref, valid_at, clip_at, count, each_patches, 0)
        heads_backward(dq_ref, dk_ref, dv_ref, q_ref, k_ref, v_ref, low_ref, parts, bias, heads)
    for i, ref in enumerate((dq_ref, dk_ref, dv_ref)):
        low_ref[...] = ref[...].astype(BF)
        times(acc_ref, low_ref, w_ref, i, transposed=True, add=i > 0)

    def body(rows):
        acc_ref[rows, :] = norm_back(xm_ref[rows, :], cot_ref[rows, :], acc_ref[rows, :], mvec[1]).astype(F32)

    over_rows(main, body)
    for dest in range(devices):
        write_chunk(sent_ref, dest, room, acc_ref[token(dest) : token(dest) + small, :])
    grad = norm_back(xe_ref[...], cot_ref[last], acc_ref[last], evec(1))
    ge_ref[...] = grad
    acc_ref[last] = nt((gate_s * grad.astype(F32)).astype(BF), ws_ref[0])
    for dest in range(devices):
        head, group = dest // groups, dest % groups
        rows = slice(main + group * chunk, main + (group + 1) * chunk)
        sent_ref[dest, :chunk, :] = take_head(acc_ref, rows, head).astype(BF)


def place_kernel(meta_ref, main_ref, extra_ref, out_ref, *, sharers):
    frame_dev, patch_dev, width = main_ref.shape[-3], out_ref.shape[1], out_ref.shape[2]
    for slot in range(out_ref.shape[0]):
        kind = meta_ref[KIND + slot]

        @pl.when(kind == 0)
        def _(slot=slot):
            out_ref[slot] = jnp.zeros_like(out_ref[slot])

        @pl.when(kind == 1)
        def _(slot=slot):
            if not sharers:
                out_ref[slot] = main_ref[slot % frame_dev]
                return
            columns, patch_t = main_ref.shape[0], main_ref.shape[2]
            small = patch_t // sharers
            parts = [main_ref[meta_ref[COLUMN] ^ f, slot % frame_dev].astype(F32) for f in range(columns)]
            pieces = [p[s * small : (s + 1) * small] for s in range(sharers) for p in parts]
            out_ref[slot] = jnp.concatenate(pieces, axis=0).astype(BF)

        @pl.when(kind == 2)
        def _(slot=slot):
            out_ref[slot] = extra_ref[meta_ref[EXTRA_AT + slot]]


SCALARS = pl.BlockSpec(memory_space=pltpu.SMEM)
ANYWHERE = pl.BlockSpec(memory_space=pl.ANY)


def params(steps=0):
    semantics = {"dimension_semantics": ("arbitrary",) * steps} if steps else {}
    return pltpu.CompilerParams(vmem_limit_bytes=VMEM_LIMIT, **semantics)


def cost(flops, elements=0):
    return pl.CostEstimate(flops=int(flops), bytes_accessed=int(elements), transcendentals=0)


def whole(array):
    return pl.BlockSpec(array.shape, lambda *_: (0,) * len(array.shape))


def shape(*dims, dtype=BF):
    return jax.ShapeDtypeStruct(dims, dtype)


def weight_call(kernel, name, operands, weights, members, outs, scratch, weigh):
    width = weights.shape[-1]
    first, count = members
    return pl.pallas_call(
        kernel,
        name=name,
        grid=(count,),
        in_specs=[SCALARS]
        + [whole(a) for a in operands[1:]]
        + [pl.BlockSpec((1, width, width), lambda i: (first + i, 0, 0))],
        out_specs=[spec for spec, _ in outs],
        out_shape=[struct for _, struct in outs],
        scratch_shapes=scratch,
        compiler_params=params(1),
        cost_estimate=cost(weigh * count, 2 * width * width * count),
    )(*operands, weights)


def full(*dims):
    return whole(shape(*dims)), shape(*dims)


def gather(lengths, frame_mask, column, latents, cotangent, columns, sharers):
    _, frame_dev, patch_dev, width = latents.shape
    main = (frame_dev, patch_dev, width)
    patch_t = patch_dev // columns
    extra = shape(columns, EXTRAS, patch_t, width)
    return pl.pallas_call(
        functools.partial(gather_kernel, sharers=sharers),
        name="gather",
        in_specs=[SCALARS] * 3 + [ANYWHERE] * 2,
        out_specs=[SCALARS] + [pl.BlockSpec(memory_space=pltpu.VMEM)] * 4,
        out_shape=[
            shape(TABLE, dtype=jnp.int32), shape(*main), extra, shape(columns, frame_dev, patch_t, width), extra,
        ],
        scratch_shapes=[
            pltpu.VMEM(main, BF),
            pltpu.VMEM((2, EXTRAS, patch_dev, width), BF),
            pltpu.SemaphoreType.DMA((2, EXTRAS + 1)),
        ],
        compiler_params=params(),
    )(lengths, frame_mask, column, latents, cotangent)


def front_main(meta, mod, x, weights):
    rows, width = x.shape
    kv = pl.BlockSpec((1, rows, width), lambda i: (jnp.maximum(i - 1, 0), 0, 0)), shape(2, rows, width)
    return weight_call(
        front_main_kernel, "front_main", (meta, mod, x), weights, (0, 3),
        [full(rows, width), kv], [pltpu.VMEM((rows, width), BF)], 2 * rows * width**2,
    )


def front_extra(meta, mod, x, weights, heads, patches):
    rows, width = x.shape
    return weight_call(
        functools.partial(front_extra_kernel, patches=patches), "front_extra", (meta, mod, x), weights, (0, 3),
        [full(heads, rows, 256)], [pltpu.VMEM((rows, width), BF), pltpu.VMEM((3, rows, width), F32)],
        4 * rows * width**2,
    )[0]


def back_main(meta, mod, x, o, weights, columns, devices):
    rows, width = x.shape
    return weight_call(
        functools.partial(back_main_kernel, columns=columns), "back_main", (meta, mod, x, o), weights,
        (3, 1), [full(devices, rows * width // (devices * 128), 128)], [pltpu.VMEM((rows, width), F32)],
        3 * rows * width**2,
    )[0]


def back_grad_main(meta, mod, got, weights, rows, columns, room):
    width = weights.shape[-1]
    return weight_call(
        functools.partial(back_grad_main_kernel, columns=columns, room=room), "back_grad_main",
        (meta, mod, got), weights, (3, 1), [full(rows, width)] * 2,
        [pltpu.VMEM((rows, width), BF), pltpu.VMEM((rows, width), F32)], 3 * rows * width**2,
    )


def front_grad_main(meta, mod, own, got, x, g, weights):
    rows, width = x.shape
    return weight_call(
        front_grad_main_kernel, "front_grad_main", (meta, mod, own, got, x, g), weights, (0, 3),
        [full(rows, width)], [pltpu.VMEM((3, rows, width), BF), pltpu.VMEM((rows, width), F32)],
        3 * rows * width**2,
    )[0]


def front_grad_extra(meta, mod, pack, x, g, weights, patches):
    rows, width = x.shape
    return weight_call(
        functools.partial(front_grad_extra_kernel, patches=patches), "front_grad_extra",
        (meta, mod, pack, x, g), weights, (0, 3), [full(rows, width)],
        [pltpu.VMEM((3, rows, width), BF), pltpu.VMEM((rows, width), F32), pltpu.VMEM((3, rows, width), F32)],
        4 * rows * width**2,
    )[0]


def attend(q, kv, other, heads):
    rows, width = q.shape
    keys = rows * (other.shape[0] + 1)
    return pl.pallas_call(
        functools.partial(attend_kernel, heads=heads),
        name="attend",
        out_shape=shape(rows, width),
        scratch_shapes=[
            pltpu.VMEM((keys, width), BF),
            pltpu.VMEM((keys, width), BF),
            pltpu.VMEM((rows, width), F32),
        ],
        compiler_params=params(),
        cost_estimate=cost(6e9),
    )(q, kv, other)


def extra_attend(pack, main):
    devices, count, patches, _ = pack.shape
    return pl.pallas_call(
        extra_attend_kernel, name="extra_attend",
        out_shape=shape(devices, extra_room(count * patches) + main.shape[1], 128),
        compiler_params=params(), cost_estimate=cost(4e9),
    )(pack, main)


def extra_attend_back(pack, got):
    return pl.pallas_call(
        extra_attend_back_kernel, name="extra_attend_back", out_shape=shape(*pack.shape),
        compiler_params=params(), cost_estimate=cost(6e9),
    )(pack, got)


def attend_back(q, kv, other, do, heads):
    rows, width = q.shape
    keys = rows * (other.shape[0] + 1)
    return pl.pallas_call(
        functools.partial(attend_back_kernel, heads=heads),
        name="attend_back",
        out_shape=[shape(3, rows, width), shape(*other.shape)],
        scratch_shapes=[
            pltpu.VMEM((keys, width), BF),
            pltpu.VMEM((keys, width), BF),
            pltpu.VMEM((rows, width), F32),
            pltpu.VMEM((keys, width), F32),
            pltpu.VMEM((keys, width), F32),
        ],
        compiler_params=params(),
        cost_estimate=cost(14e9),
    )(q, kv, other, do)


def temporal(meta, mod, got, le, cm, ce, weights, last_weight, heads, patches, groups):
    columns, block, width = cm.shape
    main, extra = columns * block, le.shape[0]
    rows = main + extra
    operands = (mod, got, le, cm, ce, weights, last_weight)
    return pl.pallas_call(
        functools.partial(temporal_kernel, heads=heads, patches=patches, groups=groups),
        name="temporal",
        in_specs=[SCALARS] + [whole(a) for a in operands],
        out_shape=[shape(*cm.shape), shape(extra, width), shape(*got.shape), shape(extra, width)],
        scratch_shapes=[pltpu.VMEM((main, width), F32), pltpu.VMEM((extra, width), F32)]
        + [pltpu.VMEM((rows, width), BF)] * 4
        + [pltpu.VMEM((rows, width), F32)] * 5,
        compiler_params=params(),
        cost_estimate=cost(34e9),
    )(meta, *operands)


def place(meta, main, extra, slots, sharers):
    return pl.pallas_call(
        functools.partial(place_kernel, sharers=sharers),
        name="place",
        in_specs=[SCALARS, whole(main), whole(extra)],
        out_shape=shape(slots, *extra.shape[1:]),
        compiler_params=params(),
        cost_estimate=cost(3e9),
    )(meta, main, extra)


def local(latents, cotangent, spatial_weights, temporal_weights, modulation, lengths, frame_mask):
    clips, frame_dev, patch_dev, width = latents.shape
    heads = width // HEAD
    frame_axis, patch_axis = lax.axis_size("frame"), lax.axis_size("patch")
    everyone = ("frame", "patch")
    frames = frame_dev * frame_axis
    sharers = patch_axis // frame_dev
    sub = patch_dev // sharers
    small = sub // frame_axis
    patch_t = patch_dev // frame_axis
    heads_col = heads // frame_axis
    groups = patch_axis // heads_col
    group_extras = -(-EXTRAS // groups)
    extras = groups * group_extras

    def swap(x, axis):
        return lax.all_to_all(x, axis, split_axis=0, concat_axis=0, tiled=True)

    column = lax.axis_index("frame")
    sources = -(-(EXTRAS - clips + 2) // frame_dev)
    main_rows = frame_dev * patch_dev

    def cross(blocks):
        got = [blocks[0]]
        for m in range(1, frame_axis):
            got.append(lax.ppermute(blocks[m], "frame", [(f, f ^ m) for f in range(frame_axis)]))
        return jnp.stack(got)

    def extras_out(x, meta):
        found = []
        for source in range(sources):
            mine = jnp.where(column == source, x[source], jnp.zeros((), BF))
            for dest in range(frame_axis):
                if dest != source:
                    mine = mine + lax.ppermute(x[dest], "frame", [(source, dest)])
            found.append(mine)
        out = found[0]
        for source in range(1, sources):
            frame = meta[FRAME : FRAME + EXTRAS][:, None, None]
            out = jnp.where(frame // frame_dev == source, found[source], out)
        out = out.reshape(EXTRAS * patch_t, width)
        return jnp.concatenate([out, jnp.zeros(((extras - EXTRAS) * patch_t, width), BF)])

    def extras_home(x):
        x = x.reshape(extras, patch_t, width)[:EXTRAS]
        found = []
        for source in range(frame_axis):
            mine = jnp.where(column == source, x, jnp.zeros((), BF))
            for dest in range(sources):
                if dest != source:
                    mine = mine + lax.ppermute(x, "frame", [(source, dest)])
            found.append(mine)
        return jnp.transpose(jnp.stack(found), (1, 0, 2, 3)).reshape(EXTRAS, patch_dev, width)

    meta, main_home, extra_home, cot_main, cot_extra = gather(
        lengths, frame_mask, column.reshape(1).astype(jnp.int32), latents, cotangent, frame_axis, sharers
    )
    main_s = swap(main_home.reshape(patch_axis, sub, width), "patch").reshape(main_rows, width)
    extra_t = extras_out(extra_home, meta)
    cot_m = cross(cot_main.reshape(frame_axis, frame_dev * patch_t, width))
    cot_e = extras_out(cot_extra, meta)
    main_s, cot_m, cot_e = lax.optimization_barrier((main_s, cot_m, cot_e))

    def rotate(array, by):
        perm = []
        for p in range(patch_axis):
            base = p // sharers * sharers
            perm.append((p, base + (p - base + by) % sharers))
        return lax.ppermute(array, "patch", perm)

    mod = modulation
    chunk = group_extras * patch_t
    pack = front_extra(meta, mod, extra_t, spatial_weights, heads, patch_t)
    pack_got = swap(pack.reshape(frame_axis * patch_axis, chunk, 256), everyone)
    pack_got = pack_got.reshape(frame_axis * patch_axis, group_extras, patch_t, 256)
    q, kv = front_main(meta, mod, main_s, spatial_weights)
    other = jnp.stack([rotate(kv, by) for by in range(1, sharers)])
    attended = attend(q, kv, other, heads)
    sent = back_main(meta, mod, main_s, attended, spatial_weights, frame_axis, frame_axis * patch_axis)
    sent, pack_got = lax.optimization_barrier((sent, pack_got))
    sent = extra_attend(pack_got, sent)

    out_m, out_e, sent, grad_e = temporal(
        meta, mod, swap(sent, everyone), extra_t, cot_m, cot_e, temporal_weights, spatial_weights[3:],
        heads, patch_t, groups,
    )

    grads = swap(sent, everyone)
    do_main, grad_s = back_grad_main(
        meta, mod, grads, spatial_weights, main_rows, frame_axis, extra_room(chunk)
    )
    own, sent = attend_back(q, kv, other, do_main, heads)
    got = jnp.stack([rotate(sent[by - 1], -by) for by in range(1, sharers)])
    dpack = extra_attend_back(pack_got, grads)
    dpack = swap(dpack.reshape(frame_axis * patch_axis, chunk, 256), everyone)
    dpack = dpack.reshape(heads, extras * patch_t, 256)
    lat_m = front_grad_main(meta, mod, own, got, main_s, grad_s, spatial_weights)
    lat_m, dpack, out_m, out_e = lax.optimization_barrier((lat_m, dpack, out_m, out_e))
    lat_e = front_grad_extra(meta, mod, dpack, extra_t, grad_e, spatial_weights, patch_t)
    lat_main = swap(lat_m.reshape(patch_axis, sub, width), "patch").reshape(frame_dev, patch_dev, width)

    out_main = cross(out_m).reshape(frame_axis, frame_dev, patch_t, width)
    slots = clips * frame_dev
    output = place(meta, out_main, extras_home(out_e), slots, sharers)
    grad = place(meta, lat_main, extras_home(lat_e), slots, 0)
    return output.reshape(latents.shape), grad.reshape(latents.shape)


def solution(mesh):
    tokens = P(None, "frame", "patch", None)
    in_specs = (tokens, tokens, P(), P(), P(), P(), P())
    return jax.shard_map(local, mesh=mesh, in_specs=in_specs, out_specs=(tokens, tokens), check_vma=False)
```

```python
import functools
import math

import jax
import jax.numpy as jnp
from jax import lax
from jax.experimental import pallas as pl
from jax.experimental.pallas import tpu as pltpu
from jax.sharding import PartitionSpec as P

HEAD = 72
EXTRAS = 5
SCALE = HEAD ** -0.5
SCALE2 = SCALE * math.log2(math.e)
BF = jnp.bfloat16
F32 = jnp.float32
VMEM_LIMIT = 56 * 1024 * 1024
LONG, COLUMN, CLIP, FRAME, VALID, LONG_VALID, KIND, EXTRA_AT, TABLE = 0, 1, 8, 16, 24, 32, 48, 64, 80


def nn(a, b):
    return lax.dot_general(a, b, (((1,), (0,)), ((), ())), preferred_element_type=F32)


def nt(a, b):
    return lax.dot_general(a, b, (((1,), (1,)), ((), ())), preferred_element_type=F32)


def tn(a, b):
    return lax.dot_general(a, b, (((0,), (0,)), ((), ())), preferred_element_type=F32)


def window(head):
    start = head * HEAD // 128 * 128
    offset = head * HEAD - start
    return start, offset, 128 if offset + HEAD <= 128 else 256


def lanes_in(width, low, high):
    lane = lax.broadcasted_iota(jnp.int32, (1, width), 1)
    return (lane >= low) & (lane < high)


def masked(x, keep):
    return jnp.where(keep, x, jnp.zeros((), x.dtype))


def take_head(x_ref, rows, head):
    start, offset, width = window(head)
    part = x_ref[rows, start : start + width].astype(F32)
    if offset:
        part = pltpu.roll(part, width - offset, 1)
    return masked(part[:, :128], lanes_in(128, 0, HEAD))


def put_head(value, head):
    start, offset, width = window(head)
    if width == 256:
        value = jnp.concatenate([value, jnp.zeros_like(value)], axis=1)
    if offset:
        value = pltpu.roll(value, offset, 1)
    return start, width, value


def room_for(count):
    return -(-count * HEAD // 128) * 128


def pack(parts):
    width = room_for(len(parts))
    out = None
    for i, part in enumerate(parts):
        if width > 128:
            part = jnp.concatenate([part, jnp.zeros((part.shape[0], width - 128), F32)], axis=1)
        if i:
            part = pltpu.roll(part, i * HEAD, 1)
        out = part if out is None else out + part
    return out


def unpack(packed, member):
    if member:
        packed = pltpu.roll(packed, packed.shape[1] - member * HEAD, 1)
    return masked(packed[:, :128], lanes_in(128, 0, HEAD))


def main_vec(meta_ref, mod_ref, block, member):
    return mod_ref[block, member, pl.ds(meta_ref[LONG], 1), :]


def extra_vec(meta_ref, mod_ref, block, member, extras, patches):
    rows = [mod_ref[block, member, pl.ds(meta_ref[CLIP + e], 1), :] for e in range(extras)]
    return jnp.concatenate([jnp.broadcast_to(r, (patches, r.shape[1])) for r in rows], axis=0)


def normed_of(x):
    average = jnp.mean(x, axis=-1, keepdims=True)
    centred = x - average
    variance = jnp.mean(centred * centred, axis=-1, keepdims=True)
    inverse = lax.rsqrt(variance + 1e-06)
    return centred * inverse, inverse


def over_rows(count, body, most=64):
    size = math.gcd(count, most)
    if count == size:
        body(slice(0, count))
        return

    def step(i, carry):
        body(pl.ds(pl.multiple_of(i * size, size), size))
        return carry

    lax.fori_loop(0, count // size, step, 0)


def modulate(x, shift, scale):
    normed, _ = normed_of(x.astype(F32))
    return (normed * (1.0 + scale) + shift).astype(BF)


def norm_back(x, grad, dmod, scale):
    normed, inverse = normed_of(x.astype(F32))
    dnormed = dmod * (1.0 + scale)
    mean_d = jnp.mean(dnormed, axis=-1, keepdims=True)
    mean_dn = jnp.mean(dnormed * normed, axis=-1, keepdims=True)
    dx = (inverse * (dnormed - mean_d - normed * mean_dn)).astype(BF)
    return (dx.astype(F32) + grad.astype(F32)).astype(BF)


def gated(x, gate, mixed):
    return (x.astype(F32) + gate * mixed).astype(BF)


def col_tiles(width):
    whole, tiles = 512, []
    start = 0
    while start < width:
        tiles.append((start, min(whole, width - start)))
        start += whole
    return tiles


def times(dest_ref, x_ref, w_ref, member, transposed=False, add=False):
    for start, size in col_tiles(w_ref.shape[-1]):
        cols = pl.ds(start, size)
        if transposed:
            product = nt(x_ref[...], w_ref[member, cols, :])
        else:
            product = nn(x_ref[...], w_ref[member, :, cols])
        if add:
            product = dest_ref[:, cols] + product
        dest_ref[:, cols] = product.astype(dest_ref.dtype)


def heads_forward(o_ref, q_ref, k_ref, v_ref, parts, bias, heads):
    for head in range(heads):
        start, offset, width = window(head)
        cols = slice(start, start + width)
        keep = lanes_in(width, offset, offset + HEAD)
        scores = [nt(masked(q_ref[rows, cols], keep), k_ref[rows, cols]) for rows in parts]
        scores = jnp.concatenate(scores, axis=0) if len(parts) > 1 else scores[0]
        if bias is not None:
            scores = scores + bias
        exponent = jnp.exp2((scores - jnp.max(scores, axis=-1, keepdims=True)) * SCALE2)
        inverse = 1.0 / jnp.sum(exponent, axis=-1, keepdims=True)
        exponent = exponent.astype(BF)
        count = exponent.shape[0] // len(parts)
        for i, rows in enumerate(parts):
            mine = slice(i * count, (i + 1) * count)
            result = nn(exponent[mine], masked(v_ref[rows, cols], keep)) * inverse[mine]
            o_ref[rows, cols] = o_ref[rows, cols] + result


def softmax_grads(q, do, k, v, bias):
    def joined(left, right):
        products = [nt(a, b) for a, b in zip(left, right)]
        return jnp.concatenate(products, axis=1) if len(products) > 1 else products[0]

    scores = joined(k, q)
    if bias is not None:
        scores = scores + bias
    exponent = jnp.exp2((scores - jnp.max(scores, axis=0, keepdims=True)) * SCALE2)
    prob = exponent * (1.0 / jnp.sum(exponent, axis=0, keepdims=True))
    dprob = joined(v, do)
    delta = jnp.sum(prob * dprob, axis=0, keepdims=True)
    dscores = prob * (dprob - delta) * SCALE
    count = scores.shape[1] // len(q)

    def split(x):
        return [x[:, i * count : (i + 1) * count] for i in range(len(q))]

    return split(dscores.astype(BF)), split(prob.astype(BF))


def heads_backward(dq_ref, dk_ref, dv_ref, q_ref, k_ref, v_ref, do_ref, parts, bias, heads):
    for head in range(heads):
        start, offset, width = window(head)
        cols = slice(start, start + width)
        keep = lanes_in(width, offset, offset + HEAD)
        q, do, k = [[masked(ref[rows, cols], keep) for rows in parts] for ref in (q_ref, do_ref, k_ref)]
        dscores, prob = softmax_grads(q, do, k, [v_ref[rows, cols] for rows in parts], bias)
        for i, rows in enumerate(parts):
            dv_ref[rows, cols] = dv_ref[rows, cols] + nn(prob[i], do[i])
            dk_ref[rows, cols] = dk_ref[rows, cols] + nn(dscores[i], q[i])
            dq_ref[rows, cols] = dq_ref[rows, cols] + tn(dscores[i], k[i])


def gather_kernel(
    lengths_ref, mask_ref, column_ref, latents_ref, cotangent_ref,
    meta_ref, main_ref, extra_ref, cot_main_ref, cot_extra_ref,
    main_in, extra_in, sems, *, sharers,
):
    clips, frame_dev, patch_dev, width = latents_ref.shape
    frames = mask_ref.shape[1]
    frame_axis = frames // frame_dev
    patch_t = patch_dev // frame_axis
    small, sub = patch_t // sharers, patch_dev // sharers
    column = column_ref[0]
    long = jnp.int32(0)
    for c in range(clips):
        long = long + jnp.where(lengths_ref[c] == frames, c, 0)
    for i in range(TABLE):
        meta_ref[i] = 0
    meta_ref[LONG] = long
    meta_ref[COLUMN] = column
    count = jnp.int32(0)
    for c in range(clips):
        for f in range(EXTRAS - clips + 2):
            used = (c != long) & (f < lengths_ref[c])
            at = jnp.where(used, count, EXTRAS)
            meta_ref[CLIP + at] = jnp.int32(c)
            meta_ref[FRAME + at] = jnp.int32(f)
            meta_ref[VALID + at] = mask_ref[c, f]
            count = count + used.astype(jnp.int32)
    for e in range(EXTRAS, 8):
        for row in (CLIP, FRAME, VALID):
            meta_ref[row + e] = 0

    copies = []
    pairs = ((latents_ref, main_ref), (cotangent_ref, main_in))
    for i, (source, main) in enumerate(pairs):
        copies.append(pltpu.make_async_copy(source.at[long], main, sems.at[i, EXTRAS]))
        copies[-1].start()
        for e in range(EXTRAS):
            frame = lax.rem(meta_ref[FRAME + e], frame_dev)
            part = source.at[meta_ref[CLIP + e], frame]
            copies.append(pltpu.make_async_copy(part, extra_in.at[i, e], sems.at[i, e]))
            copies[-1].start()

    for f in range(frames):
        meta_ref[LONG_VALID + f] = mask_ref[long, f]
    for c in range(clips):
        for f in range(frame_dev):
            frame = column * frame_dev + f
            valid = (frame < lengths_ref[c]) & (mask_ref[c, frame] == 1)
            meta_ref[KIND + c * frame_dev + f] = jnp.where(valid, jnp.where(c == long, 1, 2), 0)
    for e in range(EXTRAS):
        local_frame = meta_ref[FRAME + e] - column * frame_dev
        here = (local_frame >= 0) & (local_frame < frame_dev)
        slot = meta_ref[CLIP + e] * frame_dev + jnp.where(here, local_frame, 0)

        @pl.when(here)
        def _(e=e, slot=slot):
            meta_ref[EXTRA_AT + slot] = jnp.int32(e)

    for copy in copies:
        copy.wait()
    for i, out in enumerate((extra_ref, cot_extra_ref)):
        for e in range(EXTRAS):
            rows = extra_in[i, e].astype(F32)
            for f in range(frame_axis):
                out[f, e] = rows[f * patch_t : (f + 1) * patch_t].astype(BF)
    for j in range(frame_dev):
        rows = main_in[j].astype(F32)
        for f in range(frame_axis):
            starts = [s * sub + f * small for s in range(sharers)]
            part = jnp.concatenate([rows[at : at + small] for at in starts], axis=0)
            cot_main_ref[f ^ column, j] = part.astype(BF)


def front_main_kernel(meta_ref, mod_ref, x_ref, w_ref, q_ref, kv_ref, low_ref):
    member = pl.program_id(0)

    @pl.when(member == 0)
    def _():
        shift, scale = [main_vec(meta_ref, mod_ref, 0, i) for i in range(2)]

        def body(rows):
            low_ref[rows, :] = modulate(x_ref[rows, :], shift, scale)

        over_rows(x_ref.shape[0], body)
        times(q_ref, low_ref, w_ref, 0)

    @pl.when(member > 0)
    def _():
        times(kv_ref.at[0], low_ref, w_ref, 0)


def front_extra_kernel(meta_ref, mod_ref, x_ref, w_ref, pack_ref, low_ref, out_ref, *, patches):
    member = pl.program_id(0)
    rows = x_ref.shape[0]

    @pl.when(member == 0)
    def _():
        shift, scale = [extra_vec(meta_ref, mod_ref, 0, i, rows // patches, patches) for i in range(2)]
        low_ref[...] = modulate(x_ref[...], shift, scale)

    for start, size in col_tiles(w_ref.shape[-1]):
        cols = pl.ds(start, size)
        out_ref[member, :, cols] = nn(low_ref[...], w_ref[0, :, cols])

    @pl.when(member == 2)
    def _():
        for head in range(pack_ref.shape[0]):
            parts = [take_head(out_ref.at[i], slice(None), head) for i in range(3)]
            pack_ref[head] = pack(parts).astype(BF)


def fill_keys(k_ref, v_ref, kv_ref, other_ref):
    rows = kv_ref.shape[1]
    k_ref[:rows] = kv_ref[0]
    v_ref[:rows] = kv_ref[1]
    for i in range(other_ref.shape[0]):
        k_ref[(i + 1) * rows : (i + 2) * rows] = other_ref[i, 0]
        v_ref[(i + 1) * rows : (i + 2) * rows] = other_ref[i, 1]


def attend_kernel(q_ref, kv_ref, other_ref, o_ref, k_ref, v_ref, acc_ref, *, heads):
    fill_keys(k_ref, v_ref, kv_ref, other_ref)
    acc_ref[...] = jnp.zeros_like(acc_ref)
    heads_forward(acc_ref, q_ref, k_ref, v_ref, [slice(None)], None, heads)
    o_ref[...] = acc_ref[...].astype(BF)


def extra_rows(ref, index):
    part = ref[:, index]
    return part.reshape(part.shape[0] * part.shape[1], part.shape[2])


def extra_attend_kernel(pack_ref, o_ref):
    results = []
    for index in range(pack_ref.shape[1]):
        packed = extra_rows(pack_ref, index).astype(F32)
        q, k, v = [unpack(packed, i).astype(BF) for i in range(3)]
        scores = nt(q, k)
        exponent = jnp.exp2((scores - jnp.max(scores, axis=-1, keepdims=True)) * SCALE2)
        total = jnp.sum(exponent, axis=-1, keepdims=True)
        results.append(nn(exponent.astype(BF), v) * (1.0 / total))
    o_ref[...] = pack(results).reshape(o_ref.shape).astype(BF)


def extra_attend_back_kernel(pack_ref, got_ref, grad_ref):
    devices, _, patches, _ = pack_ref.shape
    got = got_ref[...].astype(F32).reshape(devices * patches, got_ref.shape[2])
    for index in range(pack_ref.shape[1]):
        packed = extra_rows(pack_ref, index).astype(F32)
        q, k, v = [unpack(packed, i).astype(BF) for i in range(3)]
        do = unpack(got, index).astype(BF)
        (dscores,), (prob,) = softmax_grads([q], [do], [k], [v], None)
        out = pack([tn(dscores, k), nn(dscores, q), nn(prob, do)]).astype(BF)
        grad_ref[:, index] = out.reshape(devices, patches, 256)


def write_chunk(sent_ref, dest, value):
    pieces = [value[:, at : at + 128] for at in range(0, value.shape[1], 128)]
    sent_ref[dest] = jnp.concatenate(pieces, axis=0).astype(BF)


def read_chunk(got_ref, source, out_ref, row, small):
    value = got_ref[source].astype(F32)
    for i in range(out_ref.shape[1] // 128):
        out_ref[row : row + small, i * 128 : (i + 1) * 128] = value[i * small : (i + 1) * small]


def back_main_kernel(meta_ref, mod_ref, x_ref, o_ref, w_ref, sent_ref, acc_ref, *, columns):
    times(acc_ref, o_ref, w_ref, 0)
    gate = main_vec(meta_ref, mod_ref, 0, 2)

    def body(rows):
        acc_ref[rows, :] = x_ref[rows, :].astype(F32) + gate * acc_ref[rows, :]

    over_rows(x_ref.shape[0], body)
    devices = sent_ref.shape[0]
    small = x_ref.shape[0] // devices
    patch_axis = devices // columns
    for p in range(patch_axis):
        for f in range(columns):
            row = (p * columns + f) * small
            write_chunk(sent_ref, f * patch_axis + p, acc_ref[row : row + small, :])


def back_grad_main_kernel(meta_ref, mod_ref, got_ref, w_ref, do_ref, g_ref, low_ref, acc_ref, *, columns):
    devices = got_ref.shape[0]
    small = g_ref.shape[0] // devices
    patch_axis = devices // columns
    for p in range(patch_axis):
        for f in range(columns):
            row = (p * columns + f) * small
            read_chunk(got_ref, f * patch_axis + p, acc_ref, row, small)
    gate = main_vec(meta_ref, mod_ref, 0, 2)

    def body(rows):
        g_ref[rows, :] = acc_ref[rows, :].astype(BF)
        low_ref[rows, :] = (gate * acc_ref[rows, :]).astype(BF)

    over_rows(g_ref.shape[0], body)
    times(do_ref, low_ref, w_ref, 0, transposed=True)


def attend_back_kernel(
    q_ref, kv_ref, other_ref, do_ref, own_ref, sent_ref, k_ref, v_ref, dq_ref, dk_ref, dv_ref, *, heads
):
    rows = kv_ref.shape[1]
    fill_keys(k_ref, v_ref, kv_ref, other_ref)
    for ref in (dq_ref, dk_ref, dv_ref):
        ref[...] = jnp.zeros_like(ref)
    heads_backward(dq_ref, dk_ref, dv_ref, q_ref, k_ref, v_ref, do_ref, [slice(None)], None, heads)
    own_ref[0] = dq_ref[...].astype(BF)
    own_ref[1] = dk_ref[:rows].astype(BF)
    own_ref[2] = dv_ref[:rows].astype(BF)
    for i in range(other_ref.shape[0]):
        sent_ref[i, 0] = dk_ref[(i + 1) * rows : (i + 2) * rows].astype(BF)
        sent_ref[i, 1] = dv_ref[(i + 1) * rows : (i + 2) * rows].astype(BF)


def add_product(acc_ref, d_ref, member, w_ref):
    for start, size in col_tiles(w_ref.shape[-1]):
        cols = pl.ds(start, size)
        product = nt(d_ref[member], w_ref[0, cols, :])

        @pl.when(member == 0)
        def _(cols=cols, product=product):
            acc_ref[:, cols] = product

        @pl.when(member > 0)
        def _(cols=cols, product=product):
            acc_ref[:, cols] = acc_ref[:, cols] + product


def front_grad_main_kernel(meta_ref, mod_ref, own_ref, got_ref, x_ref, g_ref, w_ref, out_ref, d_ref, acc_ref):
    member = pl.program_id(0)

    @pl.when(member == 0)
    def _():
        d_ref[0] = own_ref[0]
        for i in range(2):
            total = own_ref[1 + i].astype(F32)
            for j in range(got_ref.shape[0]):
                total = total + got_ref[j, i].astype(F32)
            d_ref[1 + i] = total.astype(BF)

    add_product(acc_ref, d_ref, member, w_ref)

    @pl.when(member == 2)
    def _():
        scale = main_vec(meta_ref, mod_ref, 0, 1)

        def body(rows):
            out_ref[rows, :] = norm_back(x_ref[rows, :], g_ref[rows, :], acc_ref[rows, :], scale)

        over_rows(x_ref.shape[0], body)


def front_grad_extra_kernel(
    meta_ref, mod_ref, pack_ref, x_ref, g_ref, w_ref, out_ref, d_ref, acc_ref, ext_ref, *, patches
):
    member = pl.program_id(0)
    rows = x_ref.shape[0]

    @pl.when(member == 0)
    def _():
        ext_ref[...] = jnp.zeros_like(ext_ref)
        for head in range(pack_ref.shape[0]):
            packed = pack_ref[head].astype(F32)
            for i in range(3):
                start, width, value = put_head(unpack(packed, i), head)
                cols = slice(start, start + width)
                ext_ref[i, :, cols] = ext_ref[i, :, cols] + value
        d_ref[...] = ext_ref[...].astype(BF)

    add_product(acc_ref, d_ref, member, w_ref)

    @pl.when(member == 2)
    def _():
        scale = extra_vec(meta_ref, mod_ref, 0, 1, rows // patches, patches)
        out_ref[...] = norm_back(x_ref[...], g_ref[...], acc_ref[...], scale)


def key_bias(meta_ref, valid_at, clip_at, tokens, count, small, keys_axis):
    part = count * small

    def spread(base, axis):
        line = (1, tokens) if axis == 1 else (tokens, 1)
        item = lax.broadcasted_iota(jnp.int32, line, axis) % part // small
        out = jnp.zeros(line, jnp.int32)
        for i in range(count):
            out = jnp.where(item == i, meta_ref[base + i], out)
        return out

    where = lax.broadcasted_iota(jnp.int32, (tokens, tokens), keys_axis)
    other = lax.broadcasted_iota(jnp.int32, (tokens, tokens), 1 - keys_axis)
    admitted = jnp.broadcast_to(spread(valid_at, keys_axis) == 1, (tokens, tokens))
    if clip_at is not None:
        admitted = admitted & (spread(clip_at, 0) == spread(clip_at, 1))
    admitted = admitted & (where % small == other % small) & (where // part == other // part)
    return jnp.where(admitted | (where == other), 0.0, -1e30).astype(F32)


def temporal_core(vecs, w_ref, parts, biases, put, most, refs, heads):
    x_ref, cot_ref, low_ref, q_ref, k_ref, v_ref, acc_ref, dq_ref, dk_ref, dv_ref = refs
    count = x_ref.shape[0]
    shift, scale, gate = vecs

    def body(rows):
        low_ref[rows, :] = modulate(x_ref[rows, :], shift, scale)

    over_rows(count, body, most)
    for i, ref in enumerate((q_ref, k_ref, v_ref)):
        times(ref, low_ref, w_ref, i)
    acc_ref[...] = jnp.zeros_like(acc_ref)
    heads_forward(acc_ref, q_ref, k_ref, v_ref, parts, biases(1), heads)
    low_ref[...] = acc_ref[...].astype(BF)
    times(acc_ref, low_ref, w_ref, 3)

    def body(rows):
        acc_ref[rows, :] = x_ref[rows, :] + gate * acc_ref[rows, :]
        low_ref[rows, :] = (gate * cot_ref[rows, :]).astype(BF)

    over_rows(count, body, most)
    put()
    times(acc_ref, low_ref, w_ref, 3, transposed=True)
    low_ref[...] = acc_ref[...].astype(BF)
    for ref in (dq_ref, dk_ref, dv_ref):
        ref[...] = jnp.zeros_like(ref)
    heads_backward(dq_ref, dk_ref, dv_ref, q_ref, k_ref, v_ref, low_ref, parts, biases(0), heads)
    for i, ref in enumerate((dq_ref, dk_ref, dv_ref)):
        low_ref[...] = ref[...].astype(BF)
        times(acc_ref, low_ref, w_ref, i, transposed=True, add=i > 0)

    def body(rows):
        acc_ref[rows, :] = norm_back(x_ref[rows, :], cot_ref[rows, :], acc_ref[rows, :], scale).astype(F32)

    over_rows(count, body, most)


def temporal_main_kernel(meta_ref, mod_ref, got_ref, c_ref, w_ref, out_ref, sent_ref, *refs, heads, patches):
    x_ref, cot_ref, acc_ref = refs[0], refs[1], refs[6]
    columns, block, _ = c_ref.shape
    main = columns * block
    frames, each = main // patches, block // patches
    column = meta_ref[COLUMN]
    devices = got_ref.shape[0]
    small = main // devices
    sharers = patches // small
    part = frames * small

    def token(source):
        return source % sharers * part + source // sharers * small

    for source in range(devices):
        read_chunk(got_ref, source, x_ref, token(source), small)
    for f in range(columns):
        values = c_ref[column ^ f].astype(F32)
        for j in range(each):
            valid = meta_ref[LONG_VALID + f * each + j] == 1
            for g in range(sharers):
                rows = pl.ds(token((f * each + j) * sharers + g), small)
                at = j * patches + g * small
                cot_ref[rows, :] = jnp.where(valid, values[at : at + small], 0.0)

    parts = [slice(g * part, (g + 1) * part) for g in range(sharers)]
    if part % 128:
        parts = [slice(0, main)]

    def biases(axis):
        bias = key_bias(meta_ref, LONG_VALID, None, main // len(parts), frames, small, axis)
        return jnp.concatenate([bias] * len(parts), axis=1 - axis)

    def put():
        for f in range(columns):
            starts = [token(f * each * sharers + i) for i in range(each * sharers)]
            pieces = [acc_ref[at : at + small, :] for at in starts]
            out_ref[column ^ f] = jnp.concatenate(pieces, axis=0).astype(BF)

    vecs = [main_vec(meta_ref, mod_ref, 1, i) for i in range(3)]
    temporal_core(vecs, w_ref, parts, biases, put, 64, refs, heads)
    for dest in range(devices):
        write_chunk(sent_ref, dest, acc_ref[token(dest) : token(dest) + small, :])


def temporal_extra_kernel(
    meta_ref, mod_ref, got_ref, l_ref, c_ref, w_ref, ws_ref, out_ref, sent_ref, g_ref, *refs,
    heads, patches, groups,
):
    x_ref, cot_ref, acc_ref = refs[0], refs[1], refs[6]
    rows = l_ref.shape[0]
    extras = rows // patches
    each = extras // groups
    devices = got_ref.shape[0]

    def vec(block, member):
        return extra_vec(meta_ref, mod_ref, block, member, extras, patches)

    acc_ref[...] = jnp.zeros_like(acc_ref)
    for source in range(devices):
        head, group = source // groups, source % groups
        packed = got_ref[source].astype(F32)
        for e in range(each):
            at = (group * each + e) * patches
            start, size, value = put_head(unpack(packed, e), head)
            cols = slice(start, start + size)
            acc_ref[at : at + patches, cols] = acc_ref[at : at + patches, cols] + value
    gate_s = vec(0, 2)
    mixed = nn(acc_ref[...].astype(BF), ws_ref[0])
    x_ref[...] = gated(l_ref[...], gate_s, mixed).astype(F32)
    values = c_ref[...].astype(F32)
    for i in range(extras):
        part = slice(i * patches, (i + 1) * patches)
        cot_ref[part, :] = jnp.where(meta_ref[VALID + i] == 1, values[part], 0.0)

    def put():
        out_ref[...] = acc_ref[...].astype(BF)

    def biases(axis):
        return key_bias(meta_ref, VALID, CLIP, rows, extras, patches, axis)

    vecs = [vec(1, i) for i in range(3)]
    temporal_core(vecs, w_ref, [slice(0, rows)], biases, put, rows, refs, heads)
    grad = acc_ref[...]
    g_ref[...] = grad.astype(BF)
    acc_ref[...] = nt((gate_s * grad).astype(BF), ws_ref[0])
    for dest in range(devices):
        head, group = dest // groups, dest % groups
        starts = [(group * each + e) * patches for e in range(each)]
        parts = [take_head(acc_ref, slice(at, at + patches), head) for at in starts]
        sent_ref[dest] = pack(parts).astype(BF)


def place_kernel(meta_ref, main_ref, extra_ref, out_ref, *, sharers):
    frame_dev, patch_dev, width = main_ref.shape[-3], out_ref.shape[1], out_ref.shape[2]
    for slot in range(out_ref.shape[0]):
        kind = meta_ref[KIND + slot]

        @pl.when(kind == 0)
        def _(slot=slot):
            out_ref[slot] = jnp.zeros_like(out_ref[slot])

        @pl.when(kind == 1)
        def _(slot=slot):
            if not sharers:
                out_ref[slot] = main_ref[slot % frame_dev]
                return
            columns, patch_t = main_ref.shape[0], main_ref.shape[2]
            small = patch_t // sharers
            parts = [main_ref[meta_ref[COLUMN] ^ f, slot % frame_dev].astype(F32) for f in range(columns)]
            pieces = [p[s * small : (s + 1) * small] for s in range(sharers) for p in parts]
            out_ref[slot] = jnp.concatenate(pieces, axis=0).astype(BF)

        @pl.when(kind == 2)
        def _(slot=slot):
            out_ref[slot] = extra_ref[meta_ref[EXTRA_AT + slot]]


SCALARS = pl.BlockSpec(memory_space=pltpu.SMEM)
ANYWHERE = pl.BlockSpec(memory_space=pl.ANY)


def params(steps=0):
    semantics = {"dimension_semantics": ("arbitrary",) * steps} if steps else {}
    return pltpu.CompilerParams(vmem_limit_bytes=VMEM_LIMIT, **semantics)


def cost(flops, elements=0):
    return pl.CostEstimate(flops=int(flops), bytes_accessed=int(elements), transcendentals=0)


def whole(array):
    return pl.BlockSpec(array.shape, lambda *_: (0,) * len(array.shape))


def shape(*dims, dtype=BF):
    return jax.ShapeDtypeStruct(dims, dtype)


def weight_call(kernel, name, operands, weights, members, outs, scratch, weigh):
    width = weights.shape[-1]
    first, count = members
    return pl.pallas_call(
        kernel,
        name=name,
        grid=(count,),
        in_specs=[SCALARS]
        + [whole(a) for a in operands[1:]]
        + [pl.BlockSpec((1, width, width), lambda i: (first + i, 0, 0))],
        out_specs=[spec for spec, _ in outs],
        out_shape=[struct for _, struct in outs],
        scratch_shapes=scratch,
        compiler_params=params(1),
        cost_estimate=cost(weigh * count, 2 * width * width * count),
    )(*operands, weights)


def full(*dims):
    return whole(shape(*dims)), shape(*dims)


def gather(lengths, frame_mask, column, latents, cotangent, columns, sharers):
    _, frame_dev, patch_dev, width = latents.shape
    main = (frame_dev, patch_dev, width)
    patch_t = patch_dev // columns
    extra = shape(columns, EXTRAS, patch_t, width)
    return pl.pallas_call(
        functools.partial(gather_kernel, sharers=sharers),
        name="gather",
        in_specs=[SCALARS] * 3 + [ANYWHERE] * 2,
        out_specs=[SCALARS] + [pl.BlockSpec(memory_space=pltpu.VMEM)] * 4,
        out_shape=[
            shape(TABLE, dtype=jnp.int32), shape(*main), extra, shape(columns, frame_dev, patch_t, width), extra,
        ],
        scratch_shapes=[
            pltpu.VMEM(main, BF),
            pltpu.VMEM((2, EXTRAS, patch_dev, width), BF),
            pltpu.SemaphoreType.DMA((2, EXTRAS + 1)),
        ],
        compiler_params=params(),
    )(lengths, frame_mask, column, latents, cotangent)


def front_main(meta, mod, x, weights):
    rows, width = x.shape
    kv = pl.BlockSpec((1, rows, width), lambda i: (jnp.maximum(i - 1, 0), 0, 0)), shape(2, rows, width)
    return weight_call(
        front_main_kernel, "front_main", (meta, mod, x), weights, (0, 3),
        [full(rows, width), kv], [pltpu.VMEM((rows, width), BF)], 2 * rows * width**2,
    )


def front_extra(meta, mod, x, weights, heads, patches):
    rows, width = x.shape
    return weight_call(
        functools.partial(front_extra_kernel, patches=patches), "front_extra", (meta, mod, x), weights, (0, 3),
        [full(heads, rows, 256)], [pltpu.VMEM((rows, width), BF), pltpu.VMEM((3, rows, width), F32)],
        4 * rows * width**2,
    )[0]


def back_main(meta, mod, x, o, weights, columns, devices):
    rows, width = x.shape
    return weight_call(
        functools.partial(back_main_kernel, columns=columns), "back_main", (meta, mod, x, o), weights,
        (3, 1), [full(devices, rows * width // (devices * 128), 128)], [pltpu.VMEM((rows, width), F32)],
        3 * rows * width**2,
    )[0]


def back_grad_main(meta, mod, got, weights, rows, columns):
    width = weights.shape[-1]
    return weight_call(
        functools.partial(back_grad_main_kernel, columns=columns), "back_grad_main",
        (meta, mod, got), weights, (3, 1), [full(rows, width)] * 2,
        [pltpu.VMEM((rows, width), BF), pltpu.VMEM((rows, width), F32)], 3 * rows * width**2,
    )


def front_grad_main(meta, mod, own, got, x, g, weights):
    rows, width = x.shape
    return weight_call(
        front_grad_main_kernel, "front_grad_main", (meta, mod, own, got, x, g), weights, (0, 3),
        [full(rows, width)], [pltpu.VMEM((3, rows, width), BF), pltpu.VMEM((rows, width), F32)],
        3 * rows * width**2,
    )[0]


def front_grad_extra(meta, mod, pack, x, g, weights, patches):
    rows, width = x.shape
    return weight_call(
        functools.partial(front_grad_extra_kernel, patches=patches), "front_grad_extra",
        (meta, mod, pack, x, g), weights, (0, 3), [full(rows, width)],
        [pltpu.VMEM((3, rows, width), BF), pltpu.VMEM((rows, width), F32), pltpu.VMEM((3, rows, width), F32)],
        4 * rows * width**2,
    )[0]


def attend(q, kv, other, heads):
    rows, width = q.shape
    keys = rows * (other.shape[0] + 1)
    return pl.pallas_call(
        functools.partial(attend_kernel, heads=heads),
        name="attend",
        out_shape=shape(rows, width),
        scratch_shapes=[
            pltpu.VMEM((keys, width), BF),
            pltpu.VMEM((keys, width), BF),
            pltpu.VMEM((rows, width), F32),
        ],
        compiler_params=params(),
        cost_estimate=cost(6e9),
    )(q, kv, other)


def extra_attend(packed):
    devices, count, patches, _ = packed.shape
    return pl.pallas_call(
        extra_attend_kernel, name="extra_attend", out_shape=shape(devices, patches, room_for(count)),
        compiler_params=params(), cost_estimate=cost(4e9),
    )(packed)


def extra_attend_back(packed, got):
    return pl.pallas_call(
        extra_attend_back_kernel, name="extra_attend_back", out_shape=shape(*packed.shape),
        compiler_params=params(), cost_estimate=cost(6e9),
    )(packed, got)


def attend_back(q, kv, other, do, heads):
    rows, width = q.shape
    keys = rows * (other.shape[0] + 1)
    return pl.pallas_call(
        functools.partial(attend_back_kernel, heads=heads),
        name="attend_back",
        out_shape=[shape(3, rows, width), shape(*other.shape)],
        scratch_shapes=[
            pltpu.VMEM((keys, width), BF),
            pltpu.VMEM((keys, width), BF),
            pltpu.VMEM((rows, width), F32),
            pltpu.VMEM((keys, width), F32),
            pltpu.VMEM((keys, width), F32),
        ],
        compiler_params=params(),
        cost_estimate=cost(14e9),
    )(q, kv, other, do)


def temporal_scratch(rows, width):
    high, low = pltpu.VMEM((rows, width), F32), pltpu.VMEM((rows, width), BF)
    return [high] * 2 + [low] * 4 + [high] * 4


def temporal_main(meta, mod, got, cot, weights, heads, patches):
    columns, block, width = cot.shape
    operands = (mod, got, cot, weights)
    return pl.pallas_call(
        functools.partial(temporal_main_kernel, heads=heads, patches=patches),
        name="temporal_main",
        in_specs=[SCALARS] + [whole(a) for a in operands],
        out_shape=[shape(*cot.shape), shape(*got.shape)],
        scratch_shapes=temporal_scratch(columns * block, width),
        compiler_params=params(),
        cost_estimate=cost(25e9),
    )(meta, *operands)


def temporal_extra(meta, mod, got, le, cot, weights, last_weight, heads, patches, groups):
    operands = (mod, got, le, cot, weights, last_weight)
    return pl.pallas_call(
        functools.partial(temporal_extra_kernel, heads=heads, patches=patches, groups=groups),
        name="temporal_extra",
        in_specs=[SCALARS] + [whole(a) for a in operands],
        out_shape=[shape(*le.shape), shape(*got.shape), shape(*le.shape)],
        scratch_shapes=temporal_scratch(*le.shape),
        compiler_params=params(),
        cost_estimate=cost(14e9),
    )(meta, *operands)


def place(meta, main, extra, slots, sharers):
    return pl.pallas_call(
        functools.partial(place_kernel, sharers=sharers),
        name="place",
        in_specs=[SCALARS, whole(main), whole(extra)],
        out_shape=shape(slots, *extra.shape[1:]),
        compiler_params=params(),
        cost_estimate=cost(3e9),
    )(meta, main, extra)


def local(latents, cotangent, spatial_weights, temporal_weights, modulation, lengths, frame_mask):
    clips, frame_dev, patch_dev, width = latents.shape
    heads = width // HEAD
    frame_axis, patch_axis = lax.axis_size("frame"), lax.axis_size("patch")
    everyone = ("frame", "patch")
    frames = frame_dev * frame_axis
    sharers = patch_axis // frame_dev
    sub = patch_dev // sharers
    small = sub // frame_axis
    patch_t = patch_dev // frame_axis
    heads_col = heads // frame_axis
    groups = patch_axis // heads_col
    group_extras = -(-EXTRAS // groups)
    extras = groups * group_extras

    def swap(x, axis):
        return lax.all_to_all(x, axis, split_axis=0, concat_axis=0, tiled=True)

    column = lax.axis_index("frame")
    sources = -(-(EXTRAS - clips + 2) // frame_dev)
    main_rows = frame_dev * patch_dev

    def cross(blocks):
        got = [blocks[0]]
        for m in range(1, frame_axis):
            got.append(lax.ppermute(blocks[m], "frame", [(f, f ^ m) for f in range(frame_axis)]))
        return jnp.stack(got)

    def extras_out(x, meta):
        found = []
        for source in range(sources):
            mine = jnp.where(column == source, x[source], jnp.zeros((), BF))
            for dest in range(frame_axis):
                if dest != source:
                    mine = mine + lax.ppermute(x[dest], "frame", [(source, dest)])
            found.append(mine)
        out = found[0]
        for source in range(1, sources):
            frame = meta[FRAME : FRAME + EXTRAS][:, None, None]
            out = jnp.where(frame // frame_dev == source, found[source], out)
        out = out.reshape(EXTRAS * patch_t, width)
        return jnp.concatenate([out, jnp.zeros(((extras - EXTRAS) * patch_t, width), BF)])

    def extras_home(x):
        x = x.reshape(extras, patch_t, width)[:EXTRAS]
        found = []
        for source in range(frame_axis):
            mine = jnp.where(column == source, x, jnp.zeros((), BF))
            for dest in range(sources):
                if dest != source:
                    mine = mine + lax.ppermute(x, "frame", [(source, dest)])
            found.append(mine)
        return jnp.transpose(jnp.stack(found), (1, 0, 2, 3)).reshape(EXTRAS, patch_dev, width)

    meta, main_home, extra_home, cot_main, cot_extra = gather(
        lengths, frame_mask, column.reshape(1).astype(jnp.int32), latents, cotangent, frame_axis, sharers
    )
    main_s = swap(main_home.reshape(patch_axis, sub, width), "patch").reshape(main_rows, width)
    extra_t = extras_out(extra_home, meta)
    extra_t, cot_main, cot_extra = lax.optimization_barrier((extra_t, cot_main, cot_extra))
    cot_m = cross(cot_main.reshape(frame_axis, frame_dev * patch_t, width))
    cot_e = extras_out(cot_extra, meta)

    def rotate(array, by):
        perm = []
        for p in range(patch_axis):
            base = p // sharers * sharers
            perm.append((p, base + (p - base + by) % sharers))
        return lax.ppermute(array, "patch", perm)

    mod = modulation
    chunk = group_extras * patch_t
    packed = front_extra(meta, mod, extra_t, spatial_weights, heads, patch_t)
    packed, main_s = lax.optimization_barrier((packed, main_s))
    pack_got = swap(packed.reshape(frame_axis * patch_axis, chunk, 256), everyone)
    pack_got = pack_got.reshape(frame_axis * patch_axis, group_extras, patch_t, 256)
    q, kv = front_main(meta, mod, main_s, spatial_weights)
    other = jnp.stack([rotate(kv, by) for by in range(1, sharers)])
    attended = attend(q, kv, other, heads)
    attended, cot_m, cot_e = lax.optimization_barrier((attended, cot_m, cot_e))
    sent = back_main(meta, mod, main_s, attended, spatial_weights, frame_axis, frame_axis * patch_axis)
    sent, pack_got = lax.optimization_barrier((sent, pack_got))
    extra_o = extra_attend(pack_got)

    out_m, sent = temporal_main(
        meta, mod, swap(sent, everyone), cot_m, temporal_weights, heads, patch_t
    )
    extra_o, _ = lax.optimization_barrier((swap(extra_o, everyone), out_m))
    out_e, sent_e, grad_e = temporal_extra(
        meta, mod, extra_o, extra_t, cot_e, temporal_weights, spatial_weights[3:], heads, patch_t, groups
    )

    do_main, grad_s = back_grad_main(
        meta, mod, swap(sent, everyone), spatial_weights, main_rows, frame_axis
    )
    own, sent = attend_back(q, kv, other, do_main, heads)
    got = jnp.stack([rotate(sent[by - 1], -by) for by in range(1, sharers)])
    dpack = extra_attend_back(pack_got, swap(sent_e, everyone))
    dpack = swap(dpack.reshape(frame_axis * patch_axis, chunk, 256), everyone)
    dpack = dpack.reshape(heads, extras * patch_t, 256)
    lat_m = front_grad_main(meta, mod, own, got, main_s, grad_s, spatial_weights)
    dpack, out_m, out_e, _ = lax.optimization_barrier((dpack, out_m, out_e, lat_m))
    lat_e = front_grad_extra(meta, mod, dpack, extra_t, grad_e, spatial_weights, patch_t)
    lat_main = swap(lat_m.reshape(patch_axis, sub, width), "patch").reshape(frame_dev, patch_dev, width)

    out_main = cross(out_m).reshape(frame_axis, frame_dev, patch_t, width)
    slots = clips * frame_dev
    output = place(meta, out_main, extras_home(out_e), slots, sharers)
    grad = place(meta, lat_main, extras_home(lat_e), slots, 0)
    return output.reshape(latents.shape), grad.reshape(latents.shape)


def solution(mesh):
    tokens = P(None, "frame", "patch", None)
    in_specs = (tokens, tokens, P(), P(), P(), P(), P())
    return jax.shard_map(local, mesh=mesh, in_specs=in_specs, out_specs=(tokens, tokens), check_vma=False)
```

```python
import functools
import math

import jax
import jax.numpy as jnp
from jax import lax
from jax.experimental import pallas as pl
from jax.experimental.pallas import tpu as pltpu
from jax.sharding import PartitionSpec as P

HEAD = 72
EXTRAS = 5
SCALE = HEAD ** -0.5
SCALE2 = SCALE * math.log2(math.e)
BF = jnp.bfloat16
F32 = jnp.float32
VMEM_LIMIT = 56 * 1024 * 1024
LONG, COLUMN, PLACE, CLIP, FRAME, VALID, LONG_VALID, KIND, EXTRA_AT, TABLE = 0, 1, 2, 8, 16, 24, 32, 48, 64, 80


def nn(a, b):
    return lax.dot_general(a, b, (((1,), (0,)), ((), ())), preferred_element_type=F32)


def nt(a, b):
    return lax.dot_general(a, b, (((1,), (1,)), ((), ())), preferred_element_type=F32)


def tn(a, b):
    return lax.dot_general(a, b, (((0,), (0,)), ((), ())), preferred_element_type=F32)


def window(head):
    start = head * HEAD // 128 * 128
    offset = head * HEAD - start
    return start, offset, 128 if offset + HEAD <= 128 else 256


def lanes_in(width, low, high):
    lane = lax.broadcasted_iota(jnp.int32, (1, width), 1)
    return (lane >= low) & (lane < high)


def masked(x, keep):
    return jnp.where(keep, x, jnp.zeros((), x.dtype))


def take_head(x_ref, rows, head):
    start, offset, width = window(head)
    part = x_ref[rows, start : start + width].astype(F32)
    if offset:
        part = pltpu.roll(part, width - offset, 1)
    return masked(part[:, :128], lanes_in(128, 0, HEAD))


def put_head(value, head):
    start, offset, width = window(head)
    if width == 256:
        value = jnp.concatenate([value, jnp.zeros_like(value)], axis=1)
    if offset:
        value = pltpu.roll(value, offset, 1)
    return start, width, value


def room_for(count):
    return -(-count * HEAD // 128) * 128


def pack(parts):
    width = room_for(len(parts))
    out = None
    for i, part in enumerate(parts):
        if width > 128:
            part = jnp.concatenate([part, jnp.zeros((part.shape[0], width - 128), F32)], axis=1)
        if i:
            part = pltpu.roll(part, i * HEAD, 1)
        out = part if out is None else out + part
    return out


def unpack(packed, member):
    if member:
        packed = pltpu.roll(packed, packed.shape[1] - member * HEAD, 1)
    return masked(packed[:, :128], lanes_in(128, 0, HEAD))


def main_vec(meta_ref, mod_ref, block, member):
    return mod_ref[block, member, pl.ds(meta_ref[LONG], 1), :]


def extra_vec(meta_ref, mod_ref, block, member, extras, patches):
    rows = [mod_ref[block, member, pl.ds(meta_ref[CLIP + e], 1), :] for e in range(extras)]
    return jnp.concatenate([jnp.broadcast_to(r, (patches, r.shape[1])) for r in rows], axis=0)


def normed_of(x):
    average = jnp.mean(x, axis=-1, keepdims=True)
    centred = x - average
    variance = jnp.mean(centred * centred, axis=-1, keepdims=True)
    inverse = lax.rsqrt(variance + 1e-06)
    return centred * inverse, inverse


def over_rows(count, body, most=64):
    size = math.gcd(count, most)
    if count == size:
        body(slice(0, count))
        return

    def step(i, carry):
        body(pl.ds(pl.multiple_of(i * size, size), size))
        return carry

    lax.fori_loop(0, count // size, step, 0)


def modulate(x, shift, scale):
    normed, _ = normed_of(x.astype(F32))
    return (normed * (1.0 + scale) + shift).astype(BF)


def norm_back(x, grad, dmod, scale):
    normed, inverse = normed_of(x.astype(F32))
    dnormed = dmod * (1.0 + scale)
    mean_d = jnp.mean(dnormed, axis=-1, keepdims=True)
    mean_dn = jnp.mean(dnormed * normed, axis=-1, keepdims=True)
    dx = (inverse * (dnormed - mean_d - normed * mean_dn)).astype(BF)
    return (dx.astype(F32) + grad.astype(F32)).astype(BF)


def gated(x, gate, mixed):
    return (x.astype(F32) + gate * mixed).astype(BF)


def col_tiles(width):
    whole, tiles = 512, []
    start = 0
    while start < width:
        tiles.append((start, min(whole, width - start)))
        start += whole
    return tiles


def times(dest_ref, x_ref, w_ref, member, transposed=False, add=False):
    for start, size in col_tiles(w_ref.shape[-1]):
        cols = pl.ds(start, size)
        if transposed:
            product = nt(x_ref[...], w_ref[member, cols, :])
        else:
            product = nn(x_ref[...], w_ref[member, :, cols])
        if add:
            product = dest_ref[:, cols] + product
        dest_ref[:, cols] = product.astype(dest_ref.dtype)


def heads_forward(o_ref, q_ref, k_ref, v_ref, parts, bias, heads):
    for head in range(heads):
        start, offset, width = window(head)
        cols = slice(start, start + width)
        keep = lanes_in(width, offset, offset + HEAD)
        scores = [nt(masked(q_ref[rows, cols], keep), k_ref[rows, cols]) for rows in parts]
        scores = jnp.concatenate(scores, axis=0) if len(parts) > 1 else scores[0]
        if bias is not None:
            scores = scores + bias
        exponent = jnp.exp2((scores - jnp.max(scores, axis=-1, keepdims=True)) * SCALE2)
        inverse = 1.0 / jnp.sum(exponent, axis=-1, keepdims=True)
        exponent = exponent.astype(BF)
        count = exponent.shape[0] // len(parts)
        for i, rows in enumerate(parts):
            mine = slice(i * count, (i + 1) * count)
            result = nn(exponent[mine], masked(v_ref[rows, cols], keep)) * inverse[mine]
            o_ref[rows, cols] = o_ref[rows, cols] + result


def softmax_grads(q, do, k, v, bias):
    def joined(left, right):
        products = [nt(a, b) for a, b in zip(left, right)]
        return jnp.concatenate(products, axis=1) if len(products) > 1 else products[0]

    scores = joined(k, q)
    if bias is not None:
        scores = scores + bias
    exponent = jnp.exp2((scores - jnp.max(scores, axis=0, keepdims=True)) * SCALE2)
    prob = exponent * (1.0 / jnp.sum(exponent, axis=0, keepdims=True))
    dprob = joined(v, do)
    delta = jnp.sum(prob * dprob, axis=0, keepdims=True)
    dscores = prob * (dprob - delta) * SCALE
    count = scores.shape[1] // len(q)

    def split(x):
        return [x[:, i * count : (i + 1) * count] for i in range(len(q))]

    return split(dscores.astype(BF)), split(prob.astype(BF))


def heads_backward(dq_ref, dk_ref, dv_ref, q_ref, k_ref, v_ref, do_ref, parts, bias, heads):
    for head in range(heads):
        start, offset, width = window(head)
        cols = slice(start, start + width)
        keep = lanes_in(width, offset, offset + HEAD)
        q, do, k = [[masked(ref[rows, cols], keep) for rows in parts] for ref in (q_ref, do_ref, k_ref)]
        dscores, prob = softmax_grads(q, do, k, [v_ref[rows, cols] for rows in parts], bias)
        for i, rows in enumerate(parts):
            dv_ref[rows, cols] = dv_ref[rows, cols] + nn(prob[i], do[i])
            dk_ref[rows, cols] = dk_ref[rows, cols] + nn(dscores[i], q[i])
            dq_ref[rows, cols] = dq_ref[rows, cols] + tn(dscores[i], k[i])


def gather_kernel(
    lengths_ref, mask_ref, place_ref, latents_ref, cotangent_ref,
    meta_ref, main_ref, extra_ref, cot_main_ref, cot_extra_ref,
    latents_in, main_in, extra_in, sems, *, sharers,
):
    clips, frame_dev, patch_dev, width = latents_ref.shape
    frames = mask_ref.shape[1]
    frame_axis = frames // frame_dev
    patch_t = patch_dev // frame_axis
    small, sub = patch_t // sharers, patch_dev // sharers
    column, place = place_ref[0], place_ref[1]
    long = jnp.int32(0)
    for c in range(clips):
        long = long + jnp.where(lengths_ref[c] == frames, c, 0)
    for i in range(TABLE):
        meta_ref[i] = 0
    meta_ref[LONG] = long
    meta_ref[COLUMN] = column
    meta_ref[PLACE] = place
    count = jnp.int32(0)
    for c in range(clips):
        for f in range(EXTRAS - clips + 2):
            used = (c != long) & (f < lengths_ref[c])
            at = jnp.where(used, count, EXTRAS)
            meta_ref[CLIP + at] = jnp.int32(c)
            meta_ref[FRAME + at] = jnp.int32(f)
            meta_ref[VALID + at] = mask_ref[c, f]
            count = count + used.astype(jnp.int32)
    for e in range(EXTRAS, 8):
        for row in (CLIP, FRAME, VALID):
            meta_ref[row + e] = 0

    copies = []
    pairs = ((latents_ref, latents_in), (cotangent_ref, main_in))
    for i, (source, main) in enumerate(pairs):
        copies.append(pltpu.make_async_copy(source.at[long], main, sems.at[i, EXTRAS]))
        copies[-1].start()
        for e in range(EXTRAS):
            frame = lax.rem(meta_ref[FRAME + e], frame_dev)
            part = source.at[meta_ref[CLIP + e], frame]
            copies.append(pltpu.make_async_copy(part, extra_in.at[i, e], sems.at[i, e]))
            copies[-1].start()

    for f in range(frames):
        meta_ref[LONG_VALID + f] = mask_ref[long, f]
    for c in range(clips):
        for f in range(frame_dev):
            frame = column * frame_dev + f
            valid = (frame < lengths_ref[c]) & (mask_ref[c, frame] == 1)
            meta_ref[KIND + c * frame_dev + f] = jnp.where(valid, jnp.where(c == long, 1, 2), 0)
    for e in range(EXTRAS):
        local_frame = meta_ref[FRAME + e] - column * frame_dev
        here = (local_frame >= 0) & (local_frame < frame_dev)
        slot = meta_ref[CLIP + e] * frame_dev + jnp.where(here, local_frame, 0)

        @pl.when(here)
        def _(e=e, slot=slot):
            meta_ref[EXTRA_AT + slot] = jnp.int32(e)

    for copy in copies:
        copy.wait()
    patch_axis = frame_dev * sharers
    for p in range(patch_axis):
        j, group = p // sharers, p % sharers
        rows = latents_in[j] if sub % 16 == 0 else latents_in[j].astype(F32)
        main_ref[place ^ p] = rows[group * sub : (group + 1) * sub].astype(BF)
    for i, out in enumerate((extra_ref, cot_extra_ref)):
        for e in range(EXTRAS):
            rows = extra_in[i, e].astype(F32)
            for f in range(frame_axis):
                out[f, e] = rows[f * patch_t : (f + 1) * patch_t].astype(BF)
    for j in range(frame_dev):
        rows = main_in[j].astype(F32)
        for f in range(frame_axis):
            starts = [s * sub + f * small for s in range(sharers)]
            part = jnp.concatenate([rows[at : at + small] for at in starts], axis=0)
            cot_main_ref[f ^ column, j] = part.astype(BF)


def front_main_kernel(meta_ref, mod_ref, x_ref, w_ref, q_ref, kv_ref, low_ref):
    member = pl.program_id(0)

    @pl.when(member == 0)
    def _():
        shift, scale = [main_vec(meta_ref, mod_ref, 0, i) for i in range(2)]

        def body(rows):
            low_ref[rows, :] = modulate(x_ref[rows, :], shift, scale)

        over_rows(x_ref.shape[0], body)
        times(q_ref, low_ref, w_ref, 0)

    @pl.when(member > 0)
    def _():
        times(kv_ref.at[0], low_ref, w_ref, 0)


def front_extra_kernel(meta_ref, mod_ref, x_ref, w_ref, pack_ref, low_ref, out_ref, *, patches):
    member = pl.program_id(0)
    rows = x_ref.shape[0]

    @pl.when(member == 0)
    def _():
        shift, scale = [extra_vec(meta_ref, mod_ref, 0, i, rows // patches, patches) for i in range(2)]
        low_ref[...] = modulate(x_ref[...], shift, scale)

    for start, size in col_tiles(w_ref.shape[-1]):
        cols = pl.ds(start, size)
        out_ref[member, :, cols] = nn(low_ref[...], w_ref[0, :, cols])

    @pl.when(member == 2)
    def _():
        for head in range(pack_ref.shape[0]):
            parts = [take_head(out_ref.at[i], slice(None), head) for i in range(3)]
            pack_ref[head] = pack(parts).astype(BF)


def fill_keys(k_ref, v_ref, kv_ref, other_ref):
    rows = kv_ref.shape[1]
    k_ref[:rows] = kv_ref[0]
    v_ref[:rows] = kv_ref[1]
    for i in range(other_ref.shape[0]):
        k_ref[(i + 1) * rows : (i + 2) * rows] = other_ref[i, 0]
        v_ref[(i + 1) * rows : (i + 2) * rows] = other_ref[i, 1]


def attend_kernel(q_ref, kv_ref, other_ref, o_ref, k_ref, v_ref, acc_ref, *, heads):
    fill_keys(k_ref, v_ref, kv_ref, other_ref)
    acc_ref[...] = jnp.zeros_like(acc_ref)
    heads_forward(acc_ref, q_ref, k_ref, v_ref, [slice(None)], None, heads)
    o_ref[...] = acc_ref[...].astype(BF)


def extra_rows(ref, index):
    part = ref[:, index]
    return part.reshape(part.shape[0] * part.shape[1], part.shape[2])


def extra_attend_kernel(pack_ref, o_ref):
    results = []
    for index in range(pack_ref.shape[1]):
        packed = extra_rows(pack_ref, index).astype(F32)
        q, k, v = [unpack(packed, i).astype(BF) for i in range(3)]
        scores = nt(q, k)
        exponent = jnp.exp2((scores - jnp.max(scores, axis=-1, keepdims=True)) * SCALE2)
        total = jnp.sum(exponent, axis=-1, keepdims=True)
        results.append(nn(exponent.astype(BF), v) * (1.0 / total))
    o_ref[...] = pack(results).reshape(o_ref.shape).astype(BF)


def extra_attend_back_kernel(pack_ref, got_ref, grad_ref):
    devices, _, patches, _ = pack_ref.shape
    got = got_ref[...].astype(F32).reshape(devices * patches, got_ref.shape[2])
    for index in range(pack_ref.shape[1]):
        packed = extra_rows(pack_ref, index).astype(F32)
        q, k, v = [unpack(packed, i).astype(BF) for i in range(3)]
        do = unpack(got, index).astype(BF)
        (dscores,), (prob,) = softmax_grads([q], [do], [k], [v], None)
        out = pack([tn(dscores, k), nn(dscores, q), nn(prob, do)]).astype(BF)
        grad_ref[:, index] = out.reshape(devices, patches, 256)


def write_chunk(sent_ref, dest, value):
    pieces = [value[:, at : at + 128] for at in range(0, value.shape[1], 128)]
    sent_ref[dest] = jnp.concatenate(pieces, axis=0).astype(BF)


def read_chunk(got_ref, source, out_ref, row, small):
    value = got_ref[source].astype(F32)
    for i in range(out_ref.shape[1] // 128):
        out_ref[row : row + small, i * 128 : (i + 1) * 128] = value[i * small : (i + 1) * small]


def back_main_kernel(meta_ref, mod_ref, x_ref, o_ref, w_ref, sent_ref, acc_ref, *, columns):
    times(acc_ref, o_ref, w_ref, 0)
    gate = main_vec(meta_ref, mod_ref, 0, 2)

    def body(rows):
        acc_ref[rows, :] = x_ref[rows, :].astype(F32) + gate * acc_ref[rows, :]

    over_rows(x_ref.shape[0], body)
    devices = sent_ref.shape[0]
    small = x_ref.shape[0] // devices
    patch_axis = devices // columns
    for p in range(patch_axis):
        for f in range(columns):
            row = (p * columns + f) * small
            write_chunk(sent_ref, f * patch_axis + (p ^ meta_ref[PLACE]), acc_ref[row : row + small, :])


def back_grad_main_kernel(meta_ref, mod_ref, got_ref, w_ref, do_ref, g_ref, low_ref, acc_ref, *, columns):
    devices = got_ref.shape[0]
    small = g_ref.shape[0] // devices
    patch_axis = devices // columns
    for p in range(patch_axis):
        for f in range(columns):
            row = (p * columns + f) * small
            read_chunk(got_ref, f * patch_axis + (p ^ meta_ref[PLACE]), acc_ref, row, small)
    gate = main_vec(meta_ref, mod_ref, 0, 2)

    def body(rows):
        g_ref[rows, :] = acc_ref[rows, :].astype(BF)
        low_ref[rows, :] = (gate * acc_ref[rows, :]).astype(BF)

    over_rows(g_ref.shape[0], body)
    times(do_ref, low_ref, w_ref, 0, transposed=True)


def attend_back_kernel(
    q_ref, kv_ref, other_ref, do_ref, own_ref, sent_ref, k_ref, v_ref, dq_ref, dk_ref, dv_ref, *, heads
):
    rows = kv_ref.shape[1]
    fill_keys(k_ref, v_ref, kv_ref, other_ref)
    for ref in (dq_ref, dk_ref, dv_ref):
        ref[...] = jnp.zeros_like(ref)
    heads_backward(dq_ref, dk_ref, dv_ref, q_ref, k_ref, v_ref, do_ref, [slice(None)], None, heads)
    own_ref[0] = dq_ref[...].astype(BF)
    own_ref[1] = dk_ref[:rows].astype(BF)
    own_ref[2] = dv_ref[:rows].astype(BF)
    for i in range(other_ref.shape[0]):
        sent_ref[i, 0] = dk_ref[(i + 1) * rows : (i + 2) * rows].astype(BF)
        sent_ref[i, 1] = dv_ref[(i + 1) * rows : (i + 2) * rows].astype(BF)


def add_product(acc_ref, d_ref, member, w_ref):
    for start, size in col_tiles(w_ref.shape[-1]):
        cols = pl.ds(start, size)
        product = nt(d_ref[member], w_ref[0, cols, :])

        @pl.when(member == 0)
        def _(cols=cols, product=product):
            acc_ref[:, cols] = product

        @pl.when(member > 0)
        def _(cols=cols, product=product):
            acc_ref[:, cols] = acc_ref[:, cols] + product


def front_grad_main_kernel(meta_ref, mod_ref, own_ref, got_ref, x_ref, g_ref, w_ref, out_ref, d_ref, acc_ref):
    member = pl.program_id(0)

    @pl.when(member == 0)
    def _():
        d_ref[0] = own_ref[0]
        for i in range(2):
            total = own_ref[1 + i].astype(F32)
            for j in range(got_ref.shape[0]):
                total = total + got_ref[j, i].astype(F32)
            d_ref[1 + i] = total.astype(BF)

    add_product(acc_ref, d_ref, member, w_ref)

    @pl.when(member == 2)
    def _():
        scale = main_vec(meta_ref, mod_ref, 0, 1)

        def body(rows):
            out_ref[rows, :] = norm_back(x_ref[rows, :], g_ref[rows, :], acc_ref[rows, :], scale)

        over_rows(x_ref.shape[0], body)


def front_grad_extra_kernel(
    meta_ref, mod_ref, pack_ref, x_ref, g_ref, w_ref, out_ref, d_ref, acc_ref, ext_ref, *, patches
):
    member = pl.program_id(0)
    rows = x_ref.shape[0]

    @pl.when(member == 0)
    def _():
        ext_ref[...] = jnp.zeros_like(ext_ref)
        for head in range(pack_ref.shape[0]):
            packed = pack_ref[head].astype(F32)
            for i in range(3):
                start, width, value = put_head(unpack(packed, i), head)
                cols = slice(start, start + width)
                ext_ref[i, :, cols] = ext_ref[i, :, cols] + value
        d_ref[...] = ext_ref[...].astype(BF)

    add_product(acc_ref, d_ref, member, w_ref)

    @pl.when(member == 2)
    def _():
        scale = extra_vec(meta_ref, mod_ref, 0, 1, rows // patches, patches)
        out_ref[...] = norm_back(x_ref[...], g_ref[...], acc_ref[...], scale)


def key_bias(meta_ref, valid_at, clip_at, tokens, count, small, keys_axis):
    part = count * small

    def spread(base, axis):
        line = (1, tokens) if axis == 1 else (tokens, 1)
        item = lax.broadcasted_iota(jnp.int32, line, axis) % part // small
        out = jnp.zeros(line, jnp.int32)
        for i in range(count):
            out = jnp.where(item == i, meta_ref[base + i], out)
        return out

    where = lax.broadcasted_iota(jnp.int32, (tokens, tokens), keys_axis)
    other = lax.broadcasted_iota(jnp.int32, (tokens, tokens), 1 - keys_axis)
    admitted = jnp.broadcast_to(spread(valid_at, keys_axis) == 1, (tokens, tokens))
    if clip_at is not None:
        admitted = admitted & (spread(clip_at, 0) == spread(clip_at, 1))
    admitted = admitted & (where % small == other % small) & (where // part == other // part)
    return jnp.where(admitted | (where == other), 0.0, -1e30).astype(F32)


def temporal_core(vecs, w_ref, parts, biases, put, most, refs, heads):
    x_ref, cot_ref, low_ref, q_ref, k_ref, v_ref, acc_ref, dq_ref, dk_ref, dv_ref = refs
    count = x_ref.shape[0]
    shift, scale, gate = vecs

    def body(rows):
        low_ref[rows, :] = modulate(x_ref[rows, :], shift, scale)

    over_rows(count, body, most)
    for i, ref in enumerate((q_ref, k_ref, v_ref)):
        times(ref, low_ref, w_ref, i)
    acc_ref[...] = jnp.zeros_like(acc_ref)
    heads_forward(acc_ref, q_ref, k_ref, v_ref, parts, biases(1), heads)
    low_ref[...] = acc_ref[...].astype(BF)
    times(acc_ref, low_ref, w_ref, 3)

    def body(rows):
        acc_ref[rows, :] = x_ref[rows, :] + gate * acc_ref[rows, :]
        low_ref[rows, :] = (gate * cot_ref[rows, :]).astype(BF)

    over_rows(count, body, most)
    put()
    times(acc_ref, low_ref, w_ref, 3, transposed=True)
    low_ref[...] = acc_ref[...].astype(BF)
    for ref in (dq_ref, dk_ref, dv_ref):
        ref[...] = jnp.zeros_like(ref)
    heads_backward(dq_ref, dk_ref, dv_ref, q_ref, k_ref, v_ref, low_ref, parts, biases(0), heads)
    for i, ref in enumerate((dq_ref, dk_ref, dv_ref)):
        low_ref[...] = ref[...].astype(BF)
        times(acc_ref, low_ref, w_ref, i, transposed=True, add=i > 0)

    def body(rows):
        acc_ref[rows, :] = norm_back(x_ref[rows, :], cot_ref[rows, :], acc_ref[rows, :], scale).astype(F32)

    over_rows(count, body, most)


def temporal_main_kernel(meta_ref, mod_ref, got_ref, c_ref, w_ref, out_ref, sent_ref, *refs, heads, patches):
    x_ref, cot_ref, acc_ref = refs[0], refs[1], refs[6]
    columns, block, _ = c_ref.shape
    main = columns * block
    frames, each = main // patches, block // patches
    column = meta_ref[COLUMN]
    devices = got_ref.shape[0]
    small = main // devices
    sharers = patches // small
    part = frames * small

    def token(source):
        return source % sharers * part + source // sharers * small

    for source in range(devices):
        read_chunk(got_ref, source, x_ref, token(source), small)
    for f in range(columns):
        values = c_ref[column ^ f].astype(F32)
        for j in range(each):
            valid = meta_ref[LONG_VALID + f * each + j] == 1
            for g in range(sharers):
                rows = pl.ds(token((f * each + j) * sharers + g), small)
                at = j * patches + g * small
                cot_ref[rows, :] = jnp.where(valid, values[at : at + small], 0.0)

    parts = [slice(g * part, (g + 1) * part) for g in range(sharers)]
    if part % 128:
        parts = [slice(0, main)]

    def biases(axis):
        bias = key_bias(meta_ref, LONG_VALID, None, main // len(parts), frames, small, axis)
        return jnp.concatenate([bias] * len(parts), axis=1 - axis)

    def put():
        for f in range(columns):
            starts = [token(f * each * sharers + i) for i in range(each * sharers)]
            pieces = [acc_ref[at : at + small, :] for at in starts]
            out_ref[column ^ f] = jnp.concatenate(pieces, axis=0).astype(BF)

    vecs = [main_vec(meta_ref, mod_ref, 1, i) for i in range(3)]
    temporal_core(vecs, w_ref, parts, biases, put, 64, refs, heads)
    for dest in range(devices):
        write_chunk(sent_ref, dest, acc_ref[token(dest) : token(dest) + small, :])


def temporal_extra_kernel(
    meta_ref, mod_ref, got_ref, l_ref, c_ref, w_ref, ws_ref, out_ref, sent_ref, g_ref, *refs,
    heads, patches, groups,
):
    x_ref, cot_ref, acc_ref = refs[0], refs[1], refs[6]
    rows = l_ref.shape[0]
    extras = rows // patches
    each = extras // groups
    devices = got_ref.shape[0]

    def vec(block, member):
        return extra_vec(meta_ref, mod_ref, block, member, extras, patches)

    acc_ref[...] = jnp.zeros_like(acc_ref)
    for source in range(devices):
        head, group = source // groups, source % groups
        packed = got_ref[source].astype(F32)
        for e in range(each):
            at = (group * each + e) * patches
            start, size, value = put_head(unpack(packed, e), head)
            cols = slice(start, start + size)
            acc_ref[at : at + patches, cols] = acc_ref[at : at + patches, cols] + value
    gate_s = vec(0, 2)
    mixed = nn(acc_ref[...].astype(BF), ws_ref[0])
    x_ref[...] = gated(l_ref[...], gate_s, mixed).astype(F32)
    values = c_ref[...].astype(F32)
    for i in range(extras):
        part = slice(i * patches, (i + 1) * patches)
        cot_ref[part, :] = jnp.where(meta_ref[VALID + i] == 1, values[part], 0.0)

    def put():
        out_ref[...] = acc_ref[...].astype(BF)

    def biases(axis):
        return key_bias(meta_ref, VALID, CLIP, rows, extras, patches, axis)

    vecs = [vec(1, i) for i in range(3)]
    temporal_core(vecs, w_ref, [slice(0, rows)], biases, put, rows, refs, heads)
    grad = acc_ref[...]
    g_ref[...] = grad.astype(BF)
    acc_ref[...] = nt((gate_s * grad).astype(BF), ws_ref[0])
    for dest in range(devices):
        head, group = dest // groups, dest % groups
        starts = [(group * each + e) * patches for e in range(each)]
        parts = [take_head(acc_ref, slice(at, at + patches), head) for at in starts]
        sent_ref[dest] = pack(parts).astype(BF)


def place_kernel(meta_ref, main_ref, extra_ref, out_ref, *, sharers, frame_dev):
    for slot in range(out_ref.shape[0]):
        kind = meta_ref[KIND + slot]

        @pl.when(kind == 0)
        def _(slot=slot):
            out_ref[slot] = jnp.zeros_like(out_ref[slot])

        @pl.when(kind == 1)
        def _(slot=slot):
            frame = slot % frame_dev
            parts, pieces = [], []
            if sharers:
                columns = main_ref.shape[0]
                small = main_ref.shape[2] // sharers
                for f in range(columns):
                    parts.append(main_ref[meta_ref[COLUMN] ^ f, frame].astype(F32))
                pieces = [p[s * small : (s + 1) * small] for s in range(sharers) for p in parts]
            else:
                groups = main_ref.shape[0] // frame_dev
                for group in range(groups):
                    pieces.append(main_ref[meta_ref[PLACE] ^ (frame * groups + group)].astype(F32))
            out_ref[slot] = jnp.concatenate(pieces, axis=0).astype(BF)

        @pl.when(kind == 2)
        def _(slot=slot):
            out_ref[slot] = extra_ref[meta_ref[EXTRA_AT + slot]]


SCALARS = pl.BlockSpec(memory_space=pltpu.SMEM)
ANYWHERE = pl.BlockSpec(memory_space=pl.ANY)


def params(steps=0):
    semantics = {"dimension_semantics": ("arbitrary",) * steps} if steps else {}
    return pltpu.CompilerParams(vmem_limit_bytes=VMEM_LIMIT, **semantics)


def cost(flops, elements=0):
    return pl.CostEstimate(flops=int(flops), bytes_accessed=int(elements), transcendentals=0)


def whole(array):
    return pl.BlockSpec(array.shape, lambda *_: (0,) * len(array.shape))


def shape(*dims, dtype=BF):
    return jax.ShapeDtypeStruct(dims, dtype)


def weight_call(kernel, name, operands, weights, members, outs, scratch, weigh):
    width = weights.shape[-1]
    first, count = members
    return pl.pallas_call(
        kernel,
        name=name,
        grid=(count,),
        in_specs=[SCALARS]
        + [whole(a) for a in operands[1:]]
        + [pl.BlockSpec((1, width, width), lambda i: (first + i, 0, 0))],
        out_specs=[spec for spec, _ in outs],
        out_shape=[struct for _, struct in outs],
        scratch_shapes=scratch,
        compiler_params=params(1),
        cost_estimate=cost(weigh * count, 2 * width * width * count),
    )(*operands, weights)


def full(*dims):
    return whole(shape(*dims)), shape(*dims)


def gather(lengths, frame_mask, places, latents, cotangent, columns, sharers):
    _, frame_dev, patch_dev, width = latents.shape
    main = (frame_dev, patch_dev, width)
    sent = shape(frame_dev * sharers, patch_dev // sharers, width)
    patch_t = patch_dev // columns
    extra = shape(columns, EXTRAS, patch_t, width)
    return pl.pallas_call(
        functools.partial(gather_kernel, sharers=sharers),
        name="gather",
        in_specs=[SCALARS] * 3 + [ANYWHERE] * 2,
        out_specs=[SCALARS] + [pl.BlockSpec(memory_space=pltpu.VMEM)] * 4,
        out_shape=[
            shape(TABLE, dtype=jnp.int32), sent, extra, shape(columns, frame_dev, patch_t, width), extra,
        ],
        scratch_shapes=[
            pltpu.VMEM(main, BF),
            pltpu.VMEM(main, BF),
            pltpu.VMEM((2, EXTRAS, patch_dev, width), BF),
            pltpu.SemaphoreType.DMA((2, EXTRAS + 1)),
        ],
        compiler_params=params(),
    )(lengths, frame_mask, places, latents, cotangent)


def front_main(meta, mod, x, weights):
    rows, width = x.shape
    kv = pl.BlockSpec((1, rows, width), lambda i: (jnp.maximum(i - 1, 0), 0, 0)), shape(2, rows, width)
    return weight_call(
        front_main_kernel, "front_main", (meta, mod, x), weights, (0, 3),
        [full(rows, width), kv], [pltpu.VMEM((rows, width), BF)], 2 * rows * width**2,
    )


def front_extra(meta, mod, x, weights, heads, patches):
    rows, width = x.shape
    return weight_call(
        functools.partial(front_extra_kernel, patches=patches), "front_extra", (meta, mod, x), weights, (0, 3),
        [full(heads, rows, 256)], [pltpu.VMEM((rows, width), BF), pltpu.VMEM((3, rows, width), F32)],
        4 * rows * width**2,
    )[0]


def back_main(meta, mod, x, o, weights, columns, devices):
    rows, width = x.shape
    return weight_call(
        functools.partial(back_main_kernel, columns=columns), "back_main", (meta, mod, x, o), weights,
        (3, 1), [full(devices, rows * width // (devices * 128), 128)], [pltpu.VMEM((rows, width), F32)],
        3 * rows * width**2,
    )[0]


def back_grad_main(meta, mod, got, weights, rows, columns):
    width = weights.shape[-1]
    return weight_call(
        functools.partial(back_grad_main_kernel, columns=columns), "back_grad_main",
        (meta, mod, got), weights, (3, 1), [full(rows, width)] * 2,
        [pltpu.VMEM((rows, width), BF), pltpu.VMEM((rows, width), F32)], 3 * rows * width**2,
    )


def front_grad_main(meta, mod, own, got, x, g, weights):
    rows, width = x.shape
    return weight_call(
        front_grad_main_kernel, "front_grad_main", (meta, mod, own, got, x, g), weights, (0, 3),
        [full(rows, width)], [pltpu.VMEM((3, rows, width), BF), pltpu.VMEM((rows, width), F32)],
        3 * rows * width**2,
    )[0]


def front_grad_extra(meta, mod, pack, x, g, weights, patches):
    rows, width = x.shape
    return weight_call(
        functools.partial(front_grad_extra_kernel, patches=patches), "front_grad_extra",
        (meta, mod, pack, x, g), weights, (0, 3), [full(rows, width)],
        [pltpu.VMEM((3, rows, width), BF), pltpu.VMEM((rows, width), F32), pltpu.VMEM((3, rows, width), F32)],
        4 * rows * width**2,
    )[0]


def attend(q, kv, other, heads):
    rows, width = q.shape
    keys = rows * (other.shape[0] + 1)
    return pl.pallas_call(
        functools.partial(attend_kernel, heads=heads),
        name="attend",
        out_shape=shape(rows, width),
        scratch_shapes=[
            pltpu.VMEM((keys, width), BF),
            pltpu.VMEM((keys, width), BF),
            pltpu.VMEM((rows, width), F32),
        ],
        compiler_params=params(),
        cost_estimate=cost(6e9),
    )(q, kv, other)


def extra_attend(packed):
    devices, count, patches, _ = packed.shape
    return pl.pallas_call(
        extra_attend_kernel, name="extra_attend", out_shape=shape(devices, patches, room_for(count)),
        compiler_params=params(), cost_estimate=cost(4e9),
    )(packed)


def extra_attend_back(packed, got):
    return pl.pallas_call(
        extra_attend_back_kernel, name="extra_attend_back", out_shape=shape(*packed.shape),
        compiler_params=params(), cost_estimate=cost(6e9),
    )(packed, got)


def attend_back(q, kv, other, do, heads):
    rows, width = q.shape
    keys = rows * (other.shape[0] + 1)
    return pl.pallas_call(
        functools.partial(attend_back_kernel, heads=heads),
        name="attend_back",
        out_shape=[shape(3, rows, width), shape(*other.shape)],
        scratch_shapes=[
            pltpu.VMEM((keys, width), BF),
            pltpu.VMEM((keys, width), BF),
            pltpu.VMEM((rows, width), F32),
            pltpu.VMEM((keys, width), F32),
            pltpu.VMEM((keys, width), F32),
        ],
        compiler_params=params(),
        cost_estimate=cost(14e9),
    )(q, kv, other, do)


def temporal_scratch(rows, width):
    high, low = pltpu.VMEM((rows, width), F32), pltpu.VMEM((rows, width), BF)
    return [high] * 2 + [low] * 4 + [high] * 4


def temporal_main(meta, mod, got, cot, weights, heads, patches):
    columns, block, width = cot.shape
    operands = (mod, got, cot, weights)
    return pl.pallas_call(
        functools.partial(temporal_main_kernel, heads=heads, patches=patches),
        name="temporal_main",
        in_specs=[SCALARS] + [whole(a) for a in operands],
        out_shape=[shape(*cot.shape), shape(*got.shape)],
        scratch_shapes=temporal_scratch(columns * block, width),
        compiler_params=params(),
        cost_estimate=cost(25e9),
    )(meta, *operands)


def temporal_extra(meta, mod, got, le, cot, weights, last_weight, heads, patches, groups):
    operands = (mod, got, le, cot, weights, last_weight)
    return pl.pallas_call(
        functools.partial(temporal_extra_kernel, heads=heads, patches=patches, groups=groups),
        name="temporal_extra",
        in_specs=[SCALARS] + [whole(a) for a in operands],
        out_shape=[shape(*le.shape), shape(*got.shape), shape(*le.shape)],
        scratch_shapes=temporal_scratch(*le.shape),
        compiler_params=params(),
        cost_estimate=cost(14e9),
    )(meta, *operands)


def place(meta, main, extra, slots, sharers, frame_dev):
    return pl.pallas_call(
        functools.partial(place_kernel, sharers=sharers, frame_dev=frame_dev),
        name="place",
        in_specs=[SCALARS, whole(main), whole(extra)],
        out_shape=shape(slots, *extra.shape[1:]),
        compiler_params=params(),
        cost_estimate=cost(3e9),
    )(meta, main, extra)


def local(latents, cotangent, spatial_weights, temporal_weights, modulation, lengths, frame_mask):
    clips, frame_dev, patch_dev, width = latents.shape
    heads = width // HEAD
    frame_axis, patch_axis = lax.axis_size("frame"), lax.axis_size("patch")
    everyone = ("frame", "patch")
    frames = frame_dev * frame_axis
    sharers = patch_axis // frame_dev
    sub = patch_dev // sharers
    small = sub // frame_axis
    patch_t = patch_dev // frame_axis
    heads_col = heads // frame_axis
    groups = patch_axis // heads_col
    group_extras = -(-EXTRAS // groups)
    extras = groups * group_extras

    def swap(x, axis):
        return lax.all_to_all(x, axis, split_axis=0, concat_axis=0, tiled=True)

    column = lax.axis_index("frame")
    sources = -(-(EXTRAS - clips + 2) // frame_dev)
    main_rows = frame_dev * patch_dev

    def cross(blocks, axis, size):
        got = [blocks[0]]
        for m in range(1, size):
            got.append(lax.ppermute(blocks[m], axis, [(i, i ^ m) for i in range(size)]))
        return jnp.stack(got)

    def extras_out(x, meta):
        found = []
        for source in range(sources):
            mine = jnp.where(column == source, x[source], jnp.zeros((), BF))
            for dest in range(frame_axis):
                if dest != source:
                    mine = mine + lax.ppermute(x[dest], "frame", [(source, dest)])
            found.append(mine)
        out = found[0]
        for source in range(1, sources):
            frame = meta[FRAME : FRAME + EXTRAS][:, None, None]
            out = jnp.where(frame // frame_dev == source, found[source], out)
        out = out.reshape(EXTRAS * patch_t, width)
        return jnp.concatenate([out, jnp.zeros(((extras - EXTRAS) * patch_t, width), BF)])

    def extras_home(x):
        x = x.reshape(extras, patch_t, width)[:EXTRAS]
        found = []
        for source in range(frame_axis):
            mine = jnp.where(column == source, x, jnp.zeros((), BF))
            for dest in range(sources):
                if dest != source:
                    mine = mine + lax.ppermute(x, "frame", [(source, dest)])
            found.append(mine)
        return jnp.transpose(jnp.stack(found), (1, 0, 2, 3)).reshape(EXTRAS, patch_dev, width)

    meta, main_home, extra_home, cot_main, cot_extra = gather(
        lengths, frame_mask, jnp.stack([column, lax.axis_index("patch")]).astype(jnp.int32), latents, cotangent, frame_axis, sharers
    )
    main_s = cross(main_home, "patch", patch_axis).reshape(main_rows, width)
    extra_t = extras_out(extra_home, meta)
    extra_t, cot_main, cot_extra = lax.optimization_barrier((extra_t, cot_main, cot_extra))
    cot_m = cross(cot_main.reshape(frame_axis, frame_dev * patch_t, width), "frame", frame_axis)
    cot_e = extras_out(cot_extra, meta)

    def rotate(array, by):
        perm = []
        for p in range(patch_axis):
            base = p // sharers * sharers
            perm.append((p, base + (p - base + by) % sharers))
        return lax.ppermute(array, "patch", perm)

    mod = modulation
    chunk = group_extras * patch_t
    packed = front_extra(meta, mod, extra_t, spatial_weights, heads, patch_t)
    packed, main_s = lax.optimization_barrier((packed, main_s))
    pack_got = swap(packed.reshape(frame_axis * patch_axis, chunk, 256), everyone)
    pack_got = pack_got.reshape(frame_axis * patch_axis, group_extras, patch_t, 256)
    q, kv = front_main(meta, mod, main_s, spatial_weights)
    other = jnp.stack([rotate(kv, by) for by in range(1, sharers)])
    attended = attend(q, kv, other, heads)
    sent = back_main(meta, mod, main_s, attended, spatial_weights, frame_axis, frame_axis * patch_axis)
    sent, pack_got = lax.optimization_barrier((sent, pack_got))
    extra_o = extra_attend(pack_got)

    out_m, sent = temporal_main(
        meta, mod, swap(sent, everyone), cot_m, temporal_weights, heads, patch_t
    )
    extra_o, _ = lax.optimization_barrier((swap(extra_o, everyone), out_m))
    out_e, sent_e, grad_e = temporal_extra(
        meta, mod, extra_o, extra_t, cot_e, temporal_weights, spatial_weights[3:], heads, patch_t, groups
    )

    grads, sent_e = lax.optimization_barrier((swap(sent, everyone), sent_e))
    do_main, grad_s = back_grad_main(meta, mod, grads, spatial_weights, main_rows, frame_axis)
    own, sent = attend_back(q, kv, other, do_main, heads)
    got = jnp.stack([rotate(sent[by - 1], -by) for by in range(1, sharers)])
    dpack = extra_attend_back(pack_got, swap(sent_e, everyone))
    dpack = swap(dpack.reshape(frame_axis * patch_axis, chunk, 256), everyone)
    dpack = dpack.reshape(heads, extras * patch_t, 256)
    lat_m = front_grad_main(meta, mod, own, got, main_s, grad_s, spatial_weights)
    dpack, out_m, out_e, _ = lax.optimization_barrier((dpack, out_m, out_e, own))
    lat_e = front_grad_extra(meta, mod, dpack, extra_t, grad_e, spatial_weights, patch_t)
    lat_main = cross(lat_m.reshape(patch_axis, sub, width), "patch", patch_axis)

    out_main = cross(out_m, "frame", frame_axis).reshape(frame_axis, frame_dev, patch_t, width)
    slots = clips * frame_dev
    output = place(meta, out_main, extras_home(out_e), slots, sharers, frame_dev)
    grad = place(meta, lat_main, extras_home(lat_e), slots, 0, frame_dev)
    return output.reshape(latents.shape), grad.reshape(latents.shape)


def solution(mesh):
    tokens = P(None, "frame", "patch", None)
    in_specs = (tokens, tokens, P(), P(), P(), P(), P())
    return jax.shard_map(local, mesh=mesh, in_specs=in_specs, out_specs=(tokens, tokens), check_vma=False)
```

```python
import functools
import math

import jax
import jax.numpy as jnp
from jax import lax
from jax.experimental import pallas as pl
from jax.experimental.pallas import tpu as pltpu
from jax.sharding import PartitionSpec as P

HEAD = 72
EXTRAS = 5
SCALE = HEAD ** -0.5
SCALE2 = SCALE * math.log2(math.e)
BF = jnp.bfloat16
F32 = jnp.float32
VMEM_LIMIT = 56 * 1024 * 1024
LONG, COLUMN, PLACE, CLIP, FRAME, VALID, LONG_VALID, KIND, EXTRA_AT, TABLE = 0, 1, 2, 8, 16, 24, 32, 48, 64, 80


def nn(a, b):
    return lax.dot_general(a, b, (((1,), (0,)), ((), ())), preferred_element_type=F32)


def nt(a, b):
    return lax.dot_general(a, b, (((1,), (1,)), ((), ())), preferred_element_type=F32)


def tn(a, b):
    return lax.dot_general(a, b, (((0,), (0,)), ((), ())), preferred_element_type=F32)


def window(head):
    start = head * HEAD // 128 * 128
    offset = head * HEAD - start
    return start, offset, 128 if offset + HEAD <= 128 else 256


def lanes_in(width, low, high):
    lane = lax.broadcasted_iota(jnp.int32, (1, width), 1)
    return (lane >= low) & (lane < high)


def masked(x, keep):
    return jnp.where(keep, x, jnp.zeros((), x.dtype))


def take_head(x_ref, rows, head):
    start, offset, width = window(head)
    part = x_ref[rows, start : start + width].astype(F32)
    if offset:
        part = pltpu.roll(part, width - offset, 1)
    return masked(part[:, :128], lanes_in(128, 0, HEAD))


def put_head(value, head):
    start, offset, width = window(head)
    if width == 256:
        value = jnp.concatenate([value, jnp.zeros_like(value)], axis=1)
    if offset:
        value = pltpu.roll(value, offset, 1)
    return start, width, value


def room_for(count):
    return -(-count * HEAD // 128) * 128


def pack(parts):
    width = room_for(len(parts))
    out = None
    for i, part in enumerate(parts):
        if width > 128:
            part = jnp.concatenate([part, jnp.zeros((part.shape[0], width - 128), F32)], axis=1)
        if i:
            part = pltpu.roll(part, i * HEAD, 1)
        out = part if out is None else out + part
    return out


def unpack(packed, member):
    if member:
        packed = pltpu.roll(packed, packed.shape[1] - member * HEAD, 1)
    return masked(packed[:, :128], lanes_in(128, 0, HEAD))


def main_vec(meta_ref, mod_ref, block, member):
    return mod_ref[block, member, pl.ds(meta_ref[LONG], 1), :]


def extra_vec(meta_ref, mod_ref, block, member, extras, patches):
    rows = [mod_ref[block, member, pl.ds(meta_ref[CLIP + e], 1), :] for e in range(extras)]
    return jnp.concatenate([jnp.broadcast_to(r, (patches, r.shape[1])) for r in rows], axis=0)


def normed_of(x):
    average = jnp.mean(x, axis=-1, keepdims=True)
    centred = x - average
    variance = jnp.mean(centred * centred, axis=-1, keepdims=True)
    inverse = lax.rsqrt(variance + 1e-06)
    return centred * inverse, inverse


def over_rows(count, body, most=64):
    size = math.gcd(count, most)
    if count == size:
        body(slice(0, count))
        return

    def step(i, carry):
        body(pl.ds(pl.multiple_of(i * size, size), size))
        return carry

    lax.fori_loop(0, count // size, step, 0)


def modulate(x, shift, scale):
    normed, _ = normed_of(x.astype(F32))
    return (normed * (1.0 + scale) + shift).astype(BF)


def norm_back(x, grad, dmod, scale):
    normed, inverse = normed_of(x.astype(F32))
    dnormed = dmod * (1.0 + scale)
    mean_d = jnp.mean(dnormed, axis=-1, keepdims=True)
    mean_dn = jnp.mean(dnormed * normed, axis=-1, keepdims=True)
    dx = (inverse * (dnormed - mean_d - normed * mean_dn)).astype(BF)
    return (dx.astype(F32) + grad.astype(F32)).astype(BF)


def gated(x, gate, mixed):
    return (x.astype(F32) + gate * mixed).astype(BF)


def col_tiles(width):
    whole, tiles = 512, []
    start = 0
    while start < width:
        tiles.append((start, min(whole, width - start)))
        start += whole
    return tiles


def times(dest_ref, x_ref, w_ref, member, transposed=False, add=False):
    for start, size in col_tiles(w_ref.shape[-1]):
        cols = pl.ds(start, size)
        if transposed:
            product = nt(x_ref[...], w_ref[member, cols, :])
        else:
            product = nn(x_ref[...], w_ref[member, :, cols])
        if add:
            product = dest_ref[:, cols] + product
        dest_ref[:, cols] = product.astype(dest_ref.dtype)


def heads_forward(o_ref, q_ref, k_ref, v_ref, parts, bias, heads):
    for head in range(heads):
        start, offset, width = window(head)
        cols = slice(start, start + width)
        keep = lanes_in(width, offset, offset + HEAD)
        scores = [nt(masked(q_ref[rows, cols], keep), k_ref[rows, cols]) for rows in parts]
        scores = jnp.concatenate(scores, axis=0) if len(parts) > 1 else scores[0]
        if bias is not None:
            scores = scores + bias
        exponent = jnp.exp2((scores - jnp.max(scores, axis=-1, keepdims=True)) * SCALE2)
        inverse = 1.0 / jnp.sum(exponent, axis=-1, keepdims=True)
        exponent = exponent.astype(BF)
        count = exponent.shape[0] // len(parts)
        for i, rows in enumerate(parts):
            mine = slice(i * count, (i + 1) * count)
            result = nn(exponent[mine], masked(v_ref[rows, cols], keep)) * inverse[mine]
            o_ref[rows, cols] = o_ref[rows, cols] + result


def softmax_grads(q, do, k, v, bias):
    def joined(left, right):
        products = [nt(a, b) for a, b in zip(left, right)]
        return jnp.concatenate(products, axis=1) if len(products) > 1 else products[0]

    scores = joined(k, q)
    if bias is not None:
        scores = scores + bias
    exponent = jnp.exp2((scores - jnp.max(scores, axis=0, keepdims=True)) * SCALE2)
    prob = exponent * (1.0 / jnp.sum(exponent, axis=0, keepdims=True))
    dprob = joined(v, do)
    delta = jnp.sum(prob * dprob, axis=0, keepdims=True)
    dscores = prob * (dprob - delta) * SCALE
    count = scores.shape[1] // len(q)

    def split(x):
        return [x[:, i * count : (i + 1) * count] for i in range(len(q))]

    return split(dscores.astype(BF)), split(prob.astype(BF))


def heads_backward(dq_ref, dk_ref, dv_ref, q_ref, k_ref, v_ref, do_ref, parts, bias, heads):
    for head in range(heads):
        start, offset, width = window(head)
        cols = slice(start, start + width)
        keep = lanes_in(width, offset, offset + HEAD)
        q, do, k = [[masked(ref[rows, cols], keep) for rows in parts] for ref in (q_ref, do_ref, k_ref)]
        dscores, prob = softmax_grads(q, do, k, [v_ref[rows, cols] for rows in parts], bias)
        for i, rows in enumerate(parts):
            dv_ref[rows, cols] = dv_ref[rows, cols] + nn(prob[i], do[i])
            dk_ref[rows, cols] = dk_ref[rows, cols] + nn(dscores[i], q[i])
            dq_ref[rows, cols] = dq_ref[rows, cols] + tn(dscores[i], k[i])


def gather_kernel(
    lengths_ref, mask_ref, place_ref, latents_ref, cotangent_ref,
    meta_ref, main_ref, extra_ref, cot_main_ref, cot_extra_ref,
    latents_in, main_in, extra_in, sems, *, sharers,
):
    clips, frame_dev, patch_dev, width = latents_ref.shape
    frames = mask_ref.shape[1]
    frame_axis = frames // frame_dev
    patch_t = patch_dev // frame_axis
    small, sub = patch_t // sharers, patch_dev // sharers
    column, place = place_ref[0], place_ref[1]
    long = jnp.int32(0)
    for c in range(clips):
        long = long + jnp.where(lengths_ref[c] == frames, c, 0)
    for i in range(TABLE):
        meta_ref[i] = 0
    meta_ref[LONG] = long
    meta_ref[COLUMN] = column
    meta_ref[PLACE] = place
    count = jnp.int32(0)
    for c in range(clips):
        for f in range(EXTRAS - clips + 2):
            used = (c != long) & (f < lengths_ref[c])
            at = jnp.where(used, count, EXTRAS)
            meta_ref[CLIP + at] = jnp.int32(c)
            meta_ref[FRAME + at] = jnp.int32(f)
            meta_ref[VALID + at] = mask_ref[c, f]
            count = count + used.astype(jnp.int32)
    for e in range(EXTRAS, 8):
        for row in (CLIP, FRAME, VALID):
            meta_ref[row + e] = 0

    copies = []
    pairs = ((latents_ref, latents_in), (cotangent_ref, main_in))
    for i, (source, main) in enumerate(pairs):
        copies.append(pltpu.make_async_copy(source.at[long], main, sems.at[i, EXTRAS]))
        copies[-1].start()
        for e in range(EXTRAS):
            frame = lax.rem(meta_ref[FRAME + e], frame_dev)
            part = source.at[meta_ref[CLIP + e], frame]
            copies.append(pltpu.make_async_copy(part, extra_in.at[i, e], sems.at[i, e]))
            copies[-1].start()

    for f in range(frames):
        meta_ref[LONG_VALID + f] = mask_ref[long, f]
    for c in range(clips):
        for f in range(frame_dev):
            frame = column * frame_dev + f
            valid = (frame < lengths_ref[c]) & (mask_ref[c, frame] == 1)
            meta_ref[KIND + c * frame_dev + f] = jnp.where(valid, jnp.where(c == long, 1, 2), 0)
    for e in range(EXTRAS):
        local_frame = meta_ref[FRAME + e] - column * frame_dev
        here = (local_frame >= 0) & (local_frame < frame_dev)
        slot = meta_ref[CLIP + e] * frame_dev + jnp.where(here, local_frame, 0)

        @pl.when(here)
        def _(e=e, slot=slot):
            meta_ref[EXTRA_AT + slot] = jnp.int32(e)

    for copy in copies:
        copy.wait()
    patch_axis = frame_dev * sharers
    for p in range(patch_axis):
        j, group = p // sharers, p % sharers
        rows = latents_in[j] if sub % 16 == 0 else latents_in[j].astype(F32)
        main_ref[place ^ p] = rows[group * sub : (group + 1) * sub].astype(BF)
    for i, out in enumerate((extra_ref, cot_extra_ref)):
        for e in range(EXTRAS):
            rows = extra_in[i, e].astype(F32)
            for f in range(frame_axis):
                out[f, e] = rows[f * patch_t : (f + 1) * patch_t].astype(BF)
    for j in range(frame_dev):
        rows = main_in[j].astype(F32)
        for f in range(frame_axis):
            starts = [s * sub + f * small for s in range(sharers)]
            part = jnp.concatenate([rows[at : at + small] for at in starts], axis=0)
            cot_main_ref[f ^ column, j] = part.astype(BF)


def front_main_kernel(meta_ref, mod_ref, x_ref, w_ref, q_ref, kv_ref, low_ref):
    member = pl.program_id(0)

    @pl.when(member == 0)
    def _():
        shift, scale = [main_vec(meta_ref, mod_ref, 0, i) for i in range(2)]

        def body(rows):
            low_ref[rows, :] = modulate(x_ref[rows, :], shift, scale)

        over_rows(x_ref.shape[0], body)
        times(q_ref, low_ref, w_ref, 0)

    @pl.when(member > 0)
    def _():
        times(kv_ref.at[0], low_ref, w_ref, 0)


def front_extra_kernel(meta_ref, mod_ref, x_ref, w_ref, pack_ref, low_ref, out_ref, *, patches):
    member = pl.program_id(0)
    rows = x_ref.shape[0]

    @pl.when(member == 0)
    def _():
        shift, scale = [extra_vec(meta_ref, mod_ref, 0, i, rows // patches, patches) for i in range(2)]
        low_ref[...] = modulate(x_ref[...], shift, scale)

    for start, size in col_tiles(w_ref.shape[-1]):
        cols = pl.ds(start, size)
        out_ref[member, :, cols] = nn(low_ref[...], w_ref[0, :, cols])

    @pl.when(member == 2)
    def _():
        for head in range(pack_ref.shape[0]):
            parts = [take_head(out_ref.at[i], slice(None), head) for i in range(3)]
            pack_ref[head] = pack(parts).astype(BF)


def fill_keys(k_ref, v_ref, kv_ref, other_ref):
    rows = kv_ref.shape[1]
    k_ref[:rows] = kv_ref[0]
    v_ref[:rows] = kv_ref[1]
    for i in range(other_ref.shape[0]):
        k_ref[(i + 1) * rows : (i + 2) * rows] = other_ref[i, 0]
        v_ref[(i + 1) * rows : (i + 2) * rows] = other_ref[i, 1]


def attend_kernel(q_ref, kv_ref, other_ref, o_ref, k_ref, v_ref, acc_ref, *, heads):
    fill_keys(k_ref, v_ref, kv_ref, other_ref)
    acc_ref[...] = jnp.zeros_like(acc_ref)
    heads_forward(acc_ref, q_ref, k_ref, v_ref, [slice(None)], None, heads)
    o_ref[...] = acc_ref[...].astype(BF)


def extra_rows(ref, index):
    part = ref[:, index]
    return part.reshape(part.shape[0] * part.shape[1], part.shape[2])


def extra_attend_kernel(pack_ref, o_ref):
    results = []
    for index in range(pack_ref.shape[1]):
        packed = extra_rows(pack_ref, index).astype(F32)
        q, k, v = [unpack(packed, i).astype(BF) for i in range(3)]
        scores = nt(q, k)
        exponent = jnp.exp2((scores - jnp.max(scores, axis=-1, keepdims=True)) * SCALE2)
        total = jnp.sum(exponent, axis=-1, keepdims=True)
        results.append(nn(exponent.astype(BF), v) * (1.0 / total))
    o_ref[...] = pack(results).reshape(o_ref.shape).astype(BF)


def extra_attend_back_kernel(pack_ref, got_ref, grad_ref):
    devices, _, patches, _ = pack_ref.shape
    got = got_ref[...].astype(F32).reshape(devices * patches, got_ref.shape[2])
    for index in range(pack_ref.shape[1]):
        packed = extra_rows(pack_ref, index).astype(F32)
        q, k, v = [unpack(packed, i).astype(BF) for i in range(3)]
        do = unpack(got, index).astype(BF)
        (dscores,), (prob,) = softmax_grads([q], [do], [k], [v], None)
        out = pack([tn(dscores, k), nn(dscores, q), nn(prob, do)]).astype(BF)
        grad_ref[:, index] = out.reshape(devices, patches, 256)


def write_chunk(sent_ref, dest, value):
    pieces = [value[:, at : at + 128] for at in range(0, value.shape[1], 128)]
    sent_ref[dest] = jnp.concatenate(pieces, axis=0).astype(BF)


def read_chunk(got_ref, source, out_ref, row, small):
    value = got_ref[source].astype(F32)
    for i in range(out_ref.shape[1] // 128):
        out_ref[row : row + small, i * 128 : (i + 1) * 128] = value[i * small : (i + 1) * small]


def back_main_kernel(meta_ref, mod_ref, x_ref, o_ref, w_ref, sent_ref, acc_ref, *, columns):
    times(acc_ref, o_ref, w_ref, 0)
    gate = main_vec(meta_ref, mod_ref, 0, 2)

    def body(rows):
        acc_ref[rows, :] = x_ref[rows, :].astype(F32) + gate * acc_ref[rows, :]

    over_rows(x_ref.shape[0], body)
    devices = sent_ref.shape[0]
    small = x_ref.shape[0] // devices
    patch_axis = devices // columns
    for p in range(patch_axis):
        for f in range(columns):
            row = (p * columns + f) * small
            write_chunk(sent_ref, f * patch_axis + (p ^ meta_ref[PLACE]), acc_ref[row : row + small, :])


def back_grad_main_kernel(meta_ref, mod_ref, got_ref, w_ref, do_ref, g_ref, low_ref, acc_ref, *, columns):
    devices = got_ref.shape[0]
    small = g_ref.shape[0] // devices
    patch_axis = devices // columns
    for p in range(patch_axis):
        for f in range(columns):
            row = (p * columns + f) * small
            read_chunk(got_ref, f * patch_axis + (p ^ meta_ref[PLACE]), acc_ref, row, small)
    gate = main_vec(meta_ref, mod_ref, 0, 2)

    def body(rows):
        g_ref[rows, :] = acc_ref[rows, :].astype(BF)
        low_ref[rows, :] = (gate * acc_ref[rows, :]).astype(BF)

    over_rows(g_ref.shape[0], body)
    times(do_ref, low_ref, w_ref, 0, transposed=True)


def attend_back_kernel(
    q_ref, kv_ref, other_ref, do_ref, own_ref, sent_ref, k_ref, v_ref, dq_ref, dk_ref, dv_ref, *, heads
):
    rows = kv_ref.shape[1]
    fill_keys(k_ref, v_ref, kv_ref, other_ref)
    for ref in (dq_ref, dk_ref, dv_ref):
        ref[...] = jnp.zeros_like(ref)
    heads_backward(dq_ref, dk_ref, dv_ref, q_ref, k_ref, v_ref, do_ref, [slice(None)], None, heads)
    own_ref[0] = dq_ref[...].astype(BF)
    own_ref[1] = dk_ref[:rows].astype(BF)
    own_ref[2] = dv_ref[:rows].astype(BF)
    for i in range(other_ref.shape[0]):
        sent_ref[i, 0] = dk_ref[(i + 1) * rows : (i + 2) * rows].astype(BF)
        sent_ref[i, 1] = dv_ref[(i + 1) * rows : (i + 2) * rows].astype(BF)


def add_product(acc_ref, d_ref, member, w_ref):
    for start, size in col_tiles(w_ref.shape[-1]):
        cols = pl.ds(start, size)
        product = nt(d_ref[member], w_ref[0, cols, :])

        @pl.when(member == 0)
        def _(cols=cols, product=product):
            acc_ref[:, cols] = product

        @pl.when(member > 0)
        def _(cols=cols, product=product):
            acc_ref[:, cols] = acc_ref[:, cols] + product


def front_grad_main_kernel(meta_ref, mod_ref, own_ref, got_ref, x_ref, g_ref, w_ref, out_ref, d_ref, acc_ref):
    member = pl.program_id(0)

    @pl.when(member == 0)
    def _():
        d_ref[0] = own_ref[0]
        for i in range(2):
            total = own_ref[1 + i].astype(F32)
            for j in range(got_ref.shape[0]):
                total = total + got_ref[j, i].astype(F32)
            d_ref[1 + i] = total.astype(BF)

    add_product(acc_ref, d_ref, member, w_ref)

    @pl.when(member == 2)
    def _():
        scale = main_vec(meta_ref, mod_ref, 0, 1)

        def body(rows):
            out_ref[rows, :] = norm_back(x_ref[rows, :], g_ref[rows, :], acc_ref[rows, :], scale)

        over_rows(x_ref.shape[0], body)


def front_grad_extra_kernel(
    meta_ref, mod_ref, pack_ref, x_ref, g_ref, w_ref, out_ref, d_ref, acc_ref, ext_ref, *, patches
):
    member = pl.program_id(0)
    rows = x_ref.shape[0]

    @pl.when(member == 0)
    def _():
        ext_ref[...] = jnp.zeros_like(ext_ref)
        for head in range(pack_ref.shape[0]):
            packed = pack_ref[head].astype(F32)
            for i in range(3):
                start, width, value = put_head(unpack(packed, i), head)
                cols = slice(start, start + width)
                ext_ref[i, :, cols] = ext_ref[i, :, cols] + value
        d_ref[...] = ext_ref[...].astype(BF)

    add_product(acc_ref, d_ref, member, w_ref)

    @pl.when(member == 2)
    def _():
        scale = extra_vec(meta_ref, mod_ref, 0, 1, rows // patches, patches)
        out_ref[...] = norm_back(x_ref[...], g_ref[...], acc_ref[...], scale)


def key_bias(meta_ref, valid_at, clip_at, tokens, count, small, keys_axis):
    part = count * small

    def spread(base, axis):
        line = (1, tokens) if axis == 1 else (tokens, 1)
        item = lax.broadcasted_iota(jnp.int32, line, axis) % part // small
        out = jnp.zeros(line, jnp.int32)
        for i in range(count):
            out = jnp.where(item == i, meta_ref[base + i], out)
        return out

    where = lax.broadcasted_iota(jnp.int32, (tokens, tokens), keys_axis)
    other = lax.broadcasted_iota(jnp.int32, (tokens, tokens), 1 - keys_axis)
    admitted = jnp.broadcast_to(spread(valid_at, keys_axis) == 1, (tokens, tokens))
    if clip_at is not None:
        admitted = admitted & (spread(clip_at, 0) == spread(clip_at, 1))
    admitted = admitted & (where % small == other % small) & (where // part == other // part)
    return jnp.where(admitted | (where == other), 0.0, -1e30).astype(F32)


def temporal_core(vecs, w_ref, parts, biases, put, most, refs, heads):
    x_ref, cot_ref, low_ref, q_ref, k_ref, v_ref, acc_ref, dq_ref, dk_ref, dv_ref = refs
    count = x_ref.shape[0]
    shift, scale, gate = vecs

    def body(rows):
        low_ref[rows, :] = modulate(x_ref[rows, :], shift, scale)

    over_rows(count, body, most)
    for i, ref in enumerate((q_ref, k_ref, v_ref)):
        times(ref, low_ref, w_ref, i)
    acc_ref[...] = jnp.zeros_like(acc_ref)
    heads_forward(acc_ref, q_ref, k_ref, v_ref, parts, biases(1), heads)
    low_ref[...] = acc_ref[...].astype(BF)
    times(acc_ref, low_ref, w_ref, 3)

    def body(rows):
        acc_ref[rows, :] = x_ref[rows, :] + gate * acc_ref[rows, :]
        low_ref[rows, :] = (gate * cot_ref[rows, :]).astype(BF)

    over_rows(count, body, most)
    put()
    times(acc_ref, low_ref, w_ref, 3, transposed=True)
    low_ref[...] = acc_ref[...].astype(BF)
    for ref in (dq_ref, dk_ref, dv_ref):
        ref[...] = jnp.zeros_like(ref)
    heads_backward(dq_ref, dk_ref, dv_ref, q_ref, k_ref, v_ref, low_ref, parts, biases(0), heads)
    for i, ref in enumerate((dq_ref, dk_ref, dv_ref)):
        low_ref[...] = ref[...].astype(BF)
        times(acc_ref, low_ref, w_ref, i, transposed=True, add=i > 0)

    def body(rows):
        acc_ref[rows, :] = norm_back(x_ref[rows, :], cot_ref[rows, :], acc_ref[rows, :], scale).astype(F32)

    over_rows(count, body, most)


def temporal_main_kernel(meta_ref, mod_ref, got_ref, c_ref, w_ref, out_ref, sent_ref, *refs, heads, patches):
    x_ref, cot_ref, acc_ref = refs[0], refs[1], refs[6]
    columns, block, _ = c_ref.shape
    main = columns * block
    frames, each = main // patches, block // patches
    column = meta_ref[COLUMN]
    devices = got_ref.shape[0]
    small = main // devices
    sharers = patches // small
    part = frames * small

    def token(source):
        return source % sharers * part + source // sharers * small

    for source in range(devices):
        read_chunk(got_ref, source, x_ref, token(source), small)
    for f in range(columns):
        values = c_ref[column ^ f].astype(F32)
        for j in range(each):
            valid = meta_ref[LONG_VALID + f * each + j] == 1
            for g in range(sharers):
                rows = pl.ds(token((f * each + j) * sharers + g), small)
                at = j * patches + g * small
                cot_ref[rows, :] = jnp.where(valid, values[at : at + small], 0.0)

    parts = [slice(g * part, (g + 1) * part) for g in range(sharers)]
    if part % 128:
        parts = [slice(0, main)]

    def biases(axis):
        bias = key_bias(meta_ref, LONG_VALID, None, main // len(parts), frames, small, axis)
        return jnp.concatenate([bias] * len(parts), axis=1 - axis)

    def put():
        for f in range(columns):
            starts = [token(f * each * sharers + i) for i in range(each * sharers)]
            pieces = [acc_ref[at : at + small, :] for at in starts]
            out_ref[column ^ f] = jnp.concatenate(pieces, axis=0).astype(BF)

    vecs = [main_vec(meta_ref, mod_ref, 1, i) for i in range(3)]
    temporal_core(vecs, w_ref, parts, biases, put, 64, refs, heads)
    for dest in range(devices):
        write_chunk(sent_ref, dest, acc_ref[token(dest) : token(dest) + small, :])


def temporal_extra_kernel(
    meta_ref, mod_ref, got_ref, l_ref, c_ref, w_ref, ws_ref, out_ref, sent_ref, g_ref, *refs,
    heads, patches, groups,
):
    x_ref, cot_ref, acc_ref = refs[0], refs[1], refs[6]
    rows = l_ref.shape[0]
    extras = rows // patches
    each = extras // groups
    devices = got_ref.shape[0]

    def vec(block, member):
        return extra_vec(meta_ref, mod_ref, block, member, extras, patches)

    acc_ref[...] = jnp.zeros_like(acc_ref)
    for source in range(devices):
        head, group = source // groups, source % groups
        packed = got_ref[source].astype(F32)
        for e in range(each):
            at = (group * each + e) * patches
            start, size, value = put_head(unpack(packed, e), head)
            cols = slice(start, start + size)
            acc_ref[at : at + patches, cols] = acc_ref[at : at + patches, cols] + value
    gate_s = vec(0, 2)
    mixed = nn(acc_ref[...].astype(BF), ws_ref[0])
    x_ref[...] = gated(l_ref[...], gate_s, mixed).astype(F32)
    values = c_ref[...].astype(F32)
    for i in range(extras):
        part = slice(i * patches, (i + 1) * patches)
        cot_ref[part, :] = jnp.where(meta_ref[VALID + i] == 1, values[part], 0.0)

    def put():
        out_ref[...] = acc_ref[...].astype(BF)

    def biases(axis):
        return key_bias(meta_ref, VALID, CLIP, rows, extras, patches, axis)

    vecs = [vec(1, i) for i in range(3)]
    temporal_core(vecs, w_ref, [slice(0, rows)], biases, put, rows, refs, heads)
    grad = acc_ref[...]
    g_ref[...] = grad.astype(BF)
    acc_ref[...] = nt((gate_s * grad).astype(BF), ws_ref[0])
    for dest in range(devices):
        head, group = dest // groups, dest % groups
        starts = [(group * each + e) * patches for e in range(each)]
        parts = [take_head(acc_ref, slice(at, at + patches), head) for at in starts]
        sent_ref[dest] = pack(parts).astype(BF)


def place_kernel(meta_ref, main_ref, extra_ref, out_ref, *, sharers, frame_dev):
    for slot in range(out_ref.shape[0]):
        kind = meta_ref[KIND + slot]

        @pl.when(kind == 0)
        def _(slot=slot):
            out_ref[slot] = jnp.zeros_like(out_ref[slot])

        @pl.when(kind == 1)
        def _(slot=slot):
            frame = slot % frame_dev
            parts, pieces = [], []
            if sharers:
                columns = main_ref.shape[0]
                small = main_ref.shape[2] // sharers
                for f in range(columns):
                    parts.append(main_ref[meta_ref[COLUMN] ^ f, frame].astype(F32))
                pieces = [p[s * small : (s + 1) * small] for s in range(sharers) for p in parts]
            else:
                groups = main_ref.shape[0] // frame_dev
                for group in range(groups):
                    pieces.append(main_ref[meta_ref[PLACE] ^ (frame * groups + group)].astype(F32))
            out_ref[slot] = jnp.concatenate(pieces, axis=0).astype(BF)

        @pl.when(kind == 2)
        def _(slot=slot):
            out_ref[slot] = extra_ref[meta_ref[EXTRA_AT + slot]]


SCALARS = pl.BlockSpec(memory_space=pltpu.SMEM)
ANYWHERE = pl.BlockSpec(memory_space=pl.ANY)


def params(steps=0):
    semantics = {"dimension_semantics": ("arbitrary",) * steps} if steps else {}
    return pltpu.CompilerParams(vmem_limit_bytes=VMEM_LIMIT, **semantics)


def cost(flops, elements=0):
    return pl.CostEstimate(flops=int(flops) // 1000, bytes_accessed=int(elements) // 1000, transcendentals=0)


def whole(array):
    return pl.BlockSpec(array.shape, lambda *_: (0,) * len(array.shape))


def shape(*dims, dtype=BF):
    return jax.ShapeDtypeStruct(dims, dtype)


def weight_call(kernel, name, operands, weights, members, outs, scratch, weigh):
    width = weights.shape[-1]
    first, count = members
    return pl.pallas_call(
        kernel,
        name=name,
        grid=(count,),
        in_specs=[SCALARS]
        + [whole(a) for a in operands[1:]]
        + [pl.BlockSpec((1, width, width), lambda i: (first + i, 0, 0))],
        out_specs=[spec for spec, _ in outs],
        out_shape=[struct for _, struct in outs],
        scratch_shapes=scratch,
        compiler_params=params(1),
        cost_estimate=cost(weigh * count, 2 * width * width * count),
    )(*operands, weights)


def full(*dims):
    return whole(shape(*dims)), shape(*dims)


def gather(lengths, frame_mask, places, latents, cotangent, columns, sharers):
    _, frame_dev, patch_dev, width = latents.shape
    main = (frame_dev, patch_dev, width)
    sent = shape(frame_dev * sharers, patch_dev // sharers, width)
    patch_t = patch_dev // columns
    extra = shape(columns, EXTRAS, patch_t, width)
    return pl.pallas_call(
        functools.partial(gather_kernel, sharers=sharers),
        name="gather",
        in_specs=[SCALARS] * 3 + [ANYWHERE] * 2,
        out_specs=[SCALARS] + [pl.BlockSpec(memory_space=pltpu.VMEM)] * 4,
        out_shape=[
            shape(TABLE, dtype=jnp.int32), sent, extra, shape(columns, frame_dev, patch_t, width), extra,
        ],
        scratch_shapes=[
            pltpu.VMEM(main, BF),
            pltpu.VMEM(main, BF),
            pltpu.VMEM((2, EXTRAS, patch_dev, width), BF),
            pltpu.SemaphoreType.DMA((2, EXTRAS + 1)),
        ],
        compiler_params=params(),
    )(lengths, frame_mask, places, latents, cotangent)


def front_main(meta, mod, x, weights):
    rows, width = x.shape
    kv = pl.BlockSpec((1, rows, width), lambda i: (jnp.maximum(i - 1, 0), 0, 0)), shape(2, rows, width)
    return weight_call(
        front_main_kernel, "front_main", (meta, mod, x), weights, (0, 3),
        [full(rows, width), kv], [pltpu.VMEM((rows, width), BF)], 2 * rows * width**2,
    )


def front_extra(meta, mod, x, weights, heads, patches):
    rows, width = x.shape
    return weight_call(
        functools.partial(front_extra_kernel, patches=patches), "front_extra", (meta, mod, x), weights, (0, 3),
        [full(heads, rows, 256)], [pltpu.VMEM((rows, width), BF), pltpu.VMEM((3, rows, width), F32)],
        4 * rows * width**2,
    )[0]


def back_main(meta, mod, x, o, weights, columns, devices):
    rows, width = x.shape
    return weight_call(
        functools.partial(back_main_kernel, columns=columns), "back_main", (meta, mod, x, o), weights,
        (3, 1), [full(devices, rows * width // (devices * 128), 128)], [pltpu.VMEM((rows, width), F32)],
        3 * rows * width**2,
    )[0]


def back_grad_main(meta, mod, got, weights, rows, columns):
    width = weights.shape[-1]
    return weight_call(
        functools.partial(back_grad_main_kernel, columns=columns), "back_grad_main",
        (meta, mod, got), weights, (3, 1), [full(rows, width)] * 2,
        [pltpu.VMEM((rows, width), BF), pltpu.VMEM((rows, width), F32)], 3 * rows * width**2,
    )


def front_grad_main(meta, mod, own, got, x, g, weights):
    rows, width = x.shape
    return weight_call(
        front_grad_main_kernel, "front_grad_main", (meta, mod, own, got, x, g), weights, (0, 3),
        [full(rows, width)], [pltpu.VMEM((3, rows, width), BF), pltpu.VMEM((rows, width), F32)],
        3 * rows * width**2,
    )[0]


def front_grad_extra(meta, mod, pack, x, g, weights, patches):
    rows, width = x.shape
    return weight_call(
        functools.partial(front_grad_extra_kernel, patches=patches), "front_grad_extra",
        (meta, mod, pack, x, g), weights, (0, 3), [full(rows, width)],
        [pltpu.VMEM((3, rows, width), BF), pltpu.VMEM((rows, width), F32), pltpu.VMEM((3, rows, width), F32)],
        4 * rows * width**2,
    )[0]


def attend(q, kv, other, heads):
    rows, width = q.shape
    keys = rows * (other.shape[0] + 1)
    return pl.pallas_call(
        functools.partial(attend_kernel, heads=heads),
        name="attend",
        out_shape=shape(rows, width),
        scratch_shapes=[
            pltpu.VMEM((keys, width), BF),
            pltpu.VMEM((keys, width), BF),
            pltpu.VMEM((rows, width), F32),
        ],
        compiler_params=params(),
        cost_estimate=cost(6e9),
    )(q, kv, other)


def extra_attend(packed):
    devices, count, patches, _ = packed.shape
    return pl.pallas_call(
        extra_attend_kernel, name="extra_attend", out_shape=shape(devices, patches, room_for(count)),
        compiler_params=params(), cost_estimate=cost(4e9),
    )(packed)


def extra_attend_back(packed, got):
    return pl.pallas_call(
        extra_attend_back_kernel, name="extra_attend_back", out_shape=shape(*packed.shape),
        compiler_params=params(), cost_estimate=cost(6e9),
    )(packed, got)


def attend_back(q, kv, other, do, heads):
    rows, width = q.shape
    keys = rows * (other.shape[0] + 1)
    return pl.pallas_call(
        functools.partial(attend_back_kernel, heads=heads),
        name="attend_back",
        out_shape=[shape(3, rows, width), shape(*other.shape)],
        scratch_shapes=[
            pltpu.VMEM((keys, width), BF),
            pltpu.VMEM((keys, width), BF),
            pltpu.VMEM((rows, width), F32),
            pltpu.VMEM((keys, width), F32),
            pltpu.VMEM((keys, width), F32),
        ],
        compiler_params=params(),
        cost_estimate=cost(14e9),
    )(q, kv, other, do)


def temporal_scratch(rows, width):
    high, low = pltpu.VMEM((rows, width), F32), pltpu.VMEM((rows, width), BF)
    return [high] * 2 + [low] * 4 + [high] * 4


def temporal_main(meta, mod, got, cot, weights, heads, patches):
    columns, block, width = cot.shape
    operands = (mod, got, cot, weights)
    return pl.pallas_call(
        functools.partial(temporal_main_kernel, heads=heads, patches=patches),
        name="temporal_main",
        in_specs=[SCALARS] + [whole(a) for a in operands],
        out_shape=[shape(*cot.shape), shape(*got.shape)],
        scratch_shapes=temporal_scratch(columns * block, width),
        compiler_params=params(),
        cost_estimate=cost(25e9),
    )(meta, *operands)


def temporal_extra(meta, mod, got, le, cot, weights, last_weight, heads, patches, groups):
    operands = (mod, got, le, cot, weights, last_weight)
    return pl.pallas_call(
        functools.partial(temporal_extra_kernel, heads=heads, patches=patches, groups=groups),
        name="temporal_extra",
        in_specs=[SCALARS] + [whole(a) for a in operands],
        out_shape=[shape(*le.shape), shape(*got.shape), shape(*le.shape)],
        scratch_shapes=temporal_scratch(*le.shape),
        compiler_params=params(),
        cost_estimate=cost(14e9),
    )(meta, *operands)


def place(meta, main, extra, slots, sharers, frame_dev):
    return pl.pallas_call(
        functools.partial(place_kernel, sharers=sharers, frame_dev=frame_dev),
        name="place",
        in_specs=[SCALARS, whole(main), whole(extra)],
        out_shape=shape(slots, *extra.shape[1:]),
        compiler_params=params(),
        cost_estimate=cost(3e9),
    )(meta, main, extra)


def local(latents, cotangent, spatial_weights, temporal_weights, modulation, lengths, frame_mask):
    clips, frame_dev, patch_dev, width = latents.shape
    heads = width // HEAD
    frame_axis, patch_axis = lax.axis_size("frame"), lax.axis_size("patch")
    everyone = ("frame", "patch")
    frames = frame_dev * frame_axis
    sharers = patch_axis // frame_dev
    sub = patch_dev // sharers
    small = sub // frame_axis
    patch_t = patch_dev // frame_axis
    heads_col = heads // frame_axis
    groups = patch_axis // heads_col
    group_extras = -(-EXTRAS // groups)
    extras = groups * group_extras

    def swap(x, axis):
        return lax.all_to_all(x, axis, split_axis=0, concat_axis=0, tiled=True)

    column = lax.axis_index("frame")
    sources = -(-(EXTRAS - clips + 2) // frame_dev)
    main_rows = frame_dev * patch_dev

    def cross(blocks, axis, size):
        got = [blocks[0]]
        for m in range(1, size):
            got.append(lax.ppermute(blocks[m], axis, [(i, i ^ m) for i in range(size)]))
        return jnp.stack(got)

    def extras_out(x, meta):
        found = []
        for source in range(sources):
            mine = jnp.where(column == source, x[source], jnp.zeros((), BF))
            for dest in range(frame_axis):
                if dest != source:
                    mine = mine + lax.ppermute(x[dest], "frame", [(source, dest)])
            found.append(mine)
        out = found[0]
        for source in range(1, sources):
            frame = meta[FRAME : FRAME + EXTRAS][:, None, None]
            out = jnp.where(frame // frame_dev == source, found[source], out)
        out = out.reshape(EXTRAS * patch_t, width)
        return jnp.concatenate([out, jnp.zeros(((extras - EXTRAS) * patch_t, width), BF)])

    def extras_home(x):
        x = x.reshape(extras, patch_t, width)[:EXTRAS]
        found = []
        for source in range(frame_axis):
            mine = jnp.where(column == source, x, jnp.zeros((), BF))
            for dest in range(sources):
                if dest != source:
                    mine = mine + lax.ppermute(x, "frame", [(source, dest)])
            found.append(mine)
        return jnp.transpose(jnp.stack(found), (1, 0, 2, 3)).reshape(EXTRAS, patch_dev, width)

    meta, main_home, extra_home, cot_main, cot_extra = gather(
        lengths, frame_mask, jnp.stack([column, lax.axis_index("patch")]).astype(jnp.int32), latents, cotangent, frame_axis, sharers
    )
    main_s = cross(main_home, "patch", patch_axis).reshape(main_rows, width)
    extra_t = extras_out(extra_home, meta)
    extra_t, cot_main, cot_extra = lax.optimization_barrier((extra_t, cot_main, cot_extra))
    cot_m = cross(cot_main.reshape(frame_axis, frame_dev * patch_t, width), "frame", frame_axis)
    cot_e = extras_out(cot_extra, meta)

    def rotate(array, by):
        perm = []
        for p in range(patch_axis):
            base = p // sharers * sharers
            perm.append((p, base + (p - base + by) % sharers))
        return lax.ppermute(array, "patch", perm)

    mod = modulation
    chunk = group_extras * patch_t
    packed = front_extra(meta, mod, extra_t, spatial_weights, heads, patch_t)
    packed, main_s = lax.optimization_barrier((packed, main_s))
    pack_got = swap(packed.reshape(frame_axis * patch_axis, chunk, 256), everyone)
    pack_got = pack_got.reshape(frame_axis * patch_axis, group_extras, patch_t, 256)
    q, kv = front_main(meta, mod, main_s, spatial_weights)
    other = jnp.stack([rotate(kv, by) for by in range(1, sharers)])
    attended = attend(q, kv, other, heads)
    sent = back_main(meta, mod, main_s, attended, spatial_weights, frame_axis, frame_axis * patch_axis)
    sent, pack_got = lax.optimization_barrier((sent, pack_got))
    extra_o = extra_attend(pack_got)

    out_m, sent = temporal_main(
        meta, mod, swap(sent, everyone), cot_m, temporal_weights, heads, patch_t
    )
    extra_o, _ = lax.optimization_barrier((swap(extra_o, everyone), out_m))
    out_e, sent_e, grad_e = temporal_extra(
        meta, mod, extra_o, extra_t, cot_e, temporal_weights, spatial_weights[3:], heads, patch_t, groups
    )

    grads, sent_e = lax.optimization_barrier((swap(sent, everyone), sent_e))
    do_main, grad_s = back_grad_main(meta, mod, grads, spatial_weights, main_rows, frame_axis)
    own, sent = attend_back(q, kv, other, do_main, heads)
    got = jnp.stack([rotate(sent[by - 1], -by) for by in range(1, sharers)])
    dpack = extra_attend_back(pack_got, swap(sent_e, everyone))
    dpack = swap(dpack.reshape(frame_axis * patch_axis, chunk, 256), everyone)
    dpack = dpack.reshape(heads, extras * patch_t, 256)
    lat_m = front_grad_main(meta, mod, own, got, main_s, grad_s, spatial_weights)
    dpack, out_m, out_e, _ = lax.optimization_barrier((dpack, out_m, out_e, own))
    lat_e = front_grad_extra(meta, mod, dpack, extra_t, grad_e, spatial_weights, patch_t)
    lat_main = cross(lat_m.reshape(patch_axis, sub, width), "patch", patch_axis)

    out_main = cross(out_m, "frame", frame_axis).reshape(frame_axis, frame_dev, patch_t, width)
    slots = clips * frame_dev
    output = place(meta, out_main, extras_home(out_e), slots, sharers, frame_dev)
    grad = place(meta, lat_main, extras_home(lat_e), slots, 0, frame_dev)
    return output.reshape(latents.shape), grad.reshape(latents.shape)


def solution(mesh):
    tokens = P(None, "frame", "patch", None)
    in_specs = (tokens, tokens, P(), P(), P(), P(), P())
    return jax.shard_map(local, mesh=mesh, in_specs=in_specs, out_specs=(tokens, tokens), check_vma=False)
```

```python
import functools
import math

import jax
import jax.numpy as jnp
from jax import lax
from jax.experimental import pallas as pl
from jax.experimental.pallas import tpu as pltpu
from jax.sharding import PartitionSpec as P

HEAD = 72
EXTRAS = 5
SCALE = HEAD ** -0.5
SCALE2 = SCALE * math.log2(math.e)
BF = jnp.bfloat16
F32 = jnp.float32
VMEM_LIMIT = 56 * 1024 * 1024
LONG, COLUMN, CLIP, FRAME, VALID, LONG_VALID, KIND, EXTRA_AT, TABLE = 0, 1, 8, 16, 24, 32, 48, 64, 80


def nn(a, b):
    return lax.dot_general(a, b, (((1,), (0,)), ((), ())), preferred_element_type=F32)


def nt(a, b):
    return lax.dot_general(a, b, (((1,), (1,)), ((), ())), preferred_element_type=F32)


def tn(a, b):
    return lax.dot_general(a, b, (((0,), (0,)), ((), ())), preferred_element_type=F32)


def window(head):
    start = head * HEAD // 128 * 128
    offset = head * HEAD - start
    return start, offset, 128 if offset + HEAD <= 128 else 256


def lanes_in(width, low, high):
    lane = lax.broadcasted_iota(jnp.int32, (1, width), 1)
    return (lane >= low) & (lane < high)


def masked(x, keep):
    return jnp.where(keep, x, jnp.zeros((), x.dtype))


def take_head(x_ref, rows, head):
    start, offset, width = window(head)
    part = x_ref[rows, start : start + width].astype(F32)
    if offset:
        part = pltpu.roll(part, width - offset, 1)
    return masked(part[:, :128], lanes_in(128, 0, HEAD))


def put_head(value, head):
    start, offset, width = window(head)
    if width == 256:
        value = jnp.concatenate([value, jnp.zeros_like(value)], axis=1)
    if offset:
        value = pltpu.roll(value, offset, 1)
    return start, width, value


def room_for(count):
    return -(-count * HEAD // 128) * 128


def pack(parts):
    width = room_for(len(parts))
    out = None
    for i, part in enumerate(parts):
        if width > 128:
            part = jnp.concatenate([part, jnp.zeros((part.shape[0], width - 128), F32)], axis=1)
        if i:
            part = pltpu.roll(part, i * HEAD, 1)
        out = part if out is None else out + part
    return out


def unpack(packed, member):
    if member:
        packed = pltpu.roll(packed, packed.shape[1] - member * HEAD, 1)
    return masked(packed[:, :128], lanes_in(128, 0, HEAD))


def main_vec(meta_ref, mod_ref, block, member):
    return mod_ref[block, member, pl.ds(meta_ref[LONG], 1), :]


def extra_vec(meta_ref, mod_ref, block, member, extras, patches):
    rows = [mod_ref[block, member, pl.ds(meta_ref[CLIP + e], 1), :] for e in range(extras)]
    return jnp.concatenate([jnp.broadcast_to(r, (patches, r.shape[1])) for r in rows], axis=0)


def normed_of(x):
    average = jnp.mean(x, axis=-1, keepdims=True)
    centred = x - average
    variance = jnp.mean(centred * centred, axis=-1, keepdims=True)
    inverse = lax.rsqrt(variance + 1e-06)
    return centred * inverse, inverse


def over_rows(count, body, most=64):
    size = math.gcd(count, most)
    if count == size:
        body(slice(0, count))
        return

    def step(i, carry):
        body(pl.ds(pl.multiple_of(i * size, size), size))
        return carry

    lax.fori_loop(0, count // size, step, 0)


def modulate(x, shift, scale):
    normed, _ = normed_of(x.astype(F32))
    return (normed * (1.0 + scale) + shift).astype(BF)


def norm_back(x, grad, dmod, scale):
    normed, inverse = normed_of(x.astype(F32))
    dnormed = dmod * (1.0 + scale)
    mean_d = jnp.mean(dnormed, axis=-1, keepdims=True)
    mean_dn = jnp.mean(dnormed * normed, axis=-1, keepdims=True)
    dx = (inverse * (dnormed - mean_d - normed * mean_dn)).astype(BF)
    return (dx.astype(F32) + grad.astype(F32)).astype(BF)


def gated(x, gate, mixed):
    return (x.astype(F32) + gate * mixed).astype(BF)


def col_tiles(width):
    whole, tiles = 512, []
    start = 0
    while start < width:
        tiles.append((start, min(whole, width - start)))
        start += whole
    return tiles


def times(dest_ref, x_ref, w_ref, member, transposed=False, add=False):
    for start, size in col_tiles(w_ref.shape[-1]):
        cols = pl.ds(start, size)
        if transposed:
            product = nt(x_ref[...], w_ref[member, cols, :])
        else:
            product = nn(x_ref[...], w_ref[member, :, cols])
        if add:
            product = dest_ref[:, cols] + product
        dest_ref[:, cols] = product.astype(dest_ref.dtype)


def heads_forward(o_ref, q_ref, k_ref, v_ref, parts, bias, heads):
    for head in range(heads):
        start, offset, width = window(head)
        cols = slice(start, start + width)
        keep = lanes_in(width, offset, offset + HEAD)
        scores = [nt(masked(q_ref[rows, cols], keep), k_ref[rows, cols]) for rows in parts]
        scores = jnp.concatenate(scores, axis=0) if len(parts) > 1 else scores[0]
        if bias is not None:
            scores = scores + bias
        exponent = jnp.exp2((scores - jnp.max(scores, axis=-1, keepdims=True)) * SCALE2)
        inverse = 1.0 / jnp.sum(exponent, axis=-1, keepdims=True)
        exponent = exponent.astype(BF)
        count = exponent.shape[0] // len(parts)
        for i, rows in enumerate(parts):
            mine = slice(i * count, (i + 1) * count)
            result = nn(exponent[mine], masked(v_ref[rows, cols], keep)) * inverse[mine]
            o_ref[rows, cols] = o_ref[rows, cols] + result


def softmax_grads(q, do, k, v, bias):
    def joined(left, right):
        products = [nt(a, b) for a, b in zip(left, right)]
        return jnp.concatenate(products, axis=1) if len(products) > 1 else products[0]

    scores = joined(k, q)
    if bias is not None:
        scores = scores + bias
    exponent = jnp.exp2((scores - jnp.max(scores, axis=0, keepdims=True)) * SCALE2)
    prob = exponent * (1.0 / jnp.sum(exponent, axis=0, keepdims=True))
    dprob = joined(v, do)
    delta = jnp.sum(prob * dprob, axis=0, keepdims=True)
    dscores = prob * (dprob - delta) * SCALE
    count = scores.shape[1] // len(q)

    def split(x):
        return [x[:, i * count : (i + 1) * count] for i in range(len(q))]

    return split(dscores.astype(BF)), split(prob.astype(BF))


def heads_backward(dq_ref, dk_ref, dv_ref, q_ref, k_ref, v_ref, do_ref, parts, bias, heads):
    for head in range(heads):
        start, offset, width = window(head)
        cols = slice(start, start + width)
        keep = lanes_in(width, offset, offset + HEAD)
        q, do, k = [[masked(ref[rows, cols], keep) for rows in parts] for ref in (q_ref, do_ref, k_ref)]
        dscores, prob = softmax_grads(q, do, k, [v_ref[rows, cols] for rows in parts], bias)
        for i, rows in enumerate(parts):
            dv_ref[rows, cols] = dv_ref[rows, cols] + nn(prob[i], do[i])
            dk_ref[rows, cols] = dk_ref[rows, cols] + nn(dscores[i], q[i])
            dq_ref[rows, cols] = dq_ref[rows, cols] + tn(dscores[i], k[i])


def gather_kernel(
    lengths_ref, mask_ref, column_ref, latents_ref, cotangent_ref,
    meta_ref, main_ref, extra_ref, cot_ref,
    main_in, extra_in, sems, *, sharers,
):
    clips, frame_dev, patch_dev, width = latents_ref.shape
    frames = mask_ref.shape[1]
    frame_axis = frames // frame_dev
    patch_t = patch_dev // frame_axis
    small, sub = patch_t // sharers, patch_dev // sharers
    column = column_ref[0]
    long = jnp.int32(0)
    for c in range(clips):
        long = long + jnp.where(lengths_ref[c] == frames, c, 0)
    for i in range(TABLE):
        meta_ref[i] = 0
    meta_ref[LONG] = long
    meta_ref[COLUMN] = column
    count = jnp.int32(0)
    for c in range(clips):
        for f in range(EXTRAS - clips + 2):
            used = (c != long) & (f < lengths_ref[c])
            at = jnp.where(used, count, EXTRAS)
            meta_ref[CLIP + at] = jnp.int32(c)
            meta_ref[FRAME + at] = jnp.int32(f)
            meta_ref[VALID + at] = mask_ref[c, f]
            count = count + used.astype(jnp.int32)
    for e in range(EXTRAS, 8):
        for row in (CLIP, FRAME, VALID):
            meta_ref[row + e] = 0

    copies = []
    pairs = ((latents_ref, main_ref), (cotangent_ref, main_in))
    for i, (source, main) in enumerate(pairs):
        copies.append(pltpu.make_async_copy(source.at[long], main, sems.at[i, EXTRAS]))
        copies[-1].start()
        for e in range(EXTRAS):
            frame = lax.rem(meta_ref[FRAME + e], frame_dev)
            part = source.at[meta_ref[CLIP + e], frame]
            copies.append(pltpu.make_async_copy(part, extra_in.at[i, e], sems.at[i, e]))
            copies[-1].start()

    for f in range(frames):
        meta_ref[LONG_VALID + f] = mask_ref[long, f]
    for c in range(clips):
        for f in range(frame_dev):
            frame = column * frame_dev + f
            valid = (frame < lengths_ref[c]) & (mask_ref[c, frame] == 1)
            meta_ref[KIND + c * frame_dev + f] = jnp.where(valid, jnp.where(c == long, 1, 2), 0)
    for e in range(EXTRAS):
        local_frame = meta_ref[FRAME + e] - column * frame_dev
        here = (local_frame >= 0) & (local_frame < frame_dev)
        slot = meta_ref[CLIP + e] * frame_dev + jnp.where(here, local_frame, 0)

        @pl.when(here)
        def _(e=e, slot=slot):
            meta_ref[EXTRA_AT + slot] = jnp.int32(e)

    for copy in copies:
        copy.wait()
    for f in range(frame_axis):
        own = slice(f * patch_t, (f + 1) * patch_t)
        parts = [[extra_in[i, e].astype(F32)[own] for e in range(EXTRAS)] for i in range(2)]
        main = []
        for j in range(frame_dev):
            rows = main_in[j].astype(F32)
            starts = [s * sub + f * small for s in range(sharers)]
            main += [rows[at : at + small] for at in starts]
        extra_ref[f ^ column] = jnp.concatenate(parts[0], axis=0).astype(BF)
        cot_ref[f ^ column] = jnp.concatenate(main + parts[1], axis=0).astype(BF)


def front_main_kernel(meta_ref, mod_ref, x_ref, w_ref, q_ref, kv_ref, low_ref):
    member = pl.program_id(0)

    @pl.when(member == 0)
    def _():
        shift, scale = [main_vec(meta_ref, mod_ref, 0, i) for i in range(2)]

        def body(rows):
            low_ref[rows, :] = modulate(x_ref[rows, :], shift, scale)

        over_rows(x_ref.shape[0], body)
        times(q_ref, low_ref, w_ref, 0)

    @pl.when(member > 0)
    def _():
        times(kv_ref.at[0], low_ref, w_ref, 0)


def own_extras(meta_ref, got_ref, first, extras, patches, frame_dev):
    rows = []
    for e in range(EXTRAS):
        source = meta_ref[COLUMN] ^ (meta_ref[FRAME + e] // frame_dev)
        at = first + e * patches
        rows.append(got_ref[source, at : at + patches, :].astype(F32))
    return rows + [jnp.zeros_like(rows[0])] * (extras - EXTRAS)


def front_extra_kernel(
    meta_ref, mod_ref, got_ref, w_ref, pack_ref, x_ref, low_ref, out_ref, *, patches, frame_dev
):
    member = pl.program_id(0)
    rows = x_ref.shape[0]

    @pl.when(member == 0)
    def _():
        x = own_extras(meta_ref, got_ref, 0, rows // patches, patches, frame_dev)
        x = jnp.concatenate(x, axis=0)
        x_ref[...] = x.astype(BF)
        shift, scale = [extra_vec(meta_ref, mod_ref, 0, i, rows // patches, patches) for i in range(2)]
        low_ref[...] = modulate(x, shift, scale)

    for start, size in col_tiles(w_ref.shape[-1]):
        cols = pl.ds(start, size)
        out_ref[member, :, cols] = nn(low_ref[...], w_ref[0, :, cols])

    @pl.when(member == 2)
    def _():
        for head in range(pack_ref.shape[0]):
            parts = [take_head(out_ref.at[i], slice(None), head) for i in range(3)]
            pack_ref[head] = pack(parts).astype(BF)


def fill_keys(k_ref, v_ref, kv_ref, other_ref):
    rows = kv_ref.shape[1]
    k_ref[:rows] = kv_ref[0]
    v_ref[:rows] = kv_ref[1]
    for i in range(other_ref.shape[0]):
        k_ref[(i + 1) * rows : (i + 2) * rows] = other_ref[i, 0]
        v_ref[(i + 1) * rows : (i + 2) * rows] = other_ref[i, 1]


def attend_kernel(q_ref, kv_ref, other_ref, o_ref, k_ref, v_ref, acc_ref, *, heads):
    fill_keys(k_ref, v_ref, kv_ref, other_ref)
    acc_ref[...] = jnp.zeros_like(acc_ref)
    heads_forward(acc_ref, q_ref, k_ref, v_ref, [slice(None)], None, heads)
    o_ref[...] = acc_ref[...].astype(BF)


def extra_rows(ref, index):
    part = ref[:, index]
    return part.reshape(part.shape[0] * part.shape[1], part.shape[2])


def extra_attend_kernel(pack_ref, o_ref):
    results = []
    for index in range(pack_ref.shape[1]):
        packed = extra_rows(pack_ref, index).astype(F32)
        q, k, v = [unpack(packed, i).astype(BF) for i in range(3)]
        scores = nt(q, k)
        exponent = jnp.exp2((scores - jnp.max(scores, axis=-1, keepdims=True)) * SCALE2)
        total = jnp.sum(exponent, axis=-1, keepdims=True)
        results.append(nn(exponent.astype(BF), v) * (1.0 / total))
    o_ref[...] = pack(results).reshape(o_ref.shape).astype(BF)


def extra_attend_back_kernel(pack_ref, got_ref, grad_ref):
    devices, _, patches, _ = pack_ref.shape
    got = got_ref[...].astype(F32).reshape(devices * patches, got_ref.shape[2])
    for index in range(pack_ref.shape[1]):
        packed = extra_rows(pack_ref, index).astype(F32)
        q, k, v = [unpack(packed, i).astype(BF) for i in range(3)]
        do = unpack(got, index).astype(BF)
        (dscores,), (prob,) = softmax_grads([q], [do], [k], [v], None)
        out = pack([tn(dscores, k), nn(dscores, q), nn(prob, do)]).astype(BF)
        grad_ref[:, index] = out.reshape(devices, patches, 256)


def write_chunk(sent_ref, dest, value):
    pieces = [value[:, at : at + 128] for at in range(0, value.shape[1], 128)]
    sent_ref[dest] = jnp.concatenate(pieces, axis=0).astype(BF)


def read_chunk(got_ref, source, out_ref, row, small):
    value = got_ref[source].astype(F32)
    for i in range(out_ref.shape[1] // 128):
        out_ref[row : row + small, i * 128 : (i + 1) * 128] = value[i * small : (i + 1) * small]


def back_main_kernel(meta_ref, mod_ref, x_ref, o_ref, w_ref, sent_ref, acc_ref, *, columns):
    times(acc_ref, o_ref, w_ref, 0)
    gate = main_vec(meta_ref, mod_ref, 0, 2)

    def body(rows):
        acc_ref[rows, :] = x_ref[rows, :].astype(F32) + gate * acc_ref[rows, :]

    over_rows(x_ref.shape[0], body)
    devices = sent_ref.shape[0]
    small = x_ref.shape[0] // devices
    patch_axis = devices // columns
    for p in range(patch_axis):
        for f in range(columns):
            row = (p * columns + f) * small
            write_chunk(sent_ref, f * patch_axis + p, acc_ref[row : row + small, :])


def back_grad_main_kernel(meta_ref, mod_ref, got_ref, w_ref, do_ref, g_ref, low_ref, acc_ref, *, columns):
    devices = got_ref.shape[0]
    small = g_ref.shape[0] // devices
    patch_axis = devices // columns
    for p in range(patch_axis):
        for f in range(columns):
            row = (p * columns + f) * small
            read_chunk(got_ref, f * patch_axis + p, acc_ref, row, small)
    gate = main_vec(meta_ref, mod_ref, 0, 2)

    def body(rows):
        g_ref[rows, :] = acc_ref[rows, :].astype(BF)
        low_ref[rows, :] = (gate * acc_ref[rows, :]).astype(BF)

    over_rows(g_ref.shape[0], body)
    times(do_ref, low_ref, w_ref, 0, transposed=True)


def attend_back_kernel(
    q_ref, kv_ref, other_ref, do_ref, own_ref, sent_ref, k_ref, v_ref, dq_ref, dk_ref, dv_ref, *, heads
):
    rows = kv_ref.shape[1]
    fill_keys(k_ref, v_ref, kv_ref, other_ref)
    for ref in (dq_ref, dk_ref, dv_ref):
        ref[...] = jnp.zeros_like(ref)
    heads_backward(dq_ref, dk_ref, dv_ref, q_ref, k_ref, v_ref, do_ref, [slice(None)], None, heads)
    own_ref[0] = dq_ref[...].astype(BF)
    own_ref[1] = dk_ref[:rows].astype(BF)
    own_ref[2] = dv_ref[:rows].astype(BF)
    for i in range(other_ref.shape[0]):
        sent_ref[i, 0] = dk_ref[(i + 1) * rows : (i + 2) * rows].astype(BF)
        sent_ref[i, 1] = dv_ref[(i + 1) * rows : (i + 2) * rows].astype(BF)


def add_product(acc_ref, d_ref, member, w_ref):
    for start, size in col_tiles(w_ref.shape[-1]):
        cols = pl.ds(start, size)
        product = nt(d_ref[member], w_ref[0, cols, :])

        @pl.when(member == 0)
        def _(cols=cols, product=product):
            acc_ref[:, cols] = product

        @pl.when(member > 0)
        def _(cols=cols, product=product):
            acc_ref[:, cols] = acc_ref[:, cols] + product


def front_grad_main_kernel(meta_ref, mod_ref, own_ref, got_ref, x_ref, g_ref, w_ref, out_ref, d_ref, acc_ref):
    member = pl.program_id(0)

    @pl.when(member == 0)
    def _():
        d_ref[0] = own_ref[0]
        for i in range(2):
            total = own_ref[1 + i].astype(F32)
            for j in range(got_ref.shape[0]):
                total = total + got_ref[j, i].astype(F32)
            d_ref[1 + i] = total.astype(BF)

    add_product(acc_ref, d_ref, member, w_ref)

    @pl.when(member == 2)
    def _():
        scale = main_vec(meta_ref, mod_ref, 0, 1)

        def body(rows):
            out_ref[rows, :] = norm_back(x_ref[rows, :], g_ref[rows, :], acc_ref[rows, :], scale)

        over_rows(x_ref.shape[0], body)


def front_grad_extra_kernel(
    meta_ref, mod_ref, pack_ref, x_ref, g_ref, w_ref, out_ref, d_ref, acc_ref, ext_ref, *, patches
):
    member = pl.program_id(0)
    rows = x_ref.shape[0]

    @pl.when(member == 0)
    def _():
        ext_ref[...] = jnp.zeros_like(ext_ref)
        for head in range(pack_ref.shape[0]):
            packed = pack_ref[head].astype(F32)
            for i in range(3):
                start, width, value = put_head(unpack(packed, i), head)
                cols = slice(start, start + width)
                ext_ref[i, :, cols] = ext_ref[i, :, cols] + value
        d_ref[...] = ext_ref[...].astype(BF)

    add_product(acc_ref, d_ref, member, w_ref)

    @pl.when(member == 2)
    def _():
        scale = extra_vec(meta_ref, mod_ref, 0, 1, rows // patches, patches)
        out = norm_back(x_ref[...], g_ref[...], acc_ref[...], scale)
        out_ref[...] = out.astype(F32)[: out_ref.shape[0]].astype(BF)


def key_bias(meta_ref, valid_at, clip_at, tokens, count, small, keys_axis):
    part = count * small

    def spread(base, axis):
        line = (1, tokens) if axis == 1 else (tokens, 1)
        item = lax.broadcasted_iota(jnp.int32, line, axis) % part // small
        out = jnp.zeros(line, jnp.int32)
        for i in range(count):
            out = jnp.where(item == i, meta_ref[base + i], out)
        return out

    where = lax.broadcasted_iota(jnp.int32, (tokens, tokens), keys_axis)
    other = lax.broadcasted_iota(jnp.int32, (tokens, tokens), 1 - keys_axis)
    admitted = jnp.broadcast_to(spread(valid_at, keys_axis) == 1, (tokens, tokens))
    if clip_at is not None:
        admitted = admitted & (spread(clip_at, 0) == spread(clip_at, 1))
    admitted = admitted & (where % small == other % small) & (where // part == other // part)
    return jnp.where(admitted | (where == other), 0.0, -1e30).astype(F32)


def temporal_core(vecs, w_ref, parts, biases, put, most, refs, heads):
    x_ref, cot_ref, low_ref, q_ref, k_ref, v_ref, acc_ref, dq_ref, dk_ref, dv_ref = refs
    count = x_ref.shape[0]
    shift, scale, gate = vecs

    def body(rows):
        low_ref[rows, :] = modulate(x_ref[rows, :], shift, scale)

    over_rows(count, body, most)
    for i, ref in enumerate((q_ref, k_ref, v_ref)):
        times(ref, low_ref, w_ref, i)
    acc_ref[...] = jnp.zeros_like(acc_ref)
    heads_forward(acc_ref, q_ref, k_ref, v_ref, parts, biases(1), heads)
    low_ref[...] = acc_ref[...].astype(BF)
    times(acc_ref, low_ref, w_ref, 3)

    def body(rows):
        acc_ref[rows, :] = x_ref[rows, :] + gate * acc_ref[rows, :]
        low_ref[rows, :] = (gate * cot_ref[rows, :]).astype(BF)

    over_rows(count, body, most)
    put()
    times(acc_ref, low_ref, w_ref, 3, transposed=True)
    low_ref[...] = acc_ref[...].astype(BF)
    for ref in (dq_ref, dk_ref, dv_ref):
        ref[...] = jnp.zeros_like(ref)
    heads_backward(dq_ref, dk_ref, dv_ref, q_ref, k_ref, v_ref, low_ref, parts, biases(0), heads)
    for i, ref in enumerate((dq_ref, dk_ref, dv_ref)):
        low_ref[...] = ref[...].astype(BF)
        times(acc_ref, low_ref, w_ref, i, transposed=True, add=i > 0)

    def body(rows):
        acc_ref[rows, :] = norm_back(x_ref[rows, :], cot_ref[rows, :], acc_ref[rows, :], scale).astype(F32)

    over_rows(count, body, most)


def temporal_main_kernel(meta_ref, mod_ref, got_ref, c_ref, w_ref, out_ref, sent_ref, *refs, heads, patches):
    x_ref, cot_ref, acc_ref = refs[0], refs[1], refs[6]
    columns = c_ref.shape[0]
    main = x_ref.shape[0]
    block = main // columns
    frames, each = main // patches, block // patches
    column = meta_ref[COLUMN]
    devices = got_ref.shape[0]
    small = main // devices
    sharers = patches // small
    part = frames * small

    def token(source):
        return source % sharers * part + source // sharers * small

    for source in range(devices):
        read_chunk(got_ref, source, x_ref, token(source), small)
    for f in range(columns):
        values = c_ref[column ^ f].astype(F32)
        for j in range(each):
            valid = meta_ref[LONG_VALID + f * each + j] == 1
            for g in range(sharers):
                rows = pl.ds(token((f * each + j) * sharers + g), small)
                at = j * patches + g * small
                cot_ref[rows, :] = jnp.where(valid, values[at : at + small], 0.0)

    parts = [slice(g * part, (g + 1) * part) for g in range(sharers)]
    if part % 128:
        parts = [slice(0, main)]

    def biases(axis):
        bias = key_bias(meta_ref, LONG_VALID, None, main // len(parts), frames, small, axis)
        return jnp.concatenate([bias] * len(parts), axis=1 - axis)

    def put():
        for f in range(columns):
            starts = [token(f * each * sharers + i) for i in range(each * sharers)]
            pieces = [acc_ref[at : at + small, :] for at in starts]
            out_ref[column ^ f] = jnp.concatenate(pieces, axis=0).astype(BF)

    vecs = [main_vec(meta_ref, mod_ref, 1, i) for i in range(3)]
    temporal_core(vecs, w_ref, parts, biases, put, 64, refs, heads)
    for dest in range(devices):
        write_chunk(sent_ref, dest, acc_ref[token(dest) : token(dest) + small, :])


def temporal_extra_kernel(
    meta_ref, mod_ref, got_ref, l_ref, c_ref, w_ref, ws_ref, out_ref, sent_ref, g_ref, *refs,
    heads, patches, groups, frame_dev,
):
    x_ref, cot_ref, acc_ref = refs[0], refs[1], refs[6]
    rows = l_ref.shape[0]
    extras = rows // patches
    each = extras // groups
    devices = got_ref.shape[0]

    def vec(block, member):
        return extra_vec(meta_ref, mod_ref, block, member, extras, patches)

    acc_ref[...] = jnp.zeros_like(acc_ref)
    for source in range(devices):
        head, group = source // groups, source % groups
        packed = got_ref[source].astype(F32)
        for e in range(each):
            at = (group * each + e) * patches
            start, size, value = put_head(unpack(packed, e), head)
            cols = slice(start, start + size)
            acc_ref[at : at + patches, cols] = acc_ref[at : at + patches, cols] + value
    gate_s = vec(0, 2)
    mixed = nn(acc_ref[...].astype(BF), ws_ref[0])
    x_ref[...] = gated(l_ref[...], gate_s, mixed).astype(F32)
    values = own_extras(meta_ref, c_ref, frame_dev * patches, extras, patches, frame_dev)
    for i in range(extras):
        part = slice(i * patches, (i + 1) * patches)
        cot_ref[part, :] = jnp.where(meta_ref[VALID + i] == 1, values[i], 0.0)

    def put():
        out_ref[...] = acc_ref[: out_ref.shape[0]].astype(BF)

    def biases(axis):
        return key_bias(meta_ref, VALID, CLIP, rows, extras, patches, axis)

    vecs = [vec(1, i) for i in range(3)]
    temporal_core(vecs, w_ref, [slice(0, rows)], biases, put, rows, refs, heads)
    grad = acc_ref[...]
    g_ref[...] = grad.astype(BF)
    acc_ref[...] = nt((gate_s * grad).astype(BF), ws_ref[0])
    for dest in range(devices):
        head, group = dest // groups, dest % groups
        starts = [(group * each + e) * patches for e in range(each)]
        parts = [take_head(acc_ref, slice(at, at + patches), head) for at in starts]
        sent_ref[dest] = pack(parts).astype(BF)


def place_kernel(meta_ref, main_ref, extra_ref, out_ref, *, sharers):
    frame_dev, patch_dev, width = main_ref.shape[-3], out_ref.shape[1], out_ref.shape[2]
    for slot in range(out_ref.shape[0]):
        kind = meta_ref[KIND + slot]

        @pl.when(kind == 0)
        def _(slot=slot):
            out_ref[slot] = jnp.zeros_like(out_ref[slot])

        @pl.when(kind == 1)
        def _(slot=slot):
            if not sharers:
                out_ref[slot] = main_ref[slot % frame_dev]
                return
            columns, patch_t = main_ref.shape[0], main_ref.shape[2]
            small = patch_t // sharers
            parts = [main_ref[meta_ref[COLUMN] ^ f, slot % frame_dev].astype(F32) for f in range(columns)]
            pieces = [p[s * small : (s + 1) * small] for s in range(sharers) for p in parts]
            out_ref[slot] = jnp.concatenate(pieces, axis=0).astype(BF)

        @pl.when(kind == 2)
        def _(slot=slot):
            e = meta_ref[EXTRA_AT + slot]
            parts = [extra_ref[meta_ref[COLUMN] ^ f, e].astype(F32) for f in range(extra_ref.shape[0])]
            out_ref[slot] = jnp.concatenate(parts, axis=0).astype(BF)


SCALARS = pl.BlockSpec(memory_space=pltpu.SMEM)
ANYWHERE = pl.BlockSpec(memory_space=pl.ANY)


def params(steps=0):
    semantics = {"dimension_semantics": ("arbitrary",) * steps} if steps else {}
    return pltpu.CompilerParams(vmem_limit_bytes=VMEM_LIMIT, **semantics)


def cost(flops, elements=0):
    return pl.CostEstimate(flops=int(flops) // 1000, bytes_accessed=int(elements) // 1000, transcendentals=0)


def whole(array):
    return pl.BlockSpec(array.shape, lambda *_: (0,) * len(array.shape))


def shape(*dims, dtype=BF):
    return jax.ShapeDtypeStruct(dims, dtype)


def weight_call(kernel, name, operands, weights, members, outs, scratch, weigh):
    width = weights.shape[-1]
    first, count = members
    return pl.pallas_call(
        kernel,
        name=name,
        grid=(count,),
        in_specs=[SCALARS]
        + [whole(a) for a in operands[1:]]
        + [pl.BlockSpec((1, width, width), lambda i: (first + i, 0, 0))],
        out_specs=[spec for spec, _ in outs],
        out_shape=[struct for _, struct in outs],
        scratch_shapes=scratch,
        compiler_params=params(1),
        cost_estimate=cost(weigh * count, 2 * width * width * count),
    )(*operands, weights)


def full(*dims):
    return whole(shape(*dims)), shape(*dims)


def gather(lengths, frame_mask, column, latents, cotangent, columns, sharers):
    _, frame_dev, patch_dev, width = latents.shape
    main = (frame_dev, patch_dev, width)
    patch_t = patch_dev // columns
    return pl.pallas_call(
        functools.partial(gather_kernel, sharers=sharers),
        name="gather",
        in_specs=[SCALARS] * 3 + [ANYWHERE] * 2,
        out_specs=[SCALARS] + [pl.BlockSpec(memory_space=pltpu.VMEM)] * 3,
        out_shape=[
            shape(TABLE, dtype=jnp.int32), shape(*main), shape(columns, EXTRAS * patch_t, width),
            shape(columns, (frame_dev + EXTRAS) * patch_t, width),
        ],
        scratch_shapes=[
            pltpu.VMEM(main, BF),
            pltpu.VMEM((2, EXTRAS, patch_dev, width), BF),
            pltpu.SemaphoreType.DMA((2, EXTRAS + 1)),
        ],
        compiler_params=params(),
    )(lengths, frame_mask, column, latents, cotangent)


def front_main(meta, mod, x, weights):
    rows, width = x.shape
    kv = pl.BlockSpec((1, rows, width), lambda i: (jnp.maximum(i - 1, 0), 0, 0)), shape(2, rows, width)
    return weight_call(
        front_main_kernel, "front_main", (meta, mod, x), weights, (0, 3),
        [full(rows, width), kv], [pltpu.VMEM((rows, width), BF)], 2 * rows * width**2,
    )


def front_extra(meta, mod, got, weights, heads, patches, extras, frame_dev):
    width = got.shape[-1]
    rows = extras * patches
    return weight_call(
        functools.partial(front_extra_kernel, patches=patches, frame_dev=frame_dev), "front_extra",
        (meta, mod, got), weights, (0, 3), [full(heads, rows, 256), full(rows, width)],
        [pltpu.VMEM((rows, width), BF), pltpu.VMEM((3, rows, width), F32)], 4 * rows * width**2,
    )


def back_main(meta, mod, x, o, weights, columns, devices):
    rows, width = x.shape
    return weight_call(
        functools.partial(back_main_kernel, columns=columns), "back_main", (meta, mod, x, o), weights,
        (3, 1), [full(devices, rows * width // (devices * 128), 128)], [pltpu.VMEM((rows, width), F32)],
        3 * rows * width**2,
    )[0]


def back_grad_main(meta, mod, got, weights, rows, columns):
    width = weights.shape[-1]
    return weight_call(
        functools.partial(back_grad_main_kernel, columns=columns), "back_grad_main",
        (meta, mod, got), weights, (3, 1), [full(rows, width)] * 2,
        [pltpu.VMEM((rows, width), BF), pltpu.VMEM((rows, width), F32)], 3 * rows * width**2,
    )


def front_grad_main(meta, mod, own, got, x, g, weights):
    rows, width = x.shape
    return weight_call(
        front_grad_main_kernel, "front_grad_main", (meta, mod, own, got, x, g), weights, (0, 3),
        [full(rows, width)], [pltpu.VMEM((3, rows, width), BF), pltpu.VMEM((rows, width), F32)],
        3 * rows * width**2,
    )[0]


def front_grad_extra(meta, mod, pack, x, g, weights, patches):
    rows, width = x.shape
    return weight_call(
        functools.partial(front_grad_extra_kernel, patches=patches), "front_grad_extra",
        (meta, mod, pack, x, g), weights, (0, 3), [full(EXTRAS * patches, width)],
        [pltpu.VMEM((3, rows, width), BF), pltpu.VMEM((rows, width), F32), pltpu.VMEM((3, rows, width), F32)],
        4 * rows * width**2,
    )[0]


def attend(q, kv, other, heads):
    rows, width = q.shape
    keys = rows * (other.shape[0] + 1)
    return pl.pallas_call(
        functools.partial(attend_kernel, heads=heads),
        name="attend",
        out_shape=shape(rows, width),
        scratch_shapes=[
            pltpu.VMEM((keys, width), BF),
            pltpu.VMEM((keys, width), BF),
            pltpu.VMEM((rows, width), F32),
        ],
        compiler_params=params(),
        cost_estimate=cost(6e9),
    )(q, kv, other)


def extra_attend(packed):
    devices, count, patches, _ = packed.shape
    return pl.pallas_call(
        extra_attend_kernel, name="extra_attend", out_shape=shape(devices, patches, room_for(count)),
        compiler_params=params(), cost_estimate=cost(4e9),
    )(packed)


def extra_attend_back(packed, got):
    return pl.pallas_call(
        extra_attend_back_kernel, name="extra_attend_back", out_shape=shape(*packed.shape),
        compiler_params=params(), cost_estimate=cost(6e9),
    )(packed, got)


def attend_back(q, kv, other, do, heads):
    rows, width = q.shape
    keys = rows * (other.shape[0] + 1)
    return pl.pallas_call(
        functools.partial(attend_back_kernel, heads=heads),
        name="attend_back",
        out_shape=[shape(3, rows, width), shape(*other.shape)],
        scratch_shapes=[
            pltpu.VMEM((keys, width), BF),
            pltpu.VMEM((keys, width), BF),
            pltpu.VMEM((rows, width), F32),
            pltpu.VMEM((keys, width), F32),
            pltpu.VMEM((keys, width), F32),
        ],
        compiler_params=params(),
        cost_estimate=cost(14e9),
    )(q, kv, other, do)


def temporal_scratch(rows, width):
    high, low = pltpu.VMEM((rows, width), F32), pltpu.VMEM((rows, width), BF)
    return [high] * 2 + [low] * 4 + [high] * 4


def temporal_main(meta, mod, got, cot, weights, heads, patches):
    columns, _, width = cot.shape
    block = got.shape[0] * got.shape[1] * got.shape[2] // (columns * width)
    operands = (mod, got, cot, weights)
    return pl.pallas_call(
        functools.partial(temporal_main_kernel, heads=heads, patches=patches),
        name="temporal_main",
        in_specs=[SCALARS] + [whole(a) for a in operands],
        out_shape=[shape(columns, block, width), shape(*got.shape)],
        scratch_shapes=temporal_scratch(columns * block, width),
        compiler_params=params(),
        cost_estimate=cost(25e9),
    )(meta, *operands)


def temporal_extra(meta, mod, got, le, cot, weights, last_weight, heads, patches, groups, frame_dev):
    operands = (mod, got, le, cot, weights, last_weight)
    return pl.pallas_call(
        functools.partial(
            temporal_extra_kernel, heads=heads, patches=patches, groups=groups, frame_dev=frame_dev
        ),
        name="temporal_extra",
        in_specs=[SCALARS] + [whole(a) for a in operands],
        out_shape=[shape(EXTRAS * patches, le.shape[1]), shape(*got.shape), shape(*le.shape)],
        scratch_shapes=temporal_scratch(*le.shape),
        compiler_params=params(),
        cost_estimate=cost(14e9),
    )(meta, *operands)


def place(meta, main, extra, slots, sharers):
    return pl.pallas_call(
        functools.partial(place_kernel, sharers=sharers),
        name="place",
        in_specs=[SCALARS, whole(main), whole(extra)],
        out_shape=shape(slots, extra.shape[0] * extra.shape[2], extra.shape[3]),
        compiler_params=params(),
        cost_estimate=cost(3e9),
    )(meta, main, extra)


def local(latents, cotangent, spatial_weights, temporal_weights, modulation, lengths, frame_mask):
    clips, frame_dev, patch_dev, width = latents.shape
    heads = width // HEAD
    frame_axis, patch_axis = lax.axis_size("frame"), lax.axis_size("patch")
    everyone = ("frame", "patch")
    frames = frame_dev * frame_axis
    sharers = patch_axis // frame_dev
    sub = patch_dev // sharers
    small = sub // frame_axis
    patch_t = patch_dev // frame_axis
    heads_col = heads // frame_axis
    groups = patch_axis // heads_col
    group_extras = -(-EXTRAS // groups)
    extras = groups * group_extras

    def swap(x, axis):
        return lax.all_to_all(x, axis, split_axis=0, concat_axis=0, tiled=True)

    column = lax.axis_index("frame")
    main_rows = frame_dev * patch_dev

    def cross(blocks):
        got = [blocks[0]]
        for m in range(1, frame_axis):
            got.append(lax.ppermute(blocks[m], "frame", [(f, f ^ m) for f in range(frame_axis)]))
        return jnp.stack(got)

    meta, main_home, extra_home, cot_home = gather(
        lengths, frame_mask, column.reshape(1).astype(jnp.int32), latents, cotangent, frame_axis, sharers
    )
    extra_got = cross(extra_home)
    main_s = swap(main_home.reshape(patch_axis, sub, width), "patch").reshape(main_rows, width)
    extra_got, cot_home = lax.optimization_barrier((extra_got, cot_home))
    cot = cross(cot_home)

    def rotate(array, by):
        perm = []
        for p in range(patch_axis):
            base = p // sharers * sharers
            perm.append((p, base + (p - base + by) % sharers))
        return lax.ppermute(array, "patch", perm)

    mod = modulation
    chunk = group_extras * patch_t
    packed, extra_t = front_extra(
        meta, mod, extra_got, spatial_weights, heads, patch_t, extras, frame_dev
    )
    packed, main_s = lax.optimization_barrier((packed, main_s))
    pack_got = swap(packed.reshape(frame_axis * patch_axis, chunk, 256), everyone)
    pack_got = pack_got.reshape(frame_axis * patch_axis, group_extras, patch_t, 256)
    q, kv = front_main(meta, mod, main_s, spatial_weights)
    other = jnp.stack([rotate(kv, by) for by in range(1, sharers)])
    q, cot = lax.optimization_barrier((q, cot))
    attended = attend(q, kv, other, heads)
    sent = back_main(meta, mod, main_s, attended, spatial_weights, frame_axis, frame_axis * patch_axis)
    sent, pack_got = lax.optimization_barrier((sent, pack_got))
    extra_o = extra_attend(pack_got)

    out_m, sent = temporal_main(
        meta, mod, swap(sent, everyone), cot, temporal_weights, heads, patch_t
    )
    extra_o, _ = lax.optimization_barrier((swap(extra_o, everyone), out_m))
    out_e, sent_e, grad_e = temporal_extra(
        meta, mod, extra_o, extra_t, cot, temporal_weights, spatial_weights[3:], heads, patch_t, groups, frame_dev
    )

    grads, sent_e = lax.optimization_barrier((swap(sent, everyone), sent_e))
    do_main, grad_s = back_grad_main(meta, mod, grads, spatial_weights, main_rows, frame_axis)
    dpack = extra_attend_back(pack_got, swap(sent_e, everyone))
    do_main, dpack = lax.optimization_barrier((do_main, dpack))
    own, sent = attend_back(q, kv, other, do_main, heads)
    got = jnp.stack([rotate(sent[by - 1], -by) for by in range(1, sharers)])
    dpack = swap(dpack.reshape(frame_axis * patch_axis, chunk, 256), everyone)
    dpack = dpack.reshape(heads, extras * patch_t, 256)
    lat_m = front_grad_main(meta, mod, own, got, main_s, grad_s, spatial_weights)
    dpack, out_m, out_e, _ = lax.optimization_barrier((dpack, out_m, out_e, own))
    lat_e = front_grad_extra(meta, mod, dpack, extra_t, grad_e, spatial_weights, patch_t)
    lat_main = swap(lat_m.reshape(patch_axis, sub, width), "patch").reshape(frame_dev, patch_dev, width)

    def parts_home(x):
        return cross([x] * frame_axis).reshape(frame_axis, EXTRAS, patch_t, width)

    out_main = cross(out_m).reshape(frame_axis, frame_dev, patch_t, width)
    slots = clips * frame_dev
    output = place(meta, out_main, parts_home(out_e), slots, sharers)
    grad = place(meta, lat_main, parts_home(lat_e), slots, 0)
    return output.reshape(latents.shape), grad.reshape(latents.shape)


def solution(mesh):
    tokens = P(None, "frame", "patch", None)
    in_specs = (tokens, tokens, P(), P(), P(), P(), P())
    return jax.shard_map(local, mesh=mesh, in_specs=in_specs, out_specs=(tokens, tokens), check_vma=False)
```

```python
import functools
import math

import jax
import jax.numpy as jnp
from jax import lax
from jax.experimental import pallas as pl
from jax.experimental.pallas import tpu as pltpu
from jax.sharding import PartitionSpec as P

HEAD = 72
EXTRAS = 5
SCALE = HEAD ** -0.5
SCALE2 = SCALE * math.log2(math.e)
BF = jnp.bfloat16
F32 = jnp.float32
VMEM_LIMIT = 56 * 1024 * 1024
LONG, COLUMN, CLIP, FRAME, VALID, LONG_VALID, KIND, EXTRA_AT, TABLE = 0, 1, 8, 16, 24, 32, 48, 64, 80


def nn(a, b):
    return lax.dot_general(a, b, (((1,), (0,)), ((), ())), preferred_element_type=F32)


def nt(a, b):
    return lax.dot_general(a, b, (((1,), (1,)), ((), ())), preferred_element_type=F32)


def tn(a, b):
    return lax.dot_general(a, b, (((0,), (0,)), ((), ())), preferred_element_type=F32)


def window(head):
    start = head * HEAD // 128 * 128
    offset = head * HEAD - start
    return start, offset, 128 if offset + HEAD <= 128 else 256


def lanes_in(width, low, high):
    lane = lax.broadcasted_iota(jnp.int32, (1, width), 1)
    return (lane >= low) & (lane < high)


def masked(x, keep):
    return jnp.where(keep, x, jnp.zeros((), x.dtype))


def room_for(count):
    return -(-count * HEAD // 128) * 128


def widened(x):
    return x if x.shape[1] == 256 else jnp.concatenate([x, jnp.zeros_like(x)], axis=1)


def moved(x, lanes):
    return pltpu.roll(x, lanes % 256, 1) if lanes % 256 else x


def head_into(x_ref, rows, head, member):
    start, offset, width = window(head)
    part = moved(widened(x_ref[rows, start : start + width].astype(F32)), member * HEAD - offset)
    return masked(part, lanes_in(256, member * HEAD, (member + 1) * HEAD))


def head_from(packed, head, member):
    start, offset, width = window(head)
    part = moved(widened(packed), offset - member * HEAD)[:, :width]
    return slice(start, start + width), masked(part, lanes_in(width, offset, offset + HEAD))


def pack(parts):
    out = sum(moved(widened(part), i * HEAD) for i, part in enumerate(parts))
    return out[:, : room_for(len(parts))]


def unpack(packed, member):
    return masked(moved(widened(packed), -member * HEAD)[:, :128], lanes_in(128, 0, HEAD))


def main_vec(meta_ref, mod_ref, block, member):
    return mod_ref[block, member, pl.ds(meta_ref[LONG], 1), :]


def extra_vec(meta_ref, mod_ref, block, member, extras, patches):
    rows = [mod_ref[block, member, pl.ds(meta_ref[CLIP + e], 1), :] for e in range(extras)]
    return jnp.concatenate([jnp.broadcast_to(r, (patches, r.shape[1])) for r in rows], axis=0)


def normed_of(x):
    average = jnp.mean(x, axis=-1, keepdims=True)
    centred = x - average
    variance = jnp.mean(centred * centred, axis=-1, keepdims=True)
    inverse = lax.rsqrt(variance + 1e-06)
    return centred * inverse, inverse


def over_rows(count, body, most=64):
    size = math.gcd(count, most)
    if count == size:
        body(slice(0, count))
        return

    def step(i, carry):
        body(pl.ds(pl.multiple_of(i * size, size), size))
        return carry

    lax.fori_loop(0, count // size, step, 0)


def modulate(x, shift, scale):
    normed, _ = normed_of(x.astype(F32))
    return (normed * (1.0 + scale) + shift).astype(BF)


def norm_back(x, grad, dmod, scale):
    normed, inverse = normed_of(x.astype(F32))
    dnormed = dmod * (1.0 + scale)
    mean_d = jnp.mean(dnormed, axis=-1, keepdims=True)
    mean_dn = jnp.mean(dnormed * normed, axis=-1, keepdims=True)
    dx = (inverse * (dnormed - mean_d - normed * mean_dn)).astype(BF)
    return (dx.astype(F32) + grad.astype(F32)).astype(BF)


def gated(x, gate, mixed):
    return (x.astype(F32) + gate * mixed).astype(BF)


def col_tiles(width):
    whole, tiles = 512, []
    start = 0
    while start < width:
        tiles.append((start, min(whole, width - start)))
        start += whole
    return tiles


def times(dest_ref, x_ref, w_ref, member, transposed=False, add=False):
    for start, size in col_tiles(w_ref.shape[-1]):
        cols = pl.ds(start, size)
        if transposed:
            product = nt(x_ref[...], w_ref[member, cols, :])
        else:
            product = nn(x_ref[...], w_ref[member, :, cols])
        if add:
            product = dest_ref[:, cols] + product
        dest_ref[:, cols] = product.astype(dest_ref.dtype)


def heads_forward(o_ref, q_ref, k_ref, v_ref, parts, bias, heads):
    for head in range(heads):
        start, offset, width = window(head)
        cols = slice(start, start + width)
        keep = lanes_in(width, offset, offset + HEAD)
        scores = [nt(masked(q_ref[rows, cols], keep), k_ref[rows, cols]) for rows in parts]
        scores = jnp.concatenate(scores, axis=0) if len(parts) > 1 else scores[0]
        if bias is not None:
            scores = scores + bias
        exponent = jnp.exp2((scores - jnp.max(scores, axis=-1, keepdims=True)) * SCALE2)
        inverse = 1.0 / jnp.sum(exponent, axis=-1, keepdims=True)
        exponent = exponent.astype(BF)
        count = exponent.shape[0] // len(parts)
        for i, rows in enumerate(parts):
            mine = slice(i * count, (i + 1) * count)
            result = nn(exponent[mine], masked(v_ref[rows, cols], keep)) * inverse[mine]
            o_ref[rows, cols] = o_ref[rows, cols] + result


def softmax_grads(q, do, k, v, bias):
    def joined(left, right):
        products = [nt(a, b) for a, b in zip(left, right)]
        return jnp.concatenate(products, axis=1) if len(products) > 1 else products[0]

    scores = joined(k, q)
    if bias is not None:
        scores = scores + bias
    exponent = jnp.exp2((scores - jnp.max(scores, axis=0, keepdims=True)) * SCALE2)
    prob = exponent * (1.0 / jnp.sum(exponent, axis=0, keepdims=True))
    dprob = joined(v, do)
    delta = jnp.sum(prob * dprob, axis=0, keepdims=True)
    dscores = prob * (dprob - delta) * SCALE
    count = scores.shape[1] // len(q)

    def split(x):
        return [x[:, i * count : (i + 1) * count] for i in range(len(q))]

    return split(dscores.astype(BF)), split(prob.astype(BF))


def heads_backward(dq_ref, dk_ref, dv_ref, q_ref, k_ref, v_ref, do_ref, parts, bias, heads):
    for head in range(heads):
        start, offset, width = window(head)
        cols = slice(start, start + width)
        keep = lanes_in(width, offset, offset + HEAD)
        q, do, k = [[masked(ref[rows, cols], keep) for rows in parts] for ref in (q_ref, do_ref, k_ref)]
        dscores, prob = softmax_grads(q, do, k, [v_ref[rows, cols] for rows in parts], bias)
        for i, rows in enumerate(parts):
            dv_ref[rows, cols] = dv_ref[rows, cols] + nn(prob[i], do[i])
            dk_ref[rows, cols] = dk_ref[rows, cols] + nn(dscores[i], q[i])
            dq_ref[rows, cols] = dq_ref[rows, cols] + tn(dscores[i], k[i])


def gather_kernel(
    lengths_ref, mask_ref, column_ref, latents_ref, cotangent_ref,
    meta_ref, main_ref, extra_ref, cot_ref,
    main_in, extra_in, sems, *, sharers,
):
    clips, frame_dev, patch_dev, width = latents_ref.shape
    frames = mask_ref.shape[1]
    frame_axis = frames // frame_dev
    patch_t = patch_dev // frame_axis
    small, sub = patch_t // sharers, patch_dev // sharers
    column = column_ref[0]
    long = jnp.int32(0)
    for c in range(clips):
        long = long + jnp.where(lengths_ref[c] == frames, c, 0)
    for i in range(TABLE):
        meta_ref[i] = 0
    meta_ref[LONG] = long
    meta_ref[COLUMN] = column
    count = jnp.int32(0)
    for c in range(clips):
        for f in range(EXTRAS - clips + 2):
            used = (c != long) & (f < lengths_ref[c])
            at = jnp.where(used, count, EXTRAS)
            meta_ref[CLIP + at] = jnp.int32(c)
            meta_ref[FRAME + at] = jnp.int32(f)
            meta_ref[VALID + at] = mask_ref[c, f]
            count = count + used.astype(jnp.int32)
    for e in range(EXTRAS, 8):
        for row in (CLIP, FRAME, VALID):
            meta_ref[row + e] = 0

    copies = []
    pairs = ((latents_ref, main_ref), (cotangent_ref, main_in))
    for i, (source, main) in enumerate(pairs):
        copies.append(pltpu.make_async_copy(source.at[long], main, sems.at[i, EXTRAS]))
        copies[-1].start()
        for e in range(EXTRAS):
            frame = lax.rem(meta_ref[FRAME + e], frame_dev)
            part = source.at[meta_ref[CLIP + e], frame]
            copies.append(pltpu.make_async_copy(part, extra_in.at[i, e], sems.at[i, e]))
            copies[-1].start()

    for f in range(frames):
        meta_ref[LONG_VALID + f] = mask_ref[long, f]
    for c in range(clips):
        for f in range(frame_dev):
            frame = column * frame_dev + f
            valid = (frame < lengths_ref[c]) & (mask_ref[c, frame] == 1)
            meta_ref[KIND + c * frame_dev + f] = jnp.where(valid, jnp.where(c == long, 1, 2), 0)
    for e in range(EXTRAS):
        local_frame = meta_ref[FRAME + e] - column * frame_dev
        here = (local_frame >= 0) & (local_frame < frame_dev)
        slot = meta_ref[CLIP + e] * frame_dev + jnp.where(here, local_frame, 0)

        @pl.when(here)
        def _(e=e, slot=slot):
            meta_ref[EXTRA_AT + slot] = jnp.int32(e)

    for copy in copies:
        copy.wait()
    for f in range(frame_axis):
        own = slice(f * patch_t, (f + 1) * patch_t)
        parts = [[extra_in[i, e].astype(F32)[own] for e in range(EXTRAS)] for i in range(2)]
        main = []
        for j in range(frame_dev):
            rows = main_in[j].astype(F32)
            starts = [s * sub + f * small for s in range(sharers)]
            main += [rows[at : at + small] for at in starts]
        extra_ref[f ^ column] = jnp.concatenate(parts[0], axis=0).astype(BF)
        cot_ref[f ^ column] = jnp.concatenate(main + parts[1], axis=0).astype(BF)


def front_main_kernel(meta_ref, mod_ref, x_ref, w_ref, q_ref, kv_ref, low_ref):
    member = pl.program_id(0)

    @pl.when(member == 0)
    def _():
        shift, scale = [main_vec(meta_ref, mod_ref, 0, i) for i in range(2)]

        def body(rows):
            low_ref[rows, :] = modulate(x_ref[rows, :], shift, scale)

        over_rows(x_ref.shape[0], body)
        times(q_ref, low_ref, w_ref, 0)

    @pl.when(member > 0)
    def _():
        times(kv_ref.at[0], low_ref, w_ref, 0)


def own_extras(meta_ref, got_ref, first, extras, patches, frame_dev):
    rows = []
    for e in range(EXTRAS):
        source = meta_ref[COLUMN] ^ (meta_ref[FRAME + e] // frame_dev)
        at = first + e * patches
        rows.append(got_ref[source, at : at + patches, :].astype(F32))
    return rows + [jnp.zeros_like(rows[0])] * (extras - EXTRAS)


def front_extra_kernel(
    meta_ref, mod_ref, got_ref, w_ref, pack_ref, x_ref, low_ref, out_ref, *, patches, frame_dev
):
    member = pl.program_id(0)
    rows = x_ref.shape[0]

    @pl.when(member == 0)
    def _():
        x = own_extras(meta_ref, got_ref, 0, rows // patches, patches, frame_dev)
        x = jnp.concatenate(x, axis=0)
        x_ref[...] = x.astype(BF)
        shift, scale = [extra_vec(meta_ref, mod_ref, 0, i, rows // patches, patches) for i in range(2)]
        low_ref[...] = modulate(x, shift, scale)

    for start, size in col_tiles(w_ref.shape[-1]):
        cols = pl.ds(start, size)
        out_ref[member, :, cols] = nn(low_ref[...], w_ref[0, :, cols])

    @pl.when(member == 2)
    def _():
        for head in range(pack_ref.shape[0]):
            pack_ref[head] = sum(head_into(out_ref.at[i], slice(None), head, i) for i in range(3)).astype(BF)


def fill_keys(k_ref, v_ref, kv_ref, other_ref):
    rows = kv_ref.shape[1]
    k_ref[:rows] = kv_ref[0]
    v_ref[:rows] = kv_ref[1]
    for i in range(other_ref.shape[0]):
        k_ref[(i + 1) * rows : (i + 2) * rows] = other_ref[i, 0]
        v_ref[(i + 1) * rows : (i + 2) * rows] = other_ref[i, 1]


def attend_kernel(q_ref, kv_ref, other_ref, o_ref, k_ref, v_ref, acc_ref, *, heads):
    fill_keys(k_ref, v_ref, kv_ref, other_ref)
    acc_ref[...] = jnp.zeros_like(acc_ref)
    heads_forward(acc_ref, q_ref, k_ref, v_ref, [slice(None)], None, heads)
    o_ref[...] = acc_ref[...].astype(BF)


def extra_rows(ref, index):
    part = ref[:, index]
    return part.reshape(part.shape[0] * part.shape[1], part.shape[2])


def extra_attend_kernel(pack_ref, o_ref):
    results = []
    for index in range(pack_ref.shape[1]):
        packed = extra_rows(pack_ref, index).astype(F32)
        q, k, v = [unpack(packed, i).astype(BF) for i in range(3)]
        scores = nt(q, k)
        exponent = jnp.exp2((scores - jnp.max(scores, axis=-1, keepdims=True)) * SCALE2)
        total = jnp.sum(exponent, axis=-1, keepdims=True)
        results.append(nn(exponent.astype(BF), v) * (1.0 / total))
    o_ref[...] = pack(results).reshape(o_ref.shape).astype(BF)


def extra_attend_back_kernel(pack_ref, got_ref, grad_ref):
    devices, _, patches, _ = pack_ref.shape
    got = got_ref[...].astype(F32).reshape(devices * patches, got_ref.shape[2])
    for index in range(pack_ref.shape[1]):
        packed = extra_rows(pack_ref, index).astype(F32)
        q, k, v = [unpack(packed, i).astype(BF) for i in range(3)]
        do = unpack(got, index).astype(BF)
        (dscores,), (prob,) = softmax_grads([q], [do], [k], [v], None)
        out = pack([tn(dscores, k), nn(dscores, q), nn(prob, do)]).astype(BF)
        grad_ref[:, index] = out.reshape(devices, patches, 256)


def write_chunk(sent_ref, dest, value):
    pieces = [value[:, at : at + 128] for at in range(0, value.shape[1], 128)]
    sent_ref[dest] = jnp.concatenate(pieces, axis=0).astype(BF)


def read_chunk(got_ref, source, out_ref, row, small):
    value = got_ref[source].astype(F32)
    for i in range(out_ref.shape[1] // 128):
        out_ref[row : row + small, i * 128 : (i + 1) * 128] = value[i * small : (i + 1) * small]


def back_main_kernel(meta_ref, mod_ref, x_ref, o_ref, w_ref, sent_ref, acc_ref, *, columns):
    times(acc_ref, o_ref, w_ref, 0)
    gate = main_vec(meta_ref, mod_ref, 0, 2)

    def body(rows):
        acc_ref[rows, :] = x_ref[rows, :].astype(F32) + gate * acc_ref[rows, :]

    over_rows(x_ref.shape[0], body)
    devices = sent_ref.shape[0]
    small = x_ref.shape[0] // devices
    patch_axis = devices // columns
    for p in range(patch_axis):
        for f in range(columns):
            row = (p * columns + f) * small
            write_chunk(sent_ref, f * patch_axis + p, acc_ref[row : row + small, :])


def back_grad_main_kernel(meta_ref, mod_ref, got_ref, w_ref, do_ref, g_ref, low_ref, acc_ref, *, columns):
    devices = got_ref.shape[0]
    small = g_ref.shape[0] // devices
    patch_axis = devices // columns
    for p in range(patch_axis):
        for f in range(columns):
            row = (p * columns + f) * small
            read_chunk(got_ref, f * patch_axis + p, acc_ref, row, small)
    gate = main_vec(meta_ref, mod_ref, 0, 2)

    def body(rows):
        g_ref[rows, :] = acc_ref[rows, :].astype(BF)
        low_ref[rows, :] = (gate * acc_ref[rows, :]).astype(BF)

    over_rows(g_ref.shape[0], body)
    times(do_ref, low_ref, w_ref, 0, transposed=True)


def attend_back_kernel(
    q_ref, kv_ref, other_ref, do_ref, own_ref, sent_ref, k_ref, v_ref, dq_ref, dk_ref, dv_ref, *, heads
):
    rows = kv_ref.shape[1]
    fill_keys(k_ref, v_ref, kv_ref, other_ref)
    for ref in (dq_ref, dk_ref, dv_ref):
        ref[...] = jnp.zeros_like(ref)
    heads_backward(dq_ref, dk_ref, dv_ref, q_ref, k_ref, v_ref, do_ref, [slice(None)], None, heads)
    own_ref[0] = dq_ref[...].astype(BF)
    own_ref[1] = dk_ref[:rows].astype(BF)
    own_ref[2] = dv_ref[:rows].astype(BF)
    for i in range(other_ref.shape[0]):
        sent_ref[i, 0] = dk_ref[(i + 1) * rows : (i + 2) * rows].astype(BF)
        sent_ref[i, 1] = dv_ref[(i + 1) * rows : (i + 2) * rows].astype(BF)


def add_product(acc_ref, d_ref, member, w_ref):
    for start, size in col_tiles(w_ref.shape[-1]):
        cols = pl.ds(start, size)
        product = nt(d_ref[member], w_ref[0, cols, :])

        @pl.when(member == 0)
        def _(cols=cols, product=product):
            acc_ref[:, cols] = product

        @pl.when(member > 0)
        def _(cols=cols, product=product):
            acc_ref[:, cols] = acc_ref[:, cols] + product


def front_grad_main_kernel(meta_ref, mod_ref, own_ref, got_ref, x_ref, g_ref, w_ref, out_ref, d_ref, acc_ref):
    member = pl.program_id(0)

    @pl.when(member == 0)
    def _():
        d_ref[0] = own_ref[0]
        for i in range(2):
            total = own_ref[1 + i].astype(F32)
            for j in range(got_ref.shape[0]):
                total = total + got_ref[j, i].astype(F32)
            d_ref[1 + i] = total.astype(BF)

    add_product(acc_ref, d_ref, member, w_ref)

    @pl.when(member == 2)
    def _():
        scale = main_vec(meta_ref, mod_ref, 0, 1)

        def body(rows):
            out_ref[rows, :] = norm_back(x_ref[rows, :], g_ref[rows, :], acc_ref[rows, :], scale)

        over_rows(x_ref.shape[0], body)


def front_grad_extra_kernel(
    meta_ref, mod_ref, pack_ref, x_ref, g_ref, w_ref, out_ref, d_ref, acc_ref, ext_ref, *, patches
):
    member = pl.program_id(0)
    rows = x_ref.shape[0]

    @pl.when(member == 0)
    def _():
        ext_ref[...] = jnp.zeros_like(ext_ref)
        for head in range(pack_ref.shape[0]):
            packed = pack_ref[head].astype(F32)
            for i in range(3):
                cols, value = head_from(packed, head, i)
                ext_ref[i, :, cols] = ext_ref[i, :, cols] + value
        d_ref[...] = ext_ref[...].astype(BF)

    add_product(acc_ref, d_ref, member, w_ref)

    @pl.when(member == 2)
    def _():
        scale = extra_vec(meta_ref, mod_ref, 0, 1, rows // patches, patches)
        out = norm_back(x_ref[...], g_ref[...], acc_ref[...], scale)
        out_ref[...] = out.astype(F32)[: out_ref.shape[0]].astype(BF)


def key_bias(meta_ref, valid_at, clip_at, tokens, count, small, keys_axis):
    part = count * small

    def spread(base, axis):
        line = (1, tokens) if axis == 1 else (tokens, 1)
        item = lax.broadcasted_iota(jnp.int32, line, axis) % part // small
        out = jnp.zeros(line, jnp.int32)
        for i in range(count):
            out = jnp.where(item == i, meta_ref[base + i], out)
        return out

    where = lax.broadcasted_iota(jnp.int32, (tokens, tokens), keys_axis)
    other = lax.broadcasted_iota(jnp.int32, (tokens, tokens), 1 - keys_axis)
    admitted = jnp.broadcast_to(spread(valid_at, keys_axis) == 1, (tokens, tokens))
    if clip_at is not None:
        admitted = admitted & (spread(clip_at, 0) == spread(clip_at, 1))
    admitted = admitted & (where % small == other % small) & (where // part == other // part)
    return jnp.where(admitted | (where == other), 0.0, -1e30).astype(F32)


def temporal_core(vecs, w_ref, parts, biases, put, most, refs, heads):
    x_ref, cot_ref, low_ref, q_ref, k_ref, v_ref, acc_ref, dq_ref, dk_ref, dv_ref = refs
    count = x_ref.shape[0]
    shift, scale, gate = vecs

    def body(rows):
        low_ref[rows, :] = modulate(x_ref[rows, :], shift, scale)

    over_rows(count, body, most)
    for i, ref in enumerate((q_ref, k_ref, v_ref)):
        times(ref, low_ref, w_ref, i)
    acc_ref[...] = jnp.zeros_like(acc_ref)
    heads_forward(acc_ref, q_ref, k_ref, v_ref, parts, biases(1), heads)
    low_ref[...] = acc_ref[...].astype(BF)
    times(acc_ref, low_ref, w_ref, 3)

    def body(rows):
        acc_ref[rows, :] = x_ref[rows, :] + gate * acc_ref[rows, :]
        low_ref[rows, :] = (gate * cot_ref[rows, :]).astype(BF)

    over_rows(count, body, most)
    put()
    times(acc_ref, low_ref, w_ref, 3, transposed=True)
    low_ref[...] = acc_ref[...].astype(BF)
    for ref in (dq_ref, dk_ref, dv_ref):
        ref[...] = jnp.zeros_like(ref)
    heads_backward(dq_ref, dk_ref, dv_ref, q_ref, k_ref, v_ref, low_ref, parts, biases(0), heads)
    for i, ref in enumerate((dq_ref, dk_ref, dv_ref)):
        low_ref[...] = ref[...].astype(BF)
        times(acc_ref, low_ref, w_ref, i, transposed=True, add=i > 0)

    def body(rows):
        acc_ref[rows, :] = norm_back(x_ref[rows, :], cot_ref[rows, :], acc_ref[rows, :], scale).astype(F32)

    over_rows(count, body, most)


def temporal_main_kernel(meta_ref, mod_ref, got_ref, c_ref, w_ref, out_ref, sent_ref, *refs, heads, patches):
    x_ref, cot_ref, acc_ref = refs[0], refs[1], refs[6]
    columns = c_ref.shape[0]
    main = x_ref.shape[0]
    block = main // columns
    frames, each = main // patches, block // patches
    column = meta_ref[COLUMN]
    devices = got_ref.shape[0]
    small = main // devices
    sharers = patches // small
    part = frames * small

    def token(source):
        return source % sharers * part + source // sharers * small

    for source in range(devices):
        read_chunk(got_ref, source, x_ref, token(source), small)
    for f in range(columns):
        values = c_ref[column ^ f].astype(F32)
        for j in range(each):
            valid = meta_ref[LONG_VALID + f * each + j] == 1
            for g in range(sharers):
                rows = pl.ds(token((f * each + j) * sharers + g), small)
                at = j * patches + g * small
                cot_ref[rows, :] = jnp.where(valid, values[at : at + small], 0.0)

    parts = [slice(g * part, (g + 1) * part) for g in range(sharers)]
    if part % 128:
        parts = [slice(0, main)]

    def biases(axis):
        bias = key_bias(meta_ref, LONG_VALID, None, main // len(parts), frames, small, axis)
        return jnp.concatenate([bias] * len(parts), axis=1 - axis)

    def put():
        for f in range(columns):
            starts = [token(f * each * sharers + i) for i in range(each * sharers)]
            pieces = [acc_ref[at : at + small, :] for at in starts]
            out_ref[column ^ f] = jnp.concatenate(pieces, axis=0).astype(BF)

    vecs = [main_vec(meta_ref, mod_ref, 1, i) for i in range(3)]
    temporal_core(vecs, w_ref, parts, biases, put, 64, refs, heads)
    for dest in range(devices):
        write_chunk(sent_ref, dest, acc_ref[token(dest) : token(dest) + small, :])


def temporal_extra_kernel(
    meta_ref, mod_ref, got_ref, l_ref, c_ref, w_ref, ws_ref, out_ref, sent_ref, g_ref, *refs,
    heads, patches, groups, frame_dev,
):
    x_ref, cot_ref, acc_ref = refs[0], refs[1], refs[6]
    rows = l_ref.shape[0]
    extras = rows // patches
    each = extras // groups
    devices = got_ref.shape[0]

    def vec(block, member):
        return extra_vec(meta_ref, mod_ref, block, member, extras, patches)

    acc_ref[...] = jnp.zeros_like(acc_ref)
    for source in range(devices):
        head, group = source // groups, source % groups
        packed = got_ref[source].astype(F32)
        for e in range(each):
            at = (group * each + e) * patches
            cols, value = head_from(packed, head, e)
            acc_ref[at : at + patches, cols] = acc_ref[at : at + patches, cols] + value
    gate_s = vec(0, 2)
    mixed = nn(acc_ref[...].astype(BF), ws_ref[0])
    x_ref[...] = gated(l_ref[...], gate_s, mixed).astype(F32)
    values = own_extras(meta_ref, c_ref, frame_dev * patches, extras, patches, frame_dev)
    for i in range(extras):
        part = slice(i * patches, (i + 1) * patches)
        cot_ref[part, :] = jnp.where(meta_ref[VALID + i] == 1, values[i], 0.0)

    def put():
        out_ref[...] = acc_ref[: out_ref.shape[0]].astype(BF)

    def biases(axis):
        return key_bias(meta_ref, VALID, CLIP, rows, extras, patches, axis)

    vecs = [vec(1, i) for i in range(3)]
    temporal_core(vecs, w_ref, [slice(0, rows)], biases, put, rows, refs, heads)
    grad = acc_ref[...]
    g_ref[...] = grad.astype(BF)
    acc_ref[...] = nt((gate_s * grad).astype(BF), ws_ref[0])
    for dest in range(devices):
        head, group = dest // groups, dest % groups
        starts = [(group * each + e) * patches for e in range(each)]
        packed = sum(head_into(acc_ref, slice(at, at + patches), head, e) for e, at in enumerate(starts))
        sent_ref[dest] = packed[:, : sent_ref.shape[2]].astype(BF)


def place_kernel(meta_ref, main_ref, extra_ref, out_ref, *, sharers):
    frame_dev, patch_dev, width = main_ref.shape[-3], out_ref.shape[1], out_ref.shape[2]
    for slot in range(out_ref.shape[0]):
        kind = meta_ref[KIND + slot]

        @pl.when(kind == 0)
        def _(slot=slot):
            out_ref[slot] = jnp.zeros_like(out_ref[slot])

        @pl.when(kind == 1)
        def _(slot=slot):
            if not sharers:
                out_ref[slot] = main_ref[slot % frame_dev]
                return
            columns, patch_t = main_ref.shape[0], main_ref.shape[2]
            small = patch_t // sharers
            parts = [main_ref[meta_ref[COLUMN] ^ f, slot % frame_dev].astype(F32) for f in range(columns)]
            pieces = [p[s * small : (s + 1) * small] for s in range(sharers) for p in parts]
            out_ref[slot] = jnp.concatenate(pieces, axis=0).astype(BF)

        @pl.when(kind == 2)
        def _(slot=slot):
            e = meta_ref[EXTRA_AT + slot]
            parts = [extra_ref[meta_ref[COLUMN] ^ f, e].astype(F32) for f in range(extra_ref.shape[0])]
            out_ref[slot] = jnp.concatenate(parts, axis=0).astype(BF)


SCALARS = pl.BlockSpec(memory_space=pltpu.SMEM)
ANYWHERE = pl.BlockSpec(memory_space=pl.ANY)


def params(steps=0):
    semantics = {"dimension_semantics": ("arbitrary",) * steps} if steps else {}
    return pltpu.CompilerParams(vmem_limit_bytes=VMEM_LIMIT, **semantics)


def cost(flops, elements=0):
    return pl.CostEstimate(flops=int(flops) // 1000, bytes_accessed=int(elements) // 1000, transcendentals=0)


def whole(array):
    return pl.BlockSpec(array.shape, lambda *_: (0,) * len(array.shape))


def shape(*dims, dtype=BF):
    return jax.ShapeDtypeStruct(dims, dtype)


def weight_call(kernel, name, operands, weights, members, outs, scratch, weigh):
    width = weights.shape[-1]
    first, count = members
    return pl.pallas_call(
        kernel,
        name=name,
        grid=(count,),
        in_specs=[SCALARS]
        + [whole(a) for a in operands[1:]]
        + [pl.BlockSpec((1, width, width), lambda i: (first + i, 0, 0))],
        out_specs=[spec for spec, _ in outs],
        out_shape=[struct for _, struct in outs],
        scratch_shapes=scratch,
        compiler_params=params(1),
        cost_estimate=cost(weigh * count, 2 * width * width * count),
    )(*operands, weights)


def full(*dims):
    return whole(shape(*dims)), shape(*dims)


def gather(lengths, frame_mask, column, latents, cotangent, columns, sharers):
    _, frame_dev, patch_dev, width = latents.shape
    main = (frame_dev, patch_dev, width)
    patch_t = patch_dev // columns
    return pl.pallas_call(
        functools.partial(gather_kernel, sharers=sharers),
        name="gather",
        in_specs=[SCALARS] * 3 + [ANYWHERE] * 2,
        out_specs=[SCALARS] + [pl.BlockSpec(memory_space=pltpu.VMEM)] * 3,
        out_shape=[
            shape(TABLE, dtype=jnp.int32), shape(*main), shape(columns, EXTRAS * patch_t, width),
            shape(columns, (frame_dev + EXTRAS) * patch_t, width),
        ],
        scratch_shapes=[
            pltpu.VMEM(main, BF),
            pltpu.VMEM((2, EXTRAS, patch_dev, width), BF),
            pltpu.SemaphoreType.DMA((2, EXTRAS + 1)),
        ],
        compiler_params=params(),
    )(lengths, frame_mask, column, latents, cotangent)


def front_main(meta, mod, x, weights):
    rows, width = x.shape
    kv = pl.BlockSpec((1, rows, width), lambda i: (jnp.maximum(i - 1, 0), 0, 0)), shape(2, rows, width)
    return weight_call(
        front_main_kernel, "front_main", (meta, mod, x), weights, (0, 3),
        [full(rows, width), kv], [pltpu.VMEM((rows, width), BF)], 2 * rows * width**2,
    )


def front_extra(meta, mod, got, weights, heads, patches, extras, frame_dev):
    width = got.shape[-1]
    rows = extras * patches
    return weight_call(
        functools.partial(front_extra_kernel, patches=patches, frame_dev=frame_dev), "front_extra",
        (meta, mod, got), weights, (0, 3), [full(heads, rows, 256), full(rows, width)],
        [pltpu.VMEM((rows, width), BF), pltpu.VMEM((3, rows, width), F32)], 4 * rows * width**2,
    )


def back_main(meta, mod, x, o, weights, columns, devices):
    rows, width = x.shape
    return weight_call(
        functools.partial(back_main_kernel, columns=columns), "back_main", (meta, mod, x, o), weights,
        (3, 1), [full(devices, rows * width // (devices * 128), 128)], [pltpu.VMEM((rows, width), F32)],
        3 * rows * width**2,
    )[0]


def back_grad_main(meta, mod, got, weights, rows, columns):
    width = weights.shape[-1]
    return weight_call(
        functools.partial(back_grad_main_kernel, columns=columns), "back_grad_main",
        (meta, mod, got), weights, (3, 1), [full(rows, width)] * 2,
        [pltpu.VMEM((rows, width), BF), pltpu.VMEM((rows, width), F32)], 3 * rows * width**2,
    )


def front_grad_main(meta, mod, own, got, x, g, weights):
    rows, width = x.shape
    return weight_call(
        front_grad_main_kernel, "front_grad_main", (meta, mod, own, got, x, g), weights, (0, 3),
        [full(rows, width)], [pltpu.VMEM((3, rows, width), BF), pltpu.VMEM((rows, width), F32)],
        3 * rows * width**2,
    )[0]


def front_grad_extra(meta, mod, pack, x, g, weights, patches):
    rows, width = x.shape
    return weight_call(
        functools.partial(front_grad_extra_kernel, patches=patches), "front_grad_extra",
        (meta, mod, pack, x, g), weights, (0, 3), [full(EXTRAS * patches, width)],
        [pltpu.VMEM((3, rows, width), BF), pltpu.VMEM((rows, width), F32), pltpu.VMEM((3, rows, width), F32)],
        4 * rows * width**2,
    )[0]


def attend(q, kv, other, heads):
    rows, width = q.shape
    keys = rows * (other.shape[0] + 1)
    return pl.pallas_call(
        functools.partial(attend_kernel, heads=heads),
        name="attend",
        out_shape=shape(rows, width),
        scratch_shapes=[
            pltpu.VMEM((keys, width), BF),
            pltpu.VMEM((keys, width), BF),
            pltpu.VMEM((rows, width), F32),
        ],
        compiler_params=params(),
        cost_estimate=cost(6e9),
    )(q, kv, other)


def extra_attend(packed):
    devices, count, patches, _ = packed.shape
    return pl.pallas_call(
        extra_attend_kernel, name="extra_attend", out_shape=shape(devices, patches, room_for(count)),
        compiler_params=params(), cost_estimate=cost(4e9),
    )(packed)


def extra_attend_back(packed, got):
    return pl.pallas_call(
        extra_attend_back_kernel, name="extra_attend_back", out_shape=shape(*packed.shape),
        compiler_params=params(), cost_estimate=cost(6e9),
    )(packed, got)


def attend_back(q, kv, other, do, heads):
    rows, width = q.shape
    keys = rows * (other.shape[0] + 1)
    return pl.pallas_call(
        functools.partial(attend_back_kernel, heads=heads),
        name="attend_back",
        out_shape=[shape(3, rows, width), shape(*other.shape)],
        scratch_shapes=[
            pltpu.VMEM((keys, width), BF),
            pltpu.VMEM((keys, width), BF),
            pltpu.VMEM((rows, width), F32),
            pltpu.VMEM((keys, width), F32),
            pltpu.VMEM((keys, width), F32),
        ],
        compiler_params=params(),
        cost_estimate=cost(14e9),
    )(q, kv, other, do)


def temporal_scratch(rows, width):
    high, low = pltpu.VMEM((rows, width), F32), pltpu.VMEM((rows, width), BF)
    return [high] * 2 + [low] * 4 + [high] * 4


def temporal_main(meta, mod, got, cot, weights, heads, patches):
    columns, _, width = cot.shape
    block = got.shape[0] * got.shape[1] * got.shape[2] // (columns * width)
    operands = (mod, got, cot, weights)
    return pl.pallas_call(
        functools.partial(temporal_main_kernel, heads=heads, patches=patches),
        name="temporal_main",
        in_specs=[SCALARS] + [whole(a) for a in operands],
        out_shape=[shape(columns, block, width), shape(*got.shape)],
        scratch_shapes=temporal_scratch(columns * block, width),
        compiler_params=params(),
        cost_estimate=cost(25e9),
    )(meta, *operands)


def temporal_extra(meta, mod, got, le, cot, weights, last_weight, heads, patches, groups, frame_dev):
    operands = (mod, got, le, cot, weights, last_weight)
    return pl.pallas_call(
        functools.partial(
            temporal_extra_kernel, heads=heads, patches=patches, groups=groups, frame_dev=frame_dev
        ),
        name="temporal_extra",
        in_specs=[SCALARS] + [whole(a) for a in operands],
        out_shape=[shape(EXTRAS * patches, le.shape[1]), shape(*got.shape), shape(*le.shape)],
        scratch_shapes=temporal_scratch(*le.shape),
        compiler_params=params(),
        cost_estimate=cost(14e9),
    )(meta, *operands)


def place(meta, main, extra, slots, sharers):
    return pl.pallas_call(
        functools.partial(place_kernel, sharers=sharers),
        name="place",
        in_specs=[SCALARS, whole(main), whole(extra)],
        out_shape=shape(slots, extra.shape[0] * extra.shape[2], extra.shape[3]),
        compiler_params=params(),
        cost_estimate=cost(3e9),
    )(meta, main, extra)


def local(latents, cotangent, spatial_weights, temporal_weights, modulation, lengths, frame_mask):
    clips, frame_dev, patch_dev, width = latents.shape
    heads = width // HEAD
    frame_axis, patch_axis = lax.axis_size("frame"), lax.axis_size("patch")
    everyone = ("frame", "patch")
    frames = frame_dev * frame_axis
    sharers = patch_axis // frame_dev
    sub = patch_dev // sharers
    small = sub // frame_axis
    patch_t = patch_dev // frame_axis
    heads_col = heads // frame_axis
    groups = patch_axis // heads_col
    group_extras = -(-EXTRAS // groups)
    extras = groups * group_extras

    def swap(x, axis):
        return lax.all_to_all(x, axis, split_axis=0, concat_axis=0, tiled=True)

    column = lax.axis_index("frame")
    main_rows = frame_dev * patch_dev

    def cross(blocks):
        got = [blocks[0]]
        for m in range(1, frame_axis):
            got.append(lax.ppermute(blocks[m], "frame", [(f, f ^ m) for f in range(frame_axis)]))
        return jnp.stack(got)

    def parts_home(x):
        return cross([x] * frame_axis).reshape(frame_axis, EXTRAS, patch_t, width)

    meta, main_home, extra_home, cot_home = gather(
        lengths, frame_mask, column.reshape(1).astype(jnp.int32), latents, cotangent, frame_axis, sharers
    )
    extra_got = cross(extra_home)
    main_s = swap(main_home.reshape(patch_axis, sub, width), "patch").reshape(main_rows, width)
    extra_got, cot_home = lax.optimization_barrier((extra_got, cot_home))
    cot = cross(cot_home)

    def rotate(array, by):
        perm = []
        for p in range(patch_axis):
            base = p // sharers * sharers
            perm.append((p, base + (p - base + by) % sharers))
        return lax.ppermute(array, "patch", perm)

    mod = modulation
    chunk = group_extras * patch_t
    packed, extra_t = front_extra(
        meta, mod, extra_got, spatial_weights, heads, patch_t, extras, frame_dev
    )
    packed, main_s = lax.optimization_barrier((packed, main_s))
    pack_got = swap(packed.reshape(frame_axis * patch_axis, chunk, 256), everyone)
    pack_got = pack_got.reshape(frame_axis * patch_axis, group_extras, patch_t, 256)
    q, kv = front_main(meta, mod, main_s, spatial_weights)
    other = jnp.stack([rotate(kv, by) for by in range(1, sharers)])
    attended = attend(q, kv, other, heads)
    sent = back_main(meta, mod, main_s, attended, spatial_weights, frame_axis, frame_axis * patch_axis)
    sent, pack_got = lax.optimization_barrier((sent, pack_got))
    extra_o = extra_attend(pack_got)

    got, cot, extra_o = lax.optimization_barrier((swap(sent, everyone), cot, extra_o))
    out_m, sent = temporal_main(meta, mod, got, cot, temporal_weights, heads, patch_t)
    extra_o, _ = lax.optimization_barrier((swap(extra_o, everyone), out_m))
    out_e, sent_e, grad_e = temporal_extra(
        meta, mod, extra_o, extra_t, cot, temporal_weights, spatial_weights[3:], heads, patch_t, groups, frame_dev
    )

    grads, sent_e = lax.optimization_barrier((swap(sent, everyone), sent_e))
    do_main, grad_s = back_grad_main(meta, mod, grads, spatial_weights, main_rows, frame_axis)
    dpack = extra_attend_back(pack_got, swap(sent_e, everyone))
    out_main, out_extra = cross(out_m), parts_home(out_e)
    do_main, dpack, out_main, out_extra = lax.optimization_barrier((do_main, dpack, out_main, out_extra))
    own, sent = attend_back(q, kv, other, do_main, heads)
    got = jnp.stack([rotate(sent[by - 1], -by) for by in range(1, sharers)])
    dpack = swap(dpack.reshape(frame_axis * patch_axis, chunk, 256), everyone)
    dpack = dpack.reshape(heads, extras * patch_t, 256)
    lat_m = front_grad_main(meta, mod, own, got, main_s, grad_s, spatial_weights)
    dpack, _ = lax.optimization_barrier((dpack, own))
    lat_e = front_grad_extra(meta, mod, dpack, extra_t, grad_e, spatial_weights, patch_t)
    lat_main = swap(lat_m.reshape(patch_axis, sub, width), "patch").reshape(frame_dev, patch_dev, width)

    out_main = out_main.reshape(frame_axis, frame_dev, patch_t, width)
    slots = clips * frame_dev
    output = place(meta, out_main, out_extra, slots, sharers)
    grad = place(meta, lat_main, parts_home(lat_e), slots, 0)
    return output.reshape(latents.shape), grad.reshape(latents.shape)


def solution(mesh):
    tokens = P(None, "frame", "patch", None)
    in_specs = (tokens, tokens, P(), P(), P(), P(), P())
    return jax.shard_map(local, mesh=mesh, in_specs=in_specs, out_specs=(tokens, tokens), check_vma=False)
```

```python
import functools
import math

import jax
import jax.numpy as jnp
from jax import lax
from jax.experimental import pallas as pl
from jax.experimental.pallas import tpu as pltpu
from jax.sharding import PartitionSpec as P

HEAD = 72
EXTRAS = 5
SCALE = HEAD ** -0.5
SCALE2 = SCALE * math.log2(math.e)
BF = jnp.bfloat16
F32 = jnp.float32
VMEM_LIMIT = 56 * 1024 * 1024
LONG, COLUMN, CLIP, FRAME, VALID, LONG_VALID, KIND, EXTRA_AT, TABLE = 0, 1, 8, 16, 24, 32, 48, 64, 80


def nn(a, b):
    return lax.dot_general(a, b, (((1,), (0,)), ((), ())), preferred_element_type=F32)


def nt(a, b):
    return lax.dot_general(a, b, (((1,), (1,)), ((), ())), preferred_element_type=F32)


def tn(a, b):
    return lax.dot_general(a, b, (((0,), (0,)), ((), ())), preferred_element_type=F32)


def window(head):
    start = head * HEAD // 128 * 128
    offset = head * HEAD - start
    return start, offset, 128 if offset + HEAD <= 128 else 256


def lanes_in(width, low, high):
    lane = lax.broadcasted_iota(jnp.int32, (1, width), 1)
    return (lane >= low) & (lane < high)


def masked(x, keep):
    return jnp.where(keep, x, jnp.zeros((), x.dtype))


def room_for(count):
    return -(-count * HEAD // 128) * 128


def widened(x):
    return x if x.shape[1] == 256 else jnp.concatenate([x, jnp.zeros_like(x)], axis=1)


def moved(x, lanes):
    return pltpu.roll(x, lanes % 256, 1) if lanes % 256 else x


def head_into(x_ref, rows, head, member):
    start, offset, width = window(head)
    part = moved(widened(x_ref[rows, start : start + width].astype(F32)), member * HEAD - offset)
    return masked(part, lanes_in(256, member * HEAD, (member + 1) * HEAD))


def head_from(packed, head, member):
    start, offset, width = window(head)
    part = moved(widened(packed), offset - member * HEAD)[:, :width]
    return slice(start, start + width), masked(part, lanes_in(width, offset, offset + HEAD))


def pack(parts):
    out = sum(moved(widened(part), i * HEAD) for i, part in enumerate(parts))
    return out[:, : room_for(len(parts))]


def unpack(packed, member):
    return masked(moved(widened(packed), -member * HEAD)[:, :128], lanes_in(128, 0, HEAD))


def main_vec(meta_ref, mod_ref, block, member):
    return mod_ref[block, member, pl.ds(meta_ref[LONG], 1), :]


def extra_vec(meta_ref, mod_ref, block, member, extras, patches):
    rows = [mod_ref[block, member, pl.ds(meta_ref[CLIP + e], 1), :] for e in range(extras)]
    return jnp.concatenate([jnp.broadcast_to(r, (patches, r.shape[1])) for r in rows], axis=0)


def normed_of(x):
    average = jnp.mean(x, axis=-1, keepdims=True)
    centred = x - average
    variance = jnp.mean(centred * centred, axis=-1, keepdims=True)
    inverse = lax.rsqrt(variance + 1e-06)
    return centred * inverse, inverse


def over_rows(count, body, most=64):
    size = math.gcd(count, most)
    if count == size:
        body(slice(0, count))
        return

    def step(i, carry):
        body(pl.ds(pl.multiple_of(i * size, size), size))
        return carry

    lax.fori_loop(0, count // size, step, 0)


def modulate(x, shift, scale):
    normed, _ = normed_of(x.astype(F32))
    return (normed * (1.0 + scale) + shift).astype(BF)


def norm_back(x, grad, dmod, scale):
    normed, inverse = normed_of(x.astype(F32))
    dnormed = dmod * (1.0 + scale)
    mean_d = jnp.mean(dnormed, axis=-1, keepdims=True)
    mean_dn = jnp.mean(dnormed * normed, axis=-1, keepdims=True)
    dx = (inverse * (dnormed - mean_d - normed * mean_dn)).astype(BF)
    return (dx.astype(F32) + grad.astype(F32)).astype(BF)


def gated(x, gate, mixed):
    return (x.astype(F32) + gate * mixed).astype(BF)


def col_tiles(width):
    whole, tiles = 512, []
    start = 0
    while start < width:
        tiles.append((start, min(whole, width - start)))
        start += whole
    return tiles


def times(dest_ref, x_ref, w_ref, member, transposed=False, add=False):
    for start, size in col_tiles(w_ref.shape[-1]):
        cols = pl.ds(start, size)
        if transposed:
            product = nt(x_ref[...], w_ref[member, cols, :])
        else:
            product = nn(x_ref[...], w_ref[member, :, cols])
        if add:
            product = dest_ref[:, cols] + product
        dest_ref[:, cols] = product.astype(dest_ref.dtype)


def heads_forward(o_ref, q_ref, k_ref, v_ref, parts, bias, heads):
    for head in range(heads):
        start, offset, width = window(head)
        cols = slice(start, start + width)
        keep = lanes_in(width, offset, offset + HEAD)
        scores = [nt(masked(q_ref[rows, cols], keep), k_ref[rows, cols]) for rows in parts]
        scores = jnp.concatenate(scores, axis=0) if len(parts) > 1 else scores[0]
        if bias is not None:
            scores = scores + bias
        exponent = jnp.exp2((scores - jnp.max(scores, axis=-1, keepdims=True)) * SCALE2)
        inverse = 1.0 / jnp.sum(exponent, axis=-1, keepdims=True)
        exponent = exponent.astype(BF)
        count = exponent.shape[0] // len(parts)
        for i, rows in enumerate(parts):
            mine = slice(i * count, (i + 1) * count)
            result = nn(exponent[mine], masked(v_ref[rows, cols], keep)) * inverse[mine]
            o_ref[rows, cols] = o_ref[rows, cols] + result


def softmax_grads(q, do, k, v, bias):
    def joined(left, right):
        products = [nt(a, b) for a, b in zip(left, right)]
        return jnp.concatenate(products, axis=1) if len(products) > 1 else products[0]

    scores = joined(k, q)
    if bias is not None:
        scores = scores + bias
    exponent = jnp.exp2((scores - jnp.max(scores, axis=0, keepdims=True)) * SCALE2)
    prob = exponent * (1.0 / jnp.sum(exponent, axis=0, keepdims=True))
    dprob = joined(v, do)
    delta = jnp.sum(prob * dprob, axis=0, keepdims=True)
    dscores = prob * (dprob - delta) * SCALE
    count = scores.shape[1] // len(q)

    def split(x):
        return [x[:, i * count : (i + 1) * count] for i in range(len(q))]

    return split(dscores.astype(BF)), split(prob.astype(BF))


def heads_backward(dq_ref, dk_ref, dv_ref, q_ref, k_ref, v_ref, do_ref, parts, bias, heads):
    for head in range(heads):
        start, offset, width = window(head)
        cols = slice(start, start + width)
        keep = lanes_in(width, offset, offset + HEAD)
        q, do, k = [[masked(ref[rows, cols], keep) for rows in parts] for ref in (q_ref, do_ref, k_ref)]
        dscores, prob = softmax_grads(q, do, k, [v_ref[rows, cols] for rows in parts], bias)
        for i, rows in enumerate(parts):
            dv_ref[rows, cols] = dv_ref[rows, cols] + nn(prob[i], do[i])
            dk_ref[rows, cols] = dk_ref[rows, cols] + nn(dscores[i], q[i])
            dq_ref[rows, cols] = dq_ref[rows, cols] + tn(dscores[i], k[i])


def gather_kernel(
    lengths_ref, mask_ref, column_ref, latents_ref, cotangent_ref,
    meta_ref, main_ref, extra_ref, cot_main_ref, cot_extra_ref,
    main_in, extra_in, sems, *, sharers,
):
    clips, frame_dev, patch_dev, width = latents_ref.shape
    frames = mask_ref.shape[1]
    frame_axis = frames // frame_dev
    patch_t = patch_dev // frame_axis
    small, sub = patch_t // sharers, patch_dev // sharers
    column = column_ref[0]
    long = jnp.int32(0)
    for c in range(clips):
        long = long + jnp.where(lengths_ref[c] == frames, c, 0)
    for i in range(TABLE):
        meta_ref[i] = 0
    meta_ref[LONG] = long
    meta_ref[COLUMN] = column
    count = jnp.int32(0)
    for c in range(clips):
        for f in range(EXTRAS - clips + 2):
            used = (c != long) & (f < lengths_ref[c])
            at = jnp.where(used, count, EXTRAS)
            meta_ref[CLIP + at] = jnp.int32(c)
            meta_ref[FRAME + at] = jnp.int32(f)
            meta_ref[VALID + at] = mask_ref[c, f]
            count = count + used.astype(jnp.int32)
    for e in range(EXTRAS, 8):
        for row in (CLIP, FRAME, VALID):
            meta_ref[row + e] = 0

    copies = []
    pairs = ((latents_ref, main_ref), (cotangent_ref, main_in))
    for i, (source, main) in enumerate(pairs):
        copies.append(pltpu.make_async_copy(source.at[long], main, sems.at[i, EXTRAS]))
        copies[-1].start()
        for e in range(EXTRAS):
            frame = lax.rem(meta_ref[FRAME + e], frame_dev)
            part = source.at[meta_ref[CLIP + e], frame]
            copies.append(pltpu.make_async_copy(part, extra_in.at[i, e], sems.at[i, e]))
            copies[-1].start()

    for f in range(frames):
        meta_ref[LONG_VALID + f] = mask_ref[long, f]
    for c in range(clips):
        for f in range(frame_dev):
            frame = column * frame_dev + f
            valid = (frame < lengths_ref[c]) & (mask_ref[c, frame] == 1)
            meta_ref[KIND + c * frame_dev + f] = jnp.where(valid, jnp.where(c == long, 1, 2), 0)
    for e in range(EXTRAS):
        local_frame = meta_ref[FRAME + e] - column * frame_dev
        here = (local_frame >= 0) & (local_frame < frame_dev)
        slot = meta_ref[CLIP + e] * frame_dev + jnp.where(here, local_frame, 0)

        @pl.when(here)
        def _(e=e, slot=slot):
            meta_ref[EXTRA_AT + slot] = jnp.int32(e)

    for copy in copies:
        copy.wait()
    for f in range(frame_axis):
        own = slice(f * patch_t, (f + 1) * patch_t)
        parts = [[extra_in[i, e].astype(F32)[own] for e in range(EXTRAS)] for i in range(2)]
        main = []
        for j in range(frame_dev):
            rows = main_in[j].astype(F32)
            starts = [s * sub + f * small for s in range(sharers)]
            main += [rows[at : at + small] for at in starts]
        extra_ref[f ^ column] = jnp.concatenate(parts[0], axis=0).astype(BF)
        cot_main_ref[f ^ column] = jnp.concatenate(main, axis=0).astype(BF)
        cot_extra_ref[f ^ column] = jnp.concatenate(parts[1], axis=0).astype(BF)


def front_main_kernel(meta_ref, mod_ref, x_ref, w_ref, q_ref, kv_ref, low_ref):
    member = pl.program_id(0)

    @pl.when(member == 0)
    def _():
        shift, scale = [main_vec(meta_ref, mod_ref, 0, i) for i in range(2)]

        def body(rows):
            low_ref[rows, :] = modulate(x_ref[rows, :], shift, scale)

        over_rows(x_ref.shape[0], body)
        times(q_ref, low_ref, w_ref, 0)

    @pl.when(member > 0)
    def _():
        times(kv_ref.at[0], low_ref, w_ref, 0)


def own_extras(meta_ref, got_ref, extras, patches, frame_dev):
    rows = []
    for e in range(EXTRAS):
        source = meta_ref[COLUMN] ^ (meta_ref[FRAME + e] // frame_dev)
        at = e * patches
        rows.append(got_ref[source, at : at + patches, :].astype(F32))
    return rows + [jnp.zeros_like(rows[0])] * (extras - EXTRAS)


def front_extra_kernel(
    meta_ref, mod_ref, got_ref, w_ref, pack_ref, x_ref, low_ref, out_ref, *, patches, frame_dev
):
    member = pl.program_id(0)
    rows = x_ref.shape[0]

    @pl.when(member == 0)
    def _():
        x = own_extras(meta_ref, got_ref, rows // patches, patches, frame_dev)
        x = jnp.concatenate(x, axis=0)
        x_ref[...] = x.astype(BF)
        shift, scale = [extra_vec(meta_ref, mod_ref, 0, i, rows // patches, patches) for i in range(2)]
        low_ref[...] = modulate(x, shift, scale)

    for start, size in col_tiles(w_ref.shape[-1]):
        cols = pl.ds(start, size)
        out_ref[member, :, cols] = nn(low_ref[...], w_ref[0, :, cols])

    @pl.when(member == 2)
    def _():
        for head in range(pack_ref.shape[0]):
            pack_ref[head] = sum(head_into(out_ref.at[i], slice(None), head, i) for i in range(3)).astype(BF)


def fill_keys(k_ref, v_ref, kv_ref, other_ref):
    rows = kv_ref.shape[1]
    k_ref[:rows] = kv_ref[0]
    v_ref[:rows] = kv_ref[1]
    for i in range(other_ref.shape[0]):
        k_ref[(i + 1) * rows : (i + 2) * rows] = other_ref[i, 0]
        v_ref[(i + 1) * rows : (i + 2) * rows] = other_ref[i, 1]


def attend_kernel(q_ref, kv_ref, other_ref, o_ref, k_ref, v_ref, acc_ref, *, heads):
    fill_keys(k_ref, v_ref, kv_ref, other_ref)
    acc_ref[...] = jnp.zeros_like(acc_ref)
    heads_forward(acc_ref, q_ref, k_ref, v_ref, [slice(None)], None, heads)
    o_ref[...] = acc_ref[...].astype(BF)


def extra_rows(ref, index):
    part = ref[:, index]
    return part.reshape(part.shape[0] * part.shape[1], part.shape[2])


def extra_attend_kernel(pack_ref, o_ref):
    results = []
    for index in range(pack_ref.shape[1]):
        packed = extra_rows(pack_ref, index).astype(F32)
        q, k, v = [unpack(packed, i).astype(BF) for i in range(3)]
        scores = nt(q, k)
        exponent = jnp.exp2((scores - jnp.max(scores, axis=-1, keepdims=True)) * SCALE2)
        total = jnp.sum(exponent, axis=-1, keepdims=True)
        results.append(nn(exponent.astype(BF), v) * (1.0 / total))
    o_ref[...] = pack(results).reshape(o_ref.shape).astype(BF)


def extra_attend_back_kernel(pack_ref, got_ref, grad_ref):
    devices, _, patches, _ = pack_ref.shape
    got = got_ref[...].astype(F32).reshape(devices * patches, got_ref.shape[2])
    for index in range(pack_ref.shape[1]):
        packed = extra_rows(pack_ref, index).astype(F32)
        q, k, v = [unpack(packed, i).astype(BF) for i in range(3)]
        do = unpack(got, index).astype(BF)
        (dscores,), (prob,) = softmax_grads([q], [do], [k], [v], None)
        out = pack([tn(dscores, k), nn(dscores, q), nn(prob, do)]).astype(BF)
        grad_ref[:, index] = out.reshape(devices, patches, 256)


def write_chunk(sent_ref, dest, value):
    pieces = [value[:, at : at + 128] for at in range(0, value.shape[1], 128)]
    sent_ref[dest] = jnp.concatenate(pieces, axis=0).astype(BF)


def read_chunk(got_ref, source, out_ref, row, small):
    value = got_ref[source].astype(F32)
    for i in range(out_ref.shape[1] // 128):
        out_ref[row : row + small, i * 128 : (i + 1) * 128] = value[i * small : (i + 1) * small]


def back_main_kernel(meta_ref, mod_ref, x_ref, o_ref, w_ref, sent_ref, acc_ref, *, columns):
    times(acc_ref, o_ref, w_ref, 0)
    gate = main_vec(meta_ref, mod_ref, 0, 2)

    def body(rows):
        acc_ref[rows, :] = x_ref[rows, :].astype(F32) + gate * acc_ref[rows, :]

    over_rows(x_ref.shape[0], body)
    devices = sent_ref.shape[0]
    small = x_ref.shape[0] // devices
    patch_axis = devices // columns
    for p in range(patch_axis):
        for f in range(columns):
            row = (p * columns + f) * small
            write_chunk(sent_ref, f * patch_axis + p, acc_ref[row : row + small, :])


def back_grad_main_kernel(meta_ref, mod_ref, got_ref, w_ref, do_ref, g_ref, low_ref, acc_ref, *, columns):
    devices = got_ref.shape[0]
    small = g_ref.shape[0] // devices
    patch_axis = devices // columns
    for p in range(patch_axis):
        for f in range(columns):
            row = (p * columns + f) * small
            read_chunk(got_ref, f * patch_axis + p, acc_ref, row, small)
    gate = main_vec(meta_ref, mod_ref, 0, 2)

    def body(rows):
        g_ref[rows, :] = acc_ref[rows, :].astype(BF)
        low_ref[rows, :] = (gate * acc_ref[rows, :]).astype(BF)

    over_rows(g_ref.shape[0], body)
    times(do_ref, low_ref, w_ref, 0, transposed=True)


def attend_back_kernel(
    q_ref, kv_ref, other_ref, do_ref, own_ref, sent_ref, k_ref, v_ref, dq_ref, dk_ref, dv_ref, *, heads
):
    rows = kv_ref.shape[1]
    fill_keys(k_ref, v_ref, kv_ref, other_ref)
    for ref in (dq_ref, dk_ref, dv_ref):
        ref[...] = jnp.zeros_like(ref)
    heads_backward(dq_ref, dk_ref, dv_ref, q_ref, k_ref, v_ref, do_ref, [slice(None)], None, heads)
    own_ref[0] = dq_ref[...].astype(BF)
    own_ref[1] = dk_ref[:rows].astype(BF)
    own_ref[2] = dv_ref[:rows].astype(BF)
    for i in range(other_ref.shape[0]):
        sent_ref[i, 0] = dk_ref[(i + 1) * rows : (i + 2) * rows].astype(BF)
        sent_ref[i, 1] = dv_ref[(i + 1) * rows : (i + 2) * rows].astype(BF)


def add_product(acc_ref, d_ref, member, w_ref):
    for start, size in col_tiles(w_ref.shape[-1]):
        cols = pl.ds(start, size)
        product = nt(d_ref[member], w_ref[0, cols, :])

        @pl.when(member == 0)
        def _(cols=cols, product=product):
            acc_ref[:, cols] = product

        @pl.when(member > 0)
        def _(cols=cols, product=product):
            acc_ref[:, cols] = acc_ref[:, cols] + product


def front_grad_main_kernel(meta_ref, mod_ref, own_ref, got_ref, x_ref, g_ref, w_ref, out_ref, d_ref, acc_ref):
    member = pl.program_id(0)

    @pl.when(member == 0)
    def _():
        d_ref[0] = own_ref[0]
        for i in range(2):
            total = own_ref[1 + i].astype(F32)
            for j in range(got_ref.shape[0]):
                total = total + got_ref[j, i].astype(F32)
            d_ref[1 + i] = total.astype(BF)

    add_product(acc_ref, d_ref, member, w_ref)

    @pl.when(member == 2)
    def _():
        scale = main_vec(meta_ref, mod_ref, 0, 1)

        def body(rows):
            out_ref[rows, :] = norm_back(x_ref[rows, :], g_ref[rows, :], acc_ref[rows, :], scale)

        over_rows(x_ref.shape[0], body)


def front_grad_extra_kernel(
    meta_ref, mod_ref, pack_ref, x_ref, g_ref, w_ref, out_ref, d_ref, acc_ref, ext_ref, *, patches
):
    member = pl.program_id(0)
    rows = x_ref.shape[0]

    @pl.when(member == 0)
    def _():
        ext_ref[...] = jnp.zeros_like(ext_ref)
        for head in range(pack_ref.shape[0]):
            packed = pack_ref[head].astype(F32)
            for i in range(3):
                cols, value = head_from(packed, head, i)
                ext_ref[i, :, cols] = ext_ref[i, :, cols] + value
        d_ref[...] = ext_ref[...].astype(BF)

    add_product(acc_ref, d_ref, member, w_ref)

    @pl.when(member == 2)
    def _():
        scale = extra_vec(meta_ref, mod_ref, 0, 1, rows // patches, patches)
        out = norm_back(x_ref[...], g_ref[...], acc_ref[...], scale)
        out_ref[...] = out.astype(F32)[: out_ref.shape[0]].astype(BF)


def key_bias(meta_ref, valid_at, clip_at, tokens, count, small, keys_axis):
    part = count * small

    def spread(base, axis):
        line = (1, tokens) if axis == 1 else (tokens, 1)
        item = lax.broadcasted_iota(jnp.int32, line, axis) % part // small
        out = jnp.zeros(line, jnp.int32)
        for i in range(count):
            out = jnp.where(item == i, meta_ref[base + i], out)
        return out

    where = lax.broadcasted_iota(jnp.int32, (tokens, tokens), keys_axis)
    other = lax.broadcasted_iota(jnp.int32, (tokens, tokens), 1 - keys_axis)
    admitted = jnp.broadcast_to(spread(valid_at, keys_axis) == 1, (tokens, tokens))
    if clip_at is not None:
        admitted = admitted & (spread(clip_at, 0) == spread(clip_at, 1))
    admitted = admitted & (where % small == other % small) & (where // part == other // part)
    return jnp.where(admitted | (where == other), 0.0, -1e30).astype(F32)


def bring(w_hbm, w_ref, sems):
    copies = [pltpu.make_async_copy(w_hbm.at[i], w_ref.at[i], sems.at[i]) for i in range(4)]
    for copy in copies:
        copy.start()
    return copies


def temporal_core(vecs, w_ref, copies, parts, biases, put, most, refs, heads):
    x_ref, cot_ref, low_ref, q_ref, k_ref, v_ref, acc_ref, dq_ref, dk_ref, dv_ref = refs
    count = x_ref.shape[0]
    shift, scale, gate = vecs

    def body(rows):
        low_ref[rows, :] = modulate(x_ref[rows, :], shift, scale)

    over_rows(count, body, most)
    for i, ref in enumerate((q_ref, k_ref, v_ref)):
        copies[i].wait()
        times(ref, low_ref, w_ref, i)
    acc_ref[...] = jnp.zeros_like(acc_ref)
    heads_forward(acc_ref, q_ref, k_ref, v_ref, parts, biases(1), heads)
    low_ref[...] = acc_ref[...].astype(BF)
    copies[3].wait()
    times(acc_ref, low_ref, w_ref, 3)

    def body(rows):
        acc_ref[rows, :] = x_ref[rows, :] + gate * acc_ref[rows, :]
        low_ref[rows, :] = (gate * cot_ref[rows, :]).astype(BF)

    over_rows(count, body, most)
    put()
    times(acc_ref, low_ref, w_ref, 3, transposed=True)
    low_ref[...] = acc_ref[...].astype(BF)
    for ref in (dq_ref, dk_ref, dv_ref):
        ref[...] = jnp.zeros_like(ref)
    heads_backward(dq_ref, dk_ref, dv_ref, q_ref, k_ref, v_ref, low_ref, parts, biases(0), heads)
    for i, ref in enumerate((dq_ref, dk_ref, dv_ref)):
        low_ref[...] = ref[...].astype(BF)
        times(acc_ref, low_ref, w_ref, i, transposed=True, add=i > 0)

    def body(rows):
        acc_ref[rows, :] = norm_back(x_ref[rows, :], cot_ref[rows, :], acc_ref[rows, :], scale).astype(F32)

    over_rows(count, body, most)


def temporal_main_kernel(
    meta_ref, mod_ref, got_ref, c_ref, w_hbm, out_ref, sent_ref, w_ref, sems, *refs, heads, patches
):
    copies = bring(w_hbm, w_ref, sems)
    x_ref, cot_ref, acc_ref = refs[0], refs[1], refs[6]
    columns = c_ref.shape[0]
    main = x_ref.shape[0]
    block = main // columns
    frames, each = main // patches, block // patches
    column = meta_ref[COLUMN]
    devices = got_ref.shape[0]
    small = main // devices
    sharers = patches // small
    part = frames * small

    def token(source):
        return source % sharers * part + source // sharers * small

    for source in range(devices):
        read_chunk(got_ref, source, x_ref, token(source), small)
    for f in range(columns):
        values = c_ref[column ^ f].astype(F32)
        for j in range(each):
            valid = meta_ref[LONG_VALID + f * each + j] == 1
            for g in range(sharers):
                rows = pl.ds(token((f * each + j) * sharers + g), small)
                at = j * patches + g * small
                cot_ref[rows, :] = jnp.where(valid, values[at : at + small], 0.0)

    parts = [slice(g * part, (g + 1) * part) for g in range(sharers)]
    if part % 128:
        parts = [slice(0, main)]

    def biases(axis):
        bias = key_bias(meta_ref, LONG_VALID, None, main // len(parts), frames, small, axis)
        return jnp.concatenate([bias] * len(parts), axis=1 - axis)

    def put():
        for f in range(columns):
            starts = [token(f * each * sharers + i) for i in range(each * sharers)]
            pieces = [acc_ref[at : at + small, :] for at in starts]
            out_ref[column ^ f] = jnp.concatenate(pieces, axis=0).astype(BF)

    vecs = [main_vec(meta_ref, mod_ref, 1, i) for i in range(3)]
    temporal_core(vecs, w_ref, copies, parts, biases, put, 64, refs, heads)
    for dest in range(devices):
        write_chunk(sent_ref, dest, acc_ref[token(dest) : token(dest) + small, :])


def temporal_extra_kernel(
    meta_ref, mod_ref, got_ref, l_ref, c_ref, ws_ref, w_hbm, out_ref, sent_ref, g_ref, w_ref, sems, *refs,
    heads, patches, groups, frame_dev,
):
    copies = bring(w_hbm, w_ref, sems)
    x_ref, cot_ref, acc_ref = refs[0], refs[1], refs[6]
    rows = l_ref.shape[0]
    extras = rows // patches
    each = extras // groups
    devices = got_ref.shape[0]

    def vec(block, member):
        return extra_vec(meta_ref, mod_ref, block, member, extras, patches)

    acc_ref[...] = jnp.zeros_like(acc_ref)
    for source in range(devices):
        head, group = source // groups, source % groups
        packed = got_ref[source].astype(F32)
        for e in range(each):
            at = (group * each + e) * patches
            cols, value = head_from(packed, head, e)
            acc_ref[at : at + patches, cols] = acc_ref[at : at + patches, cols] + value
    gate_s = vec(0, 2)
    mixed = nn(acc_ref[...].astype(BF), ws_ref[0])
    x_ref[...] = gated(l_ref[...], gate_s, mixed).astype(F32)
    values = own_extras(meta_ref, c_ref, extras, patches, frame_dev)
    for i in range(extras):
        part = slice(i * patches, (i + 1) * patches)
        cot_ref[part, :] = jnp.where(meta_ref[VALID + i] == 1, values[i], 0.0)

    def put():
        out_ref[...] = acc_ref[: out_ref.shape[0]].astype(BF)

    def biases(axis):
        return key_bias(meta_ref, VALID, CLIP, rows, extras, patches, axis)

    vecs = [vec(1, i) for i in range(3)]
    temporal_core(vecs, w_ref, copies, [slice(0, rows)], biases, put, rows, refs, heads)
    grad = acc_ref[...]
    g_ref[...] = grad.astype(BF)
    acc_ref[...] = nt((gate_s * grad).astype(BF), ws_ref[0])
    for dest in range(devices):
        head, group = dest // groups, dest % groups
        starts = [(group * each + e) * patches for e in range(each)]
        packed = sum(head_into(acc_ref, slice(at, at + patches), head, e) for e, at in enumerate(starts))
        sent_ref[dest] = packed[:, : sent_ref.shape[2]].astype(BF)


def place_kernel(meta_ref, main_ref, extra_ref, out_ref, *, sharers):
    frame_dev, patch_dev, width = main_ref.shape[-3], out_ref.shape[1], out_ref.shape[2]
    for slot in range(out_ref.shape[0]):
        kind = meta_ref[KIND + slot]

        @pl.when(kind == 0)
        def _(slot=slot):
            out_ref[slot] = jnp.zeros_like(out_ref[slot])

        @pl.when(kind == 1)
        def _(slot=slot):
            if not sharers:
                out_ref[slot] = main_ref[slot % frame_dev]
                return
            columns, patch_t = main_ref.shape[0], main_ref.shape[2]
            small = patch_t // sharers
            parts = [main_ref[meta_ref[COLUMN] ^ f, slot % frame_dev].astype(F32) for f in range(columns)]
            pieces = [p[s * small : (s + 1) * small] for s in range(sharers) for p in parts]
            out_ref[slot] = jnp.concatenate(pieces, axis=0).astype(BF)

        @pl.when(kind == 2)
        def _(slot=slot):
            e = meta_ref[EXTRA_AT + slot]
            parts = [extra_ref[meta_ref[COLUMN] ^ f, e].astype(F32) for f in range(extra_ref.shape[0])]
            out_ref[slot] = jnp.concatenate(parts, axis=0).astype(BF)


SCALARS = pl.BlockSpec(memory_space=pltpu.SMEM)
ANYWHERE = pl.BlockSpec(memory_space=pl.ANY)


def params(steps=0):
    semantics = {"dimension_semantics": ("arbitrary",) * steps} if steps else {}
    return pltpu.CompilerParams(vmem_limit_bytes=VMEM_LIMIT, **semantics)


def cost(flops, elements=0):
    return pl.CostEstimate(flops=int(flops) // 1000, bytes_accessed=int(elements) // 1000, transcendentals=0)


def whole(array):
    return pl.BlockSpec(array.shape, lambda *_: (0,) * len(array.shape))


def shape(*dims, dtype=BF):
    return jax.ShapeDtypeStruct(dims, dtype)


def weight_call(kernel, name, operands, weights, members, outs, scratch, weigh):
    width = weights.shape[-1]
    first, count = members
    return pl.pallas_call(
        kernel,
        name=name,
        grid=(count,),
        in_specs=[SCALARS]
        + [whole(a) for a in operands[1:]]
        + [pl.BlockSpec((1, width, width), lambda i: (first + i, 0, 0))],
        out_specs=[spec for spec, _ in outs],
        out_shape=[struct for _, struct in outs],
        scratch_shapes=scratch,
        compiler_params=params(1),
        cost_estimate=cost(weigh * count, 2 * width * width * count),
    )(*operands, weights)


def full(*dims):
    return whole(shape(*dims)), shape(*dims)


def gather(lengths, frame_mask, column, latents, cotangent, columns, sharers):
    _, frame_dev, patch_dev, width = latents.shape
    main = (frame_dev, patch_dev, width)
    patch_t = patch_dev // columns
    return pl.pallas_call(
        functools.partial(gather_kernel, sharers=sharers),
        name="gather",
        in_specs=[SCALARS] * 3 + [ANYWHERE] * 2,
        out_specs=[SCALARS] + [pl.BlockSpec(memory_space=pltpu.VMEM)] * 4,
        out_shape=[
            shape(TABLE, dtype=jnp.int32), shape(*main), shape(columns, EXTRAS * patch_t, width),
            shape(columns, frame_dev * patch_t, width), shape(columns, EXTRAS * patch_t, width),
        ],
        scratch_shapes=[
            pltpu.VMEM(main, BF),
            pltpu.VMEM((2, EXTRAS, patch_dev, width), BF),
            pltpu.SemaphoreType.DMA((2, EXTRAS + 1)),
        ],
        compiler_params=params(),
    )(lengths, frame_mask, column, latents, cotangent)


def front_main(meta, mod, x, weights):
    rows, width = x.shape
    kv = pl.BlockSpec((1, rows, width), lambda i: (jnp.maximum(i - 1, 0), 0, 0)), shape(2, rows, width)
    return weight_call(
        front_main_kernel, "front_main", (meta, mod, x), weights, (0, 3),
        [full(rows, width), kv], [pltpu.VMEM((rows, width), BF)], 2 * rows * width**2,
    )


def front_extra(meta, mod, got, weights, heads, patches, extras, frame_dev):
    width = got.shape[-1]
    rows = extras * patches
    return weight_call(
        functools.partial(front_extra_kernel, patches=patches, frame_dev=frame_dev), "front_extra",
        (meta, mod, got), weights, (0, 3), [full(heads, rows, 256), full(rows, width)],
        [pltpu.VMEM((rows, width), BF), pltpu.VMEM((3, rows, width), F32)], 4 * rows * width**2,
    )


def back_main(meta, mod, x, o, weights, columns, devices):
    rows, width = x.shape
    return weight_call(
        functools.partial(back_main_kernel, columns=columns), "back_main", (meta, mod, x, o), weights,
        (3, 1), [full(devices, rows * width // (devices * 128), 128)], [pltpu.VMEM((rows, width), F32)],
        3 * rows * width**2,
    )[0]


def back_grad_main(meta, mod, got, weights, rows, columns):
    width = weights.shape[-1]
    return weight_call(
        functools.partial(back_grad_main_kernel, columns=columns), "back_grad_main",
        (meta, mod, got), weights, (3, 1), [full(rows, width)] * 2,
        [pltpu.VMEM((rows, width), BF), pltpu.VMEM((rows, width), F32)], 3 * rows * width**2,
    )


def front_grad_main(meta, mod, own, got, x, g, weights):
    rows, width = x.shape
    return weight_call(
        front_grad_main_kernel, "front_grad_main", (meta, mod, own, got, x, g), weights, (0, 3),
        [full(rows, width)], [pltpu.VMEM((3, rows, width), BF), pltpu.VMEM((rows, width), F32)],
        3 * rows * width**2,
    )[0]


def front_grad_extra(meta, mod, pack, x, g, weights, patches):
    rows, width = x.shape
    return weight_call(
        functools.partial(front_grad_extra_kernel, patches=patches), "front_grad_extra",
        (meta, mod, pack, x, g), weights, (0, 3), [full(EXTRAS * patches, width)],
        [pltpu.VMEM((3, rows, width), BF), pltpu.VMEM((rows, width), F32), pltpu.VMEM((3, rows, width), F32)],
        4 * rows * width**2,
    )[0]


def attend(q, kv, other, heads):
    rows, width = q.shape
    keys = rows * (other.shape[0] + 1)
    return pl.pallas_call(
        functools.partial(attend_kernel, heads=heads),
        name="attend",
        out_shape=shape(rows, width),
        scratch_shapes=[
            pltpu.VMEM((keys, width), BF),
            pltpu.VMEM((keys, width), BF),
            pltpu.VMEM((rows, width), F32),
        ],
        compiler_params=params(),
        cost_estimate=cost(6e9),
    )(q, kv, other)


def extra_attend(packed):
    devices, count, patches, _ = packed.shape
    return pl.pallas_call(
        extra_attend_kernel, name="extra_attend", out_shape=shape(devices, patches, room_for(count)),
        compiler_params=params(), cost_estimate=cost(4e9),
    )(packed)


def extra_attend_back(packed, got):
    return pl.pallas_call(
        extra_attend_back_kernel, name="extra_attend_back", out_shape=shape(*packed.shape),
        compiler_params=params(), cost_estimate=cost(6e9),
    )(packed, got)


def attend_back(q, kv, other, do, heads):
    rows, width = q.shape
    keys = rows * (other.shape[0] + 1)
    return pl.pallas_call(
        functools.partial(attend_back_kernel, heads=heads),
        name="attend_back",
        out_shape=[shape(3, rows, width), shape(*other.shape)],
        scratch_shapes=[
            pltpu.VMEM((keys, width), BF),
            pltpu.VMEM((keys, width), BF),
            pltpu.VMEM((rows, width), F32),
            pltpu.VMEM((keys, width), F32),
            pltpu.VMEM((keys, width), F32),
        ],
        compiler_params=params(),
        cost_estimate=cost(14e9),
    )(q, kv, other, do)


def temporal_scratch(rows, width):
    high, low = pltpu.VMEM((rows, width), F32), pltpu.VMEM((rows, width), BF)
    weights = [pltpu.VMEM((4, width, width), BF), pltpu.SemaphoreType.DMA((4,))]
    return weights + [high] * 2 + [low] * 4 + [high] * 4


def temporal_main(meta, mod, got, cot, weights, heads, patches):
    columns, _, width = cot.shape
    block = got.shape[0] * got.shape[1] * got.shape[2] // (columns * width)
    operands = (mod, got, cot)
    return pl.pallas_call(
        functools.partial(temporal_main_kernel, heads=heads, patches=patches),
        name="temporal_main",
        in_specs=[SCALARS] + [whole(a) for a in operands] + [ANYWHERE],
        out_shape=[shape(columns, block, width), shape(*got.shape)],
        scratch_shapes=temporal_scratch(columns * block, width),
        compiler_params=params(),
        cost_estimate=cost(25e9),
    )(meta, *operands, weights)


def temporal_extra(meta, mod, got, le, cot, weights, last_weight, heads, patches, groups, frame_dev):
    operands = (mod, got, le, cot, last_weight)
    return pl.pallas_call(
        functools.partial(
            temporal_extra_kernel, heads=heads, patches=patches, groups=groups, frame_dev=frame_dev
        ),
        name="temporal_extra",
        in_specs=[SCALARS] + [whole(a) for a in operands] + [ANYWHERE],
        out_shape=[shape(EXTRAS * patches, le.shape[1]), shape(*got.shape), shape(*le.shape)],
        scratch_shapes=temporal_scratch(*le.shape),
        compiler_params=params(),
        cost_estimate=cost(14e9),
    )(meta, *operands, weights)


def place(meta, main, extra, slots, sharers):
    return pl.pallas_call(
        functools.partial(place_kernel, sharers=sharers),
        name="place",
        in_specs=[SCALARS, whole(main), whole(extra)],
        out_shape=shape(slots, extra.shape[0] * extra.shape[2], extra.shape[3]),
        compiler_params=params(),
        cost_estimate=cost(3e9),
    )(meta, main, extra)


def local(latents, cotangent, spatial_weights, temporal_weights, modulation, lengths, frame_mask):
    clips, frame_dev, patch_dev, width = latents.shape
    heads = width // HEAD
    frame_axis, patch_axis = lax.axis_size("frame"), lax.axis_size("patch")
    everyone = ("frame", "patch")
    frames = frame_dev * frame_axis
    sharers = patch_axis // frame_dev
    sub = patch_dev // sharers
    small = sub // frame_axis
    patch_t = patch_dev // frame_axis
    heads_col = heads // frame_axis
    groups = patch_axis // heads_col
    group_extras = -(-EXTRAS // groups)
    extras = groups * group_extras

    def swap(x, axis):
        return lax.all_to_all(x, axis, split_axis=0, concat_axis=0, tiled=True)

    column = lax.axis_index("frame")
    main_rows = frame_dev * patch_dev

    sources = -(-(EXTRAS - clips + 2) // frame_dev)

    def cross(blocks, chosen=lambda sender, receiver: True):
        got = [blocks[0]]
        for m in range(1, frame_axis):
            pairs = [(f, f ^ m) for f in range(frame_axis) if chosen(f, f ^ m)]
            got.append(lax.ppermute(blocks[m], "frame", pairs))
        return jnp.stack(got)

    def from_extras(sender, receiver):
        return sender < sources

    def to_extras(sender, receiver):
        return receiver < sources

    def parts_home(x):
        return cross([x] * frame_axis, to_extras).reshape(frame_axis, EXTRAS, patch_t, width)

    meta, main_home, extra_home, cot_main, cot_extra = gather(
        lengths, frame_mask, column.reshape(1).astype(jnp.int32), latents, cotangent, frame_axis, sharers
    )
    extra_got = cross(extra_home, from_extras)
    main_s = swap(main_home.reshape(patch_axis, sub, width), "patch").reshape(main_rows, width)
    extra_got, cot_main, cot_extra = lax.optimization_barrier((extra_got, cot_main, cot_extra))
    cot_m, cot_e = cross(cot_main), cross(cot_extra, from_extras)

    def rotate(array, by):
        perm = []
        for p in range(patch_axis):
            base = p // sharers * sharers
            perm.append((p, base + (p - base + by) % sharers))
        return lax.ppermute(array, "patch", perm)

    mod = modulation
    chunk = group_extras * patch_t
    packed, extra_t = front_extra(
        meta, mod, extra_got, spatial_weights, heads, patch_t, extras, frame_dev
    )
    packed, main_s = lax.optimization_barrier((packed, main_s))
    pack_got = swap(packed.reshape(frame_axis * patch_axis, chunk, 256), everyone)
    pack_got = pack_got.reshape(frame_axis * patch_axis, group_extras, patch_t, 256)
    q, kv = front_main(meta, mod, main_s, spatial_weights)
    other = jnp.stack([rotate(kv, by) for by in range(1, sharers)])
    attended = attend(q, kv, other, heads)
    sent = back_main(meta, mod, main_s, attended, spatial_weights, frame_axis, frame_axis * patch_axis)
    sent, pack_got = lax.optimization_barrier((sent, pack_got))
    extra_o = extra_attend(pack_got)

    got, cot_m, cot_e, extra_o = lax.optimization_barrier((swap(sent, everyone), cot_m, cot_e, extra_o))
    out_m, sent = temporal_main(meta, mod, got, cot_m, temporal_weights, heads, patch_t)
    extra_o, _ = lax.optimization_barrier((swap(extra_o, everyone), out_m))
    out_e, sent_e, grad_e = temporal_extra(
        meta, mod, extra_o, extra_t, cot_e, temporal_weights, spatial_weights[3:], heads, patch_t, groups, frame_dev
    )

    grads, sent_e = lax.optimization_barrier((swap(sent, everyone), sent_e))
    do_main, grad_s = back_grad_main(meta, mod, grads, spatial_weights, main_rows, frame_axis)
    dpack = extra_attend_back(pack_got, swap(sent_e, everyone))
    out_main, out_extra = cross(out_m), parts_home(out_e)
    do_main, dpack, out_main, out_extra = lax.optimization_barrier((do_main, dpack, out_main, out_extra))
    own, sent = attend_back(q, kv, other, do_main, heads)
    got = jnp.stack([rotate(sent[by - 1], -by) for by in range(1, sharers)])
    dpack = swap(dpack.reshape(frame_axis * patch_axis, chunk, 256), everyone)
    dpack = dpack.reshape(heads, extras * patch_t, 256)
    lat_m = front_grad_main(meta, mod, own, got, main_s, grad_s, spatial_weights)
    dpack, _ = lax.optimization_barrier((dpack, own))
    lat_e = front_grad_extra(meta, mod, dpack, extra_t, grad_e, spatial_weights, patch_t)
    lat_main = swap(lat_m.reshape(patch_axis, sub, width), "patch").reshape(frame_dev, patch_dev, width)

    out_main = out_main.reshape(frame_axis, frame_dev, patch_t, width)
    slots = clips * frame_dev
    output = place(meta, out_main, out_extra, slots, sharers)
    grad = place(meta, lat_main, parts_home(lat_e), slots, 0)
    return output.reshape(latents.shape), grad.reshape(latents.shape)


def solution(mesh):
    tokens = P(None, "frame", "patch", None)
    in_specs = (tokens, tokens, P(), P(), P(), P(), P())
    return jax.shard_map(local, mesh=mesh, in_specs=in_specs, out_specs=(tokens, tokens), check_vma=False)
```

```python
import functools
import math

import jax
import jax.numpy as jnp
from jax import lax
from jax.experimental import pallas as pl
from jax.experimental.pallas import tpu as pltpu
from jax.sharding import PartitionSpec as P

HEAD = 72
EXTRAS = 5
SCALE = HEAD ** -0.5
SCALE2 = SCALE * math.log2(math.e)
BF = jnp.bfloat16
F32 = jnp.float32
VMEM_LIMIT = 56 * 1024 * 1024
LONG, COLUMN, CLIP, FRAME, VALID, LONG_VALID, KIND, EXTRA_AT, TABLE = 0, 1, 8, 16, 24, 32, 48, 64, 80


def nn(a, b):
    return lax.dot_general(a, b, (((1,), (0,)), ((), ())), preferred_element_type=F32)


def nt(a, b):
    return lax.dot_general(a, b, (((1,), (1,)), ((), ())), preferred_element_type=F32)


def tn(a, b):
    return lax.dot_general(a, b, (((0,), (0,)), ((), ())), preferred_element_type=F32)


def window(head):
    start = head * HEAD // 128 * 128
    offset = head * HEAD - start
    return start, offset, 128 if offset + HEAD <= 128 else 256


def lanes_in(width, low, high):
    lane = lax.broadcasted_iota(jnp.int32, (1, width), 1)
    return (lane >= low) & (lane < high)


def masked(x, keep):
    return jnp.where(keep, x, jnp.zeros((), x.dtype))


def room_for(count):
    return -(-count * HEAD // 128) * 128


def widened(x):
    return x if x.shape[1] == 256 else jnp.concatenate([x, jnp.zeros_like(x)], axis=1)


def moved(x, lanes):
    return pltpu.roll(x, lanes % 256, 1) if lanes % 256 else x


def head_into(x_ref, rows, head, member):
    start, offset, width = window(head)
    part = moved(widened(x_ref[rows, start : start + width].astype(F32)), member * HEAD - offset)
    return masked(part, lanes_in(256, member * HEAD, (member + 1) * HEAD))


def head_from(packed, head, member):
    start, offset, width = window(head)
    part = moved(widened(packed), offset - member * HEAD)[:, :width]
    return slice(start, start + width), masked(part, lanes_in(width, offset, offset + HEAD))


def pack(parts):
    out = sum(moved(widened(part), i * HEAD) for i, part in enumerate(parts))
    return out[:, : room_for(len(parts))]


def unpack(packed, member):
    return masked(moved(widened(packed), -member * HEAD)[:, :128], lanes_in(128, 0, HEAD))


def main_vec(meta_ref, mod_ref, block, member):
    return mod_ref[block, member, pl.ds(meta_ref[LONG], 1), :]


def extra_vec(meta_ref, mod_ref, block, member, extras, patches):
    rows = [mod_ref[block, member, pl.ds(meta_ref[CLIP + e], 1), :] for e in range(extras)]
    return jnp.concatenate([jnp.broadcast_to(r, (patches, r.shape[1])) for r in rows], axis=0)


def normed_of(x):
    average = jnp.mean(x, axis=-1, keepdims=True)
    centred = x - average
    variance = jnp.mean(centred * centred, axis=-1, keepdims=True)
    inverse = lax.rsqrt(variance + 1e-06)
    return centred * inverse, inverse


def over_rows(count, body, most=64):
    size = math.gcd(count, most)
    if count == size:
        body(slice(0, count))
        return

    def step(i, carry):
        body(pl.ds(pl.multiple_of(i * size, size), size))
        return carry

    lax.fori_loop(0, count // size, step, 0)


def modulate(x, shift, scale):
    normed, _ = normed_of(x.astype(F32))
    return (normed * (1.0 + scale) + shift).astype(BF)


def norm_back(x, grad, dmod, scale):
    normed, inverse = normed_of(x.astype(F32))
    dnormed = dmod * (1.0 + scale)
    mean_d = jnp.mean(dnormed, axis=-1, keepdims=True)
    mean_dn = jnp.mean(dnormed * normed, axis=-1, keepdims=True)
    dx = (inverse * (dnormed - mean_d - normed * mean_dn)).astype(BF)
    return (dx.astype(F32) + grad.astype(F32)).astype(BF)


def gated(x, gate, mixed):
    return (x.astype(F32) + gate * mixed).astype(BF)


def col_tiles(width):
    whole, tiles = 512, []
    start = 0
    while start < width:
        tiles.append((start, min(whole, width - start)))
        start += whole
    return tiles


def times(dest_ref, x_ref, w_ref, member, transposed=False, add=False):
    for start, size in col_tiles(w_ref.shape[-1]):
        cols = pl.ds(start, size)
        if transposed:
            product = nt(x_ref[...], w_ref[member, cols, :])
        else:
            product = nn(x_ref[...], w_ref[member, :, cols])
        if add:
            product = dest_ref[:, cols] + product
        dest_ref[:, cols] = product.astype(dest_ref.dtype)


def heads_forward(o_ref, q_ref, k_ref, v_ref, parts, bias, heads):
    for head in range(heads):
        start, offset, width = window(head)
        cols = slice(start, start + width)
        keep = lanes_in(width, offset, offset + HEAD)
        scores = [nt(masked(q_ref[rows, cols], keep), k_ref[rows, cols]) for rows in parts]
        scores = jnp.concatenate(scores, axis=0) if len(parts) > 1 else scores[0]
        if bias is not None:
            scores = scores + bias
        exponent = jnp.exp2((scores - jnp.max(scores, axis=-1, keepdims=True)) * SCALE2)
        inverse = 1.0 / jnp.sum(exponent, axis=-1, keepdims=True)
        exponent = exponent.astype(BF)
        count = exponent.shape[0] // len(parts)
        for i, rows in enumerate(parts):
            mine = slice(i * count, (i + 1) * count)
            result = nn(exponent[mine], masked(v_ref[rows, cols], keep)) * inverse[mine]
            o_ref[rows, cols] = o_ref[rows, cols] + result


def softmax_grads(q, do, k, v, bias):
    def joined(left, right):
        products = [nt(a, b) for a, b in zip(left, right)]
        return jnp.concatenate(products, axis=1) if len(products) > 1 else products[0]

    scores = joined(k, q)
    if bias is not None:
        scores = scores + bias
    exponent = jnp.exp2((scores - jnp.max(scores, axis=0, keepdims=True)) * SCALE2)
    prob = exponent * (1.0 / jnp.sum(exponent, axis=0, keepdims=True))
    dprob = joined(v, do)
    delta = jnp.sum(prob * dprob, axis=0, keepdims=True)
    dscores = prob * (dprob - delta) * SCALE
    count = scores.shape[1] // len(q)

    def split(x):
        return [x[:, i * count : (i + 1) * count] for i in range(len(q))]

    return split(dscores.astype(BF)), split(prob.astype(BF))


def heads_backward(dq_ref, dk_ref, dv_ref, q_ref, k_ref, v_ref, do_ref, parts, bias, heads):
    for head in range(heads):
        start, offset, width = window(head)
        cols = slice(start, start + width)
        keep = lanes_in(width, offset, offset + HEAD)
        q, do, k = [[masked(ref[rows, cols], keep) for rows in parts] for ref in (q_ref, do_ref, k_ref)]
        dscores, prob = softmax_grads(q, do, k, [v_ref[rows, cols] for rows in parts], bias)
        for i, rows in enumerate(parts):
            dv_ref[rows, cols] = dv_ref[rows, cols] + nn(prob[i], do[i])
            dk_ref[rows, cols] = dk_ref[rows, cols] + nn(dscores[i], q[i])
            dq_ref[rows, cols] = dq_ref[rows, cols] + tn(dscores[i], k[i])


def gather_kernel(
    lengths_ref, mask_ref, column_ref, latents_ref, cotangent_ref,
    meta_ref, main_ref, extra_ref, cot_ref,
    main_in, extra_in, sems, *, sharers,
):
    clips, frame_dev, patch_dev, width = latents_ref.shape
    frames = mask_ref.shape[1]
    frame_axis = frames // frame_dev
    patch_t = patch_dev // frame_axis
    small, sub = patch_t // sharers, patch_dev // sharers
    column = column_ref[0]
    long = jnp.int32(0)
    for c in range(clips):
        long = long + jnp.where(lengths_ref[c] == frames, c, 0)
    for i in range(TABLE):
        meta_ref[i] = 0
    meta_ref[LONG] = long
    meta_ref[COLUMN] = column
    count = jnp.int32(0)
    for c in range(clips):
        for f in range(EXTRAS - clips + 2):
            used = (c != long) & (f < lengths_ref[c])
            at = jnp.where(used, count, EXTRAS)
            meta_ref[CLIP + at] = jnp.int32(c)
            meta_ref[FRAME + at] = jnp.int32(f)
            meta_ref[VALID + at] = mask_ref[c, f]
            count = count + used.astype(jnp.int32)
    for e in range(EXTRAS, 8):
        for row in (CLIP, FRAME, VALID):
            meta_ref[row + e] = 0

    copies = []
    pairs = ((latents_ref, main_ref), (cotangent_ref, main_in))
    for i, (source, main) in enumerate(pairs):
        copies.append(pltpu.make_async_copy(source.at[long], main, sems.at[i, EXTRAS]))
        copies[-1].start()
        for e in range(EXTRAS):
            frame = lax.rem(meta_ref[FRAME + e], frame_dev)
            part = source.at[meta_ref[CLIP + e], frame]
            copies.append(pltpu.make_async_copy(part, extra_in.at[i, e], sems.at[i, e]))
            copies[-1].start()

    for f in range(frames):
        meta_ref[LONG_VALID + f] = mask_ref[long, f]
    for c in range(clips):
        for f in range(frame_dev):
            frame = column * frame_dev + f
            valid = (frame < lengths_ref[c]) & (mask_ref[c, frame] == 1)
            meta_ref[KIND + c * frame_dev + f] = jnp.where(valid, jnp.where(c == long, 1, 2), 0)
    for e in range(EXTRAS):
        local_frame = meta_ref[FRAME + e] - column * frame_dev
        here = (local_frame >= 0) & (local_frame < frame_dev)
        slot = meta_ref[CLIP + e] * frame_dev + jnp.where(here, local_frame, 0)

        @pl.when(here)
        def _(e=e, slot=slot):
            meta_ref[EXTRA_AT + slot] = jnp.int32(e)

    for copy in copies:
        copy.wait()
    for f in range(frame_axis):
        own = slice(f * patch_t, (f + 1) * patch_t)
        parts = [[extra_in[i, e].astype(F32)[own] for e in range(EXTRAS)] for i in range(2)]
        main = []
        for j in range(frame_dev):
            rows = main_in[j].astype(F32)
            starts = [s * sub + f * small for s in range(sharers)]
            main += [rows[at : at + small] for at in starts]
        extra_ref[f ^ column] = jnp.concatenate(parts[0], axis=0).astype(BF)
        cot_ref[f ^ column] = jnp.concatenate(main + parts[1], axis=0).astype(BF)


def front_main_kernel(meta_ref, mod_ref, x_ref, w_ref, q_ref, kv_ref, low_ref):
    member = pl.program_id(0)

    @pl.when(member == 0)
    def _():
        shift, scale = [main_vec(meta_ref, mod_ref, 0, i) for i in range(2)]

        def body(rows):
            low_ref[rows, :] = modulate(x_ref[rows, :], shift, scale)

        over_rows(x_ref.shape[0], body)
        times(q_ref, low_ref, w_ref, 0)

    @pl.when(member > 0)
    def _():
        times(kv_ref.at[0], low_ref, w_ref, 0)


def own_extras(meta_ref, got_ref, first, extras, patches, frame_dev):
    rows = []
    for e in range(EXTRAS):
        source = meta_ref[COLUMN] ^ (meta_ref[FRAME + e] // frame_dev)
        at = first + e * patches
        rows.append(got_ref[source, at : at + patches, :].astype(F32))
    return rows + [jnp.zeros_like(rows[0])] * (extras - EXTRAS)


def front_extra_kernel(
    meta_ref, mod_ref, got_ref, w_ref, pack_ref, x_ref, low_ref, out_ref, *, patches, frame_dev
):
    member = pl.program_id(0)
    rows = x_ref.shape[0]

    @pl.when(member == 0)
    def _():
        x = own_extras(meta_ref, got_ref, 0, rows // patches, patches, frame_dev)
        x = jnp.concatenate(x, axis=0)
        x_ref[...] = x.astype(BF)
        shift, scale = [extra_vec(meta_ref, mod_ref, 0, i, rows // patches, patches) for i in range(2)]
        low_ref[...] = modulate(x, shift, scale)

    for start, size in col_tiles(w_ref.shape[-1]):
        cols = pl.ds(start, size)
        out_ref[member, :, cols] = nn(low_ref[...], w_ref[0, :, cols])

    @pl.when(member == 2)
    def _():
        for head in range(pack_ref.shape[0]):
            pack_ref[head] = sum(head_into(out_ref.at[i], slice(None), head, i) for i in range(3)).astype(BF)


def fill_keys(k_ref, v_ref, kv_ref, other_ref):
    rows = kv_ref.shape[1]
    k_ref[:rows] = kv_ref[0]
    v_ref[:rows] = kv_ref[1]
    for i in range(other_ref.shape[0]):
        k_ref[(i + 1) * rows : (i + 2) * rows] = other_ref[i, 0]
        v_ref[(i + 1) * rows : (i + 2) * rows] = other_ref[i, 1]


def attend_kernel(q_ref, kv_ref, other_ref, o_ref, k_ref, v_ref, acc_ref, *, heads):
    fill_keys(k_ref, v_ref, kv_ref, other_ref)
    acc_ref[...] = jnp.zeros_like(acc_ref)
    heads_forward(acc_ref, q_ref, k_ref, v_ref, [slice(None)], None, heads)
    o_ref[...] = acc_ref[...].astype(BF)


def extra_rows(ref, index):
    part = ref[:, index]
    return part.reshape(part.shape[0] * part.shape[1], part.shape[2])


def extra_attend_kernel(pack_ref, main_ref, sent_ref):
    devices, count, patches, _ = pack_ref.shape
    sent_ref[:, extra_room(patches, count) :, :] = main_ref[...]
    results = []
    for index in range(count):
        packed = extra_rows(pack_ref, index).astype(F32)
        q, k, v = [unpack(packed, i).astype(BF) for i in range(3)]
        scores = nt(q, k)
        exponent = jnp.exp2((scores - jnp.max(scores, axis=-1, keepdims=True)) * SCALE2)
        total = jnp.sum(exponent, axis=-1, keepdims=True)
        results.append(nn(exponent.astype(BF), v) * (1.0 / total))
    packed = pack(results)
    for i in range(packed.shape[1] // 128):
        piece = packed[:, i * 128 : (i + 1) * 128].reshape(devices, patches, 128)
        sent_ref[:, i * patches : (i + 1) * patches, :] = piece.astype(BF)


def extra_attend_back_kernel(pack_ref, got_ref, grad_ref):
    devices, _, patches, _ = pack_ref.shape
    got = got_ref[...].astype(F32).reshape(devices * patches, got_ref.shape[2])
    for index in range(pack_ref.shape[1]):
        packed = extra_rows(pack_ref, index).astype(F32)
        q, k, v = [unpack(packed, i).astype(BF) for i in range(3)]
        do = unpack(got, index).astype(BF)
        (dscores,), (prob,) = softmax_grads([q], [do], [k], [v], None)
        out = pack([tn(dscores, k), nn(dscores, q), nn(prob, do)]).astype(BF)
        grad_ref[:, index] = out.reshape(devices, patches, 256)


def extra_room(patches, count):
    return -(-patches * (room_for(count) // 128) // 16) * 16


def write_chunk(sent_ref, dest, value):
    pieces = [value[:, at : at + 128] for at in range(0, value.shape[1], 128)]
    sent_ref[dest] = jnp.concatenate(pieces, axis=0).astype(BF)


def read_chunk(got_ref, source, out_ref, row, small, room=0):
    count = out_ref.shape[1] // 128
    value = got_ref[source, room : room + count * small, :].astype(F32)
    for i in range(count):
        out_ref[row : row + small, i * 128 : (i + 1) * 128] = value[i * small : (i + 1) * small]


def back_main_kernel(meta_ref, mod_ref, x_ref, o_ref, w_ref, sent_ref, acc_ref, *, columns):
    times(acc_ref, o_ref, w_ref, 0)
    gate = main_vec(meta_ref, mod_ref, 0, 2)

    def body(rows):
        acc_ref[rows, :] = x_ref[rows, :].astype(F32) + gate * acc_ref[rows, :]

    over_rows(x_ref.shape[0], body)
    devices = sent_ref.shape[0]
    small = x_ref.shape[0] // devices
    patch_axis = devices // columns
    for p in range(patch_axis):
        for f in range(columns):
            row = (p * columns + f) * small
            write_chunk(sent_ref, f * patch_axis + p, acc_ref[row : row + small, :])


def back_grad_main_kernel(meta_ref, mod_ref, got_ref, w_ref, do_ref, g_ref, low_ref, acc_ref, *, columns):
    devices = got_ref.shape[0]
    small = g_ref.shape[0] // devices
    patch_axis = devices // columns
    for p in range(patch_axis):
        for f in range(columns):
            row = (p * columns + f) * small
            read_chunk(got_ref, f * patch_axis + p, acc_ref, row, small)
    gate = main_vec(meta_ref, mod_ref, 0, 2)

    def body(rows):
        g_ref[rows, :] = acc_ref[rows, :].astype(BF)
        low_ref[rows, :] = (gate * acc_ref[rows, :]).astype(BF)

    over_rows(g_ref.shape[0], body)
    times(do_ref, low_ref, w_ref, 0, transposed=True)


def attend_back_kernel(
    q_ref, kv_ref, other_ref, do_ref, own_ref, sent_ref, k_ref, v_ref, dq_ref, dk_ref, dv_ref, *, heads
):
    rows = kv_ref.shape[1]
    fill_keys(k_ref, v_ref, kv_ref, other_ref)
    for ref in (dq_ref, dk_ref, dv_ref):
        ref[...] = jnp.zeros_like(ref)
    heads_backward(dq_ref, dk_ref, dv_ref, q_ref, k_ref, v_ref, do_ref, [slice(None)], None, heads)
    own_ref[0] = dq_ref[...].astype(BF)
    own_ref[1] = dk_ref[:rows].astype(BF)
    own_ref[2] = dv_ref[:rows].astype(BF)
    for i in range(other_ref.shape[0]):
        sent_ref[i, 0] = dk_ref[(i + 1) * rows : (i + 2) * rows].astype(BF)
        sent_ref[i, 1] = dv_ref[(i + 1) * rows : (i + 2) * rows].astype(BF)


def add_product(acc_ref, d_ref, member, w_ref):
    for start, size in col_tiles(w_ref.shape[-1]):
        cols = pl.ds(start, size)
        product = nt(d_ref[member], w_ref[0, cols, :])

        @pl.when(member == 0)
        def _(cols=cols, product=product):
            acc_ref[:, cols] = product

        @pl.when(member > 0)
        def _(cols=cols, product=product):
            acc_ref[:, cols] = acc_ref[:, cols] + product


def front_grad_main_kernel(meta_ref, mod_ref, own_ref, got_ref, x_ref, g_ref, w_ref, out_ref, d_ref, acc_ref):
    member = pl.program_id(0)

    @pl.when(member == 0)
    def _():
        d_ref[0] = own_ref[0]
        for i in range(2):
            total = own_ref[1 + i].astype(F32)
            for j in range(got_ref.shape[0]):
                total = total + got_ref[j, i].astype(F32)
            d_ref[1 + i] = total.astype(BF)

    add_product(acc_ref, d_ref, member, w_ref)

    @pl.when(member == 2)
    def _():
        scale = main_vec(meta_ref, mod_ref, 0, 1)

        def body(rows):
            out_ref[rows, :] = norm_back(x_ref[rows, :], g_ref[rows, :], acc_ref[rows, :], scale)

        over_rows(x_ref.shape[0], body)


def front_grad_extra_kernel(
    meta_ref, mod_ref, pack_ref, x_ref, g_ref, w_ref, out_ref, d_ref, acc_ref, ext_ref, *, patches
):
    member = pl.program_id(0)
    rows = x_ref.shape[0]

    @pl.when(member == 0)
    def _():
        ext_ref[...] = jnp.zeros_like(ext_ref)
        for head in range(pack_ref.shape[0]):
            packed = pack_ref[head].astype(F32)
            for i in range(3):
                cols, value = head_from(packed, head, i)
                ext_ref[i, :, cols] = ext_ref[i, :, cols] + value
        d_ref[...] = ext_ref[...].astype(BF)

    add_product(acc_ref, d_ref, member, w_ref)

    @pl.when(member == 2)
    def _():
        scale = extra_vec(meta_ref, mod_ref, 0, 1, rows // patches, patches)
        out = norm_back(x_ref[...], g_ref[...], acc_ref[...], scale)
        out_ref[...] = out.astype(F32)[: out_ref.shape[0]].astype(BF)


def key_bias(meta_ref, valid_at, clip_at, tokens, count, small, keys_axis):
    part = count * small

    def spread(base, axis):
        line = (1, tokens) if axis == 1 else (tokens, 1)
        item = lax.broadcasted_iota(jnp.int32, line, axis) % part // small
        out = jnp.zeros(line, jnp.int32)
        for i in range(count):
            out = jnp.where(item == i, meta_ref[base + i], out)
        return out

    where = lax.broadcasted_iota(jnp.int32, (tokens, tokens), keys_axis)
    other = lax.broadcasted_iota(jnp.int32, (tokens, tokens), 1 - keys_axis)
    admitted = jnp.broadcast_to(spread(valid_at, keys_axis) == 1, (tokens, tokens))
    if clip_at is not None:
        admitted = admitted & (spread(clip_at, 0) == spread(clip_at, 1))
    admitted = admitted & (where % small == other % small) & (where // part == other // part)
    return jnp.where(admitted | (where == other), 0.0, -1e30).astype(F32)


def bring(w_hbm, w_ref, sems):
    copies = [pltpu.make_async_copy(w_hbm.at[i], w_ref.at[i], sems.at[i]) for i in range(4)]
    for copy in copies:
        copy.start()
    return copies


def temporal_core(vecs, w_ref, copies, parts, biases, put, most, refs, heads):
    x_ref, cot_ref, low_ref, q_ref, k_ref, v_ref, acc_ref, dq_ref, dk_ref, dv_ref = refs
    count = x_ref.shape[0]
    shift, scale, gate = vecs

    def body(rows):
        low_ref[rows, :] = modulate(x_ref[rows, :], shift, scale)

    over_rows(count, body, most)
    for i, ref in enumerate((q_ref, k_ref, v_ref)):
        copies[i].wait()
        times(ref, low_ref, w_ref, i)
    acc_ref[...] = jnp.zeros_like(acc_ref)
    heads_forward(acc_ref, q_ref, k_ref, v_ref, parts, biases(1), heads)
    low_ref[...] = acc_ref[...].astype(BF)
    copies[3].wait()
    times(acc_ref, low_ref, w_ref, 3)

    def body(rows):
        acc_ref[rows, :] = x_ref[rows, :] + gate * acc_ref[rows, :]
        low_ref[rows, :] = (gate * cot_ref[rows, :]).astype(BF)

    over_rows(count, body, most)
    put()
    times(acc_ref, low_ref, w_ref, 3, transposed=True)
    low_ref[...] = acc_ref[...].astype(BF)
    for ref in (dq_ref, dk_ref, dv_ref):
        ref[...] = jnp.zeros_like(ref)
    heads_backward(dq_ref, dk_ref, dv_ref, q_ref, k_ref, v_ref, low_ref, parts, biases(0), heads)
    for i, ref in enumerate((dq_ref, dk_ref, dv_ref)):
        low_ref[...] = ref[...].astype(BF)
        times(acc_ref, low_ref, w_ref, i, transposed=True, add=i > 0)

    def body(rows):
        acc_ref[rows, :] = norm_back(x_ref[rows, :], cot_ref[rows, :], acc_ref[rows, :], scale).astype(F32)

    over_rows(count, body, most)


def temporal_main_kernel(
    meta_ref, mod_ref, got_ref, c_ref, w_hbm, out_ref, sent_ref, w_ref, sems, *refs, heads, patches
):
    copies = bring(w_hbm, w_ref, sems)
    x_ref, cot_ref, acc_ref = refs[0], refs[1], refs[6]
    columns = c_ref.shape[0]
    main = x_ref.shape[0]
    block = main // columns
    frames, each = main // patches, block // patches
    column = meta_ref[COLUMN]
    devices = got_ref.shape[0]
    small = main // devices
    room = got_ref.shape[1] - small * (x_ref.shape[1] // 128)
    sharers = patches // small
    part = frames * small

    def token(source):
        return source % sharers * part + source // sharers * small

    for source in range(devices):
        read_chunk(got_ref, source, x_ref, token(source), small, room)
    for f in range(columns):
        values = c_ref[column ^ f].astype(F32)
        for j in range(each):
            valid = meta_ref[LONG_VALID + f * each + j] == 1
            for g in range(sharers):
                rows = pl.ds(token((f * each + j) * sharers + g), small)
                at = j * patches + g * small
                cot_ref[rows, :] = jnp.where(valid, values[at : at + small], 0.0)

    parts = [slice(g * part, (g + 1) * part) for g in range(sharers)]
    if part % 128:
        parts = [slice(0, main)]

    def biases(axis):
        bias = key_bias(meta_ref, LONG_VALID, None, main // len(parts), frames, small, axis)
        return jnp.concatenate([bias] * len(parts), axis=1 - axis)

    def put():
        for f in range(columns):
            starts = [token(f * each * sharers + i) for i in range(each * sharers)]
            pieces = [acc_ref[at : at + small, :] for at in starts]
            out_ref[column ^ f] = jnp.concatenate(pieces, axis=0).astype(BF)

    vecs = [main_vec(meta_ref, mod_ref, 1, i) for i in range(3)]
    temporal_core(vecs, w_ref, copies, parts, biases, put, 64, refs, heads)
    for dest in range(devices):
        write_chunk(sent_ref, dest, acc_ref[token(dest) : token(dest) + small, :])


def temporal_extra_kernel(
    meta_ref, mod_ref, got_ref, l_ref, c_ref, w_hbm, ws_hbm, out_ref, sent_ref, g_ref,
    ws_ref, ws_sem, w_ref, sems, *refs, heads, patches, groups, frame_dev,
):
    last_copy = pltpu.make_async_copy(ws_hbm.at[3], ws_ref, ws_sem)
    last_copy.start()
    copies = bring(w_hbm, w_ref, sems)
    x_ref, cot_ref, acc_ref = refs[0], refs[1], refs[6]
    rows = l_ref.shape[0]
    extras = rows // patches
    each = extras // groups
    devices = got_ref.shape[0]

    def vec(block, member):
        return extra_vec(meta_ref, mod_ref, block, member, extras, patches)

    acc_ref[...] = jnp.zeros_like(acc_ref)
    for source in range(devices):
        head, group = source // groups, source % groups
        pieces = got_ref[source, : patches * (room_for(each) // 128), :].astype(F32)
        pieces = [pieces[at : at + patches] for at in range(0, pieces.shape[0], patches)]
        packed = jnp.concatenate(pieces, axis=1) if len(pieces) > 1 else pieces[0]
        for e in range(each):
            at = (group * each + e) * patches
            cols, value = head_from(packed, head, e)
            acc_ref[at : at + patches, cols] = acc_ref[at : at + patches, cols] + value
    gate_s = vec(0, 2)
    last_copy.wait()
    mixed = nn(acc_ref[...].astype(BF), ws_ref[...])
    x_ref[...] = gated(l_ref[...], gate_s, mixed).astype(F32)
    values = own_extras(meta_ref, c_ref, frame_dev * patches, extras, patches, frame_dev)
    for i in range(extras):
        part = slice(i * patches, (i + 1) * patches)
        cot_ref[part, :] = jnp.where(meta_ref[VALID + i] == 1, values[i], 0.0)

    def put():
        out_ref[...] = acc_ref[: out_ref.shape[0]].astype(BF)

    def biases(axis):
        return key_bias(meta_ref, VALID, CLIP, rows, extras, patches, axis)

    vecs = [vec(1, i) for i in range(3)]
    temporal_core(vecs, w_ref, copies, [slice(0, rows)], biases, put, rows, refs, heads)
    grad = acc_ref[...]
    g_ref[...] = grad.astype(BF)
    acc_ref[...] = nt((gate_s * grad).astype(BF), ws_ref[...])
    for dest in range(devices):
        head, group = dest // groups, dest % groups
        starts = [(group * each + e) * patches for e in range(each)]
        packed = sum(head_into(acc_ref, slice(at, at + patches), head, e) for e, at in enumerate(starts))
        sent_ref[dest] = packed[:, : sent_ref.shape[2]].astype(BF)


def place_kernel(meta_ref, main_ref, extra_ref, out_ref, *, sharers):
    frame_dev, patch_dev, width = main_ref.shape[-3], out_ref.shape[1], out_ref.shape[2]
    for slot in range(out_ref.shape[0]):
        kind = meta_ref[KIND + slot]

        @pl.when(kind == 0)
        def _(slot=slot):
            out_ref[slot] = jnp.zeros_like(out_ref[slot])

        @pl.when(kind == 1)
        def _(slot=slot):
            if not sharers:
                out_ref[slot] = main_ref[slot % frame_dev]
                return
            columns, patch_t = main_ref.shape[0], main_ref.shape[2]
            small = patch_t // sharers
            parts = [main_ref[meta_ref[COLUMN] ^ f, slot % frame_dev].astype(F32) for f in range(columns)]
            pieces = [p[s * small : (s + 1) * small] for s in range(sharers) for p in parts]
            out_ref[slot] = jnp.concatenate(pieces, axis=0).astype(BF)

        @pl.when(kind == 2)
        def _(slot=slot):
            e = meta_ref[EXTRA_AT + slot]
            parts = [extra_ref[meta_ref[COLUMN] ^ f, e].astype(F32) for f in range(extra_ref.shape[0])]
            out_ref[slot] = jnp.concatenate(parts, axis=0).astype(BF)


SCALARS = pl.BlockSpec(memory_space=pltpu.SMEM)
ANYWHERE = pl.BlockSpec(memory_space=pl.ANY)


def params(steps=0):
    semantics = {"dimension_semantics": ("arbitrary",) * steps} if steps else {}
    return pltpu.CompilerParams(vmem_limit_bytes=VMEM_LIMIT, **semantics)


def cost(flops, elements=0):
    return pl.CostEstimate(flops=int(flops) // 1000, bytes_accessed=int(elements) // 1000, transcendentals=0)


def whole(array):
    return pl.BlockSpec(array.shape, lambda *_: (0,) * len(array.shape))


def shape(*dims, dtype=BF):
    return jax.ShapeDtypeStruct(dims, dtype)


def weight_call(kernel, name, operands, weights, members, outs, scratch, weigh):
    width = weights.shape[-1]
    first, count = members
    return pl.pallas_call(
        kernel,
        name=name,
        grid=(count,),
        in_specs=[SCALARS]
        + [whole(a) for a in operands[1:]]
        + [pl.BlockSpec((1, width, width), lambda i: (first + i, 0, 0))],
        out_specs=[spec for spec, _ in outs],
        out_shape=[struct for _, struct in outs],
        scratch_shapes=scratch,
        compiler_params=params(1),
        cost_estimate=cost(weigh * count, 2 * width * width * count),
    )(*operands, weights)


def full(*dims):
    return whole(shape(*dims)), shape(*dims)


def gather(lengths, frame_mask, column, latents, cotangent, columns, sharers):
    _, frame_dev, patch_dev, width = latents.shape
    main = (frame_dev, patch_dev, width)
    patch_t = patch_dev // columns
    return pl.pallas_call(
        functools.partial(gather_kernel, sharers=sharers),
        name="gather",
        in_specs=[SCALARS] * 3 + [ANYWHERE] * 2,
        out_specs=[SCALARS] + [pl.BlockSpec(memory_space=pltpu.VMEM)] * 3,
        out_shape=[
            shape(TABLE, dtype=jnp.int32), shape(*main), shape(columns, EXTRAS * patch_t, width),
            shape(columns, (frame_dev + EXTRAS) * patch_t, width),
        ],
        scratch_shapes=[
            pltpu.VMEM(main, BF),
            pltpu.VMEM((2, EXTRAS, patch_dev, width), BF),
            pltpu.SemaphoreType.DMA((2, EXTRAS + 1)),
        ],
        compiler_params=params(),
    )(lengths, frame_mask, column, latents, cotangent)


def front_main(meta, mod, x, weights):
    rows, width = x.shape
    kv = pl.BlockSpec((1, rows, width), lambda i: (jnp.maximum(i - 1, 0), 0, 0)), shape(2, rows, width)
    return weight_call(
        front_main_kernel, "front_main", (meta, mod, x), weights, (0, 3),
        [full(rows, width), kv], [pltpu.VMEM((rows, width), BF)], 2 * rows * width**2,
    )


def front_extra(meta, mod, got, weights, heads, patches, extras, frame_dev):
    width = got.shape[-1]
    rows = extras * patches
    return weight_call(
        functools.partial(front_extra_kernel, patches=patches, frame_dev=frame_dev), "front_extra",
        (meta, mod, got), weights, (0, 3), [full(heads, rows, 256), full(rows, width)],
        [pltpu.VMEM((rows, width), BF), pltpu.VMEM((3, rows, width), F32)], 4 * rows * width**2,
    )


def back_main(meta, mod, x, o, weights, columns, devices):
    rows, width = x.shape
    return weight_call(
        functools.partial(back_main_kernel, columns=columns), "back_main", (meta, mod, x, o), weights,
        (3, 1), [full(devices, rows * width // (devices * 128), 128)], [pltpu.VMEM((rows, width), F32)],
        3 * rows * width**2,
    )[0]


def back_grad_main(meta, mod, got, weights, rows, columns):
    width = weights.shape[-1]
    return weight_call(
        functools.partial(back_grad_main_kernel, columns=columns), "back_grad_main",
        (meta, mod, got), weights, (3, 1), [full(rows, width)] * 2,
        [pltpu.VMEM((rows, width), BF), pltpu.VMEM((rows, width), F32)], 3 * rows * width**2,
    )


def front_grad_main(meta, mod, own, got, x, g, weights):
    rows, width = x.shape
    return weight_call(
        front_grad_main_kernel, "front_grad_main", (meta, mod, own, got, x, g), weights, (0, 3),
        [full(rows, width)], [pltpu.VMEM((3, rows, width), BF), pltpu.VMEM((rows, width), F32)],
        3 * rows * width**2,
    )[0]


def front_grad_extra(meta, mod, pack, x, g, weights, patches):
    rows, width = x.shape
    return weight_call(
        functools.partial(front_grad_extra_kernel, patches=patches), "front_grad_extra",
        (meta, mod, pack, x, g), weights, (0, 3), [full(EXTRAS * patches, width)],
        [pltpu.VMEM((3, rows, width), BF), pltpu.VMEM((rows, width), F32), pltpu.VMEM((3, rows, width), F32)],
        4 * rows * width**2,
    )[0]


def attend(q, kv, other, heads):
    rows, width = q.shape
    keys = rows * (other.shape[0] + 1)
    return pl.pallas_call(
        functools.partial(attend_kernel, heads=heads),
        name="attend",
        out_shape=shape(rows, width),
        scratch_shapes=[
            pltpu.VMEM((keys, width), BF),
            pltpu.VMEM((keys, width), BF),
            pltpu.VMEM((rows, width), F32),
        ],
        compiler_params=params(),
        cost_estimate=cost(6e9),
    )(q, kv, other)


def extra_attend(packed, main):
    devices, count, patches, _ = packed.shape
    return pl.pallas_call(
        extra_attend_kernel, name="extra_attend",
        out_shape=shape(devices, extra_room(patches, count) + main.shape[1], 128),
        compiler_params=params(), cost_estimate=cost(4e9),
    )(packed, main)


def extra_attend_back(packed, got):
    return pl.pallas_call(
        extra_attend_back_kernel, name="extra_attend_back", out_shape=shape(*packed.shape),
        compiler_params=params(), cost_estimate=cost(6e9),
    )(packed, got)


def attend_back(q, kv, other, do, heads):
    rows, width = q.shape
    keys = rows * (other.shape[0] + 1)
    return pl.pallas_call(
        functools.partial(attend_back_kernel, heads=heads),
        name="attend_back",
        out_shape=[shape(3, rows, width), shape(*other.shape)],
        scratch_shapes=[
            pltpu.VMEM((keys, width), BF),
            pltpu.VMEM((keys, width), BF),
            pltpu.VMEM((rows, width), F32),
            pltpu.VMEM((keys, width), F32),
            pltpu.VMEM((keys, width), F32),
        ],
        compiler_params=params(),
        cost_estimate=cost(14e9),
    )(q, kv, other, do)


def temporal_scratch(rows, width):
    high, low = pltpu.VMEM((rows, width), F32), pltpu.VMEM((rows, width), BF)
    weights = [pltpu.VMEM((4, width, width), BF), pltpu.SemaphoreType.DMA((4,))]
    return weights + [high] * 2 + [low] * 4 + [high] * 4


def temporal_main(meta, mod, got, cot, weights, heads, patches, block):
    columns, _, width = cot.shape
    devices = got.shape[0]
    operands = (mod, got, cot)
    sent = shape(devices, columns * block * width // (devices * 128), 128)
    return pl.pallas_call(
        functools.partial(temporal_main_kernel, heads=heads, patches=patches),
        name="temporal_main",
        in_specs=[SCALARS] + [whole(a) for a in operands] + [ANYWHERE],
        out_shape=[shape(columns, block, width), sent],
        scratch_shapes=temporal_scratch(columns * block, width),
        compiler_params=params(),
        cost_estimate=cost(25e9),
    )(meta, *operands, weights)


def temporal_extra(meta, mod, got, le, cot, weights, spatial_weights, heads, patches, groups, frame_dev):
    operands = (mod, got, le, cot)
    rows, width = le.shape
    sent = shape(got.shape[0], patches, room_for(rows // (patches * groups)))
    return pl.pallas_call(
        functools.partial(
            temporal_extra_kernel, heads=heads, patches=patches, groups=groups, frame_dev=frame_dev
        ),
        name="temporal_extra",
        in_specs=[SCALARS] + [whole(a) for a in operands] + [ANYWHERE] * 2,
        out_shape=[shape(EXTRAS * patches, width), sent, shape(*le.shape)],
        scratch_shapes=[pltpu.VMEM((width, width), BF), pltpu.SemaphoreType.DMA]
        + temporal_scratch(rows, width),
        compiler_params=params(),
        cost_estimate=cost(14e9),
    )(meta, *operands, weights, spatial_weights)


def place(meta, main, extra, slots, sharers):
    return pl.pallas_call(
        functools.partial(place_kernel, sharers=sharers),
        name="place",
        in_specs=[SCALARS, whole(main), whole(extra)],
        out_shape=shape(slots, extra.shape[0] * extra.shape[2], extra.shape[3]),
        compiler_params=params(),
        cost_estimate=cost(3e9),
    )(meta, main, extra)


def local(latents, cotangent, spatial_weights, temporal_weights, modulation, lengths, frame_mask):
    clips, frame_dev, patch_dev, width = latents.shape
    heads = width // HEAD
    frame_axis, patch_axis = lax.axis_size("frame"), lax.axis_size("patch")
    everyone = ("frame", "patch")
    frames = frame_dev * frame_axis
    sharers = patch_axis // frame_dev
    sub = patch_dev // sharers
    small = sub // frame_axis
    patch_t = patch_dev // frame_axis
    heads_col = heads // frame_axis
    groups = patch_axis // heads_col
    group_extras = -(-EXTRAS // groups)
    extras = groups * group_extras

    def swap(x, axis):
        return lax.all_to_all(x, axis, split_axis=0, concat_axis=0, tiled=True)

    column = lax.axis_index("frame")
    main_rows = frame_dev * patch_dev

    def cross(blocks):
        got = [blocks[0]]
        for m in range(1, frame_axis):
            got.append(lax.ppermute(blocks[m], "frame", [(f, f ^ m) for f in range(frame_axis)]))
        return jnp.stack(got)

    def parts_home(x):
        return cross([x] * frame_axis).reshape(frame_axis, EXTRAS, patch_t, width)

    meta, main_home, extra_home, cot_home = gather(
        lengths, frame_mask, column.reshape(1).astype(jnp.int32), latents, cotangent, frame_axis, sharers
    )
    extra_got = cross(extra_home)
    main_s = swap(main_home.reshape(patch_axis, sub, width), "patch").reshape(main_rows, width)
    extra_got, cot_home = lax.optimization_barrier((extra_got, cot_home))
    cot = cross(cot_home)

    def rotate(array, by):
        perm = []
        for p in range(patch_axis):
            base = p // sharers * sharers
            perm.append((p, base + (p - base + by) % sharers))
        return lax.ppermute(array, "patch", perm)

    mod = modulation
    chunk = group_extras * patch_t
    packed, extra_t = front_extra(
        meta, mod, extra_got, spatial_weights, heads, patch_t, extras, frame_dev
    )
    packed, main_s = lax.optimization_barrier((packed, main_s))
    pack_got = swap(packed.reshape(frame_axis * patch_axis, chunk, 256), everyone)
    pack_got = pack_got.reshape(frame_axis * patch_axis, group_extras, patch_t, 256)
    q, kv = front_main(meta, mod, main_s, spatial_weights)
    other = jnp.stack([rotate(kv, by) for by in range(1, sharers)])
    attended = attend(q, kv, other, heads)
    sent = back_main(meta, mod, main_s, attended, spatial_weights, frame_axis, frame_axis * patch_axis)
    sent, pack_got = lax.optimization_barrier((sent, pack_got))
    sent = extra_attend(pack_got, sent)

    got, cot = lax.optimization_barrier((swap(sent, everyone), cot))
    out_m, sent = temporal_main(
        meta, mod, got, cot, temporal_weights, heads, patch_t, frame_dev * patch_t
    )
    got, _ = lax.optimization_barrier((got, out_m))
    out_e, sent_e, grad_e = temporal_extra(
        meta, mod, got, extra_t, cot, temporal_weights, spatial_weights, heads, patch_t, groups, frame_dev
    )

    grads, sent_e = lax.optimization_barrier((swap(sent, everyone), sent_e))
    do_main, grad_s = back_grad_main(meta, mod, grads, spatial_weights, main_rows, frame_axis)
    dpack = extra_attend_back(pack_got, swap(sent_e, everyone))
    out_main, out_extra = cross(out_m), parts_home(out_e)
    do_main, dpack, out_main, out_extra = lax.optimization_barrier((do_main, dpack, out_main, out_extra))
    own, sent = attend_back(q, kv, other, do_main, heads)
    got = jnp.stack([rotate(sent[by - 1], -by) for by in range(1, sharers)])
    dpack = swap(dpack.reshape(frame_axis * patch_axis, chunk, 256), everyone)
    dpack = dpack.reshape(heads, extras * patch_t, 256)
    lat_m = front_grad_main(meta, mod, own, got, main_s, grad_s, spatial_weights)
    dpack, _ = lax.optimization_barrier((dpack, own))
    lat_e = front_grad_extra(meta, mod, dpack, extra_t, grad_e, spatial_weights, patch_t)
    lat_main = swap(lat_m.reshape(patch_axis, sub, width), "patch").reshape(frame_dev, patch_dev, width)

    out_main = out_main.reshape(frame_axis, frame_dev, patch_t, width)
    slots = clips * frame_dev
    output = place(meta, out_main, out_extra, slots, sharers)
    grad = place(meta, lat_main, parts_home(lat_e), slots, 0)
    return output.reshape(latents.shape), grad.reshape(latents.shape)


def solution(mesh):
    tokens = P(None, "frame", "patch", None)
    in_specs = (tokens, tokens, P(), P(), P(), P(), P())
    return jax.shard_map(local, mesh=mesh, in_specs=in_specs, out_specs=(tokens, tokens), check_vma=False)
```

```python
import functools
import math

import jax
import jax.numpy as jnp
from jax import lax
from jax.experimental import pallas as pl
from jax.experimental.pallas import tpu as pltpu
from jax.sharding import PartitionSpec as P

HEAD = 72
EXTRAS = 5
SCALE = HEAD ** -0.5
SCALE2 = SCALE * math.log2(math.e)
BF = jnp.bfloat16
F32 = jnp.float32
VMEM_LIMIT = 56 * 1024 * 1024
LONG, COLUMN, CLIP, FRAME, VALID, LONG_VALID, KIND, EXTRA_AT, TABLE = 0, 1, 8, 16, 24, 32, 48, 64, 80


def nn(a, b):
    return lax.dot_general(a, b, (((1,), (0,)), ((), ())), preferred_element_type=F32)


def nt(a, b):
    return lax.dot_general(a, b, (((1,), (1,)), ((), ())), preferred_element_type=F32)


def tn(a, b):
    return lax.dot_general(a, b, (((0,), (0,)), ((), ())), preferred_element_type=F32)


def window(head):
    start = head * HEAD // 128 * 128
    offset = head * HEAD - start
    return start, offset, 128 if offset + HEAD <= 128 else 256


def lanes_in(width, low, high):
    lane = lax.broadcasted_iota(jnp.int32, (1, width), 1)
    return (lane >= low) & (lane < high)


def masked(x, keep):
    return jnp.where(keep, x, jnp.zeros((), x.dtype))


def room_for(count):
    return -(-count * HEAD // 128) * 128


def widened(x):
    return x if x.shape[1] == 256 else jnp.concatenate([x, jnp.zeros_like(x)], axis=1)


def moved(x, lanes):
    return pltpu.roll(x, lanes % 256, 1) if lanes % 256 else x


def head_into(x_ref, rows, head, member):
    start, offset, width = window(head)
    part = moved(widened(x_ref[rows, start : start + width].astype(F32)), member * HEAD - offset)
    return masked(part, lanes_in(256, member * HEAD, (member + 1) * HEAD))


def head_from(packed, head, member):
    start, offset, width = window(head)
    part = moved(widened(packed), offset - member * HEAD)[:, :width]
    return slice(start, start + width), masked(part, lanes_in(width, offset, offset + HEAD))


def pack(parts):
    out = sum(moved(widened(part), i * HEAD) for i, part in enumerate(parts))
    return out[:, : room_for(len(parts))]


def unpack(packed, member):
    return masked(moved(widened(packed), -member * HEAD)[:, :128], lanes_in(128, 0, HEAD))


def main_vec(meta_ref, mod_ref, block, member):
    return mod_ref[block, member, pl.ds(meta_ref[LONG], 1), :]


def extra_vec(meta_ref, mod_ref, block, member, extras, patches):
    rows = [mod_ref[block, member, pl.ds(meta_ref[CLIP + e], 1), :] for e in range(extras)]
    return jnp.concatenate([jnp.broadcast_to(r, (patches, r.shape[1])) for r in rows], axis=0)


def normed_of(x):
    average = jnp.mean(x, axis=-1, keepdims=True)
    centred = x - average
    variance = jnp.mean(centred * centred, axis=-1, keepdims=True)
    inverse = lax.rsqrt(variance + 1e-06)
    return centred * inverse, inverse


def over_rows(count, body, most=64):
    size = math.gcd(count, most)
    if count == size:
        body(slice(0, count))
        return

    def step(i, carry):
        body(pl.ds(pl.multiple_of(i * size, size), size))
        return carry

    lax.fori_loop(0, count // size, step, 0)


def modulate(x, shift, scale):
    normed, _ = normed_of(x.astype(F32))
    return (normed * (1.0 + scale) + shift).astype(BF)


def norm_back(x, grad, dmod, scale):
    normed, inverse = normed_of(x.astype(F32))
    dnormed = dmod * (1.0 + scale)
    mean_d = jnp.mean(dnormed, axis=-1, keepdims=True)
    mean_dn = jnp.mean(dnormed * normed, axis=-1, keepdims=True)
    dx = (inverse * (dnormed - mean_d - normed * mean_dn)).astype(BF)
    return (dx.astype(F32) + grad.astype(F32)).astype(BF)


def gated(x, gate, mixed):
    return (x.astype(F32) + gate * mixed).astype(BF)


def col_tiles(width):
    whole, tiles = 512, []
    start = 0
    while start < width:
        tiles.append((start, min(whole, width - start)))
        start += whole
    return tiles


def times(dest_ref, x_ref, w_ref, member, transposed=False, add=False):
    for start, size in col_tiles(w_ref.shape[-1]):
        cols = pl.ds(start, size)
        if transposed:
            product = nt(x_ref[...], w_ref[member, cols, :])
        else:
            product = nn(x_ref[...], w_ref[member, :, cols])
        if add:
            product = dest_ref[:, cols] + product
        dest_ref[:, cols] = product.astype(dest_ref.dtype)


def heads_forward(o_ref, q_ref, k_ref, v_ref, parts, bias, heads):
    for head in range(heads):
        start, offset, width = window(head)
        cols = slice(start, start + width)
        keep = lanes_in(width, offset, offset + HEAD)
        scores = [nt(masked(q_ref[rows, cols], keep), k_ref[rows, cols]) for rows in parts]
        scores = jnp.concatenate(scores, axis=0) if len(parts) > 1 else scores[0]
        if bias is not None:
            scores = scores + bias
        exponent = jnp.exp2((scores - jnp.max(scores, axis=-1, keepdims=True)) * SCALE2)
        inverse = 1.0 / jnp.sum(exponent, axis=-1, keepdims=True)
        exponent = exponent.astype(BF)
        count = exponent.shape[0] // len(parts)
        for i, rows in enumerate(parts):
            mine = slice(i * count, (i + 1) * count)
            result = nn(exponent[mine], masked(v_ref[rows, cols], keep)) * inverse[mine]
            o_ref[rows, cols] = o_ref[rows, cols] + result


def softmax_grads(q, do, k, v, bias):
    def joined(left, right):
        products = [nt(a, b) for a, b in zip(left, right)]
        return jnp.concatenate(products, axis=1) if len(products) > 1 else products[0]

    scores = joined(k, q)
    if bias is not None:
        scores = scores + bias
    exponent = jnp.exp2((scores - jnp.max(scores, axis=0, keepdims=True)) * SCALE2)
    prob = exponent * (1.0 / jnp.sum(exponent, axis=0, keepdims=True))
    dprob = joined(v, do)
    delta = jnp.sum(prob * dprob, axis=0, keepdims=True)
    dscores = prob * (dprob - delta) * SCALE
    count = scores.shape[1] // len(q)

    def split(x):
        return [x[:, i * count : (i + 1) * count] for i in range(len(q))]

    return split(dscores.astype(BF)), split(prob.astype(BF))


def heads_backward(dq_ref, dk_ref, dv_ref, q_ref, k_ref, v_ref, do_ref, parts, bias, heads):
    for head in range(heads):
        start, offset, width = window(head)
        cols = slice(start, start + width)
        keep = lanes_in(width, offset, offset + HEAD)
        q, do, k = [[masked(ref[rows, cols], keep) for rows in parts] for ref in (q_ref, do_ref, k_ref)]
        dscores, prob = softmax_grads(q, do, k, [v_ref[rows, cols] for rows in parts], bias)
        for i, rows in enumerate(parts):
            dv_ref[rows, cols] = dv_ref[rows, cols] + nn(prob[i], do[i])
            dk_ref[rows, cols] = dk_ref[rows, cols] + nn(dscores[i], q[i])
            dq_ref[rows, cols] = dq_ref[rows, cols] + tn(dscores[i], k[i])


def gather_kernel(
    lengths_ref, mask_ref, column_ref, latents_ref, cotangent_ref,
    meta_ref, main_ref, extra_ref, cot_main_ref, cot_extra_ref,
    main_in, extra_in, sems, *, sharers,
):
    clips, frame_dev, patch_dev, width = latents_ref.shape
    frames = mask_ref.shape[1]
    frame_axis = frames // frame_dev
    patch_t = patch_dev // frame_axis
    small, sub = patch_t // sharers, patch_dev // sharers
    column = column_ref[0]
    long = jnp.int32(0)
    for c in range(clips):
        long = long + jnp.where(lengths_ref[c] == frames, c, 0)
    for i in range(TABLE):
        meta_ref[i] = 0
    meta_ref[LONG] = long
    meta_ref[COLUMN] = column
    count = jnp.int32(0)
    for c in range(clips):
        for f in range(EXTRAS - clips + 2):
            used = (c != long) & (f < lengths_ref[c])
            at = jnp.where(used, count, EXTRAS)
            meta_ref[CLIP + at] = jnp.int32(c)
            meta_ref[FRAME + at] = jnp.int32(f)
            meta_ref[VALID + at] = mask_ref[c, f]
            count = count + used.astype(jnp.int32)
    for e in range(EXTRAS, 8):
        for row in (CLIP, FRAME, VALID):
            meta_ref[row + e] = 0

    copies = []
    pairs = ((latents_ref, main_ref), (cotangent_ref, main_in))
    for i, (source, main) in enumerate(pairs):
        copies.append(pltpu.make_async_copy(source.at[long], main, sems.at[i, EXTRAS]))
        copies[-1].start()
        for e in range(EXTRAS):
            frame = lax.rem(meta_ref[FRAME + e], frame_dev)
            part = source.at[meta_ref[CLIP + e], frame]
            copies.append(pltpu.make_async_copy(part, extra_in.at[i, e], sems.at[i, e]))
            copies[-1].start()

    for f in range(frames):
        meta_ref[LONG_VALID + f] = mask_ref[long, f]
    for c in range(clips):
        for f in range(frame_dev):
            frame = column * frame_dev + f
            valid = (frame < lengths_ref[c]) & (mask_ref[c, frame] == 1)
            meta_ref[KIND + c * frame_dev + f] = jnp.where(valid, jnp.where(c == long, 1, 2), 0)
    for e in range(EXTRAS):
        local_frame = meta_ref[FRAME + e] - column * frame_dev
        here = (local_frame >= 0) & (local_frame < frame_dev)
        slot = meta_ref[CLIP + e] * frame_dev + jnp.where(here, local_frame, 0)

        @pl.when(here)
        def _(e=e, slot=slot):
            meta_ref[EXTRA_AT + slot] = jnp.int32(e)

    for copy in copies:
        copy.wait()
    for f in range(frame_axis):
        own = slice(f * patch_t, (f + 1) * patch_t)
        parts = [[extra_in[i, e].astype(F32)[own] for e in range(EXTRAS)] for i in range(2)]
        main = []
        for j in range(frame_dev):
            rows = main_in[j].astype(F32)
            starts = [s * sub + f * small for s in range(sharers)]
            main += [rows[at : at + small] for at in starts]
        extra_ref[f ^ column] = jnp.concatenate(parts[0], axis=0).astype(BF)
        cot_main_ref[f ^ column] = jnp.concatenate(main, axis=0).astype(BF)
        cot_extra_ref[f ^ column] = jnp.concatenate(parts[1], axis=0).astype(BF)


def front_main_kernel(meta_ref, mod_ref, x_ref, w_ref, q_ref, kv_ref, low_ref):
    member = pl.program_id(0)

    @pl.when(member == 0)
    def _():
        shift, scale = [main_vec(meta_ref, mod_ref, 0, i) for i in range(2)]

        def body(rows):
            low_ref[rows, :] = modulate(x_ref[rows, :], shift, scale)

        over_rows(x_ref.shape[0], body)
        times(q_ref, low_ref, w_ref, 0)

    @pl.when(member > 0)
    def _():
        times(kv_ref.at[0], low_ref, w_ref, 0)


def own_extras(meta_ref, got_ref, extras, patches, frame_dev):
    rows = []
    for e in range(EXTRAS):
        source = meta_ref[COLUMN] ^ (meta_ref[FRAME + e] // frame_dev)
        at = e * patches
        rows.append(got_ref[source, at : at + patches, :].astype(F32))
    return rows + [jnp.zeros_like(rows[0])] * (extras - EXTRAS)


def front_extra_kernel(
    meta_ref, mod_ref, got_ref, w_ref, pack_ref, x_ref, low_ref, out_ref, *, patches, frame_dev
):
    member = pl.program_id(0)
    rows = x_ref.shape[0]

    @pl.when(member == 0)
    def _():
        x = own_extras(meta_ref, got_ref, rows // patches, patches, frame_dev)
        x = jnp.concatenate(x, axis=0)
        x_ref[...] = x.astype(BF)
        shift, scale = [extra_vec(meta_ref, mod_ref, 0, i, rows // patches, patches) for i in range(2)]
        low_ref[...] = modulate(x, shift, scale)

    for start, size in col_tiles(w_ref.shape[-1]):
        cols = pl.ds(start, size)
        out_ref[member, :, cols] = nn(low_ref[...], w_ref[0, :, cols])

    @pl.when(member == 2)
    def _():
        for head in range(pack_ref.shape[0]):
            pack_ref[head] = sum(head_into(out_ref.at[i], slice(None), head, i) for i in range(3)).astype(BF)


def fill_keys(k_ref, v_ref, kv_ref, other_ref):
    rows = kv_ref.shape[1]
    k_ref[:rows] = kv_ref[0]
    v_ref[:rows] = kv_ref[1]
    for i in range(other_ref.shape[0]):
        k_ref[(i + 1) * rows : (i + 2) * rows] = other_ref[i, 0]
        v_ref[(i + 1) * rows : (i + 2) * rows] = other_ref[i, 1]


def attend_kernel(q_ref, kv_ref, other_ref, o_ref, k_ref, v_ref, acc_ref, *, heads):
    fill_keys(k_ref, v_ref, kv_ref, other_ref)
    acc_ref[...] = jnp.zeros_like(acc_ref)
    heads_forward(acc_ref, q_ref, k_ref, v_ref, [slice(None)], None, heads)
    o_ref[...] = acc_ref[...].astype(BF)


def extra_rows(ref, index):
    part = ref[:, index]
    return part.reshape(part.shape[0] * part.shape[1], part.shape[2])


def extra_attend_kernel(pack_ref, main_ref, sent_ref):
    devices, count, patches, _ = pack_ref.shape
    sent_ref[:, extra_room(patches, count) :, :] = main_ref[...]
    results = []
    for index in range(count):
        packed = extra_rows(pack_ref, index).astype(F32)
        q, k, v = [unpack(packed, i).astype(BF) for i in range(3)]
        scores = nt(q, k)
        exponent = jnp.exp2((scores - jnp.max(scores, axis=-1, keepdims=True)) * SCALE2)
        total = jnp.sum(exponent, axis=-1, keepdims=True)
        results.append(nn(exponent.astype(BF), v) * (1.0 / total))
    packed = pack(results)
    for i in range(packed.shape[1] // 128):
        piece = packed[:, i * 128 : (i + 1) * 128].reshape(devices, patches, 128)
        sent_ref[:, i * patches : (i + 1) * patches, :] = piece.astype(BF)


def extra_attend_back_kernel(pack_ref, got_ref, grad_ref):
    devices, _, patches, _ = pack_ref.shape
    got = got_ref[...].astype(F32).reshape(devices * patches, got_ref.shape[2])
    for index in range(pack_ref.shape[1]):
        packed = extra_rows(pack_ref, index).astype(F32)
        q, k, v = [unpack(packed, i).astype(BF) for i in range(3)]
        do = unpack(got, index).astype(BF)
        (dscores,), (prob,) = softmax_grads([q], [do], [k], [v], None)
        out = pack([tn(dscores, k), nn(dscores, q), nn(prob, do)]).astype(BF)
        grad_ref[:, index] = out.reshape(devices, patches, 256)


def extra_room(patches, count):
    return -(-patches * (room_for(count) // 128) // 16) * 16


def write_chunk(sent_ref, dest, value):
    pieces = [value[:, at : at + 128] for at in range(0, value.shape[1], 128)]
    sent_ref[dest] = jnp.concatenate(pieces, axis=0).astype(BF)


def read_chunk(got_ref, source, out_ref, row, small, room=0):
    count = out_ref.shape[1] // 128
    value = got_ref[source, room : room + count * small, :].astype(F32)
    for i in range(count):
        out_ref[row : row + small, i * 128 : (i + 1) * 128] = value[i * small : (i + 1) * small]


def back_main_kernel(meta_ref, mod_ref, x_ref, o_ref, w_ref, sent_ref, acc_ref, *, columns):
    times(acc_ref, o_ref, w_ref, 0)
    gate = main_vec(meta_ref, mod_ref, 0, 2)

    def body(rows):
        acc_ref[rows, :] = x_ref[rows, :].astype(F32) + gate * acc_ref[rows, :]

    over_rows(x_ref.shape[0], body)
    devices = sent_ref.shape[0]
    small = x_ref.shape[0] // devices
    patch_axis = devices // columns
    for p in range(patch_axis):
        for f in range(columns):
            row = (p * columns + f) * small
            write_chunk(sent_ref, f * patch_axis + p, acc_ref[row : row + small, :])


def back_grad_main_kernel(meta_ref, mod_ref, got_ref, w_ref, do_ref, g_ref, low_ref, acc_ref, *, columns):
    devices = got_ref.shape[0]
    small = g_ref.shape[0] // devices
    patch_axis = devices // columns
    for p in range(patch_axis):
        for f in range(columns):
            row = (p * columns + f) * small
            read_chunk(got_ref, f * patch_axis + p, acc_ref, row, small)
    gate = main_vec(meta_ref, mod_ref, 0, 2)

    def body(rows):
        g_ref[rows, :] = acc_ref[rows, :].astype(BF)
        low_ref[rows, :] = (gate * acc_ref[rows, :]).astype(BF)

    over_rows(g_ref.shape[0], body)
    times(do_ref, low_ref, w_ref, 0, transposed=True)


def attend_back_kernel(
    q_ref, kv_ref, other_ref, do_ref, own_ref, sent_ref, k_ref, v_ref, dq_ref, dk_ref, dv_ref, *, heads
):
    rows = kv_ref.shape[1]
    fill_keys(k_ref, v_ref, kv_ref, other_ref)
    for ref in (dq_ref, dk_ref, dv_ref):
        ref[...] = jnp.zeros_like(ref)
    heads_backward(dq_ref, dk_ref, dv_ref, q_ref, k_ref, v_ref, do_ref, [slice(None)], None, heads)
    own_ref[0] = dq_ref[...].astype(BF)
    own_ref[1] = dk_ref[:rows].astype(BF)
    own_ref[2] = dv_ref[:rows].astype(BF)
    for i in range(other_ref.shape[0]):
        sent_ref[i, 0] = dk_ref[(i + 1) * rows : (i + 2) * rows].astype(BF)
        sent_ref[i, 1] = dv_ref[(i + 1) * rows : (i + 2) * rows].astype(BF)


def add_product(acc_ref, d_ref, member, w_ref):
    for start, size in col_tiles(w_ref.shape[-1]):
        cols = pl.ds(start, size)
        product = nt(d_ref[member], w_ref[0, cols, :])

        @pl.when(member == 0)
        def _(cols=cols, product=product):
            acc_ref[:, cols] = product

        @pl.when(member > 0)
        def _(cols=cols, product=product):
            acc_ref[:, cols] = acc_ref[:, cols] + product


def front_grad_main_kernel(meta_ref, mod_ref, own_ref, got_ref, x_ref, g_ref, w_ref, out_ref, d_ref, acc_ref):
    member = pl.program_id(0)

    @pl.when(member == 0)
    def _():
        d_ref[0] = own_ref[0]
        for i in range(2):
            total = own_ref[1 + i].astype(F32)
            for j in range(got_ref.shape[0]):
                total = total + got_ref[j, i].astype(F32)
            d_ref[1 + i] = total.astype(BF)

    add_product(acc_ref, d_ref, member, w_ref)

    @pl.when(member == 2)
    def _():
        scale = main_vec(meta_ref, mod_ref, 0, 1)

        def body(rows):
            out_ref[rows, :] = norm_back(x_ref[rows, :], g_ref[rows, :], acc_ref[rows, :], scale)

        over_rows(x_ref.shape[0], body)


def front_grad_extra_kernel(
    meta_ref, mod_ref, pack_ref, x_ref, g_ref, w_ref, out_ref, d_ref, acc_ref, ext_ref, *, patches
):
    member = pl.program_id(0)
    rows = x_ref.shape[0]

    @pl.when(member == 0)
    def _():
        ext_ref[...] = jnp.zeros_like(ext_ref)
        for head in range(pack_ref.shape[0]):
            packed = pack_ref[head].astype(F32)
            for i in range(3):
                cols, value = head_from(packed, head, i)
                ext_ref[i, :, cols] = ext_ref[i, :, cols] + value
        d_ref[...] = ext_ref[...].astype(BF)

    add_product(acc_ref, d_ref, member, w_ref)

    @pl.when(member == 2)
    def _():
        scale = extra_vec(meta_ref, mod_ref, 0, 1, rows // patches, patches)
        out = norm_back(x_ref[...], g_ref[...], acc_ref[...], scale)
        out_ref[...] = out.astype(F32)[: out_ref.shape[0]].astype(BF)


def key_bias(meta_ref, valid_at, clip_at, tokens, count, small, keys_axis):
    part = count * small

    def spread(base, axis):
        line = (1, tokens) if axis == 1 else (tokens, 1)
        item = lax.broadcasted_iota(jnp.int32, line, axis) % part // small
        out = jnp.zeros(line, jnp.int32)
        for i in range(count):
            out = jnp.where(item == i, meta_ref[base + i], out)
        return out

    where = lax.broadcasted_iota(jnp.int32, (tokens, tokens), keys_axis)
    other = lax.broadcasted_iota(jnp.int32, (tokens, tokens), 1 - keys_axis)
    admitted = jnp.broadcast_to(spread(valid_at, keys_axis) == 1, (tokens, tokens))
    if clip_at is not None:
        admitted = admitted & (spread(clip_at, 0) == spread(clip_at, 1))
    admitted = admitted & (where % small == other % small) & (where // part == other // part)
    return jnp.where(admitted | (where == other), 0.0, -1e30).astype(F32)


def bring(w_hbm, w_ref, sems):
    copies = [pltpu.make_async_copy(w_hbm.at[i], w_ref.at[i], sems.at[i]) for i in range(4)]
    for copy in copies:
        copy.start()
    return copies


def temporal_core(vecs, w_ref, copies, parts, biases, put, most, refs, heads):
    x_ref, cot_ref, low_ref, q_ref, k_ref, v_ref, acc_ref, dq_ref, dk_ref, dv_ref = refs
    count = x_ref.shape[0]
    shift, scale, gate = vecs

    def body(rows):
        low_ref[rows, :] = modulate(x_ref[rows, :], shift, scale)

    over_rows(count, body, most)
    for i, ref in enumerate((q_ref, k_ref, v_ref)):
        copies[i].wait()
        times(ref, low_ref, w_ref, i)
    acc_ref[...] = jnp.zeros_like(acc_ref)
    heads_forward(acc_ref, q_ref, k_ref, v_ref, parts, biases(1), heads)
    low_ref[...] = acc_ref[...].astype(BF)
    copies[3].wait()
    times(acc_ref, low_ref, w_ref, 3)

    def body(rows):
        acc_ref[rows, :] = x_ref[rows, :] + gate * acc_ref[rows, :]
        low_ref[rows, :] = (gate * cot_ref[rows, :]).astype(BF)

    over_rows(count, body, most)
    put()
    times(acc_ref, low_ref, w_ref, 3, transposed=True)
    low_ref[...] = acc_ref[...].astype(BF)
    for ref in (dq_ref, dk_ref, dv_ref):
        ref[...] = jnp.zeros_like(ref)
    heads_backward(dq_ref, dk_ref, dv_ref, q_ref, k_ref, v_ref, low_ref, parts, biases(0), heads)
    for i, ref in enumerate((dq_ref, dk_ref, dv_ref)):
        low_ref[...] = ref[...].astype(BF)
        times(acc_ref, low_ref, w_ref, i, transposed=True, add=i > 0)

    def body(rows):
        acc_ref[rows, :] = norm_back(x_ref[rows, :], cot_ref[rows, :], acc_ref[rows, :], scale).astype(F32)

    over_rows(count, body, most)


def temporal_main_kernel(
    meta_ref, mod_ref, got_ref, c_ref, w_hbm, out_ref, sent_ref, w_ref, sems, *refs, heads, patches
):
    copies = bring(w_hbm, w_ref, sems)
    x_ref, cot_ref, acc_ref = refs[0], refs[1], refs[6]
    columns = c_ref.shape[0]
    main = x_ref.shape[0]
    block = main // columns
    frames, each = main // patches, block // patches
    column = meta_ref[COLUMN]
    devices = got_ref.shape[0]
    small = main // devices
    room = got_ref.shape[1] - small * (x_ref.shape[1] // 128)
    sharers = patches // small
    part = frames * small

    def token(source):
        return source % sharers * part + source // sharers * small

    for source in range(devices):
        read_chunk(got_ref, source, x_ref, token(source), small, room)
    for f in range(columns):
        values = c_ref[column ^ f].astype(F32)
        for j in range(each):
            valid = meta_ref[LONG_VALID + f * each + j] == 1
            for g in range(sharers):
                rows = pl.ds(token((f * each + j) * sharers + g), small)
                at = j * patches + g * small
                cot_ref[rows, :] = jnp.where(valid, values[at : at + small], 0.0)

    parts = [slice(g * part, (g + 1) * part) for g in range(sharers)]
    if part % 128:
        parts = [slice(0, main)]

    def biases(axis):
        bias = key_bias(meta_ref, LONG_VALID, None, main // len(parts), frames, small, axis)
        return jnp.concatenate([bias] * len(parts), axis=1 - axis)

    def put():
        for f in range(columns):
            starts = [token(f * each * sharers + i) for i in range(each * sharers)]
            pieces = [acc_ref[at : at + small, :] for at in starts]
            out_ref[column ^ f] = jnp.concatenate(pieces, axis=0).astype(BF)

    vecs = [main_vec(meta_ref, mod_ref, 1, i) for i in range(3)]
    temporal_core(vecs, w_ref, copies, parts, biases, put, 64, refs, heads)
    for dest in range(devices):
        write_chunk(sent_ref, dest, acc_ref[token(dest) : token(dest) + small, :])


def temporal_extra_kernel(
    meta_ref, mod_ref, got_ref, l_ref, c_ref, w_hbm, ws_hbm, out_ref, sent_ref, g_ref,
    ws_ref, ws_sem, w_ref, sems, *refs, heads, patches, groups, frame_dev,
):
    last_copy = pltpu.make_async_copy(ws_hbm.at[3], ws_ref, ws_sem)
    last_copy.start()
    copies = bring(w_hbm, w_ref, sems)
    x_ref, cot_ref, acc_ref = refs[0], refs[1], refs[6]
    rows = l_ref.shape[0]
    extras = rows // patches
    each = extras // groups
    devices = got_ref.shape[0]

    def vec(block, member):
        return extra_vec(meta_ref, mod_ref, block, member, extras, patches)

    acc_ref[...] = jnp.zeros_like(acc_ref)
    for source in range(devices):
        head, group = source // groups, source % groups
        pieces = got_ref[source, : patches * (room_for(each) // 128), :].astype(F32)
        pieces = [pieces[at : at + patches] for at in range(0, pieces.shape[0], patches)]
        packed = jnp.concatenate(pieces, axis=1) if len(pieces) > 1 else pieces[0]
        for e in range(each):
            at = (group * each + e) * patches
            cols, value = head_from(packed, head, e)
            acc_ref[at : at + patches, cols] = acc_ref[at : at + patches, cols] + value
    gate_s = vec(0, 2)
    last_copy.wait()
    mixed = nn(acc_ref[...].astype(BF), ws_ref[...])
    x_ref[...] = gated(l_ref[...], gate_s, mixed).astype(F32)
    values = own_extras(meta_ref, c_ref, extras, patches, frame_dev)
    for i in range(extras):
        part = slice(i * patches, (i + 1) * patches)
        cot_ref[part, :] = jnp.where(meta_ref[VALID + i] == 1, values[i], 0.0)

    def put():
        out_ref[...] = acc_ref[: out_ref.shape[0]].astype(BF)

    def biases(axis):
        return key_bias(meta_ref, VALID, CLIP, rows, extras, patches, axis)

    vecs = [vec(1, i) for i in range(3)]
    temporal_core(vecs, w_ref, copies, [slice(0, rows)], biases, put, rows, refs, heads)
    grad = acc_ref[...]
    g_ref[...] = grad.astype(BF)
    acc_ref[...] = nt((gate_s * grad).astype(BF), ws_ref[...])
    for dest in range(devices):
        head, group = dest // groups, dest % groups
        starts = [(group * each + e) * patches for e in range(each)]
        packed = sum(head_into(acc_ref, slice(at, at + patches), head, e) for e, at in enumerate(starts))
        sent_ref[dest] = packed[:, : sent_ref.shape[2]].astype(BF)


def place_kernel(meta_ref, main_ref, extra_ref, out_ref, *, sharers):
    frame_dev, patch_dev, width = main_ref.shape[-3], out_ref.shape[1], out_ref.shape[2]
    for slot in range(out_ref.shape[0]):
        kind = meta_ref[KIND + slot]

        @pl.when(kind == 0)
        def _(slot=slot):
            out_ref[slot] = jnp.zeros_like(out_ref[slot])

        @pl.when(kind == 1)
        def _(slot=slot):
            if not sharers:
                out_ref[slot] = main_ref[slot % frame_dev]
                return
            columns, patch_t = main_ref.shape[0], main_ref.shape[2]
            small = patch_t // sharers
            parts = [main_ref[meta_ref[COLUMN] ^ f, slot % frame_dev].astype(F32) for f in range(columns)]
            pieces = [p[s * small : (s + 1) * small] for s in range(sharers) for p in parts]
            out_ref[slot] = jnp.concatenate(pieces, axis=0).astype(BF)

        @pl.when(kind == 2)
        def _(slot=slot):
            e = meta_ref[EXTRA_AT + slot]
            parts = [extra_ref[meta_ref[COLUMN] ^ f, e].astype(F32) for f in range(extra_ref.shape[0])]
            out_ref[slot] = jnp.concatenate(parts, axis=0).astype(BF)


SCALARS = pl.BlockSpec(memory_space=pltpu.SMEM)
ANYWHERE = pl.BlockSpec(memory_space=pl.ANY)


def params(steps=0):
    semantics = {"dimension_semantics": ("arbitrary",) * steps} if steps else {}
    return pltpu.CompilerParams(vmem_limit_bytes=VMEM_LIMIT, **semantics)


def cost(flops, elements=0):
    return pl.CostEstimate(flops=int(flops) // 1000, bytes_accessed=int(elements) // 1000, transcendentals=0)


def whole(array):
    return pl.BlockSpec(array.shape, lambda *_: (0,) * len(array.shape))


def shape(*dims, dtype=BF):
    return jax.ShapeDtypeStruct(dims, dtype)


def weight_call(kernel, name, operands, weights, members, outs, scratch, weigh):
    width = weights.shape[-1]
    first, count = members
    return pl.pallas_call(
        kernel,
        name=name,
        grid=(count,),
        in_specs=[SCALARS]
        + [whole(a) for a in operands[1:]]
        + [pl.BlockSpec((1, width, width), lambda i: (first + i, 0, 0))],
        out_specs=[spec for spec, _ in outs],
        out_shape=[struct for _, struct in outs],
        scratch_shapes=scratch,
        compiler_params=params(1),
        cost_estimate=cost(weigh * count, 2 * width * width * count),
    )(*operands, weights)


def full(*dims):
    return whole(shape(*dims)), shape(*dims)


def gather(lengths, frame_mask, column, latents, cotangent, columns, sharers):
    _, frame_dev, patch_dev, width = latents.shape
    main = (frame_dev, patch_dev, width)
    patch_t = patch_dev // columns
    return pl.pallas_call(
        functools.partial(gather_kernel, sharers=sharers),
        name="gather",
        in_specs=[SCALARS] * 3 + [ANYWHERE] * 2,
        out_specs=[SCALARS] + [pl.BlockSpec(memory_space=pltpu.VMEM)] * 4,
        out_shape=[
            shape(TABLE, dtype=jnp.int32), shape(*main), shape(columns, EXTRAS * patch_t, width),
            shape(columns, frame_dev * patch_t, width), shape(columns, EXTRAS * patch_t, width),
        ],
        scratch_shapes=[
            pltpu.VMEM(main, BF),
            pltpu.VMEM((2, EXTRAS, patch_dev, width), BF),
            pltpu.SemaphoreType.DMA((2, EXTRAS + 1)),
        ],
        compiler_params=params(),
    )(lengths, frame_mask, column, latents, cotangent)


def front_main(meta, mod, x, weights):
    rows, width = x.shape
    kv = pl.BlockSpec((1, rows, width), lambda i: (jnp.maximum(i - 1, 0), 0, 0)), shape(2, rows, width)
    return weight_call(
        front_main_kernel, "front_main", (meta, mod, x), weights, (0, 3),
        [full(rows, width), kv], [pltpu.VMEM((rows, width), BF)], 2 * rows * width**2,
    )


def front_extra(meta, mod, got, weights, heads, patches, extras, frame_dev):
    width = got.shape[-1]
    rows = extras * patches
    return weight_call(
        functools.partial(front_extra_kernel, patches=patches, frame_dev=frame_dev), "front_extra",
        (meta, mod, got), weights, (0, 3), [full(heads, rows, 256), full(rows, width)],
        [pltpu.VMEM((rows, width), BF), pltpu.VMEM((3, rows, width), F32)], 4 * rows * width**2,
    )


def back_main(meta, mod, x, o, weights, columns, devices):
    rows, width = x.shape
    return weight_call(
        functools.partial(back_main_kernel, columns=columns), "back_main", (meta, mod, x, o), weights,
        (3, 1), [full(devices, rows * width // (devices * 128), 128)], [pltpu.VMEM((rows, width), F32)],
        3 * rows * width**2,
    )[0]


def back_grad_main(meta, mod, got, weights, rows, columns):
    width = weights.shape[-1]
    return weight_call(
        functools.partial(back_grad_main_kernel, columns=columns), "back_grad_main",
        (meta, mod, got), weights, (3, 1), [full(rows, width)] * 2,
        [pltpu.VMEM((rows, width), BF), pltpu.VMEM((rows, width), F32)], 3 * rows * width**2,
    )


def front_grad_main(meta, mod, own, got, x, g, weights):
    rows, width = x.shape
    return weight_call(
        front_grad_main_kernel, "front_grad_main", (meta, mod, own, got, x, g), weights, (0, 3),
        [full(rows, width)], [pltpu.VMEM((3, rows, width), BF), pltpu.VMEM((rows, width), F32)],
        3 * rows * width**2,
    )[0]


def front_grad_extra(meta, mod, pack, x, g, weights, patches):
    rows, width = x.shape
    return weight_call(
        functools.partial(front_grad_extra_kernel, patches=patches), "front_grad_extra",
        (meta, mod, pack, x, g), weights, (0, 3), [full(EXTRAS * patches, width)],
        [pltpu.VMEM((3, rows, width), BF), pltpu.VMEM((rows, width), F32), pltpu.VMEM((3, rows, width), F32)],
        4 * rows * width**2,
    )[0]


def attend(q, kv, other, heads):
    rows, width = q.shape
    keys = rows * (other.shape[0] + 1)
    return pl.pallas_call(
        functools.partial(attend_kernel, heads=heads),
        name="attend",
        out_shape=shape(rows, width),
        scratch_shapes=[
            pltpu.VMEM((keys, width), BF),
            pltpu.VMEM((keys, width), BF),
            pltpu.VMEM((rows, width), F32),
        ],
        compiler_params=params(),
        cost_estimate=cost(6e9),
    )(q, kv, other)


def extra_attend(packed, main):
    devices, count, patches, _ = packed.shape
    return pl.pallas_call(
        extra_attend_kernel, name="extra_attend",
        out_shape=shape(devices, extra_room(patches, count) + main.shape[1], 128),
        compiler_params=params(), cost_estimate=cost(4e9),
    )(packed, main)


def extra_attend_back(packed, got):
    return pl.pallas_call(
        extra_attend_back_kernel, name="extra_attend_back", out_shape=shape(*packed.shape),
        compiler_params=params(), cost_estimate=cost(6e9),
    )(packed, got)


def attend_back(q, kv, other, do, heads):
    rows, width = q.shape
    keys = rows * (other.shape[0] + 1)
    return pl.pallas_call(
        functools.partial(attend_back_kernel, heads=heads),
        name="attend_back",
        out_shape=[shape(3, rows, width), shape(*other.shape)],
        scratch_shapes=[
            pltpu.VMEM((keys, width), BF),
            pltpu.VMEM((keys, width), BF),
            pltpu.VMEM((rows, width), F32),
            pltpu.VMEM((keys, width), F32),
            pltpu.VMEM((keys, width), F32),
        ],
        compiler_params=params(),
        cost_estimate=cost(14e9),
    )(q, kv, other, do)


def temporal_scratch(rows, width):
    high, low = pltpu.VMEM((rows, width), F32), pltpu.VMEM((rows, width), BF)
    weights = [pltpu.VMEM((4, width, width), BF), pltpu.SemaphoreType.DMA((4,))]
    return weights + [high] * 2 + [low] * 4 + [high] * 4


def temporal_main(meta, mod, got, cot, weights, heads, patches, block):
    columns, _, width = cot.shape
    devices = got.shape[0]
    operands = (mod, got, cot)
    sent = shape(devices, columns * block * width // (devices * 128), 128)
    return pl.pallas_call(
        functools.partial(temporal_main_kernel, heads=heads, patches=patches),
        name="temporal_main",
        in_specs=[SCALARS] + [whole(a) for a in operands] + [ANYWHERE],
        out_shape=[shape(columns, block, width), sent],
        scratch_shapes=temporal_scratch(columns * block, width),
        compiler_params=params(),
        cost_estimate=cost(25e9),
    )(meta, *operands, weights)


def temporal_extra(meta, mod, got, le, cot, weights, spatial_weights, heads, patches, groups, frame_dev):
    operands = (mod, got, le, cot)
    rows, width = le.shape
    sent = shape(got.shape[0], patches, room_for(rows // (patches * groups)))
    return pl.pallas_call(
        functools.partial(
            temporal_extra_kernel, heads=heads, patches=patches, groups=groups, frame_dev=frame_dev
        ),
        name="temporal_extra",
        in_specs=[SCALARS] + [whole(a) for a in operands] + [ANYWHERE] * 2,
        out_shape=[shape(EXTRAS * patches, width), sent, shape(*le.shape)],
        scratch_shapes=[pltpu.VMEM((width, width), BF), pltpu.SemaphoreType.DMA]
        + temporal_scratch(rows, width),
        compiler_params=params(),
        cost_estimate=cost(14e9),
    )(meta, *operands, weights, spatial_weights)


def place(meta, main, extra, slots, sharers):
    return pl.pallas_call(
        functools.partial(place_kernel, sharers=sharers),
        name="place",
        in_specs=[SCALARS, whole(main), whole(extra)],
        out_shape=shape(slots, extra.shape[0] * extra.shape[2], extra.shape[3]),
        compiler_params=params(),
        cost_estimate=cost(3e9),
    )(meta, main, extra)


def local(latents, cotangent, spatial_weights, temporal_weights, modulation, lengths, frame_mask):
    clips, frame_dev, patch_dev, width = latents.shape
    heads = width // HEAD
    frame_axis, patch_axis = lax.axis_size("frame"), lax.axis_size("patch")
    everyone = ("frame", "patch")
    frames = frame_dev * frame_axis
    sharers = patch_axis // frame_dev
    sub = patch_dev // sharers
    small = sub // frame_axis
    patch_t = patch_dev // frame_axis
    heads_col = heads // frame_axis
    groups = patch_axis // heads_col
    group_extras = -(-EXTRAS // groups)
    extras = groups * group_extras

    def swap(x, axis):
        return lax.all_to_all(x, axis, split_axis=0, concat_axis=0, tiled=True)

    column = lax.axis_index("frame")
    main_rows = frame_dev * patch_dev

    def cross(blocks):
        got = [blocks[0]]
        for m in range(1, frame_axis):
            got.append(lax.ppermute(blocks[m], "frame", [(f, f ^ m) for f in range(frame_axis)]))
        return jnp.stack(got)

    def parts_home(x):
        return cross([x] * frame_axis).reshape(frame_axis, EXTRAS, patch_t, width)

    meta, main_home, extra_home, cot_main, cot_extra = gather(
        lengths, frame_mask, column.reshape(1).astype(jnp.int32), latents, cotangent, frame_axis, sharers
    )
    extra_got = cross(extra_home)
    main_s = swap(main_home.reshape(patch_axis, sub, width), "patch").reshape(main_rows, width)
    extra_got, cot_main, cot_extra = lax.optimization_barrier((extra_got, cot_main, cot_extra))
    cot_m, cot_e = cross(cot_main), cross(cot_extra)

    def rotate(array, by):
        perm = []
        for p in range(patch_axis):
            base = p // sharers * sharers
            perm.append((p, base + (p - base + by) % sharers))
        return lax.ppermute(array, "patch", perm)

    mod = modulation
    chunk = group_extras * patch_t
    packed, extra_t = front_extra(
        meta, mod, extra_got, spatial_weights, heads, patch_t, extras, frame_dev
    )
    packed, main_s = lax.optimization_barrier((packed, main_s))
    pack_got = swap(packed.reshape(frame_axis * patch_axis, chunk, 256), everyone)
    pack_got = pack_got.reshape(frame_axis * patch_axis, group_extras, patch_t, 256)
    q, kv = front_main(meta, mod, main_s, spatial_weights)
    other = jnp.stack([rotate(kv, by) for by in range(1, sharers)])
    attended = attend(q, kv, other, heads)
    sent = back_main(meta, mod, main_s, attended, spatial_weights, frame_axis, frame_axis * patch_axis)
    sent, pack_got = lax.optimization_barrier((sent, pack_got))
    sent = extra_attend(pack_got, sent)

    got, cot_m = lax.optimization_barrier((swap(sent, everyone), cot_m))
    out_m, sent = temporal_main(
        meta, mod, got, cot_m, temporal_weights, heads, patch_t, frame_dev * patch_t
    )
    got, _ = lax.optimization_barrier((got, out_m))
    out_e, sent_e, grad_e = temporal_extra(
        meta, mod, got, extra_t, cot_e, temporal_weights, spatial_weights, heads, patch_t, groups, frame_dev
    )

    grads, sent_e = lax.optimization_barrier((swap(sent, everyone), sent_e))
    do_main, grad_s = back_grad_main(meta, mod, grads, spatial_weights, main_rows, frame_axis)
    dpack = extra_attend_back(pack_got, swap(sent_e, everyone))
    out_main, out_extra = cross(out_m), parts_home(out_e)
    do_main, dpack, out_main, out_extra = lax.optimization_barrier((do_main, dpack, out_main, out_extra))
    own, sent = attend_back(q, kv, other, do_main, heads)
    got = jnp.stack([rotate(sent[by - 1], -by) for by in range(1, sharers)])
    dpack = swap(dpack.reshape(frame_axis * patch_axis, chunk, 256), everyone)
    dpack = dpack.reshape(heads, extras * patch_t, 256)
    lat_m = front_grad_main(meta, mod, own, got, main_s, grad_s, spatial_weights)
    dpack, _ = lax.optimization_barrier((dpack, own))
    lat_e = front_grad_extra(meta, mod, dpack, extra_t, grad_e, spatial_weights, patch_t)
    lat_main = swap(lat_m.reshape(patch_axis, sub, width), "patch").reshape(frame_dev, patch_dev, width)

    out_main = out_main.reshape(frame_axis, frame_dev, patch_t, width)
    slots = clips * frame_dev
    output = place(meta, out_main, out_extra, slots, sharers)
    grad = place(meta, lat_main, parts_home(lat_e), slots, 0)
    return output.reshape(latents.shape), grad.reshape(latents.shape)


def solution(mesh):
    tokens = P(None, "frame", "patch", None)
    in_specs = (tokens, tokens, P(), P(), P(), P(), P())
    return jax.shard_map(local, mesh=mesh, in_specs=in_specs, out_specs=(tokens, tokens), check_vma=False)
```

```python
import functools
import math

import jax
import jax.numpy as jnp
from jax import lax
from jax.experimental import pallas as pl
from jax.experimental.pallas import tpu as pltpu
from jax.sharding import PartitionSpec as P

HEAD = 72
EXTRAS = 5
SCALE = HEAD ** -0.5
SCALE2 = SCALE * math.log2(math.e)
BF = jnp.bfloat16
F32 = jnp.float32
VMEM_LIMIT = 56 * 1024 * 1024
LONG, COLUMN, CLIP, FRAME, VALID, LONG_VALID, KIND, EXTRA_AT, TABLE = 0, 1, 8, 16, 24, 32, 48, 64, 80


def nn(a, b):
    return lax.dot_general(a, b, (((1,), (0,)), ((), ())), preferred_element_type=F32)


def nt(a, b):
    return lax.dot_general(a, b, (((1,), (1,)), ((), ())), preferred_element_type=F32)


def tn(a, b):
    return lax.dot_general(a, b, (((0,), (0,)), ((), ())), preferred_element_type=F32)


def window(head):
    start = head * HEAD // 128 * 128
    offset = head * HEAD - start
    return start, offset, 128 if offset + HEAD <= 128 else 256


def lanes_in(width, low, high):
    lane = lax.broadcasted_iota(jnp.int32, (1, width), 1)
    return (lane >= low) & (lane < high)


def masked(x, keep):
    return jnp.where(keep, x, jnp.zeros((), x.dtype))


def room_for(count):
    return -(-count * HEAD // 128) * 128


def widened(x):
    return x if x.shape[1] == 256 else jnp.concatenate([x, jnp.zeros_like(x)], axis=1)


def moved(x, lanes):
    return pltpu.roll(x, lanes % 256, 1) if lanes % 256 else x


def head_into(x_ref, rows, head, member):
    start, offset, width = window(head)
    part = moved(widened(x_ref[rows, start : start + width].astype(F32)), member * HEAD - offset)
    return masked(part, lanes_in(256, member * HEAD, (member + 1) * HEAD))


def head_from(packed, head, member):
    start, offset, width = window(head)
    part = moved(widened(packed), offset - member * HEAD)[:, :width]
    return slice(start, start + width), masked(part, lanes_in(width, offset, offset + HEAD))


def pack(parts):
    out = sum(moved(widened(part), i * HEAD) for i, part in enumerate(parts))
    return out[:, : room_for(len(parts))]


def unpack(packed, member):
    return masked(moved(widened(packed), -member * HEAD)[:, :128], lanes_in(128, 0, HEAD))


def main_vec(meta_ref, mod_ref, block, member):
    return mod_ref[block, member, pl.ds(meta_ref[LONG], 1), :]


def extra_vec(meta_ref, mod_ref, block, member, extras, patches):
    rows = [mod_ref[block, member, pl.ds(meta_ref[CLIP + e], 1), :] for e in range(extras)]
    return jnp.concatenate([jnp.broadcast_to(r, (patches, r.shape[1])) for r in rows], axis=0)


def normed_of(x):
    average = jnp.mean(x, axis=-1, keepdims=True)
    centred = x - average
    variance = jnp.mean(centred * centred, axis=-1, keepdims=True)
    inverse = lax.rsqrt(variance + 1e-06)
    return centred * inverse, inverse


def over_rows(count, body, most=64):
    size = math.gcd(count, most)
    if count == size:
        body(slice(0, count))
        return

    def step(i, carry):
        body(pl.ds(pl.multiple_of(i * size, size), size))
        return carry

    lax.fori_loop(0, count // size, step, 0)


def modulate(x, shift, scale):
    normed, _ = normed_of(x.astype(F32))
    return (normed * (1.0 + scale) + shift).astype(BF)


def norm_back(x, grad, dmod, scale):
    normed, inverse = normed_of(x.astype(F32))
    dnormed = dmod * (1.0 + scale)
    mean_d = jnp.mean(dnormed, axis=-1, keepdims=True)
    mean_dn = jnp.mean(dnormed * normed, axis=-1, keepdims=True)
    dx = (inverse * (dnormed - mean_d - normed * mean_dn)).astype(BF)
    return (dx.astype(F32) + grad.astype(F32)).astype(BF)


def gated(x, gate, mixed):
    return (x.astype(F32) + gate * mixed).astype(BF)


def col_tiles(width):
    whole, tiles = 512, []
    start = 0
    while start < width:
        tiles.append((start, min(whole, width - start)))
        start += whole
    return tiles


def times(dest_ref, x_ref, w_ref, member, transposed=False, add=False):
    for start, size in col_tiles(w_ref.shape[-1]):
        cols = pl.ds(start, size)
        if transposed:
            product = nt(x_ref[...], w_ref[member, cols, :])
        else:
            product = nn(x_ref[...], w_ref[member, :, cols])
        if add:
            product = dest_ref[:, cols] + product
        dest_ref[:, cols] = product.astype(dest_ref.dtype)


def heads_forward(o_ref, q_ref, k_ref, v_ref, parts, bias, heads):
    for head in range(heads):
        start, offset, width = window(head)
        cols = slice(start, start + width)
        keep = lanes_in(width, offset, offset + HEAD)
        scores = [nt(masked(q_ref[rows, cols], keep), k_ref[rows, cols]) for rows in parts]
        scores = jnp.concatenate(scores, axis=0) if len(parts) > 1 else scores[0]
        if bias is not None:
            scores = scores + bias
        exponent = jnp.exp2((scores - jnp.max(scores, axis=-1, keepdims=True)) * SCALE2)
        inverse = 1.0 / jnp.sum(exponent, axis=-1, keepdims=True)
        exponent = exponent.astype(BF)
        count = exponent.shape[0] // len(parts)
        for i, rows in enumerate(parts):
            mine = slice(i * count, (i + 1) * count)
            result = nn(exponent[mine], masked(v_ref[rows, cols], keep)) * inverse[mine]
            o_ref[rows, cols] = o_ref[rows, cols] + result


def softmax_grads(q, do, k, v, bias):
    def joined(left, right):
        products = [nt(a, b) for a, b in zip(left, right)]
        return jnp.concatenate(products, axis=1) if len(products) > 1 else products[0]

    scores = joined(k, q)
    if bias is not None:
        scores = scores + bias
    exponent = jnp.exp2((scores - jnp.max(scores, axis=0, keepdims=True)) * SCALE2)
    prob = exponent * (1.0 / jnp.sum(exponent, axis=0, keepdims=True))
    dprob = joined(v, do)
    delta = jnp.sum(prob * dprob, axis=0, keepdims=True)
    dscores = prob * (dprob - delta)
    count = scores.shape[1] // len(q)

    def split(x):
        return [x[:, i * count : (i + 1) * count] for i in range(len(q))]

    return split(dscores.astype(BF)), split(prob.astype(BF))


def heads_backward(dq_ref, dk_ref, dv_ref, q_ref, k_ref, v_ref, do_ref, parts, bias, heads):
    for head in range(heads):
        start, offset, width = window(head)
        cols = slice(start, start + width)
        keep = lanes_in(width, offset, offset + HEAD)
        q, do, k = [[masked(ref[rows, cols], keep) for rows in parts] for ref in (q_ref, do_ref, k_ref)]
        dscores, prob = softmax_grads(q, do, k, [v_ref[rows, cols] for rows in parts], bias)
        for i, rows in enumerate(parts):
            dv_ref[rows, cols] = dv_ref[rows, cols] + nn(prob[i], do[i])
            dk_ref[rows, cols] = dk_ref[rows, cols] + nn(dscores[i], q[i])
            dq_ref[rows, cols] = dq_ref[rows, cols] + tn(dscores[i], k[i])


def gather_kernel(
    lengths_ref, mask_ref, column_ref, latents_ref, cotangent_ref,
    meta_ref, main_ref, extra_ref, cot_ref,
    main_in, extra_in, sems, *, sharers,
):
    clips, frame_dev, patch_dev, width = latents_ref.shape
    frames = mask_ref.shape[1]
    frame_axis = frames // frame_dev
    patch_t = patch_dev // frame_axis
    small, sub = patch_t // sharers, patch_dev // sharers
    column = column_ref[0]
    long = jnp.int32(0)
    for c in range(clips):
        long = long + jnp.where(lengths_ref[c] == frames, c, 0)
    for i in range(TABLE):
        meta_ref[i] = 0
    meta_ref[LONG] = long
    meta_ref[COLUMN] = column
    count = jnp.int32(0)
    for c in range(clips):
        for f in range(EXTRAS - clips + 2):
            used = (c != long) & (f < lengths_ref[c])
            at = jnp.where(used, count, EXTRAS)
            meta_ref[CLIP + at] = jnp.int32(c)
            meta_ref[FRAME + at] = jnp.int32(f)
            meta_ref[VALID + at] = mask_ref[c, f]
            count = count + used.astype(jnp.int32)
    for e in range(EXTRAS, 8):
        for row in (CLIP, FRAME, VALID):
            meta_ref[row + e] = 0

    copies = []
    pairs = ((latents_ref, main_ref), (cotangent_ref, main_in))
    for i, (source, main) in enumerate(pairs):
        copies.append(pltpu.make_async_copy(source.at[long], main, sems.at[i, EXTRAS]))
        copies[-1].start()
        for e in range(EXTRAS):
            frame = lax.rem(meta_ref[FRAME + e], frame_dev)
            part = source.at[meta_ref[CLIP + e], frame]
            copies.append(pltpu.make_async_copy(part, extra_in.at[i, e], sems.at[i, e]))
            copies[-1].start()

    for f in range(frames):
        meta_ref[LONG_VALID + f] = mask_ref[long, f]
    for c in range(clips):
        for f in range(frame_dev):
            frame = column * frame_dev + f
            valid = (frame < lengths_ref[c]) & (mask_ref[c, frame] == 1)
            meta_ref[KIND + c * frame_dev + f] = jnp.where(valid, jnp.where(c == long, 1, 2), 0)
    for e in range(EXTRAS):
        local_frame = meta_ref[FRAME + e] - column * frame_dev
        here = (local_frame >= 0) & (local_frame < frame_dev)
        slot = meta_ref[CLIP + e] * frame_dev + jnp.where(here, local_frame, 0)

        @pl.when(here)
        def _(e=e, slot=slot):
            meta_ref[EXTRA_AT + slot] = jnp.int32(e)

    for copy in copies:
        copy.wait()
    for f in range(frame_axis):
        own = slice(f * patch_t, (f + 1) * patch_t)
        parts = [[extra_in[i, e].astype(F32)[own] for e in range(EXTRAS)] for i in range(2)]
        main = []
        for j in range(frame_dev):
            rows = main_in[j].astype(F32)
            starts = [s * sub + f * small for s in range(sharers)]
            main += [rows[at : at + small] for at in starts]
        extra_ref[f ^ column] = jnp.concatenate(parts[0], axis=0).astype(BF)
        cot_ref[f ^ column] = jnp.concatenate(main + parts[1], axis=0).astype(BF)


def front_main_kernel(meta_ref, mod_ref, x_ref, w_ref, q_ref, kv_ref, low_ref):
    member = pl.program_id(0)

    @pl.when(member == 0)
    def _():
        shift, scale = [main_vec(meta_ref, mod_ref, 0, i) for i in range(2)]

        def body(rows):
            low_ref[rows, :] = modulate(x_ref[rows, :], shift, scale)

        over_rows(x_ref.shape[0], body)
        times(q_ref, low_ref, w_ref, 0)

    @pl.when(member > 0)
    def _():
        times(kv_ref.at[0], low_ref, w_ref, 0)


def own_extras(meta_ref, got_ref, first, extras, patches, frame_dev):
    rows = []
    for e in range(EXTRAS):
        source = meta_ref[COLUMN] ^ (meta_ref[FRAME + e] // frame_dev)
        at = first + e * patches
        rows.append(got_ref[source, at : at + patches, :].astype(F32))
    return rows + [jnp.zeros_like(rows[0])] * (extras - EXTRAS)


def front_extra_kernel(
    meta_ref, mod_ref, got_ref, w_ref, pack_ref, x_ref, low_ref, out_ref, *, patches, frame_dev
):
    member = pl.program_id(0)
    rows = x_ref.shape[0]

    @pl.when(member == 0)
    def _():
        x = own_extras(meta_ref, got_ref, 0, rows // patches, patches, frame_dev)
        x = jnp.concatenate(x, axis=0)
        x_ref[...] = x.astype(BF)
        shift, scale = [extra_vec(meta_ref, mod_ref, 0, i, rows // patches, patches) for i in range(2)]
        low_ref[...] = modulate(x, shift, scale)

    for start, size in col_tiles(w_ref.shape[-1]):
        cols = pl.ds(start, size)
        out_ref[member, :, cols] = nn(low_ref[...], w_ref[0, :, cols])

    @pl.when(member == 2)
    def _():
        for head in range(pack_ref.shape[0]):
            pack_ref[head] = sum(head_into(out_ref.at[i], slice(None), head, i) for i in range(3)).astype(BF)


def fill_keys(k_ref, v_ref, kv_ref, other_ref):
    rows = kv_ref.shape[1]
    k_ref[:rows] = kv_ref[0]
    v_ref[:rows] = kv_ref[1]
    for i in range(other_ref.shape[0]):
        k_ref[(i + 1) * rows : (i + 2) * rows] = other_ref[i, 0]
        v_ref[(i + 1) * rows : (i + 2) * rows] = other_ref[i, 1]


def attend_kernel(q_ref, kv_ref, other_ref, o_ref, k_ref, v_ref, acc_ref, *, heads):
    fill_keys(k_ref, v_ref, kv_ref, other_ref)
    acc_ref[...] = jnp.zeros_like(acc_ref)
    heads_forward(acc_ref, q_ref, k_ref, v_ref, [slice(None)], None, heads)
    o_ref[...] = acc_ref[...].astype(BF)


def extra_rows(ref, index):
    part = ref[:, index]
    return part.reshape(part.shape[0] * part.shape[1], part.shape[2])


def extra_attend_kernel(pack_ref, main_ref, sent_ref):
    devices, count, patches, _ = pack_ref.shape
    sent_ref[:, extra_room(patches, count) :, :] = main_ref[...]
    results = []
    for index in range(count):
        packed = extra_rows(pack_ref, index).astype(F32)
        q, k, v = [unpack(packed, i).astype(BF) for i in range(3)]
        scores = nt(q, k)
        exponent = jnp.exp2((scores - jnp.max(scores, axis=-1, keepdims=True)) * SCALE2)
        total = jnp.sum(exponent, axis=-1, keepdims=True)
        results.append(nn(exponent.astype(BF), v) * (1.0 / total))
    packed = pack(results)
    for i in range(packed.shape[1] // 128):
        piece = packed[:, i * 128 : (i + 1) * 128].reshape(devices, patches, 128)
        sent_ref[:, i * patches : (i + 1) * patches, :] = piece.astype(BF)


def extra_attend_back_kernel(pack_ref, got_ref, grad_ref):
    devices, _, patches, _ = pack_ref.shape
    got = got_ref[...].astype(F32).reshape(devices * patches, got_ref.shape[2])
    for index in range(pack_ref.shape[1]):
        packed = extra_rows(pack_ref, index).astype(F32)
        q, k, v = [unpack(packed, i).astype(BF) for i in range(3)]
        do = unpack(got, index).astype(BF)
        (dscores,), (prob,) = softmax_grads([q], [do], [k], [v], None)
        out = pack([tn(dscores, k) * SCALE, nn(dscores, q) * SCALE, nn(prob, do)]).astype(BF)
        grad_ref[:, index] = out.reshape(devices, patches, 256)


def extra_room(patches, count):
    return -(-patches * (room_for(count) // 128) // 16) * 16


def write_chunk(sent_ref, dest, value):
    pieces = [value[:, at : at + 128] for at in range(0, value.shape[1], 128)]
    sent_ref[dest] = jnp.concatenate(pieces, axis=0).astype(BF)


def read_chunk(got_ref, source, out_ref, row, small, room=0):
    count = out_ref.shape[1] // 128
    value = got_ref[source, room : room + count * small, :].astype(F32)
    for i in range(count):
        out_ref[row : row + small, i * 128 : (i + 1) * 128] = value[i * small : (i + 1) * small]


def back_main_kernel(meta_ref, mod_ref, x_ref, o_ref, w_ref, sent_ref, acc_ref, *, columns):
    times(acc_ref, o_ref, w_ref, 0)
    gate = main_vec(meta_ref, mod_ref, 0, 2)

    def body(rows):
        acc_ref[rows, :] = x_ref[rows, :].astype(F32) + gate * acc_ref[rows, :]

    over_rows(x_ref.shape[0], body)
    devices = sent_ref.shape[0]
    small = x_ref.shape[0] // devices
    patch_axis = devices // columns
    for p in range(patch_axis):
        for f in range(columns):
            row = (p * columns + f) * small
            write_chunk(sent_ref, f * patch_axis + p, acc_ref[row : row + small, :])


def back_grad_main_kernel(meta_ref, mod_ref, got_ref, w_ref, do_ref, g_ref, low_ref, acc_ref, *, columns):
    devices = got_ref.shape[0]
    small = g_ref.shape[0] // devices
    patch_axis = devices // columns
    for p in range(patch_axis):
        for f in range(columns):
            row = (p * columns + f) * small
            read_chunk(got_ref, f * patch_axis + p, acc_ref, row, small)
    gate = main_vec(meta_ref, mod_ref, 0, 2)

    def body(rows):
        g_ref[rows, :] = acc_ref[rows, :].astype(BF)
        low_ref[rows, :] = (gate * acc_ref[rows, :]).astype(BF)

    over_rows(g_ref.shape[0], body)
    times(do_ref, low_ref, w_ref, 0, transposed=True)


def attend_back_kernel(
    q_ref, kv_ref, other_ref, do_ref, own_ref, sent_ref, k_ref, v_ref, dq_ref, dk_ref, dv_ref, *, heads
):
    rows = kv_ref.shape[1]
    fill_keys(k_ref, v_ref, kv_ref, other_ref)
    for ref in (dq_ref, dk_ref, dv_ref):
        ref[...] = jnp.zeros_like(ref)
    heads_backward(dq_ref, dk_ref, dv_ref, q_ref, k_ref, v_ref, do_ref, [slice(None)], None, heads)
    own_ref[0] = (dq_ref[...] * SCALE).astype(BF)
    own_ref[1] = (dk_ref[:rows] * SCALE).astype(BF)
    own_ref[2] = dv_ref[:rows].astype(BF)
    for i in range(other_ref.shape[0]):
        sent_ref[i, 0] = (dk_ref[(i + 1) * rows : (i + 2) * rows] * SCALE).astype(BF)
        sent_ref[i, 1] = dv_ref[(i + 1) * rows : (i + 2) * rows].astype(BF)


def add_product(acc_ref, d_ref, member, w_ref):
    for start, size in col_tiles(w_ref.shape[-1]):
        cols = pl.ds(start, size)
        product = nt(d_ref[member], w_ref[0, cols, :])

        @pl.when(member == 0)
        def _(cols=cols, product=product):
            acc_ref[:, cols] = product

        @pl.when(member > 0)
        def _(cols=cols, product=product):
            acc_ref[:, cols] = acc_ref[:, cols] + product


def front_grad_main_kernel(meta_ref, mod_ref, own_ref, got_ref, x_ref, g_ref, w_ref, out_ref, d_ref, acc_ref):
    member = pl.program_id(0)

    @pl.when(member == 0)
    def _():
        d_ref[0] = own_ref[0]
        for i in range(2):
            total = own_ref[1 + i].astype(F32)
            for j in range(got_ref.shape[0]):
                total = total + got_ref[j, i].astype(F32)
            d_ref[1 + i] = total.astype(BF)

    add_product(acc_ref, d_ref, member, w_ref)

    @pl.when(member == 2)
    def _():
        scale = main_vec(meta_ref, mod_ref, 0, 1)

        def body(rows):
            out_ref[rows, :] = norm_back(x_ref[rows, :], g_ref[rows, :], acc_ref[rows, :], scale)

        over_rows(x_ref.shape[0], body)


def front_grad_extra_kernel(
    meta_ref, mod_ref, pack_ref, x_ref, g_ref, w_ref, out_ref, d_ref, acc_ref, ext_ref, *, patches
):
    member = pl.program_id(0)
    rows = x_ref.shape[0]

    @pl.when(member == 0)
    def _():
        ext_ref[...] = jnp.zeros_like(ext_ref)
        for head in range(pack_ref.shape[0]):
            packed = pack_ref[head].astype(F32)
            for i in range(3):
                cols, value = head_from(packed, head, i)
                ext_ref[i, :, cols] = ext_ref[i, :, cols] + value
        d_ref[...] = ext_ref[...].astype(BF)

    add_product(acc_ref, d_ref, member, w_ref)

    @pl.when(member == 2)
    def _():
        scale = extra_vec(meta_ref, mod_ref, 0, 1, rows // patches, patches)
        out = norm_back(x_ref[...], g_ref[...], acc_ref[...], scale)
        out_ref[...] = out.astype(F32)[: out_ref.shape[0]].astype(BF)


def key_bias(meta_ref, valid_at, clip_at, tokens, count, small, keys_axis):
    part = count * small

    def spread(base, axis):
        line = (1, tokens) if axis == 1 else (tokens, 1)
        item = lax.broadcasted_iota(jnp.int32, line, axis) % part // small
        out = jnp.zeros(line, jnp.int32)
        for i in range(count):
            out = jnp.where(item == i, meta_ref[base + i], out)
        return out

    where = lax.broadcasted_iota(jnp.int32, (tokens, tokens), keys_axis)
    other = lax.broadcasted_iota(jnp.int32, (tokens, tokens), 1 - keys_axis)
    admitted = jnp.broadcast_to(spread(valid_at, keys_axis) == 1, (tokens, tokens))
    if clip_at is not None:
        admitted = admitted & (spread(clip_at, 0) == spread(clip_at, 1))
    admitted = admitted & (where % small == other % small) & (where // part == other // part)
    return jnp.where(admitted | (where == other), 0.0, -1e30).astype(F32)


def bring(w_hbm, w_ref, sems):
    copies = [pltpu.make_async_copy(w_hbm.at[i], w_ref.at[i], sems.at[i]) for i in range(4)]
    for copy in copies:
        copy.start()
    return copies


def temporal_core(vecs, w_ref, copies, parts, biases, put, most, refs, heads):
    x_ref, cot_ref, low_ref, q_ref, k_ref, v_ref, acc_ref, dq_ref, dk_ref, dv_ref = refs
    count = x_ref.shape[0]
    shift, scale, gate = vecs

    def body(rows):
        low_ref[rows, :] = modulate(x_ref[rows, :], shift, scale)

    over_rows(count, body, most)
    for i, ref in enumerate((q_ref, k_ref, v_ref)):
        copies[i].wait()
        times(ref, low_ref, w_ref, i)
    acc_ref[...] = jnp.zeros_like(acc_ref)
    heads_forward(acc_ref, q_ref, k_ref, v_ref, parts, biases(1), heads)
    low_ref[...] = acc_ref[...].astype(BF)
    copies[3].wait()
    times(acc_ref, low_ref, w_ref, 3)

    def body(rows):
        acc_ref[rows, :] = x_ref[rows, :] + gate * acc_ref[rows, :]
        low_ref[rows, :] = (gate * cot_ref[rows, :]).astype(BF)

    over_rows(count, body, most)
    put()
    times(acc_ref, low_ref, w_ref, 3, transposed=True)
    low_ref[...] = acc_ref[...].astype(BF)
    for ref in (dq_ref, dk_ref, dv_ref):
        ref[...] = jnp.zeros_like(ref)
    heads_backward(dq_ref, dk_ref, dv_ref, q_ref, k_ref, v_ref, low_ref, parts, biases(0), heads)
    for i, ref in enumerate((dq_ref, dk_ref, dv_ref)):
        low_ref[...] = (ref[...] * SCALE if i < 2 else ref[...]).astype(BF)
        times(acc_ref, low_ref, w_ref, i, transposed=True, add=i > 0)

    def body(rows):
        acc_ref[rows, :] = norm_back(x_ref[rows, :], cot_ref[rows, :], acc_ref[rows, :], scale).astype(F32)

    over_rows(count, body, most)


def temporal_main_kernel(
    meta_ref, mod_ref, got_ref, c_ref, w_hbm, out_ref, sent_ref, w_ref, sems, *refs, heads, patches
):
    copies = bring(w_hbm, w_ref, sems)
    x_ref, cot_ref, acc_ref = refs[0], refs[1], refs[6]
    columns = c_ref.shape[0]
    main = x_ref.shape[0]
    block = main // columns
    frames, each = main // patches, block // patches
    column = meta_ref[COLUMN]
    devices = got_ref.shape[0]
    small = main // devices
    room = got_ref.shape[1] - small * (x_ref.shape[1] // 128)
    sharers = patches // small
    part = frames * small

    def token(source):
        return source % sharers * part + source // sharers * small

    for source in range(devices):
        read_chunk(got_ref, source, x_ref, token(source), small, room)
    for f in range(columns):
        values = c_ref[column ^ f].astype(F32)
        for j in range(each):
            valid = meta_ref[LONG_VALID + f * each + j] == 1
            for g in range(sharers):
                rows = pl.ds(token((f * each + j) * sharers + g), small)
                at = j * patches + g * small
                cot_ref[rows, :] = jnp.where(valid, values[at : at + small], 0.0)

    parts = [slice(g * part, (g + 1) * part) for g in range(sharers)]
    if part % 128:
        parts = [slice(0, main)]

    def biases(axis):
        bias = key_bias(meta_ref, LONG_VALID, None, main // len(parts), frames, small, axis)
        return jnp.concatenate([bias] * len(parts), axis=1 - axis)

    def put():
        for f in range(columns):
            starts = [token(f * each * sharers + i) for i in range(each * sharers)]
            pieces = [acc_ref[at : at + small, :] for at in starts]
            out_ref[column ^ f] = jnp.concatenate(pieces, axis=0).astype(BF)

    vecs = [main_vec(meta_ref, mod_ref, 1, i) for i in range(3)]
    temporal_core(vecs, w_ref, copies, parts, biases, put, 64, refs, heads)
    for dest in range(devices):
        write_chunk(sent_ref, dest, acc_ref[token(dest) : token(dest) + small, :])


def temporal_extra_kernel(
    meta_ref, mod_ref, got_ref, l_ref, c_ref, w_hbm, ws_hbm, out_ref, sent_ref, g_ref,
    ws_ref, ws_sem, w_ref, sems, *refs, heads, patches, groups, frame_dev,
):
    last_copy = pltpu.make_async_copy(ws_hbm.at[3], ws_ref, ws_sem)
    last_copy.start()
    copies = bring(w_hbm, w_ref, sems)
    x_ref, cot_ref, acc_ref = refs[0], refs[1], refs[6]
    rows = l_ref.shape[0]
    extras = rows // patches
    each = extras // groups
    devices = got_ref.shape[0]

    def vec(block, member):
        return extra_vec(meta_ref, mod_ref, block, member, extras, patches)

    acc_ref[...] = jnp.zeros_like(acc_ref)
    for source in range(devices):
        head, group = source // groups, source % groups
        pieces = got_ref[source, : patches * (room_for(each) // 128), :].astype(F32)
        pieces = [pieces[at : at + patches] for at in range(0, pieces.shape[0], patches)]
        packed = jnp.concatenate(pieces, axis=1) if len(pieces) > 1 else pieces[0]
        for e in range(each):
            at = (group * each + e) * patches
            cols, value = head_from(packed, head, e)
            acc_ref[at : at + patches, cols] = acc_ref[at : at + patches, cols] + value
    gate_s = vec(0, 2)
    last_copy.wait()
    mixed = nn(acc_ref[...].astype(BF), ws_ref[...])
    x_ref[...] = gated(l_ref[...], gate_s, mixed).astype(F32)
    values = own_extras(meta_ref, c_ref, frame_dev * patches, extras, patches, frame_dev)
    for i in range(extras):
        part = slice(i * patches, (i + 1) * patches)
        cot_ref[part, :] = jnp.where(meta_ref[VALID + i] == 1, values[i], 0.0)

    def put():
        out_ref[...] = acc_ref[: out_ref.shape[0]].astype(BF)

    def biases(axis):
        return key_bias(meta_ref, VALID, CLIP, rows, extras, patches, axis)

    vecs = [vec(1, i) for i in range(3)]
    temporal_core(vecs, w_ref, copies, [slice(0, rows)], biases, put, rows, refs, heads)
    grad = acc_ref[...]
    g_ref[...] = grad.astype(BF)
    acc_ref[...] = nt((gate_s * grad).astype(BF), ws_ref[...])
    for dest in range(devices):
        head, group = dest // groups, dest % groups
        starts = [(group * each + e) * patches for e in range(each)]
        packed = sum(head_into(acc_ref, slice(at, at + patches), head, e) for e, at in enumerate(starts))
        sent_ref[dest] = packed[:, : sent_ref.shape[2]].astype(BF)


def place_kernel(meta_ref, main_ref, extra_ref, out_ref, *, sharers):
    frame_dev, patch_dev, width = main_ref.shape[-3], out_ref.shape[1], out_ref.shape[2]
    for slot in range(out_ref.shape[0]):
        kind = meta_ref[KIND + slot]

        @pl.when(kind == 0)
        def _(slot=slot):
            out_ref[slot] = jnp.zeros_like(out_ref[slot])

        @pl.when(kind == 1)
        def _(slot=slot):
            if not sharers:
                out_ref[slot] = main_ref[slot % frame_dev]
                return
            columns, patch_t = main_ref.shape[0], main_ref.shape[2]
            small = patch_t // sharers
            parts = [main_ref[meta_ref[COLUMN] ^ f, slot % frame_dev].astype(F32) for f in range(columns)]
            pieces = [p[s * small : (s + 1) * small] for s in range(sharers) for p in parts]
            out_ref[slot] = jnp.concatenate(pieces, axis=0).astype(BF)

        @pl.when(kind == 2)
        def _(slot=slot):
            e = meta_ref[EXTRA_AT + slot]
            parts = [extra_ref[meta_ref[COLUMN] ^ f, e].astype(F32) for f in range(extra_ref.shape[0])]
            out_ref[slot] = jnp.concatenate(parts, axis=0).astype(BF)


SCALARS = pl.BlockSpec(memory_space=pltpu.SMEM)
ANYWHERE = pl.BlockSpec(memory_space=pl.ANY)


def params(steps=0):
    semantics = {"dimension_semantics": ("arbitrary",) * steps} if steps else {}
    return pltpu.CompilerParams(vmem_limit_bytes=VMEM_LIMIT, **semantics)


def cost(flops, elements=0):
    return pl.CostEstimate(flops=int(flops) // 1000, bytes_accessed=int(elements) // 1000, transcendentals=0)


def whole(array):
    return pl.BlockSpec(array.shape, lambda *_: (0,) * len(array.shape))


def shape(*dims, dtype=BF):
    return jax.ShapeDtypeStruct(dims, dtype)


def weight_call(kernel, name, operands, weights, members, outs, scratch, weigh):
    width = weights.shape[-1]
    first, count = members
    return pl.pallas_call(
        kernel,
        name=name,
        grid=(count,),
        in_specs=[SCALARS]
        + [whole(a) for a in operands[1:]]
        + [pl.BlockSpec((1, width, width), lambda i: (first + i, 0, 0))],
        out_specs=[spec for spec, _ in outs],
        out_shape=[struct for _, struct in outs],
        scratch_shapes=scratch,
        compiler_params=params(1),
        cost_estimate=cost(weigh * count, 2 * width * width * count),
    )(*operands, weights)


def full(*dims):
    return whole(shape(*dims)), shape(*dims)


def gather(lengths, frame_mask, column, latents, cotangent, columns, sharers):
    _, frame_dev, patch_dev, width = latents.shape
    main = (frame_dev, patch_dev, width)
    patch_t = patch_dev // columns
    return pl.pallas_call(
        functools.partial(gather_kernel, sharers=sharers),
        name="gather",
        in_specs=[SCALARS] * 3 + [ANYWHERE] * 2,
        out_specs=[SCALARS] + [pl.BlockSpec(memory_space=pltpu.VMEM)] * 3,
        out_shape=[
            shape(TABLE, dtype=jnp.int32), shape(*main), shape(columns, EXTRAS * patch_t, width),
            shape(columns, (frame_dev + EXTRAS) * patch_t, width),
        ],
        scratch_shapes=[
            pltpu.VMEM(main, BF),
            pltpu.VMEM((2, EXTRAS, patch_dev, width), BF),
            pltpu.SemaphoreType.DMA((2, EXTRAS + 1)),
        ],
        compiler_params=params(),
    )(lengths, frame_mask, column, latents, cotangent)


def front_main(meta, mod, x, weights):
    rows, width = x.shape
    kv = pl.BlockSpec((1, rows, width), lambda i: (jnp.maximum(i - 1, 0), 0, 0)), shape(2, rows, width)
    return weight_call(
        front_main_kernel, "front_main", (meta, mod, x), weights, (0, 3),
        [full(rows, width), kv], [pltpu.VMEM((rows, width), BF)], 2 * rows * width**2,
    )


def front_extra(meta, mod, got, weights, heads, patches, extras, frame_dev):
    width = got.shape[-1]
    rows = extras * patches
    return weight_call(
        functools.partial(front_extra_kernel, patches=patches, frame_dev=frame_dev), "front_extra",
        (meta, mod, got), weights, (0, 3), [full(heads, rows, 256), full(rows, width)],
        [pltpu.VMEM((rows, width), BF), pltpu.VMEM((3, rows, width), F32)], 4 * rows * width**2,
    )


def back_main(meta, mod, x, o, weights, columns, devices):
    rows, width = x.shape
    return weight_call(
        functools.partial(back_main_kernel, columns=columns), "back_main", (meta, mod, x, o), weights,
        (3, 1), [full(devices, rows * width // (devices * 128), 128)], [pltpu.VMEM((rows, width), F32)],
        3 * rows * width**2,
    )[0]


def back_grad_main(meta, mod, got, weights, rows, columns):
    width = weights.shape[-1]
    return weight_call(
        functools.partial(back_grad_main_kernel, columns=columns), "back_grad_main",
        (meta, mod, got), weights, (3, 1), [full(rows, width)] * 2,
        [pltpu.VMEM((rows, width), BF), pltpu.VMEM((rows, width), F32)], 3 * rows * width**2,
    )


def front_grad_main(meta, mod, own, got, x, g, weights):
    rows, width = x.shape
    return weight_call(
        front_grad_main_kernel, "front_grad_main", (meta, mod, own, got, x, g), weights, (0, 3),
        [full(rows, width)], [pltpu.VMEM((3, rows, width), BF), pltpu.VMEM((rows, width), F32)],
        3 * rows * width**2,
    )[0]


def front_grad_extra(meta, mod, pack, x, g, weights, patches):
    rows, width = x.shape
    return weight_call(
        functools.partial(front_grad_extra_kernel, patches=patches), "front_grad_extra",
        (meta, mod, pack, x, g), weights, (0, 3), [full(EXTRAS * patches, width)],
        [pltpu.VMEM((3, rows, width), BF), pltpu.VMEM((rows, width), F32), pltpu.VMEM((3, rows, width), F32)],
        4 * rows * width**2,
    )[0]


def attend(q, kv, other, heads):
    rows, width = q.shape
    keys = rows * (other.shape[0] + 1)
    return pl.pallas_call(
        functools.partial(attend_kernel, heads=heads),
        name="attend",
        out_shape=shape(rows, width),
        scratch_shapes=[
            pltpu.VMEM((keys, width), BF),
            pltpu.VMEM((keys, width), BF),
            pltpu.VMEM((rows, width), F32),
        ],
        compiler_params=params(),
        cost_estimate=cost(6e9),
    )(q, kv, other)


def extra_attend(packed, main):
    devices, count, patches, _ = packed.shape
    return pl.pallas_call(
        extra_attend_kernel, name="extra_attend",
        out_shape=shape(devices, extra_room(patches, count) + main.shape[1], 128),
        compiler_params=params(), cost_estimate=cost(4e9),
    )(packed, main)


def extra_attend_back(packed, got):
    return pl.pallas_call(
        extra_attend_back_kernel, name="extra_attend_back", out_shape=shape(*packed.shape),
        compiler_params=params(), cost_estimate=cost(6e9),
    )(packed, got)


def attend_back(q, kv, other, do, heads):
    rows, width = q.shape
    keys = rows * (other.shape[0] + 1)
    return pl.pallas_call(
        functools.partial(attend_back_kernel, heads=heads),
        name="attend_back",
        out_shape=[shape(3, rows, width), shape(*other.shape)],
        scratch_shapes=[
            pltpu.VMEM((keys, width), BF),
            pltpu.VMEM((keys, width), BF),
            pltpu.VMEM((rows, width), F32),
            pltpu.VMEM((keys, width), F32),
            pltpu.VMEM((keys, width), F32),
        ],
        compiler_params=params(),
        cost_estimate=cost(14e9),
    )(q, kv, other, do)


def temporal_scratch(rows, width):
    high, low = pltpu.VMEM((rows, width), F32), pltpu.VMEM((rows, width), BF)
    weights = [pltpu.VMEM((4, width, width), BF), pltpu.SemaphoreType.DMA((4,))]
    return weights + [high] * 2 + [low] * 4 + [high] * 4


def temporal_main(meta, mod, got, cot, weights, heads, patches, block):
    columns, _, width = cot.shape
    devices = got.shape[0]
    operands = (mod, got, cot)
    sent = shape(devices, columns * block * width // (devices * 128), 128)
    return pl.pallas_call(
        functools.partial(temporal_main_kernel, heads=heads, patches=patches),
        name="temporal_main",
        in_specs=[SCALARS] + [whole(a) for a in operands] + [ANYWHERE],
        out_shape=[shape(columns, block, width), sent],
        scratch_shapes=temporal_scratch(columns * block, width),
        compiler_params=params(),
        cost_estimate=cost(25e9),
    )(meta, *operands, weights)


def temporal_extra(meta, mod, got, le, cot, weights, spatial_weights, heads, patches, groups, frame_dev):
    operands = (mod, got, le, cot)
    rows, width = le.shape
    sent = shape(got.shape[0], patches, room_for(rows // (patches * groups)))
    return pl.pallas_call(
        functools.partial(
            temporal_extra_kernel, heads=heads, patches=patches, groups=groups, frame_dev=frame_dev
        ),
        name="temporal_extra",
        in_specs=[SCALARS] + [whole(a) for a in operands] + [ANYWHERE] * 2,
        out_shape=[shape(EXTRAS * patches, width), sent, shape(*le.shape)],
        scratch_shapes=[pltpu.VMEM((width, width), BF), pltpu.SemaphoreType.DMA]
        + temporal_scratch(rows, width),
        compiler_params=params(),
        cost_estimate=cost(14e9),
    )(meta, *operands, weights, spatial_weights)


def place(meta, main, extra, slots, sharers):
    return pl.pallas_call(
        functools.partial(place_kernel, sharers=sharers),
        name="place",
        in_specs=[SCALARS, whole(main), whole(extra)],
        out_shape=shape(slots, extra.shape[0] * extra.shape[2], extra.shape[3]),
        compiler_params=params(),
        cost_estimate=cost(3e9),
    )(meta, main, extra)


def local(latents, cotangent, spatial_weights, temporal_weights, modulation, lengths, frame_mask):
    clips, frame_dev, patch_dev, width = latents.shape
    heads = width // HEAD
    frame_axis, patch_axis = lax.axis_size("frame"), lax.axis_size("patch")
    everyone = ("frame", "patch")
    frames = frame_dev * frame_axis
    sharers = patch_axis // frame_dev
    sub = patch_dev // sharers
    small = sub // frame_axis
    patch_t = patch_dev // frame_axis
    heads_col = heads // frame_axis
    groups = patch_axis // heads_col
    group_extras = -(-EXTRAS // groups)
    extras = groups * group_extras

    def swap(x, axis):
        return lax.all_to_all(x, axis, split_axis=0, concat_axis=0, tiled=True)

    column = lax.axis_index("frame")
    main_rows = frame_dev * patch_dev

    def cross(blocks):
        got = [blocks[0]]
        for m in range(1, frame_axis):
            got.append(lax.ppermute(blocks[m], "frame", [(f, f ^ m) for f in range(frame_axis)]))
        return jnp.stack(got)

    def parts_home(x):
        return cross([x] * frame_axis).reshape(frame_axis, EXTRAS, patch_t, width)

    meta, main_home, extra_home, cot_home = gather(
        lengths, frame_mask, column.reshape(1).astype(jnp.int32), latents, cotangent, frame_axis, sharers
    )
    extra_got = cross(extra_home)
    main_s = swap(main_home.reshape(patch_axis, sub, width), "patch").reshape(main_rows, width)
    extra_got, cot_home = lax.optimization_barrier((extra_got, cot_home))
    cot = cross(cot_home)

    def rotate(array, by):
        perm = []
        for p in range(patch_axis):
            base = p // sharers * sharers
            perm.append((p, base + (p - base + by) % sharers))
        return lax.ppermute(array, "patch", perm)

    mod = modulation
    chunk = group_extras * patch_t
    packed, extra_t = front_extra(
        meta, mod, extra_got, spatial_weights, heads, patch_t, extras, frame_dev
    )
    packed, main_s = lax.optimization_barrier((packed, main_s))
    pack_got = swap(packed.reshape(frame_axis * patch_axis, chunk, 256), everyone)
    pack_got = pack_got.reshape(frame_axis * patch_axis, group_extras, patch_t, 256)
    q, kv = front_main(meta, mod, main_s, spatial_weights)
    other = jnp.stack([rotate(kv, by) for by in range(1, sharers)])
    attended = attend(q, kv, other, heads)
    sent = back_main(meta, mod, main_s, attended, spatial_weights, frame_axis, frame_axis * patch_axis)
    sent, pack_got = lax.optimization_barrier((sent, pack_got))
    sent = extra_attend(pack_got, sent)

    got, cot = lax.optimization_barrier((swap(sent, everyone), cot))
    out_m, sent = temporal_main(
        meta, mod, got, cot, temporal_weights, heads, patch_t, frame_dev * patch_t
    )
    got, _ = lax.optimization_barrier((got, out_m))
    out_e, sent_e, grad_e = temporal_extra(
        meta, mod, got, extra_t, cot, temporal_weights, spatial_weights, heads, patch_t, groups, frame_dev
    )

    grads, sent_e = lax.optimization_barrier((swap(sent, everyone), sent_e))
    do_main, grad_s = back_grad_main(meta, mod, grads, spatial_weights, main_rows, frame_axis)
    dpack = extra_attend_back(pack_got, swap(sent_e, everyone))
    out_main, out_extra = cross(out_m), parts_home(out_e)
    do_main, dpack, out_main, out_extra = lax.optimization_barrier((do_main, dpack, out_main, out_extra))
    own, sent = attend_back(q, kv, other, do_main, heads)
    got = jnp.stack([rotate(sent[by - 1], -by) for by in range(1, sharers)])
    dpack = swap(dpack.reshape(frame_axis * patch_axis, chunk, 256), everyone)
    dpack = dpack.reshape(heads, extras * patch_t, 256)
    lat_m = front_grad_main(meta, mod, own, got, main_s, grad_s, spatial_weights)
    dpack, _ = lax.optimization_barrier((dpack, own))
    lat_e = front_grad_extra(meta, mod, dpack, extra_t, grad_e, spatial_weights, patch_t)
    lat_main = swap(lat_m.reshape(patch_axis, sub, width), "patch").reshape(frame_dev, patch_dev, width)

    out_main = out_main.reshape(frame_axis, frame_dev, patch_t, width)
    slots = clips * frame_dev
    output = place(meta, out_main, out_extra, slots, sharers)
    grad = place(meta, lat_main, parts_home(lat_e), slots, 0)
    return output.reshape(latents.shape), grad.reshape(latents.shape)


def solution(mesh):
    tokens = P(None, "frame", "patch", None)
    in_specs = (tokens, tokens, P(), P(), P(), P(), P())
    return jax.shard_map(local, mesh=mesh, in_specs=in_specs, out_specs=(tokens, tokens), check_vma=False)
```
